128 devices in a mesh: outer: 8 (over x, core), inner: 16 (over z, y).
Axes of the slice: x: 4, y: 4, z: 4, core: 2. Of those that a mesh axis runs over, the one named last changes fastest.
Arguments:
- query_in: bfloat16 [16384, 2048], P(('outer', 'inner')), may hold values from -5 to 5
- key_in: bfloat16 [16384, 2048], P(('outer', 'inner')), may hold values from -5 to 5
- value_in: bfloat16 [16384, 2048], P(('outer', 'inner')), may hold values from -384 to 384
- w_out: bfloat16 [2048, 2048], replicated, may hold values from -0.125 to 0.125
- cotangent: bfloat16 [16384, 2048], P(('outer', 'inner')), may hold values from -96 to 96
Outputs:
- output: bfloat16 [16384, 2048], P(('outer', 'inner'))
- query_grad: bfloat16 [16384, 2048], P(('outer', 'inner'))
- key_grad: bfloat16 [16384, 2048], P(('outer', 'inner'))
- value_grad: bfloat16 [16384, 2048], P(('outer', 'inner'))
- w_out_grad: float32 [2048, 2048], P(('outer', 'inner'))
The draws below stay inside these ranges and needn't reach their ends.
All inputs are finite; a program needn't handle non-finite values.
Results may differ from the reference program's by a relative error of at most 0.035.
Values may be sent and summed in bfloat16 or wider, within the bound.
No kernel may reach another device: no remote copies, remote signals or barrier semaphores. Data moves between devices by JAX's collectives and lax.ppermute only.
A program may use at most 128 MiB of HBM per device.

```python
import math
from functools import reduce
import jax
import jax.numpy as jnp
from jax import lax

HEADS = 16
D = 2048
BLOCK = 128
LEVELS = 3
TOKENS = 16384


def draw_query_in(key, part):
    key = jax.random.fold_in(key, 11)
    second_key = jax.random.fold_in(key, 1)
    return jnp.clip(jax.random.normal(second_key, (TOKENS, D)), -5.0, 5.0).astype(jnp.bfloat16)


def draw_key_in(key, part):
    key = jax.random.fold_in(key, 12)
    second_key = jax.random.fold_in(key, 1)
    return jnp.clip(jax.random.normal(second_key, (TOKENS, D)), -5.0, 5.0).astype(jnp.bfloat16)


def with_spikes(values, key, source, target, shards_of, factor):
    owner, partner = [(jnp.arange(values.shape[position]) // (values.shape[position] // shards_of)).reshape([-1 if axis == position else 1 for axis in range(values.ndim)]) for position in (source, target)]
    chosen = jax.random.permutation(key, shards_of)[partner]
    strong = (owner == chosen) | (owner == (partner + shards_of // 2) % shards_of)
    return jnp.where(strong, factor * values, values)


def levels(key, dims, shards, smallest, largest):
    def one(axis_at, shards_of):
        heights = jax.random.uniform(jax.random.fold_in(jax.random.fold_in(key, 6), axis_at), (shards_of,), jnp.float32, smallest / len(shards), largest / len(shards))
        return jnp.repeat(jnp.exp(heights), dims[axis_at] // shards_of).reshape((-1,) + (1,) * (len(dims) - axis_at - 1))

    level = one(*shards[0])
    for cut in shards[1:]:
        level = level * one(*cut)
    return level


def noise(key, dims, scale, bound, shards=(), held_as=jnp.bfloat16):
    values = scale * jax.random.normal(key, dims, jnp.float32)
    if shards:
        values = values * levels(key, dims, shards, -0.22, 0.18)
    return jnp.clip(values, -bound, bound).astype(held_as)


def heavy_noise(stream_key, dims, deviation, bound, cuts, heavy, dtype=jnp.bfloat16):
    values = deviation * jax.random.normal(stream_key, dims, jnp.float32)
    if cuts:
        values = values * levels(stream_key, dims, cuts, -0.22, 0.18)
    return jnp.clip(with_spikes(values, jax.random.fold_in(stream_key, 3), *heavy), -bound, bound).astype(dtype)


def setup_inputs(seed: int = 0) -> dict:
    key_list = jax.random.split(jax.random.key(seed), 6)
    return {
        "query_in": draw_query_in(jax.random.fold_in(key_list[5], 71), 0),
        "key_in": draw_key_in(jax.random.fold_in(key_list[5], 71), 0),
        "value_in": heavy_noise(key_list[2], (TOKENS, D), 16.0, 384.0, ((0, 128),), (0, 1, 128, 5.5)),
        "w_out": noise(key_list[3], (D, D), D ** -0.5, 0.125),
        "cotangent": noise(key_list[4], (TOKENS, D), 16.0, 96.0, ((0, 128),)),
    }


def rounded(matrix):
    return lax.optimization_barrier(matrix.astype(jnp.bfloat16))

def by_head(matrix):
    return matrix.reshape(matrix.shape[:-1] + (HEADS, matrix.shape[-1] // HEADS))

def halved_rows(matrix):
    paired = matrix.reshape(matrix.shape[0] // 2, 2, matrix.shape[1])
    summed = paired[:, 0].astype(jnp.float32) + paired[:, 1].astype(jnp.float32)
    return rounded(summed * 0.5)

def sibling_local(matrix, count, block_rows):
    blocks = matrix.reshape(count // 2, 2, block_rows, matrix.shape[-1])
    return jnp.flip(blocks, axis=1).reshape(count, block_rows, matrix.shape[-1])

def level_forward(query_blocks, key_blocks, value_blocks, factor):
    count, query_rows, columns = query_blocks.shape
    scale = 1.0 / math.sqrt(columns // HEADS)
    scores = jnp.einsum('bqhd,bkhd->bhqk', by_head(query_blocks).astype(jnp.float32), by_head(key_blocks).astype(jnp.float32)) * scale
    maxima = lax.optimization_barrier(jnp.max(scores, axis=-1))
    expscore = jnp.exp(scores - maxima[..., None])
    weights_bf = rounded(expscore).astype(jnp.float32)
    weighted = jnp.einsum('bhqk,bkhd->bqhd', weights_bf, by_head(value_blocks).astype(jnp.float32))
    totals = lax.optimization_barrier(jnp.sum(expscore, axis=-1))
    row_count = count * query_rows
    return (weighted.reshape(row_count, columns) * factor, jnp.transpose(totals, (0, 2, 1)).reshape(row_count, HEADS) * factor, jnp.transpose(maxima, (0, 2, 1)).reshape(row_count, HEADS))

def merge_levels(level_stats):
    maxima_fine = [jnp.repeat(stats[2], 2 ** height, axis=0) for height, stats in enumerate(level_stats)]
    peak = reduce(jnp.maximum, maxima_fine)
    totals = jnp.zeros(peak.shape, jnp.float32)
    summed = jnp.zeros(peak.shape + (level_stats[0][0].shape[1] // HEADS,), jnp.float32)
    for height, stats in enumerate(level_stats):
        factor = 2 ** height
        lift = jnp.exp(maxima_fine[height] - peak)
        totals = totals + lift * jnp.repeat(stats[1], factor, axis=0)
        summed = summed + lift[..., None] * by_head(jnp.repeat(stats[0], factor, axis=0))
    attended = rounded((summed / totals[..., None]).reshape(peak.shape[0], -1))
    return (attended, peak + jnp.log(totals))

def coarse_terms(att_grad, delta, log_total, maxima, factor):
    cover = jnp.exp(jnp.repeat(maxima, factor, axis=0) - log_total)
    token_count, columns = att_grad.shape
    row_count = token_count // factor
    scaled = by_head(att_grad).astype(jnp.float32) * cover[..., None]
    coarse_grad = lax.optimization_barrier(jnp.sum(scaled.reshape(row_count, factor, HEADS, columns // HEADS), axis=1)).reshape(row_count, columns)
    residual = lax.optimization_barrier(jnp.sum((cover * delta).reshape(row_count, factor, HEADS), axis=1))
    return (rounded(coarse_grad), residual)

def level_backward(query_blocks, key_blocks, value_blocks, grad_blocks, residual_blocks, maxima_blocks, factor):
    count, query_rows, columns = query_blocks.shape
    scale = 1.0 / math.sqrt(columns // HEADS)
    query_heads = by_head(query_blocks).astype(jnp.float32)
    key_heads = by_head(key_blocks).astype(jnp.float32)
    grad_heads = by_head(grad_blocks).astype(jnp.float32)
    scores = jnp.einsum('bqhd,bkhd->bhqk', query_heads, key_heads) * scale
    expscore = jnp.exp(scores - jnp.transpose(maxima_blocks, (0, 2, 1))[..., None])
    weights_bf = rounded(expscore).astype(jnp.float32)
    value_part = jnp.einsum('bhqk,bqhd->bkhd', weights_bf, grad_heads) * factor
    inner = jnp.einsum('bqhd,bkhd->bhqk', grad_heads, by_head(value_blocks).astype(jnp.float32))
    score_grad = rounded(expscore * (inner - jnp.transpose(residual_blocks, (0, 2, 1))[..., None]) * (factor * scale)).astype(jnp.float32)
    query_part = jnp.einsum('bhqk,bkhd->bqhd', score_grad, key_heads)
    key_part = jnp.einsum('bhqk,bqhd->bkhd', score_grad, query_heads)
    key_count = key_blocks.shape[1]
    return (query_part.reshape(count * query_rows, columns), key_part.reshape(count, key_count, columns), value_part.reshape(count, key_count, columns))

def group_pass(group_query, group_key, group_value, group_att_grad):
    token_count, columns = group_query.shape
    block_rows = BLOCK
    level_query, level_key, level_value = ([group_query], [group_key], [group_value])
    for height in range(1, LEVELS + 1):
        level_query.append(halved_rows(level_query[-1]))
        level_key.append(halved_rows(level_key[-1]))
        level_value.append(halved_rows(level_value[-1]))
    plans = []
    level_stats = []
    for height in range(LEVELS + 1):
        row_count = token_count >> height
        count = row_count // block_rows
        query_blocks = level_query[height].reshape(count, block_rows, columns)
        far_keys = sibling_local(level_key[height], count, block_rows)
        far_values = sibling_local(level_value[height], count, block_rows)
        if height == 0:
            key_blocks = jnp.concatenate([level_key[height].reshape(count, block_rows, columns), far_keys], axis=1)
            value_blocks = jnp.concatenate([level_value[height].reshape(count, block_rows, columns), far_values], axis=1)
        else:
            key_blocks, value_blocks = (far_keys, far_values)
        plans.append((query_blocks, key_blocks, value_blocks))
        level_stats.append(level_forward(query_blocks, key_blocks, value_blocks, 2.0 ** height))
    attended, log_total = merge_levels(level_stats)
    delta = lax.optimization_barrier(jnp.sum(by_head(group_att_grad).astype(jnp.float32) * by_head(attended).astype(jnp.float32), axis=-1))
    query_total = jnp.zeros((token_count, columns), jnp.float32)
    key_total = jnp.zeros((token_count, columns), jnp.float32)
    value_total = jnp.zeros((token_count, columns), jnp.float32)
    for height in range(LEVELS + 1):
        factor = 2 ** height
        row_count = token_count >> height
        count = row_count // block_rows
        query_blocks, key_blocks, value_blocks = plans[height]
        maxima = level_stats[height][2]
        coarse_grad, residual = coarse_terms(group_att_grad, delta, log_total, maxima, factor)
        query_part, key_part, value_part = level_backward(query_blocks, key_blocks, value_blocks, coarse_grad.reshape(count, block_rows, columns), residual.reshape(count, block_rows, HEADS), maxima.reshape(count, block_rows, HEADS), float(factor))
        if height == 0:
            own_key, far_key = (key_part[:, :block_rows], key_part[:, block_rows:])
            own_value, far_value = (value_part[:, :block_rows], value_part[:, block_rows:])
        else:
            own_key, far_key = (0.0, key_part)
            own_value, far_value = (0.0, value_part)
        key_level = (own_key + sibling_local(far_key.reshape(row_count, columns), count, block_rows)).reshape(row_count, columns)
        value_level = (own_value + sibling_local(far_value.reshape(row_count, columns), count, block_rows)).reshape(row_count, columns)
        query_total = query_total + jnp.repeat(query_part, factor, axis=0) / factor
        key_total = key_total + jnp.repeat(key_level, factor, axis=0) / factor
        value_total = value_total + jnp.repeat(value_level, factor, axis=0) / factor
    return (attended, query_total.astype(jnp.bfloat16), key_total.astype(jnp.bfloat16), value_total.astype(jnp.bfloat16))

def reference(query_in, key_in, value_in, w_out, cotangent):
    token_count, columns = query_in.shape
    group_tokens = BLOCK * 2 ** (LEVELS + 1)
    weight_full = w_out.astype(jnp.float32)
    cot_full = cotangent.astype(jnp.float32)
    att_grad = rounded(jnp.dot(cot_full, weight_full.T, preferred_element_type=jnp.float32))

    def one_group(inputs):
        return group_pass(inputs[0], inputs[1], inputs[2], inputs[3])

    def grouped(matrix):
        return matrix.reshape(token_count // group_tokens, group_tokens, columns)
    attended, query_grad, key_grad, value_grad = lax.map(one_group, (grouped(query_in), grouped(key_in), grouped(value_in), grouped(att_grad)))
    attended = attended.reshape(token_count, columns).astype(jnp.float32)
    output = jnp.dot(attended, weight_full, preferred_element_type=jnp.float32).astype(jnp.bfloat16)
    w_out_grad = jnp.dot(attended.T, cot_full, preferred_element_type=jnp.float32) / math.sqrt(token_count)
    return (output, query_grad.reshape(token_count, columns), key_grad.reshape(token_count, columns), value_grad.reshape(token_count, columns), w_out_grad)
```

```python
import functools
import math

import jax
import jax.numpy as jnp
from jax import lax
from jax.experimental import pallas as pl
from jax.experimental.pallas import tpu as pltpu
from jax.sharding import PartitionSpec as P

HEADS = 16
BLOCK = 128
LEVELS = 3
WIDTH = 128
BF16 = jnp.bfloat16
F32 = jnp.float32
VMEM_LIMIT = 56 * 1024 * 1024
CHUNK = 256


def nt(a, b):
    return lax.dot_general(a, b, (((1,), (1,)), ((), ())), preferred_element_type=F32)


def nn(a, b):
    return lax.dot_general(a, b, (((1,), (0,)), ((), ())), preferred_element_type=F32)


def tn(a, b):
    return lax.dot_general(a, b, (((0,), (0,)), ((), ())), preferred_element_type=F32)


def wide(stat, columns=WIDTH):
    return jnp.broadcast_to(stat, (stat.shape[0], columns))


def evens(ref, base, rows):
    return ref[pl.ds(base, rows, stride=2), :]


def odds(ref, base, rows):
    return ref[pl.ds(base + 1, rows, stride=2), :]


def put_twice(ref, base, value):
    rows = value.shape[0]
    ref[pl.ds(base, rows, stride=2), :] = value
    ref[pl.ds(base + 1, rows, stride=2), :] = value


def level_rows(tokens):
    out, base = [], 0
    for height in range(LEVELS + 1):
        out.append((base, tokens >> height))
        base += tokens >> height
    return out, base


def vmem_call(body, out_shape, n_in, scratch=(), cost=None, name=None):
    spec = pl.BlockSpec(memory_space=pltpu.VMEM)
    return pl.pallas_call(
        body,
        out_shape=out_shape,
        in_specs=[spec] * n_in,
        out_specs=jax.tree.map(lambda _: spec, out_shape),
        scratch_shapes=list(scratch),
        compiler_params=pltpu.CompilerParams(vmem_limit_bytes=VMEM_LIMIT),
        cost_estimate=cost,
        name=name,
    )


def cost(flops, nbytes):
    return pl.CostEstimate(flops=int(flops), bytes_accessed=int(nbytes), transcendentals=0)


def pack_body(q_ref, k_ref, v_ref, out_ref):
    for h in range(HEADS):
        for x, ref in enumerate((q_ref, k_ref, v_ref)):
            out_ref[h, x * BLOCK : (x + 1) * BLOCK, :] = ref[:, h * WIDTH : (h + 1) * WIDTH]


def pack(q, k, v):
    return vmem_call(
        pack_body,
        jax.ShapeDtypeStruct((HEADS, 3 * BLOCK, WIDTH), BF16),
        3,
        cost=cost(0, 6 * q.size * 2),
        name="pack_qkv",
    )(q, k, v)


def forward_body(blocks, in_ref, grad_ref, out_ref, lse_ref, top_ref, lev_ref, fq, mu, du, nu):
    tokens = blocks * BLOCK
    spans, _ = level_rows(tokens)
    scale = 1.0 / math.sqrt(WIDTH)
    for b in range(blocks):
        out_ref[b, 0:BLOCK, :] = grad_ref[:, b * WIDTH : (b + 1) * WIDTH]
        for x in range(3):
            part = in_ref[b, x * BLOCK : (x + 1) * BLOCK, :]
            lev_ref[x, b * BLOCK : (b + 1) * BLOCK, :] = part
            fq[x, b * BLOCK : (b + 1) * BLOCK, :] = part.astype(F32)
    for height in range(1, LEVELS + 1):
        below, _ = spans[height - 1]
        base, rows = spans[height]
        step = min(CHUNK, rows)
        for x in range(3):
            for r in range(0, rows, step):
                mean = (
                    evens(fq.at[x], below + 2 * r, step) + odds(fq.at[x], below + 2 * r, step)
                ) * 0.5
                mean = mean.astype(BF16)
                lev_ref[x, base + r : base + r + step, :] = mean
                fq[x, base + r : base + r + step, :] = mean.astype(F32)

    def attend(q, k, v, factor):
        scores = nt(q, k) * scale
        top = wide(jnp.max(scores, axis=1, keepdims=True))
        shift = jnp.concatenate([top] * (k.shape[0] // WIDTH), axis=1)
        expo = jnp.exp(scores - shift)
        denom = wide(jnp.sum(expo, axis=1, keepdims=True))
        numer = nn(expo.astype(BF16), v)
        if factor != 1:
            denom, numer = denom * factor, numer * factor
        return top, denom, numer

    def merge(height, row, stats):
        top, denom, numer = stats
        base, _ = spans[height]
        rows = top.shape[0]
        at = slice(base + row, base + row + rows)
        top_ref[at, :] = top
        if height < LEVELS:
            up = mu[at, :]
            peak = jnp.maximum(top, up)
            mine, theirs = jnp.exp(top - peak), jnp.exp(up - peak)
            denom = mine * denom + theirs * du[at, :]
            numer = mine * numer + theirs * nu[at, :]
            top = peak
        return top, denom, numer

    for height in range(LEVELS, 0, -1):
        base, rows = spans[height]
        fine, _ = spans[height - 1]
        for row in range(0, rows, BLOCK):
            far = base + (row ^ BLOCK)
            stats = attend(
                lev_ref[0, base + row : base + row + BLOCK, :],
                lev_ref[1, far : far + BLOCK, :],
                lev_ref[2, far : far + BLOCK, :],
                float(2**height),
            )
            merged = merge(height, row, stats)
            for ref, value in zip((mu, du, nu), merged):
                put_twice(ref, fine + 2 * row, value)
    for row in range(0, tokens, 2 * BLOCK):
        at = slice(row, row + 2 * BLOCK)
        stats = attend(lev_ref[0, at, :], lev_ref[1, at, :], lev_ref[2, at, :], 1)
        peak, total, summed = merge(0, row, stats)
        attended = (summed / total).astype(BF16)
        lse_ref[at, :] = peak + jnp.log(total)
        out_ref[row // BLOCK, BLOCK:, :] = attended[:BLOCK]
        out_ref[row // BLOCK + 1, BLOCK:, :] = attended[BLOCK:]


def forward(qkv, att_grad):
    blocks = qkv.shape[0]
    tokens = blocks * BLOCK
    spans, total_rows = level_rows(tokens)
    finer = total_rows - spans[LEVELS][1]
    out_shape = (
        jax.ShapeDtypeStruct((blocks, 2 * BLOCK, WIDTH), BF16),
        jax.ShapeDtypeStruct((tokens, WIDTH), F32),
        jax.ShapeDtypeStruct((total_rows, WIDTH), F32),
        jax.ShapeDtypeStruct((3, total_rows, WIDTH), BF16),
    )
    return vmem_call(
        functools.partial(forward_body, blocks),
        out_shape,
        2,
        scratch=[
            pltpu.VMEM((3, total_rows, WIDTH), F32),
            pltpu.VMEM((finer, WIDTH), F32),
            pltpu.VMEM((finer, WIDTH), F32),
            pltpu.VMEM((finer, WIDTH), F32),
        ],
        cost=cost(4 * tokens * 384 * WIDTH, 8 << 20),
        name="head_forward",
    )(qkv, att_grad)


def backward_body(
    blocks, got_ref, sent_ref, lse_ref, top_ref, lev_ref, out_ref, ys, ds, rs, cg, res, up
):
    tokens = blocks * BLOCK
    spans, _ = level_rows(tokens)
    scale = 1.0 / math.sqrt(WIDTH)
    for b in range(blocks):
        at = slice(b * BLOCK, (b + 1) * BLOCK)
        grad = got_ref[b, :BLOCK, :].astype(F32)
        delta = wide(
            jnp.sum(grad * sent_ref[b, BLOCK:, :].astype(F32), axis=1, keepdims=True)
        )
        lse = lse_ref[at, :]
        ys[at, :], ds[at, :], rs[at, :] = grad, delta, lse
        cover = jnp.exp(top_ref[at, :] - lse)
        cg[at, :] = (cover * grad).astype(BF16)
        res[at, :] = cover * delta
    for height in range(1, LEVELS + 1):
        below, _ = spans[height - 1]
        base, rows = spans[height]
        for r in range(0, rows, BLOCK):
            at = slice(base + r, base + r + BLOCK)
            first = below + 2 * r
            lo, hi = evens(rs, first, BLOCK), odds(rs, first, BLOCK)
            low = jnp.minimum(lo, hi)
            lo, hi = jnp.exp(low - lo), jnp.exp(low - hi)
            grad = lo * evens(ys, first, BLOCK) + hi * odds(ys, first, BLOCK)
            delta = lo * evens(ds, first, BLOCK) + hi * odds(ds, first, BLOCK)
            if height < LEVELS:
                ys[at, :], ds[at, :], rs[at, :] = grad, delta, low
            cover = jnp.exp(top_ref[at, :] - low)
            cg[at, :] = (cover * grad).astype(BF16)
            res[at, :] = cover * delta

    def gradients(rows, keys):
        q, grad = lev_ref[0, rows, :], cg[rows, :]
        k, v = lev_ref[1, keys, :], lev_ref[2, keys, :]
        times = k.shape[0] // WIDTH
        top = jnp.concatenate([top_ref[rows, :]] * times, axis=1)
        resid = jnp.concatenate([res[rows, :]] * times, axis=1)
        expo = jnp.exp(nt(q, k) * scale - top)
        sgrad = (expo * (nt(grad, v) - resid) * scale).astype(BF16)
        return nn(sgrad, k), tn(sgrad, q), tn(expo.astype(BF16), grad)

    for height in range(LEVELS, 0, -1):
        base, rows = spans[height]
        fine, _ = spans[height - 1]
        for row in range(0, rows, BLOCK):
            near, far = base + row, base + (row ^ BLOCK)
            near = slice(near, near + BLOCK)
            far = slice(far, far + BLOCK)
            q_part, k_part, v_part = gradients(near, far)
            for x, (at, first, value) in enumerate(
                (
                    (near, row, q_part),
                    (far, row ^ BLOCK, k_part),
                    (far, row ^ BLOCK, v_part),
                )
            ):
                if height < LEVELS:
                    value = value + up[x, at, :]
                put_twice(up.at[x], fine + 2 * first, value)
    for row in range(0, tokens, 2 * BLOCK):
        at = slice(row, row + 2 * BLOCK)
        for x, value in enumerate(gradients(at, at)):
            value = (value + up[x, at, :]).astype(BF16)
            for half in range(2):
                out_ref[row // BLOCK + half, x * BLOCK : (x + 1) * BLOCK, :] = value[
                    half * BLOCK : (half + 1) * BLOCK
                ]


def backward(got, sent, lse, tops, lev):
    blocks = got.shape[0]
    tokens = blocks * BLOCK
    spans, total_rows = level_rows(tokens)
    finer = total_rows - spans[LEVELS][1]
    return vmem_call(
        functools.partial(backward_body, blocks),
        jax.ShapeDtypeStruct((blocks, 3 * BLOCK, WIDTH), BF16),
        5,
        scratch=[
            pltpu.VMEM((finer, WIDTH), F32),
            pltpu.VMEM((finer, WIDTH), F32),
            pltpu.VMEM((finer, WIDTH), F32),
            pltpu.VMEM((total_rows, WIDTH), BF16),
            pltpu.VMEM((total_rows, WIDTH), F32),
            pltpu.VMEM((3, finer, WIDTH), F32),
        ],
        cost=cost(10 * tokens * 384 * WIDTH, 12 << 20),
        name="head_backward",
    )(got, sent, lse, tops, lev)


def tile_body(groups, per, grads_ref, att_ref, cot_ref, out_ref, lhs):
    rows = per * WIDTH
    chunk = rows // HEADS
    lanes = chunk // 16
    for o in range(groups):
        for j in range(per):
            lhs[o * BLOCK : (o + 1) * BLOCK, j * WIDTH : (j + 1) * WIDTH] = att_ref[o * per + j]
    out_ref[:, : 3 * BLOCK, :] = grads_ref[...]
    width = cot_ref.shape[1]
    step = 512
    for first in range(0, width, step):
        part = tn(lhs[...], cot_ref[:, first : first + step]).astype(BF16)
        for i in range(HEADS):
            for c in range(step // WIDTH):
                at = 3 * BLOCK + (first // WIDTH + c) * chunk
                out_ref[i, at : at + chunk, :] = part[
                    i * chunk : (i + 1) * chunk, c * WIDTH : (c + 1) * WIDTH
                ]


def with_tile(grads, att, cot):
    per = HEADS // (cot.shape[0] // BLOCK)
    groups = cot.shape[0] // BLOCK
    chunk = per * WIDTH // HEADS
    extra = chunk * (cot.shape[1] // WIDTH)
    return vmem_call(
        functools.partial(tile_body, groups, per),
        jax.ShapeDtypeStruct((HEADS, 3 * BLOCK + extra, WIDTH), BF16),
        3,
        scratch=[pltpu.VMEM((groups * BLOCK, per * WIDTH), BF16)],
        cost=cost(2 * cot.shape[0] * per * WIDTH * cot.shape[1], 10 << 20),
        name="projection_tile",
    )(grads, att, cot)


def unpack_body(scale, in_ref, q_ref, k_ref, v_ref, w_ref):
    chunk, width = w_ref.shape
    for h in range(HEADS):
        for x, ref in enumerate((q_ref, k_ref, v_ref)):
            ref[:, h * WIDTH : (h + 1) * WIDTH] = in_ref[h, x * BLOCK : (x + 1) * BLOCK, :]
    for c in range(width // WIDTH):
        at = 3 * BLOCK + c * chunk
        total = in_ref[0, at : at + chunk, :].astype(F32)
        for h in range(1, HEADS):
            total = total + in_ref[h, at : at + chunk, :].astype(F32)
        w_ref[:, c * WIDTH : (c + 1) * WIDTH] = total * scale


def unpack(got, scale):
    chunk = (got.shape[1] - 3 * BLOCK) // HEADS
    width = HEADS * WIDTH
    return vmem_call(
        functools.partial(unpack_body, scale),
        (jax.ShapeDtypeStruct((BLOCK, width), BF16),) * 3
        + (jax.ShapeDtypeStruct((chunk, width), F32),),
        1,
        cost=cost(0, 6 << 20),
        name="unpack_grads",
    )(got)


def swap(value, axis):
    return lax.all_to_all(value, axis, 0, 0, tiled=True)


def on_device(query_in, key_in, value_in, w_out, cotangent):
    tokens = query_in.shape[0] * lax.axis_size(("outer", "inner"))
    cot_outer = lax.all_gather(cotangent, "outer", axis=0, tiled=True)
    qkv = swap(pack(query_in, key_in, value_in), "inner")
    att_grad = jnp.einsum("te,de->td", cotangent, w_out, preferred_element_type=F32).astype(BF16)
    sent, lse, tops, lev = forward(qkv, att_grad)
    got = swap(sent, "inner")
    att = got[:, BLOCK:, :]
    att_outer = swap(att, "outer")
    grads = backward(got, sent, lse, tops, lev)
    flat = jnp.transpose(att, (1, 0, 2)).reshape(BLOCK, HEADS * WIDTH)
    output = jnp.dot(flat, w_out, preferred_element_type=F32).astype(BF16)
    last = swap(with_tile(grads, att_outer, cot_outer), "inner")
    query_grad, key_grad, value_grad, w_out_grad = unpack(last, 1.0 / math.sqrt(tokens))
    return output, query_grad, key_grad, value_grad, w_out_grad


def solution(mesh):
    rows = P(("outer", "inner"), None)
    return jax.shard_map(
        on_device,
        mesh=mesh,
        in_specs=(rows, rows, rows, P(), rows),
        out_specs=(rows,) * 5,
        check_vma=False,
    )
```

```python
import functools
import math

import jax
import jax.numpy as jnp
from jax import lax
from jax.experimental import pallas as pl
from jax.experimental.pallas import tpu as pltpu
from jax.sharding import PartitionSpec as P

HEADS = 16
BLOCK = 128
LEVELS = 3
WIDTH = 128
BF16 = jnp.bfloat16
F32 = jnp.float32
CHUNK = 256


def nt(a, b):
    return lax.dot_general(a, b, (((1,), (1,)), ((), ())), preferred_element_type=F32)


def nn(a, b):
    return lax.dot_general(a, b, (((1,), (0,)), ((), ())), preferred_element_type=F32)


def tn(a, b):
    return lax.dot_general(a, b, (((0,), (0,)), ((), ())), preferred_element_type=F32)


def wide(stat, columns=WIDTH):
    return jnp.broadcast_to(stat, (stat.shape[0], columns))


def evens(ref, base, rows):
    return ref[pl.ds(base, rows, stride=2), :]


def odds(ref, base, rows):
    return ref[pl.ds(base + 1, rows, stride=2), :]


def put_twice(ref, base, value):
    rows = value.shape[0]
    ref[pl.ds(base, rows, stride=2), :] = value
    ref[pl.ds(base + 1, rows, stride=2), :] = value


def level_rows(tokens):
    out, base = [], 0
    for height in range(LEVELS + 1):
        out.append((base, tokens >> height))
        base += tokens >> height
    return out, base


def vmem_call(body, out_shape, n_in, mib, scratch=(), cost=None, name=None):
    spec = pl.BlockSpec(memory_space=pltpu.VMEM)
    return pl.pallas_call(
        body,
        out_shape=out_shape,
        in_specs=[spec] * n_in,
        out_specs=jax.tree.map(lambda _: spec, out_shape),
        scratch_shapes=list(scratch),
        compiler_params=pltpu.CompilerParams(vmem_limit_bytes=mib << 20),
        cost_estimate=cost,
        name=name,
    )


def cost(flops, nbytes):
    return pl.CostEstimate(flops=int(flops), bytes_accessed=int(nbytes), transcendentals=0)


def pack_body(q_ref, k_ref, v_ref, out_ref):
    for h in range(HEADS):
        for x, ref in enumerate((q_ref, k_ref, v_ref)):
            out_ref[h, x * BLOCK : (x + 1) * BLOCK, :] = ref[:, h * WIDTH : (h + 1) * WIDTH]


def pack(q, k, v):
    return vmem_call(
        pack_body,
        jax.ShapeDtypeStruct((HEADS, 3 * BLOCK, WIDTH), BF16),
        3,
        4,
        cost=cost(0, 6 * q.size * 2),
        name="pack_qkv",
    )(q, k, v)


def forward_body(blocks, in_ref, grad_ref, out_ref, lse_ref, top_ref, lev_ref, fq, mu, du, nu):
    tokens = blocks * BLOCK
    spans, _ = level_rows(tokens)
    scale = 1.0 / math.sqrt(WIDTH)
    for b in range(blocks):
        out_ref[b, 0:BLOCK, :] = grad_ref[:, b * WIDTH : (b + 1) * WIDTH]
        for x in range(3):
            part = in_ref[b, x * BLOCK : (x + 1) * BLOCK, :]
            lev_ref[x, b * BLOCK : (b + 1) * BLOCK, :] = part
            fq[x, b * BLOCK : (b + 1) * BLOCK, :] = part.astype(F32)
    for height in range(1, LEVELS + 1):
        below, _ = spans[height - 1]
        base, rows = spans[height]
        step = min(CHUNK, rows)
        for x in range(3):
            for r in range(0, rows, step):
                mean = (
                    evens(fq.at[x], below + 2 * r, step) + odds(fq.at[x], below + 2 * r, step)
                ) * 0.5
                mean = mean.astype(BF16)
                lev_ref[x, base + r : base + r + step, :] = mean
                fq[x, base + r : base + r + step, :] = mean.astype(F32)

    def attend(q, k, v, factor):
        scores = nt(q, k) * scale
        top = wide(jnp.max(scores, axis=1, keepdims=True))
        shift = jnp.concatenate([top] * (k.shape[0] // WIDTH), axis=1)
        expo = jnp.exp(scores - shift)
        denom = wide(jnp.sum(expo, axis=1, keepdims=True))
        numer = nn(expo.astype(BF16), v)
        if factor != 1:
            denom, numer = denom * factor, numer * factor
        return top, denom, numer

    def merge(height, row, stats):
        top, denom, numer = stats
        base, _ = spans[height]
        rows = top.shape[0]
        at = slice(base + row, base + row + rows)
        top_ref[at, :] = top
        if height < LEVELS:
            up = mu[at, :]
            peak = jnp.maximum(top, up)
            mine, theirs = jnp.exp(top - peak), jnp.exp(up - peak)
            denom = mine * denom + theirs * du[at, :]
            numer = mine * numer + theirs * nu[at, :]
            top = peak
        return top, denom, numer

    for height in range(LEVELS, 0, -1):
        base, rows = spans[height]
        fine, _ = spans[height - 1]
        for row in range(0, rows, BLOCK):
            far = base + (row ^ BLOCK)
            stats = attend(
                lev_ref[0, base + row : base + row + BLOCK, :],
                lev_ref[1, far : far + BLOCK, :],
                lev_ref[2, far : far + BLOCK, :],
                float(2**height),
            )
            merged = merge(height, row, stats)
            for ref, value in zip((mu, du, nu), merged):
                put_twice(ref, fine + 2 * row, value)
    for row in range(0, tokens, 2 * BLOCK):
        at = slice(row, row + 2 * BLOCK)
        stats = attend(lev_ref[0, at, :], lev_ref[1, at, :], lev_ref[2, at, :], 1)
        peak, total, summed = merge(0, row, stats)
        attended = (summed / total).astype(BF16)
        lse_ref[at, :] = peak + jnp.log(total)
        out_ref[row // BLOCK, BLOCK:, :] = attended[:BLOCK]
        out_ref[row // BLOCK + 1, BLOCK:, :] = attended[BLOCK:]


def forward(qkv, att_grad):
    blocks = qkv.shape[0]
    tokens = blocks * BLOCK
    spans, total_rows = level_rows(tokens)
    finer = total_rows - spans[LEVELS][1]
    out_shape = (
        jax.ShapeDtypeStruct((blocks, 2 * BLOCK, WIDTH), BF16),
        jax.ShapeDtypeStruct((tokens, WIDTH), F32),
        jax.ShapeDtypeStruct((total_rows, WIDTH), F32),
        jax.ShapeDtypeStruct((3, total_rows, WIDTH), BF16),
    )
    return vmem_call(
        functools.partial(forward_body, blocks),
        out_shape,
        2,
        26,
        scratch=[
            pltpu.VMEM((3, total_rows, WIDTH), F32),
            pltpu.VMEM((finer, WIDTH), F32),
            pltpu.VMEM((finer, WIDTH), F32),
            pltpu.VMEM((finer, WIDTH), F32),
        ],
        cost=cost(4 * tokens * 384 * WIDTH, 8 << 20),
        name="head_forward",
    )(qkv, att_grad)


def backward_body(
    blocks, got_ref, sent_ref, lse_ref, top_ref, lev_ref, out_ref, ys, ds, rs, cg, res, up
):
    tokens = blocks * BLOCK
    spans, _ = level_rows(tokens)
    scale = 1.0 / math.sqrt(WIDTH)
    for b in range(blocks):
        at = slice(b * BLOCK, (b + 1) * BLOCK)
        grad = got_ref[b, :BLOCK, :].astype(F32)
        delta = wide(
            jnp.sum(grad * sent_ref[b, BLOCK:, :].astype(F32), axis=1, keepdims=True)
        )
        lse = lse_ref[at, :]
        ys[at, :], ds[at, :], rs[at, :] = grad, delta, lse
        cover = jnp.exp(top_ref[at, :] - lse)
        cg[at, :] = (cover * grad).astype(BF16)
        res[at, :] = cover * delta
    for height in range(1, LEVELS + 1):
        below, _ = spans[height - 1]
        base, rows = spans[height]
        for r in range(0, rows, BLOCK):
            at = slice(base + r, base + r + BLOCK)
            first = below + 2 * r
            lo, hi = evens(rs, first, BLOCK), odds(rs, first, BLOCK)
            low = jnp.minimum(lo, hi)
            lo, hi = jnp.exp(low - lo), jnp.exp(low - hi)
            grad = lo * evens(ys, first, BLOCK) + hi * odds(ys, first, BLOCK)
            delta = lo * evens(ds, first, BLOCK) + hi * odds(ds, first, BLOCK)
            if height < LEVELS:
                ys[at, :], ds[at, :], rs[at, :] = grad, delta, low
            cover = jnp.exp(top_ref[at, :] - low)
            cg[at, :] = (cover * grad).astype(BF16)
            res[at, :] = cover * delta

    def gradients(rows, keys):
        q, grad = lev_ref[0, rows, :], cg[rows, :]
        k, v = lev_ref[1, keys, :], lev_ref[2, keys, :]
        times = k.shape[0] // WIDTH
        top = jnp.concatenate([top_ref[rows, :]] * times, axis=1)
        resid = jnp.concatenate([res[rows, :]] * times, axis=1)
        expo = jnp.exp(nt(q, k) * scale - top)
        sgrad = (expo * (nt(grad, v) - resid) * scale).astype(BF16)
        return nn(sgrad, k), tn(sgrad, q), tn(expo.astype(BF16), grad)

    for height in range(LEVELS, 0, -1):
        base, rows = spans[height]
        fine, _ = spans[height - 1]
        for row in range(0, rows, BLOCK):
            near, far = base + row, base + (row ^ BLOCK)
            near = slice(near, near + BLOCK)
            far = slice(far, far + BLOCK)
            q_part, k_part, v_part = gradients(near, far)
            for x, (at, first, value) in enumerate(
                (
                    (near, row, q_part),
                    (far, row ^ BLOCK, k_part),
                    (far, row ^ BLOCK, v_part),
                )
            ):
                if height < LEVELS:
                    value = value + up[x, at, :]
                put_twice(up.at[x], fine + 2 * first, value)
    for row in range(0, tokens, 2 * BLOCK):
        at = slice(row, row + 2 * BLOCK)
        for x, value in enumerate(gradients(at, at)):
            value = (value + up[x, at, :]).astype(BF16)
            for half in range(2):
                out_ref[row // BLOCK + half, x * BLOCK : (x + 1) * BLOCK, :] = value[
                    half * BLOCK : (half + 1) * BLOCK
                ]


def backward(got, sent, lse, tops, lev):
    blocks = got.shape[0]
    tokens = blocks * BLOCK
    spans, total_rows = level_rows(tokens)
    finer = total_rows - spans[LEVELS][1]
    return vmem_call(
        functools.partial(backward_body, blocks),
        jax.ShapeDtypeStruct((blocks, 3 * BLOCK, WIDTH), BF16),
        5,
        28,
        scratch=[
            pltpu.VMEM((finer, WIDTH), F32),
            pltpu.VMEM((finer, WIDTH), F32),
            pltpu.VMEM((finer, WIDTH), F32),
            pltpu.VMEM((total_rows, WIDTH), BF16),
            pltpu.VMEM((total_rows, WIDTH), F32),
            pltpu.VMEM((3, finer, WIDTH), F32),
        ],
        cost=cost(10 * tokens * 384 * WIDTH, 12 << 20),
        name="head_backward",
    )(got, sent, lse, tops, lev)


def tile_body(groups, per, grads_ref, att_ref, cot_ref, out_ref, lhs):
    rows = per * WIDTH
    chunk = rows // HEADS
    lanes = chunk // 16
    for o in range(groups):
        for j in range(per):
            lhs[o * BLOCK : (o + 1) * BLOCK, j * WIDTH : (j + 1) * WIDTH] = att_ref[o * per + j]
    out_ref[:, : 3 * BLOCK, :] = grads_ref[...]
    width = cot_ref.shape[1]
    step = 512
    for first in range(0, width, step):
        part = tn(lhs[...], cot_ref[:, first : first + step]).astype(BF16)
        for i in range(HEADS):
            for c in range(step // WIDTH):
                at = 3 * BLOCK + (first // WIDTH + c) * chunk
                out_ref[i, at : at + chunk, :] = part[
                    i * chunk : (i + 1) * chunk, c * WIDTH : (c + 1) * WIDTH
                ]


def with_tile(grads, att, cot):
    per = HEADS // (cot.shape[0] // BLOCK)
    groups = cot.shape[0] // BLOCK
    chunk = per * WIDTH // HEADS
    extra = chunk * (cot.shape[1] // WIDTH)
    return vmem_call(
        functools.partial(tile_body, groups, per),
        jax.ShapeDtypeStruct((HEADS, 3 * BLOCK + extra, WIDTH), BF16),
        3,
        12,
        scratch=[pltpu.VMEM((groups * BLOCK, per * WIDTH), BF16)],
        cost=cost(2 * cot.shape[0] * per * WIDTH * cot.shape[1], 10 << 20),
        name="projection_tile",
    )(grads, att, cot)


def unpack_body(scale, in_ref, q_ref, k_ref, v_ref, w_ref):
    chunk, width = w_ref.shape
    for h in range(HEADS):
        for x, ref in enumerate((q_ref, k_ref, v_ref)):
            ref[:, h * WIDTH : (h + 1) * WIDTH] = in_ref[h, x * BLOCK : (x + 1) * BLOCK, :]
    for c in range(width // WIDTH):
        at = 3 * BLOCK + c * chunk
        total = in_ref[0, at : at + chunk, :].astype(F32)
        for h in range(1, HEADS):
            total = total + in_ref[h, at : at + chunk, :].astype(F32)
        w_ref[:, c * WIDTH : (c + 1) * WIDTH] = total * scale


def unpack(got, scale):
    chunk = (got.shape[1] - 3 * BLOCK) // HEADS
    width = HEADS * WIDTH
    return vmem_call(
        functools.partial(unpack_body, scale),
        (jax.ShapeDtypeStruct((BLOCK, width), BF16),) * 3
        + (jax.ShapeDtypeStruct((chunk, width), F32),),
        1,
        6,
        cost=cost(0, 6 << 20),
        name="unpack_grads",
    )(got)


def split_body(got_ref, att_ref, flat_ref):
    for h in range(HEADS):
        part = got_ref[h, BLOCK:, :]
        att_ref[h] = part
        flat_ref[:, h * WIDTH : (h + 1) * WIDTH] = part


def split(got):
    return vmem_call(
        split_body,
        (
            jax.ShapeDtypeStruct((HEADS, BLOCK, WIDTH), BF16),
            jax.ShapeDtypeStruct((BLOCK, HEADS * WIDTH), BF16),
        ),
        1,
        3,
        cost=cost(0, 2 << 20),
        name="split_attended",
    )(got)


def swap(value, axis):
    return lax.all_to_all(value, axis, 0, 0, tiled=True)


def on_device(query_in, key_in, value_in, w_out, cotangent):
    tokens = query_in.shape[0] * lax.axis_size(("outer", "inner"))
    cot_outer = lax.all_gather(cotangent, "outer", axis=0, tiled=True)
    qkv = swap(pack(query_in, key_in, value_in), "inner")
    att_grad = jnp.einsum("te,de->td", cotangent, w_out, preferred_element_type=F32).astype(BF16)
    sent, lse, tops, lev = forward(qkv, att_grad)
    got = swap(sent, "inner")
    att, flat = split(got)
    att_outer = swap(att, "outer")
    grads = backward(got, sent, lse, tops, lev)
    output = jnp.dot(flat, w_out, preferred_element_type=F32).astype(BF16)
    last = swap(with_tile(grads, att_outer, cot_outer), "inner")
    query_grad, key_grad, value_grad, w_out_grad = unpack(last, 1.0 / math.sqrt(tokens))
    return output, query_grad, key_grad, value_grad, w_out_grad


def solution(mesh):
    rows = P(("outer", "inner"), None)
    return jax.shard_map(
        on_device,
        mesh=mesh,
        in_specs=(rows, rows, rows, P(), rows),
        out_specs=(rows,) * 5,
        check_vma=False,
    )
```

```python
import functools
import math

import jax
import jax.numpy as jnp
from jax import lax
from jax.experimental import pallas as pl
from jax.experimental.pallas import tpu as pltpu
from jax.sharding import PartitionSpec as P

HEADS = 16
BLOCK = 128
LEVELS = 3
WIDTH = 128
BF16 = jnp.bfloat16
F32 = jnp.float32
CHUNK = 256


def nt(a, b):
    return lax.dot_general(a, b, (((1,), (1,)), ((), ())), preferred_element_type=F32)


def nn(a, b):
    return lax.dot_general(a, b, (((1,), (0,)), ((), ())), preferred_element_type=F32)


def tn(a, b):
    return lax.dot_general(a, b, (((0,), (0,)), ((), ())), preferred_element_type=F32)


def wide(stat, columns=WIDTH):
    return jnp.broadcast_to(stat, (stat.shape[0], columns))


def evens(ref, base, rows):
    return ref[pl.ds(base, rows, stride=2), :]


def odds(ref, base, rows):
    return ref[pl.ds(base + 1, rows, stride=2), :]


def put_twice(ref, base, value):
    rows = value.shape[0]
    ref[pl.ds(base, rows, stride=2), :] = value
    ref[pl.ds(base + 1, rows, stride=2), :] = value


def level_rows(tokens):
    out, base = [], 0
    for height in range(LEVELS + 1):
        out.append((base, tokens >> height))
        base += tokens >> height
    return out, base


def kernel_call(body, outs, in_places, mib, scratch=(), cost=None, name=None):
    spec = {
        "vmem": pl.BlockSpec(memory_space=pltpu.VMEM),
        "hbm": pl.BlockSpec(memory_space=pl.ANY),
    }
    shapes = [
        pltpu.HBM(shape, dtype) if place == "hbm" else jax.ShapeDtypeStruct(shape, dtype)
        for shape, dtype, place in outs
    ]
    call = pl.pallas_call(
        body,
        out_shape=shapes,
        in_specs=[spec[place] for place in in_places],
        out_specs=[spec[place] for _, _, place in outs],
        scratch_shapes=list(scratch),
        compiler_params=pltpu.CompilerParams(vmem_limit_bytes=mib << 20),
        cost_estimate=cost,
        name=name,
    )

    def run(*operands):
        operands = [
            pltpu.with_memory_space_constraint(x, pltpu.HBM) if place == "hbm" else x
            for x, place in zip(operands, in_places)
        ]
        return call(*operands)

    return run


def dma(count):
    return pltpu.SemaphoreType.DMA((count,))


def cost(flops, nbytes):
    return pl.CostEstimate(flops=int(flops), bytes_accessed=int(nbytes), transcendentals=0)


def pack_body(q_ref, k_ref, v_ref, out_ref, sems):
    copies = []
    for x, ref in enumerate((q_ref, k_ref, v_ref)):
        for h in range(HEADS):
            copies.append(
                pltpu.make_async_copy(
                    ref.at[:, h * WIDTH : (h + 1) * WIDTH],
                    out_ref.at[h, x * BLOCK : (x + 1) * BLOCK, :],
                    sems.at[x * HEADS + h],
                )
            )
            copies[-1].start()
    for copy in copies:
        copy.wait()


def pack(q, k, v):
    return kernel_call(
        pack_body,
        [((HEADS, 3 * BLOCK, WIDTH), BF16, "hbm")],
        ["hbm"] * 3,
        2,
        scratch=[dma(3 * HEADS)],
        cost=cost(0, 6 * q.size * 2),
        name="pack_qkv",
    )(q, k, v)[0]


def att_grad_body(chunks, cot_ref, w_ref, out_ref, held, sems):
    rows = held.shape[0] // chunks
    copies = []
    for c in range(chunks):
        at = slice(c * rows, (c + 1) * rows)
        copies.append(pltpu.make_async_copy(w_ref.at[at, :], held.at[at, :], sems.at[c]))
        copies[-1].start()
    for c, copy in enumerate(copies):
        at = slice(c * rows, (c + 1) * rows)
        copy.wait()
        out_ref[:, at] = nt(cot_ref[...], held[at, :]).astype(BF16)


def attended_gradient(cot, w_out):
    chunks = 8
    return kernel_call(
        functools.partial(att_grad_body, chunks),
        [(cot.shape, BF16, "vmem")],
        ["vmem", "hbm"],
        14,
        scratch=[pltpu.VMEM(w_out.shape, BF16), dma(chunks)],
        cost=cost(2 * cot.size * w_out.shape[0], 9 << 20),
        name="attended_gradient",
    )(cot, w_out)[0]


def output_body(chunks, att_ref, w_ref, out_ref, lhs, held, sems, att_sems):
    columns = held.shape[2]
    copies, parts = [], []
    for h in range(HEADS):
        parts.append(
            pltpu.make_async_copy(
                att_ref.at[h], lhs.at[:, h * WIDTH : (h + 1) * WIDTH], att_sems.at[h]
            )
        )
        parts[-1].start()
    for c in range(chunks):
        at = slice(c * columns, (c + 1) * columns)
        copies.append(pltpu.make_async_copy(w_ref.at[:, at], held.at[c], sems.at[c]))
        copies[-1].start()
    for part in parts:
        part.wait()
    for c, copy in enumerate(copies):
        copy.wait()
        out_ref[:, c * columns : (c + 1) * columns] = nn(lhs[...], held[c]).astype(BF16)


def project(att, w_out):
    chunks = 8
    rows, columns = w_out.shape
    return kernel_call(
        functools.partial(output_body, chunks),
        [((BLOCK, columns), BF16, "vmem")],
        ["hbm", "hbm"],
        14,
        scratch=[
            pltpu.VMEM((BLOCK, rows), BF16),
            pltpu.VMEM((chunks, rows, columns // chunks), BF16),
            dma(chunks),
            dma(HEADS),
        ],
        cost=cost(2 * BLOCK * rows * columns, 9 << 20),
        name="output_projection",
    )(att, w_out)[0]


def forward_body(
    blocks, in_ref, grad_ref, out_ref, att_out, lse_out, top_out, lev_out,
    lse_ref, top_ref, lev_ref, fq, mu, du, nu, sems,
):
    tokens = blocks * BLOCK
    spans, _ = level_rows(tokens)
    copies = []

    def send(source, target):
        copies.append(pltpu.make_async_copy(source, target, sems.at[len(copies)]))
        copies[-1].start()

    scale = 1.0 / math.sqrt(WIDTH)
    for b in range(blocks):
        out_ref[b, 0:BLOCK, :] = grad_ref[:, b * WIDTH : (b + 1) * WIDTH]
        for x in range(3):
            part = in_ref[b, x * BLOCK : (x + 1) * BLOCK, :]
            lev_ref[x, b * BLOCK : (b + 1) * BLOCK, :] = part
            fq[x, b * BLOCK : (b + 1) * BLOCK, :] = part.astype(F32)
    for height in range(1, LEVELS + 1):
        below, _ = spans[height - 1]
        base, rows = spans[height]
        step = min(CHUNK, rows)
        for x in range(3):
            for r in range(0, rows, step):
                mean = (
                    evens(fq.at[x], below + 2 * r, step) + odds(fq.at[x], below + 2 * r, step)
                ) * 0.5
                mean = mean.astype(BF16)
                lev_ref[x, base + r : base + r + step, :] = mean
                fq[x, base + r : base + r + step, :] = mean.astype(F32)

    send(lev_ref, lev_out)

    def attend(q, k, v, factor):
        scores = nt(q, k) * scale
        top = wide(jnp.max(scores, axis=1, keepdims=True))
        shift = jnp.concatenate([top] * (k.shape[0] // WIDTH), axis=1)
        expo = jnp.exp(scores - shift)
        denom = wide(jnp.sum(expo, axis=1, keepdims=True))
        numer = nn(expo.astype(BF16), v)
        if factor != 1:
            denom, numer = denom * factor, numer * factor
        return top, denom, numer

    def merge(height, row, stats):
        top, denom, numer = stats
        base, _ = spans[height]
        rows = top.shape[0]
        at = slice(base + row, base + row + rows)
        top_ref[at, :] = top
        if height < LEVELS:
            up = mu[at, :]
            peak = jnp.maximum(top, up)
            mine, theirs = jnp.exp(top - peak), jnp.exp(up - peak)
            denom = mine * denom + theirs * du[at, :]
            numer = mine * numer + theirs * nu[at, :]
            top = peak
        return top, denom, numer

    for height in range(LEVELS, 0, -1):
        base, rows = spans[height]
        fine, _ = spans[height - 1]
        for row in range(0, rows, BLOCK):
            far = base + (row ^ BLOCK)
            stats = attend(
                lev_ref[0, base + row : base + row + BLOCK, :],
                lev_ref[1, far : far + BLOCK, :],
                lev_ref[2, far : far + BLOCK, :],
                float(2**height),
            )
            merged = merge(height, row, stats)
            for ref, value in zip((mu, du, nu), merged):
                put_twice(ref, fine + 2 * row, value)
        at = slice(base, base + rows)
        send(top_ref.at[at, :], top_out.at[at, :])
    for row in range(0, tokens, 2 * BLOCK):
        at = slice(row, row + 2 * BLOCK)
        stats = attend(lev_ref[0, at, :], lev_ref[1, at, :], lev_ref[2, at, :], 1)
        peak, total, summed = merge(0, row, stats)
        attended = (summed / total).astype(BF16)
        lse_ref[at, :] = peak + jnp.log(total)
        pair = slice(row // BLOCK, row // BLOCK + 2)
        out_ref[row // BLOCK, BLOCK:, :] = attended[:BLOCK]
        out_ref[row // BLOCK + 1, BLOCK:, :] = attended[BLOCK:]
        send(top_ref.at[at, :], top_out.at[at, :])
        send(lse_ref.at[at, :], lse_out.at[at, :])
        send(out_ref.at[pair, BLOCK:, :], att_out.at[pair, :, :])
    for copy in copies:
        copy.wait()


def forward(qkv, att_grad):
    blocks = qkv.shape[0]
    tokens = blocks * BLOCK
    spans, total_rows = level_rows(tokens)
    finer = total_rows - spans[LEVELS][1]
    outs = [
        ((blocks, 2 * BLOCK, WIDTH), BF16, "vmem"),
        ((blocks, BLOCK, WIDTH), BF16, "hbm"),
        ((tokens, WIDTH), F32, "hbm"),
        ((total_rows, WIDTH), F32, "hbm"),
        ((3, total_rows, WIDTH), BF16, "hbm"),
    ]
    return kernel_call(
        functools.partial(forward_body, blocks),
        outs,
        ["vmem"] * 2,
        32,
        scratch=[
            pltpu.VMEM((tokens, WIDTH), F32),
            pltpu.VMEM((total_rows, WIDTH), F32),
            pltpu.VMEM((3, total_rows, WIDTH), BF16),
            pltpu.VMEM((3, total_rows, WIDTH), F32),
            pltpu.VMEM((finer, WIDTH), F32),
            pltpu.VMEM((finer, WIDTH), F32),
            pltpu.VMEM((finer, WIDTH), F32),
            dma(1 + LEVELS + 3 * blocks // 2),
        ],
        cost=cost(4 * tokens * 384 * WIDTH, 8 << 20),
        name="head_forward",
    )(qkv, att_grad)


def backward_body(
    blocks, grad_in, att_in, lse_in, top_in, lev_in, out_ref,
    grad_ref, att_ref, lse_ref, top_ref, lev_ref, ys, ds, rs, cg, res, up, sems,
):
    tokens = blocks * BLOCK
    spans, total_rows = level_rows(tokens)
    scale = 1.0 / math.sqrt(WIDTH)
    parts, count = 4, [0]

    def fetch(source, target):
        copy = pltpu.make_async_copy(source, target, sems.at[count[0]])
        count[0] += 1
        copy.start()
        return copy

    first_loads = []
    for p in range(parts):
        some = slice(p * blocks // parts, (p + 1) * blocks // parts)
        at = slice(p * tokens // parts, (p + 1) * tokens // parts)
        first_loads.append(
            [
                fetch(grad_in.at[some, :, :], grad_ref.at[some, :, :]),
                fetch(att_in.at[some, :, :], att_ref.at[some, :, :]),
                fetch(lse_in.at[at, :], lse_ref.at[at, :]),
                fetch(top_in.at[at, :], top_ref.at[at, :]),
            ]
        )
    coarse = slice(tokens, total_rows)
    later_loads = [
        fetch(top_in.at[coarse, :], top_ref.at[coarse, :]),
        fetch(lev_in.at[:, coarse, :], lev_ref.at[:, coarse, :]),
        fetch(lev_in.at[:, :tokens, :], lev_ref.at[:, :tokens, :]),
    ]
    for b in range(blocks):
        if b % (blocks // parts) == 0:
            for copy in first_loads[b // (blocks // parts)]:
                copy.wait()
        at = slice(b * BLOCK, (b + 1) * BLOCK)
        grad = grad_ref[b].astype(F32)
        delta = wide(jnp.sum(grad * att_ref[b].astype(F32), axis=1, keepdims=True))
        lse = lse_ref[at, :]
        ys[at, :], ds[at, :], rs[at, :] = grad, delta, lse
        cover = jnp.exp(top_ref[at, :] - lse)
        cg[at, :] = (cover * grad).astype(BF16)
        res[at, :] = cover * delta
    later_loads[0].wait()
    for height in range(1, LEVELS + 1):
        below, _ = spans[height - 1]
        base, rows = spans[height]
        for r in range(0, rows, BLOCK):
            at = slice(base + r, base + r + BLOCK)
            first = below + 2 * r
            lo, hi = evens(rs, first, BLOCK), odds(rs, first, BLOCK)
            low = jnp.minimum(lo, hi)
            lo, hi = jnp.exp(low - lo), jnp.exp(low - hi)
            grad = lo * evens(ys, first, BLOCK) + hi * odds(ys, first, BLOCK)
            delta = lo * evens(ds, first, BLOCK) + hi * odds(ds, first, BLOCK)
            if height < LEVELS:
                ys[at, :], ds[at, :], rs[at, :] = grad, delta, low
            cover = jnp.exp(top_ref[at, :] - low)
            cg[at, :] = (cover * grad).astype(BF16)
            res[at, :] = cover * delta

    def gradients(rows, keys):
        q, grad = lev_ref[0, rows, :], cg[rows, :]
        k, v = lev_ref[1, keys, :], lev_ref[2, keys, :]
        times = k.shape[0] // WIDTH
        top = jnp.concatenate([top_ref[rows, :]] * times, axis=1)
        resid = jnp.concatenate([res[rows, :]] * times, axis=1)
        expo = jnp.exp(nt(q, k) * scale - top)
        sgrad = (expo * (nt(grad, v) - resid) * scale).astype(BF16)
        return nn(sgrad, k), tn(sgrad, q), tn(expo.astype(BF16), grad)

    later_loads[1].wait()
    for height in range(LEVELS, 0, -1):
        base, rows = spans[height]
        fine, _ = spans[height - 1]
        for row in range(0, rows, BLOCK):
            near, far = base + row, base + (row ^ BLOCK)
            near = slice(near, near + BLOCK)
            far = slice(far, far + BLOCK)
            q_part, k_part, v_part = gradients(near, far)
            for x, (at, first, value) in enumerate(
                (
                    (near, row, q_part),
                    (far, row ^ BLOCK, k_part),
                    (far, row ^ BLOCK, v_part),
                )
            ):
                if height < LEVELS:
                    value = value + up[x, at, :]
                put_twice(up.at[x], fine + 2 * first, value)
    later_loads[2].wait()
    for row in range(0, tokens, 2 * BLOCK):
        at = slice(row, row + 2 * BLOCK)
        for x, value in enumerate(gradients(at, at)):
            value = (value + up[x, at, :]).astype(BF16)
            for half in range(2):
                out_ref[row // BLOCK + half, x * BLOCK : (x + 1) * BLOCK, :] = value[
                    half * BLOCK : (half + 1) * BLOCK
                ]


def backward(grad, att, lse, tops, lev):
    blocks = grad.shape[0]
    tokens = blocks * BLOCK
    spans, total_rows = level_rows(tokens)
    finer = total_rows - spans[LEVELS][1]
    return kernel_call(
        functools.partial(backward_body, blocks),
        [((blocks, 3 * BLOCK, WIDTH), BF16, "vmem")],
        ["hbm"] * 5,
        36,
        scratch=[
            pltpu.VMEM(grad.shape, BF16),
            pltpu.VMEM(att.shape, BF16),
            pltpu.VMEM(lse.shape, F32),
            pltpu.VMEM(tops.shape, F32),
            pltpu.VMEM(lev.shape, BF16),
            pltpu.VMEM((finer, WIDTH), F32),
            pltpu.VMEM((finer, WIDTH), F32),
            pltpu.VMEM((finer, WIDTH), F32),
            pltpu.VMEM((total_rows, WIDTH), BF16),
            pltpu.VMEM((total_rows, WIDTH), F32),
            pltpu.VMEM((3, finer, WIDTH), F32),
            dma(19),
        ],
        cost=cost(10 * tokens * 384 * WIDTH, 12 << 20),
        name="head_backward",
    )(grad, att, lse, tops, lev)[0]


def tile_body(groups, per, chunks, grads_ref, att_ref, cot_ref, _, out_ref, lhs, held, sems):
    rows = per * WIDTH
    chunk = rows // HEADS
    width = held.shape[2]
    copies = []
    for c in range(chunks):
        at = slice(c * width, (c + 1) * width)
        copies.append(pltpu.make_async_copy(cot_ref.at[:, at], held.at[c], sems.at[c]))
        copies[-1].start()
    out_ref[:, : 3 * BLOCK, :] = grads_ref[...]
    for o in range(groups):
        for j in range(per):
            lhs[o * BLOCK : (o + 1) * BLOCK, j * WIDTH : (j + 1) * WIDTH] = att_ref[o * per + j]
    for c, copy in enumerate(copies):
        copy.wait()
        part = tn(lhs[...], held[c]).astype(BF16)
        for i in range(HEADS):
            for j in range(width // WIDTH):
                at = 3 * BLOCK + (c * width // WIDTH + j) * chunk
                out_ref[i, at : at + chunk, :] = part[
                    i * chunk : (i + 1) * chunk, j * WIDTH : (j + 1) * WIDTH
                ]


def with_tile(grads, att, cot, after):
    chunks = 4
    groups = cot.shape[0] // BLOCK
    per = HEADS // groups
    chunk = per * WIDTH // HEADS
    extra = chunk * (cot.shape[1] // WIDTH)
    return kernel_call(
        functools.partial(tile_body, groups, per, chunks),
        [((HEADS, 3 * BLOCK + extra, WIDTH), BF16, "vmem")],
        ["vmem", "vmem", "hbm", "hbm"],
        16,
        scratch=[
            pltpu.VMEM((groups * BLOCK, per * WIDTH), BF16),
            pltpu.VMEM((chunks, cot.shape[0], cot.shape[1] // chunks), BF16),
            dma(chunks),
        ],
        cost=cost(2 * cot.shape[0] * per * WIDTH * cot.shape[1], 10 << 20),
        name="projection_tile",
    )(grads, att, cot, after)[0]


def unpack_body(scale, in_ref, q_ref, k_ref, v_ref, w_ref):
    chunk, width = w_ref.shape
    for h in range(HEADS):
        for x, ref in enumerate((q_ref, k_ref, v_ref)):
            ref[:, h * WIDTH : (h + 1) * WIDTH] = in_ref[h, x * BLOCK : (x + 1) * BLOCK, :]
    for c in range(width // WIDTH):
        at = 3 * BLOCK + c * chunk
        total = in_ref[0, at : at + chunk, :].astype(F32)
        for h in range(1, HEADS):
            total = total + in_ref[h, at : at + chunk, :].astype(F32)
        w_ref[:, c * WIDTH : (c + 1) * WIDTH] = total * scale


def unpack(got, scale):
    chunk = (got.shape[1] - 3 * BLOCK) // HEADS
    width = HEADS * WIDTH
    return kernel_call(
        functools.partial(unpack_body, scale),
        [((BLOCK, width), BF16, "vmem")] * 3 + [((chunk, width), F32, "vmem")],
        ["vmem"],
        8,
        cost=cost(0, 6 << 20),
        name="unpack_grads",
    )(got)


def split_body(got_ref, grad_ref, att_ref, sems):
    copies = [
        pltpu.make_async_copy(got_ref.at[:, BLOCK:, :], att_ref, sems.at[0]),
        pltpu.make_async_copy(got_ref.at[:, :BLOCK, :], grad_ref, sems.at[1]),
    ]
    for copy in copies:
        copy.start()
    for copy in copies:
        copy.wait()


def split(got):
    return kernel_call(
        split_body,
        [((HEADS, BLOCK, WIDTH), BF16, "hbm")] * 2,
        ["vmem"],
        2,
        scratch=[dma(2)],
        cost=cost(0, 2 << 20),
        name="split_attended",
    )(got)


def swap(value, axis):
    return lax.all_to_all(value, axis, 0, 0, tiled=True)


def on_device(query_in, key_in, value_in, w_out, cotangent):
    tokens = query_in.shape[0] * lax.axis_size(("outer", "inner"))
    cot_outer = lax.all_gather(cotangent, "outer", axis=0, tiled=True)
    qkv = swap(pack(query_in, key_in, value_in), "inner")
    att_grad = attended_gradient(cotangent, w_out)
    sent, att_own, lse, tops, lev = forward(qkv, att_grad)
    grad, att = split(swap(sent, "inner"))
    att_outer = swap(att, "outer")
    grads = backward(grad, att_own, lse, tops, lev)
    output = project(att, w_out)
    last = swap(with_tile(grads, att_outer, cot_outer, output), "inner")
    query_grad, key_grad, value_grad, w_out_grad = unpack(last, 1.0 / math.sqrt(tokens))
    return output, query_grad, key_grad, value_grad, w_out_grad


def solution(mesh):
    rows = P(("outer", "inner"), None)
    return jax.shard_map(
        on_device,
        mesh=mesh,
        in_specs=(rows, rows, rows, P(), rows),
        out_specs=(rows,) * 5,
        check_vma=False,
    )
```

```python
import functools
import math

import jax
import jax.numpy as jnp
from jax import lax
from jax.experimental import pallas as pl
from jax.experimental.pallas import tpu as pltpu
from jax.sharding import PartitionSpec as P

HEADS = 16
BLOCK = 128
LEVELS = 3
WIDTH = 128
BF16 = jnp.bfloat16
F32 = jnp.float32
CHUNK = 256


def nt(a, b):
    return lax.dot_general(a, b, (((1,), (1,)), ((), ())), preferred_element_type=F32)


def nn(a, b):
    return lax.dot_general(a, b, (((1,), (0,)), ((), ())), preferred_element_type=F32)


def tn(a, b):
    return lax.dot_general(a, b, (((0,), (0,)), ((), ())), preferred_element_type=F32)


def wide(stat, columns=WIDTH):
    return jnp.broadcast_to(stat, (stat.shape[0], columns))


def evens(ref, base, rows):
    return ref[pl.ds(base, rows, stride=2), :]


def odds(ref, base, rows):
    return ref[pl.ds(base + 1, rows, stride=2), :]


def put_twice(ref, base, value):
    rows = value.shape[0]
    ref[pl.ds(base, rows, stride=2), :] = value
    ref[pl.ds(base + 1, rows, stride=2), :] = value


def level_rows(tokens):
    out, base = [], 0
    for height in range(LEVELS + 1):
        out.append((base, tokens >> height))
        base += tokens >> height
    return out, base


def kernel_call(body, outs, in_places, mib, scratch=(), cost=None, name=None):
    spec = {
        "vmem": pl.BlockSpec(memory_space=pltpu.VMEM),
        "hbm": pl.BlockSpec(memory_space=pl.ANY),
    }
    shapes = [
        pltpu.HBM(shape, dtype) if place == "hbm" else jax.ShapeDtypeStruct(shape, dtype)
        for shape, dtype, place in outs
    ]
    call = pl.pallas_call(
        body,
        out_shape=shapes,
        in_specs=[spec[place] for place in in_places],
        out_specs=[spec[place] for _, _, place in outs],
        scratch_shapes=list(scratch),
        compiler_params=pltpu.CompilerParams(vmem_limit_bytes=mib << 20),
        cost_estimate=cost,
        name=name,
    )

    def run(*operands):
        operands = [
            pltpu.with_memory_space_constraint(x, pltpu.HBM) if place == "hbm" else x
            for x, place in zip(operands, in_places)
        ]
        return call(*operands)

    return run


def dma(count):
    return pltpu.SemaphoreType.DMA((count,))


def cost(flops, nbytes):
    return pl.CostEstimate(flops=int(flops), bytes_accessed=int(nbytes), transcendentals=0)


def pack_body(q_ref, k_ref, v_ref, out_ref, held, packed, in_sems, out_sems):
    loads = [
        pltpu.make_async_copy(ref, held.at[x], in_sems.at[x])
        for x, ref in enumerate((q_ref, k_ref, v_ref))
    ]
    for load in loads:
        load.start()
    stores = []
    for x, load in enumerate(loads):
        load.wait()
        rows = slice(x * BLOCK, (x + 1) * BLOCK)
        for h in range(HEADS):
            packed[h, rows, :] = held[x, :, h * WIDTH : (h + 1) * WIDTH]
        stores.append(
            pltpu.make_async_copy(packed.at[:, rows, :], out_ref.at[:, rows, :], out_sems.at[x])
        )
        stores[-1].start()
    for store in stores:
        store.wait()


def pack(q, k, v):
    packed = (HEADS, 3 * BLOCK, WIDTH)
    return kernel_call(
        pack_body,
        [(packed, BF16, "hbm")],
        ["hbm"] * 3,
        6,
        scratch=[pltpu.VMEM((3,) + q.shape, BF16), pltpu.VMEM(packed, BF16), dma(3), dma(3)],
        cost=cost(0, 6 * q.size * 2),
        name="pack_qkv",
    )(q, k, v)[0]


def att_grad_body(chunks, cot_ref, w_ref, out_ref, held, sems):
    rows = held.shape[0] // chunks
    copies = []
    for c in range(chunks):
        at = slice(c * rows, (c + 1) * rows)
        copies.append(pltpu.make_async_copy(w_ref.at[at, :], held.at[at, :], sems.at[c]))
        copies[-1].start()
    for c, copy in enumerate(copies):
        at = slice(c * rows, (c + 1) * rows)
        copy.wait()
        out_ref[:, at] = nt(cot_ref[...], held[at, :]).astype(BF16)


def attended_gradient(cot, w_out):
    chunks = 4
    return kernel_call(
        functools.partial(att_grad_body, chunks),
        [(cot.shape, BF16, "vmem")],
        ["vmem", "hbm"],
        14,
        scratch=[pltpu.VMEM(w_out.shape, BF16), dma(chunks)],
        cost=cost(2 * cot.size * w_out.shape[0], 9 << 20),
        name="attended_gradient",
    )(cot, w_out)[0]


def output_body(chunks, att_ref, w_ref, out_ref, att, lhs, held, total, att_sem, sems):
    rows = held.shape[0] // chunks
    att_copy = pltpu.make_async_copy(att_ref, att, att_sem.at[0])
    att_copy.start()
    copies = []
    for c in range(chunks):
        at = slice(c * rows, (c + 1) * rows)
        copies.append(pltpu.make_async_copy(w_ref.at[at, :], held.at[at, :], sems.at[c]))
        copies[-1].start()
    att_copy.wait()
    for h in range(HEADS):
        lhs[:, h * WIDTH : (h + 1) * WIDTH] = att[h]
    for c, copy in enumerate(copies):
        at = slice(c * rows, (c + 1) * rows)
        copy.wait()
        part = nn(lhs[:, at], held[at, :])
        if c == 0:
            total[...] = part
        elif c < chunks - 1:
            total[...] += part
        else:
            out_ref[...] = (total[...] + part).astype(BF16)


def project(att, w_out):
    chunks = 8
    rows, columns = w_out.shape
    return kernel_call(
        functools.partial(output_body, chunks),
        [((BLOCK, columns), BF16, "vmem")],
        ["hbm", "hbm"],
        16,
        scratch=[
            pltpu.VMEM(att.shape, BF16),
            pltpu.VMEM((BLOCK, rows), BF16),
            pltpu.VMEM((rows, columns), BF16),
            pltpu.VMEM((BLOCK, columns), F32),
            dma(1),
            dma(chunks),
        ],
        cost=cost(2 * BLOCK * rows * columns, 9 << 20),
        name="output_projection",
    )(att, w_out)[0]


def forward_body(
    blocks, in_ref, grad_ref, out_ref, att_out, lse_out, lev_out,
    lse_ref, lev_ref, fq, mu, du, nu, sems,
):
    tokens = blocks * BLOCK
    spans, _ = level_rows(tokens)
    copies = []

    def send(source, target):
        copies.append(pltpu.make_async_copy(source, target, sems.at[len(copies)]))
        copies[-1].start()

    scale = 1.0 / math.sqrt(WIDTH)
    for b in range(blocks):
        out_ref[b, 0:BLOCK, :] = grad_ref[:, b * WIDTH : (b + 1) * WIDTH]
        for x in range(3):
            part = in_ref[b, x * BLOCK : (x + 1) * BLOCK, :]
            lev_ref[x, b * BLOCK : (b + 1) * BLOCK, :] = part
            fq[x, b * BLOCK : (b + 1) * BLOCK, :] = part.astype(F32)
    for height in range(1, LEVELS + 1):
        below, _ = spans[height - 1]
        base, rows = spans[height]
        step = min(CHUNK, rows)
        for x in range(3):
            for r in range(0, rows, step):
                mean = (
                    evens(fq.at[x], below + 2 * r, step) + odds(fq.at[x], below + 2 * r, step)
                ) * 0.5
                mean = mean.astype(BF16)
                lev_ref[x, base + r : base + r + step, :] = mean
                fq[x, base + r : base + r + step, :] = mean.astype(F32)

    send(lev_ref, lev_out)

    def attend(q, k, v, factor):
        scores = nt(q, k) * scale
        top = wide(jnp.max(scores, axis=1, keepdims=True))
        shift = jnp.concatenate([top] * (k.shape[0] // WIDTH), axis=1)
        expo = jnp.exp(scores - shift)
        denom = wide(jnp.sum(expo, axis=1, keepdims=True))
        numer = nn(expo.astype(BF16), v)
        if factor != 1:
            denom, numer = denom * factor, numer * factor
        return top, denom, numer

    def merge(height, row, stats):
        top, denom, numer = stats
        base, _ = spans[height]
        rows = top.shape[0]
        at = slice(base + row, base + row + rows)
        if height < LEVELS:
            up = mu[at, :]
            peak = jnp.maximum(top, up)
            mine, theirs = jnp.exp(top - peak), jnp.exp(up - peak)
            denom = mine * denom + theirs * du[at, :]
            numer = mine * numer + theirs * nu[at, :]
            top = peak
        return top, denom, numer

    for height in range(LEVELS, 0, -1):
        base, rows = spans[height]
        fine, _ = spans[height - 1]
        for row in range(0, rows, BLOCK):
            far = base + (row ^ BLOCK)
            stats = attend(
                lev_ref[0, base + row : base + row + BLOCK, :],
                lev_ref[1, far : far + BLOCK, :],
                lev_ref[2, far : far + BLOCK, :],
                float(2**height),
            )
            merged = merge(height, row, stats)
            for ref, value in zip((mu, du, nu), merged):
                put_twice(ref, fine + 2 * row, value)
    for row in range(0, tokens, 2 * BLOCK):
        at = slice(row, row + 2 * BLOCK)
        stats = attend(lev_ref[0, at, :], lev_ref[1, at, :], lev_ref[2, at, :], 1)
        peak, total, summed = merge(0, row, stats)
        attended = (summed / total).astype(BF16)
        lse_ref[at, :] = peak + jnp.log(total)
        pair = slice(row // BLOCK, row // BLOCK + 2)
        out_ref[row // BLOCK, BLOCK:, :] = attended[:BLOCK]
        out_ref[row // BLOCK + 1, BLOCK:, :] = attended[BLOCK:]
        send(lse_ref.at[at, :], lse_out.at[at, :])
        send(out_ref.at[pair, BLOCK:, :], att_out.at[pair, :, :])
    for copy in copies:
        copy.wait()


def forward(qkv, att_grad):
    blocks = qkv.shape[0]
    tokens = blocks * BLOCK
    spans, total_rows = level_rows(tokens)
    finer = total_rows - spans[LEVELS][1]
    outs = [
        ((blocks, 2 * BLOCK, WIDTH), BF16, "vmem"),
        ((blocks, BLOCK, WIDTH), BF16, "hbm"),
        ((tokens, WIDTH), F32, "hbm"),
        ((3, total_rows, WIDTH), BF16, "hbm"),
    ]
    return kernel_call(
        functools.partial(forward_body, blocks),
        outs,
        ["vmem"] * 2,
        32,
        scratch=[
            pltpu.VMEM((tokens, WIDTH), F32),
            pltpu.VMEM((3, total_rows, WIDTH), BF16),
            pltpu.VMEM((3, total_rows, WIDTH), F32),
            pltpu.VMEM((finer, WIDTH), F32),
            pltpu.VMEM((finer, WIDTH), F32),
            pltpu.VMEM((finer, WIDTH), F32),
            dma(1 + blocks),
        ],
        cost=cost(4 * tokens * 384 * WIDTH, 8 << 20),
        name="head_forward",
    )(qkv, att_grad)


def backward_body(
    blocks, grad_in, att_in, lse_in, lev_in, out_ref,
    att_ref, lev_ref, ys, ds, rs, cg, up, sems,
):
    tokens = blocks * BLOCK
    spans, total_rows = level_rows(tokens)
    scale = 1.0 / math.sqrt(WIDTH)
    parts, count = 4, [0]

    def fetch(source, target):
        copy = pltpu.make_async_copy(source, target, sems.at[count[0]])
        count[0] += 1
        copy.start()
        return copy

    first_loads = []
    for p in range(parts):
        some = slice(p * blocks // parts, (p + 1) * blocks // parts)
        at = slice(p * tokens // parts, (p + 1) * tokens // parts)
        first_loads.append(
            [
                fetch(grad_in.at[at, :], cg.at[at, :]),
                fetch(att_in.at[some, :, :], att_ref.at[some, :, :]),
                fetch(lse_in.at[at, :], rs.at[at, :]),
            ]
        )
    coarse = slice(tokens, total_rows)
    later_loads = [
        fetch(lev_in.at[:, coarse, :], lev_ref.at[:, coarse, :]),
        fetch(lev_in.at[:, :tokens, :], lev_ref.at[:, :tokens, :]),
    ]
    for b in range(blocks):
        if b % (blocks // parts) == 0:
            for copy in first_loads[b // (blocks // parts)]:
                copy.wait()
        at = slice(b * BLOCK, (b + 1) * BLOCK)
        grad = cg[at, :].astype(F32)
        ys[at, :] = grad
        ds[at, :] = wide(jnp.sum(grad * att_ref[b].astype(F32), axis=1, keepdims=True))
    for height in range(1, LEVELS + 1):
        below, _ = spans[height - 1]
        base, rows = spans[height]
        for r in range(0, rows, BLOCK):
            at = slice(base + r, base + r + BLOCK)
            first = below + 2 * r
            lo, hi = evens(rs, first, BLOCK), odds(rs, first, BLOCK)
            low = jnp.minimum(lo, hi)
            lo, hi = jnp.exp(low - lo), jnp.exp(low - hi)
            grad = lo * evens(ys, first, BLOCK) + hi * odds(ys, first, BLOCK)
            delta = lo * evens(ds, first, BLOCK) + hi * odds(ds, first, BLOCK)
            ys[at, :], ds[at, :], rs[at, :] = grad, delta, low
            cg[at, :] = grad.astype(BF16)

    def gradients(rows, keys):
        q, grad = lev_ref[0, rows, :], cg[rows, :]
        k, v = lev_ref[1, keys, :], lev_ref[2, keys, :]
        times = k.shape[0] // WIDTH
        low = jnp.concatenate([rs[rows, :]] * times, axis=1)
        resid = jnp.concatenate([ds[rows, :]] * times, axis=1)
        expo = jnp.exp(nt(q, k) * scale - low)
        sgrad = (expo * (nt(grad, v) - resid) * scale).astype(BF16)
        return nn(sgrad, k), tn(sgrad, q), tn(expo.astype(BF16), grad)

    later_loads[0].wait()
    for height in range(LEVELS, 0, -1):
        base, rows = spans[height]
        fine, _ = spans[height - 1]
        for row in range(0, rows, BLOCK):
            near, far = base + row, base + (row ^ BLOCK)
            near = slice(near, near + BLOCK)
            far = slice(far, far + BLOCK)
            q_part, k_part, v_part = gradients(near, far)
            for x, (at, first, value) in enumerate(
                (
                    (near, row, q_part),
                    (far, row ^ BLOCK, k_part),
                    (far, row ^ BLOCK, v_part),
                )
            ):
                if height < LEVELS:
                    value = value + up[x, at, :]
                put_twice(up.at[x], fine + 2 * first, value)
    later_loads[1].wait()
    for row in range(0, tokens, 2 * BLOCK):
        at = slice(row, row + 2 * BLOCK)
        for x, value in enumerate(gradients(at, at)):
            value = (value + up[x, at, :]).astype(BF16)
            for half in range(2):
                out_ref[row // BLOCK + half, x * BLOCK : (x + 1) * BLOCK, :] = value[
                    half * BLOCK : (half + 1) * BLOCK
                ]


def backward(grad, att, lse, lev):
    blocks = att.shape[0]
    tokens = blocks * BLOCK
    spans, total_rows = level_rows(tokens)
    finer = total_rows - spans[LEVELS][1]
    return kernel_call(
        functools.partial(backward_body, blocks),
        [((blocks, 3 * BLOCK, WIDTH), BF16, "vmem")],
        ["hbm"] * 4,
        32,
        scratch=[
            pltpu.VMEM(att.shape, BF16),
            pltpu.VMEM(lev.shape, BF16),
            pltpu.VMEM((total_rows, WIDTH), F32),
            pltpu.VMEM((total_rows, WIDTH), F32),
            pltpu.VMEM((total_rows, WIDTH), F32),
            pltpu.VMEM((total_rows, WIDTH), BF16),
            pltpu.VMEM((3, finer, WIDTH), F32),
            dma(14),
        ],
        cost=cost(10 * tokens * 384 * WIDTH, 12 << 20),
        name="head_backward",
    )(grad.reshape(tokens, WIDTH), att, lse, lev)[0]


def tile_body(groups, per, chunks, grads_ref, att_ref, cot_ref, _, out_ref, lhs, held, sems):
    rows = per * WIDTH
    chunk = rows // HEADS
    width = held.shape[2]
    copies = []
    for c in range(chunks):
        at = slice(c * width, (c + 1) * width)
        copies.append(pltpu.make_async_copy(cot_ref.at[:, at], held.at[c], sems.at[c]))
        copies[-1].start()
    out_ref[:, : 3 * BLOCK, :] = grads_ref[...]
    for o in range(groups):
        for j in range(per):
            lhs[o * BLOCK : (o + 1) * BLOCK, j * WIDTH : (j + 1) * WIDTH] = att_ref[o * per + j]
    for c, copy in enumerate(copies):
        copy.wait()
        part = tn(lhs[...], held[c]).astype(BF16)
        for i in range(HEADS):
            for j in range(width // WIDTH):
                at = 3 * BLOCK + (c * width // WIDTH + j) * chunk
                out_ref[i, at : at + chunk, :] = part[
                    i * chunk : (i + 1) * chunk, j * WIDTH : (j + 1) * WIDTH
                ]


def with_tile(grads, att, cot, after):
    chunks = 4
    groups = cot.shape[0] // BLOCK
    per = HEADS // groups
    chunk = per * WIDTH // HEADS
    extra = chunk * (cot.shape[1] // WIDTH)
    return kernel_call(
        functools.partial(tile_body, groups, per, chunks),
        [((HEADS, 3 * BLOCK + extra, WIDTH), BF16, "vmem")],
        ["vmem", "vmem", "hbm", "hbm"],
        16,
        scratch=[
            pltpu.VMEM((groups * BLOCK, per * WIDTH), BF16),
            pltpu.VMEM((chunks, cot.shape[0], cot.shape[1] // chunks), BF16),
            dma(chunks),
        ],
        cost=cost(2 * cot.shape[0] * per * WIDTH * cot.shape[1], 10 << 20),
        name="projection_tile",
    )(grads, att, cot, after)[0]


def unpack_body(scale, in_ref, q_ref, k_ref, v_ref, w_ref):
    chunk, width = w_ref.shape
    for h in range(HEADS):
        for x, ref in enumerate((q_ref, k_ref, v_ref)):
            ref[:, h * WIDTH : (h + 1) * WIDTH] = in_ref[h, x * BLOCK : (x + 1) * BLOCK, :]
    for c in range(width // WIDTH):
        at = 3 * BLOCK + c * chunk
        total = in_ref[0, at : at + chunk, :].astype(F32)
        for h in range(1, HEADS):
            total = total + in_ref[h, at : at + chunk, :].astype(F32)
        w_ref[:, c * WIDTH : (c + 1) * WIDTH] = total * scale


def unpack(got, scale):
    chunk = (got.shape[1] - 3 * BLOCK) // HEADS
    width = HEADS * WIDTH
    return kernel_call(
        functools.partial(unpack_body, scale),
        [((BLOCK, width), BF16, "vmem")] * 3 + [((chunk, width), F32, "vmem")],
        ["vmem"],
        8,
        cost=cost(0, 6 << 20),
        name="unpack_grads",
    )(got)


def split_body(got_ref, grad_ref, att_ref, sems):
    copies = [
        pltpu.make_async_copy(got_ref.at[:, BLOCK:, :], att_ref, sems.at[0]),
        pltpu.make_async_copy(got_ref.at[:, :BLOCK, :], grad_ref, sems.at[1]),
    ]
    for copy in copies:
        copy.start()
    for copy in copies:
        copy.wait()


def split(got):
    return kernel_call(
        split_body,
        [((HEADS, BLOCK, WIDTH), BF16, "hbm")] * 2,
        ["vmem"],
        2,
        scratch=[dma(2)],
        cost=cost(0, 2 << 20),
        name="split_attended",
    )(got)


def swap(value, axis):
    return lax.all_to_all(value, axis, 0, 0, tiled=True)


def on_device(query_in, key_in, value_in, w_out, cotangent):
    tokens = query_in.shape[0] * lax.axis_size(("outer", "inner"))
    cot_outer = lax.all_gather(cotangent, "outer", axis=0, tiled=True)
    qkv = swap(pack(query_in, key_in, value_in), "inner")
    att_grad = attended_gradient(cotangent, w_out)
    sent, att_own, lse, lev = forward(qkv, att_grad)
    grad, att = split(swap(sent, "inner"))
    att_outer = swap(att, "outer")
    grads = backward(grad, att_own, lse, lev)
    output = project(att, w_out)
    last = swap(with_tile(grads, att_outer, cot_outer, output), "inner")
    query_grad, key_grad, value_grad, w_out_grad = unpack(last, 1.0 / math.sqrt(tokens))
    return output, query_grad, key_grad, value_grad, w_out_grad


def solution(mesh):
    rows = P(("outer", "inner"), None)
    return jax.shard_map(
        on_device,
        mesh=mesh,
        in_specs=(rows, rows, rows, P(), rows),
        out_specs=(rows,) * 5,
        check_vma=False,
    )
```

```python
import functools
import math

import jax
import jax.numpy as jnp
from jax import lax
from jax.experimental import pallas as pl
from jax.experimental.pallas import tpu as pltpu
from jax.sharding import PartitionSpec as P

HEADS = 16
BLOCK = 128
LEVELS = 3
WIDTH = 128
BF16 = jnp.bfloat16
F32 = jnp.float32
CHUNK = 256


def nt(a, b):
    return lax.dot_general(a, b, (((1,), (1,)), ((), ())), preferred_element_type=F32)


def nn(a, b):
    return lax.dot_general(a, b, (((1,), (0,)), ((), ())), preferred_element_type=F32)


def tn(a, b):
    return lax.dot_general(a, b, (((0,), (0,)), ((), ())), preferred_element_type=F32)


def wide(stat, columns=WIDTH):
    return jnp.broadcast_to(stat, (stat.shape[0], columns))


def evens(ref, base, rows):
    return ref[pl.ds(base, rows, stride=2), :]


def odds(ref, base, rows):
    return ref[pl.ds(base + 1, rows, stride=2), :]


def put_twice(ref, base, value):
    rows = value.shape[0]
    ref[pl.ds(base, rows, stride=2), :] = value
    ref[pl.ds(base + 1, rows, stride=2), :] = value


def level_rows(tokens):
    out, base = [], 0
    for height in range(LEVELS + 1):
        out.append((base, tokens >> height))
        base += tokens >> height
    return out, base


def kernel_call(body, outs, in_places, mib, scratch=(), cost=None, name=None):
    spec = {
        "vmem": pl.BlockSpec(memory_space=pltpu.VMEM),
        "hbm": pl.BlockSpec(memory_space=pl.ANY),
    }
    shapes = [
        pltpu.HBM(shape, dtype) if place == "hbm" else jax.ShapeDtypeStruct(shape, dtype)
        for shape, dtype, place in outs
    ]
    call = pl.pallas_call(
        body,
        out_shape=shapes,
        in_specs=[spec[place] for place in in_places],
        out_specs=[spec[place] for _, _, place in outs],
        scratch_shapes=list(scratch),
        compiler_params=pltpu.CompilerParams(vmem_limit_bytes=mib << 20),
        cost_estimate=cost,
        name=name,
    )

    def run(*operands):
        operands = [
            pltpu.with_memory_space_constraint(x, pltpu.HBM) if place == "hbm" else x
            for x, place in zip(operands, in_places)
        ]
        return call(*operands)

    return run


def dma(count):
    return pltpu.SemaphoreType.DMA((count,))


def cost(flops, nbytes):
    return pl.CostEstimate(flops=int(flops), bytes_accessed=int(nbytes), transcendentals=0)


def pack_body(q_ref, k_ref, v_ref, out_ref, held, packed, in_sems, out_sems):
    loads = [
        pltpu.make_async_copy(ref, held.at[x], in_sems.at[x])
        for x, ref in enumerate((q_ref, k_ref, v_ref))
    ]
    for load in loads:
        load.start()
    stores = []
    for x, load in enumerate(loads):
        load.wait()
        rows = slice(x * BLOCK, (x + 1) * BLOCK)
        for h in range(HEADS):
            packed[h, rows, :] = held[x, :, h * WIDTH : (h + 1) * WIDTH]
        stores.append(
            pltpu.make_async_copy(packed.at[:, rows, :], out_ref.at[:, rows, :], out_sems.at[x])
        )
        stores[-1].start()
    for store in stores:
        store.wait()


def pack(q, k, v):
    packed = (HEADS, 3 * BLOCK, WIDTH)
    return kernel_call(
        pack_body,
        [(packed, BF16, "hbm")],
        ["hbm"] * 3,
        6,
        scratch=[pltpu.VMEM((3,) + q.shape, BF16), pltpu.VMEM(packed, BF16), dma(3), dma(3)],
        cost=cost(0, 6 * q.size * 2),
        name="pack_qkv",
    )(q, k, v)[0]


def att_grad_body(chunks, cot_ref, w_ref, out_ref, held, sems):
    rows = held.shape[0] // chunks
    copies = []
    for c in range(chunks):
        at = slice(c * rows, (c + 1) * rows)
        copies.append(pltpu.make_async_copy(w_ref.at[at, :], held.at[at, :], sems.at[c]))
        copies[-1].start()
    for c, copy in enumerate(copies):
        at = slice(c * rows, (c + 1) * rows)
        copy.wait()
        out_ref[:, at] = nt(cot_ref[...], held[at, :]).astype(BF16)


def attended_gradient(cot, w_out):
    chunks = 4
    return kernel_call(
        functools.partial(att_grad_body, chunks),
        [(cot.shape, BF16, "vmem")],
        ["vmem", "hbm"],
        14,
        scratch=[pltpu.VMEM(w_out.shape, BF16), dma(chunks)],
        cost=cost(2 * cot.size * w_out.shape[0], 9 << 20),
        name="attended_gradient",
    )(cot, w_out)[0]


def forward_body(
    blocks, in_ref, grad_ref, out_ref, att_out, lse_out, lev_out,
    lse_ref, lev_ref, fq, mu, du, nu, sems,
):
    tokens = blocks * BLOCK
    spans, _ = level_rows(tokens)
    copies = []

    def send(source, target):
        copies.append(pltpu.make_async_copy(source, target, sems.at[len(copies)]))
        copies[-1].start()

    scale = 1.0 / math.sqrt(WIDTH)
    for b in range(blocks):
        out_ref[b, 0:BLOCK, :] = grad_ref[:, b * WIDTH : (b + 1) * WIDTH]
        for x in range(3):
            part = in_ref[b, x * BLOCK : (x + 1) * BLOCK, :]
            lev_ref[x, b * BLOCK : (b + 1) * BLOCK, :] = part
            fq[x, b * BLOCK : (b + 1) * BLOCK, :] = part.astype(F32)
    for height in range(1, LEVELS + 1):
        below, _ = spans[height - 1]
        base, rows = spans[height]
        step = min(CHUNK, rows)
        for x in range(3):
            for r in range(0, rows, step):
                mean = (
                    evens(fq.at[x], below + 2 * r, step) + odds(fq.at[x], below + 2 * r, step)
                ) * 0.5
                mean = mean.astype(BF16)
                lev_ref[x, base + r : base + r + step, :] = mean
                fq[x, base + r : base + r + step, :] = mean.astype(F32)

    send(lev_ref, lev_out)

    def attend(q, k, v, factor):
        scores = nt(q, k) * scale
        top = wide(jnp.max(scores, axis=1, keepdims=True))
        shift = jnp.concatenate([top] * (k.shape[0] // WIDTH), axis=1)
        expo = jnp.exp(scores - shift)
        denom = wide(jnp.sum(expo, axis=1, keepdims=True))
        numer = nn(expo.astype(BF16), v)
        if factor != 1:
            denom, numer = denom * factor, numer * factor
        return top, denom, numer

    def merge(height, row, stats):
        top, denom, numer = stats
        base, _ = spans[height]
        rows = top.shape[0]
        at = slice(base + row, base + row + rows)
        if height < LEVELS:
            up = mu[at, :]
            peak = jnp.maximum(top, up)
            mine, theirs = jnp.exp(top - peak), jnp.exp(up - peak)
            denom = mine * denom + theirs * du[at, :]
            numer = mine * numer + theirs * nu[at, :]
            top = peak
        return top, denom, numer

    for height in range(LEVELS, 0, -1):
        base, rows = spans[height]
        fine, _ = spans[height - 1]
        for row in range(0, rows, BLOCK):
            far = base + (row ^ BLOCK)
            stats = attend(
                lev_ref[0, base + row : base + row + BLOCK, :],
                lev_ref[1, far : far + BLOCK, :],
                lev_ref[2, far : far + BLOCK, :],
                float(2**height),
            )
            merged = merge(height, row, stats)
            for ref, value in zip((mu, du, nu), merged):
                put_twice(ref, fine + 2 * row, value)
    for row in range(0, tokens, 2 * BLOCK):
        at = slice(row, row + 2 * BLOCK)
        stats = attend(lev_ref[0, at, :], lev_ref[1, at, :], lev_ref[2, at, :], 1)
        peak, total, summed = merge(0, row, stats)
        attended = (summed / total).astype(BF16)
        lse_ref[at, :] = peak + jnp.log(total)
        pair = slice(row // BLOCK, row // BLOCK + 2)
        out_ref[row // BLOCK, BLOCK:, :] = attended[:BLOCK]
        out_ref[row // BLOCK + 1, BLOCK:, :] = attended[BLOCK:]
        send(lse_ref.at[at, :], lse_out.at[at, :])
        send(out_ref.at[pair, BLOCK:, :], att_out.at[pair, :, :])
    for copy in copies:
        copy.wait()


def forward(qkv, att_grad):
    blocks = qkv.shape[0]
    tokens = blocks * BLOCK
    spans, total_rows = level_rows(tokens)
    finer = total_rows - spans[LEVELS][1]
    outs = [
        ((blocks, 2 * BLOCK, WIDTH), BF16, "vmem"),
        ((blocks, BLOCK, WIDTH), BF16, "hbm"),
        ((tokens, WIDTH), F32, "hbm"),
        ((3, total_rows, WIDTH), BF16, "hbm"),
    ]
    return kernel_call(
        functools.partial(forward_body, blocks),
        outs,
        ["vmem"] * 2,
        32,
        scratch=[
            pltpu.VMEM((tokens, WIDTH), F32),
            pltpu.VMEM((3, total_rows, WIDTH), BF16),
            pltpu.VMEM((3, total_rows, WIDTH), F32),
            pltpu.VMEM((finer, WIDTH), F32),
            pltpu.VMEM((finer, WIDTH), F32),
            pltpu.VMEM((finer, WIDTH), F32),
            dma(1 + blocks),
        ],
        cost=cost(4 * tokens * 384 * WIDTH, 8 << 20),
        name="head_forward",
    )(qkv, att_grad)


def backward_body(
    blocks, grad_in, att_in, lse_in, lev_in, rows_in, w_in, cot_in, out_ref, output_ref, cot_ref,
    att_ref, lev_ref, ys, ds, rs, cg, up, rows_ref, w_ref, sems,
):
    tokens = blocks * BLOCK
    spans, total_rows = level_rows(tokens)
    scale = 1.0 / math.sqrt(WIDTH)
    parts, count = 4, [0]

    def fetch(source, target):
        copy = pltpu.make_async_copy(source, target, sems.at[count[0]])
        count[0] += 1
        copy.start()
        return copy

    first_loads = []
    for p in range(parts):
        some = slice(p * blocks // parts, (p + 1) * blocks // parts)
        at = slice(p * tokens // parts, (p + 1) * tokens // parts)
        first_loads.append(
            [
                fetch(grad_in.at[at, :], cg.at[at, :]),
                fetch(att_in.at[some, :, :], att_ref.at[some, :, :]),
                fetch(lse_in.at[at, :], rs.at[at, :]),
            ]
        )
    coarse = slice(tokens, total_rows)
    later_loads = [
        fetch(lev_in.at[:, coarse, :], lev_ref.at[:, coarse, :]),
        fetch(lev_in.at[:, :tokens, :], lev_ref.at[:, :tokens, :]),
        fetch(rows_in, rows_ref),
        fetch(w_in, w_ref),
        fetch(cot_in, cot_ref),
    ]
    for b in range(blocks):
        if b % (blocks // parts) == 0:
            for copy in first_loads[b // (blocks // parts)]:
                copy.wait()
        at = slice(b * BLOCK, (b + 1) * BLOCK)
        grad = cg[at, :].astype(F32)
        ys[at, :] = grad
        ds[at, :] = wide(jnp.sum(grad * att_ref[b].astype(F32), axis=1, keepdims=True))
    for height in range(1, LEVELS + 1):
        below, _ = spans[height - 1]
        base, rows = spans[height]
        for r in range(0, rows, BLOCK):
            at = slice(base + r, base + r + BLOCK)
            first = below + 2 * r
            lo, hi = evens(rs, first, BLOCK), odds(rs, first, BLOCK)
            low = jnp.minimum(lo, hi)
            lo, hi = jnp.exp(low - lo), jnp.exp(low - hi)
            grad = lo * evens(ys, first, BLOCK) + hi * odds(ys, first, BLOCK)
            delta = lo * evens(ds, first, BLOCK) + hi * odds(ds, first, BLOCK)
            ys[at, :], ds[at, :], rs[at, :] = grad, delta, low
            cg[at, :] = grad.astype(BF16)

    def gradients(rows, keys):
        q, grad = lev_ref[0, rows, :], cg[rows, :]
        k, v = lev_ref[1, keys, :], lev_ref[2, keys, :]
        times = k.shape[0] // WIDTH
        low = jnp.concatenate([rs[rows, :]] * times, axis=1)
        resid = jnp.concatenate([ds[rows, :]] * times, axis=1)
        expo = jnp.exp(nt(q, k) * scale - low)
        sgrad = (expo * (nt(grad, v) - resid) * scale).astype(BF16)
        return nn(sgrad, k), tn(sgrad, q), tn(expo.astype(BF16), grad)

    later_loads[0].wait()
    for height in range(LEVELS, 0, -1):
        base, rows = spans[height]
        fine, _ = spans[height - 1]
        for row in range(0, rows, BLOCK):
            near, far = base + row, base + (row ^ BLOCK)
            near = slice(near, near + BLOCK)
            far = slice(far, far + BLOCK)
            q_part, k_part, v_part = gradients(near, far)
            for x, (at, first, value) in enumerate(
                (
                    (near, row, q_part),
                    (far, row ^ BLOCK, k_part),
                    (far, row ^ BLOCK, v_part),
                )
            ):
                if height < LEVELS:
                    value = value + up[x, at, :]
                put_twice(up.at[x], fine + 2 * first, value)
    later_loads[1].wait()
    for row in range(0, tokens, 2 * BLOCK):
        at = slice(row, row + 2 * BLOCK)
        for x, value in enumerate(gradients(at, at)):
            value = (value + up[x, at, :]).astype(BF16)
            for half in range(2):
                out_ref[row // BLOCK + half, x * BLOCK : (x + 1) * BLOCK, :] = value[
                    half * BLOCK : (half + 1) * BLOCK
                ]
    later_loads[2].wait()
    later_loads[3].wait()
    rows = jnp.concatenate([rows_ref[h] for h in range(HEADS)], axis=1)
    width = w_ref.shape[1]
    for first in range(0, width, 512):
        at = slice(first, first + 512)
        output_ref[:, at] = nn(rows, w_ref[:, at]).astype(BF16)
    later_loads[4].wait()


def backward(grad, att, lse, lev, rows, w_out, cot):
    blocks = att.shape[0]
    tokens = blocks * BLOCK
    spans, total_rows = level_rows(tokens)
    finer = total_rows - spans[LEVELS][1]
    return kernel_call(
        functools.partial(backward_body, blocks),
        [
            ((blocks, 3 * BLOCK, WIDTH), BF16, "vmem"),
            ((BLOCK, w_out.shape[1]), BF16, "vmem"),
            (cot.shape, BF16, "vmem"),
        ],
        ["hbm"] * 7,
        44,
        scratch=[
            pltpu.VMEM(att.shape, BF16),
            pltpu.VMEM(lev.shape, BF16),
            pltpu.VMEM((total_rows, WIDTH), F32),
            pltpu.VMEM((total_rows, WIDTH), F32),
            pltpu.VMEM((total_rows, WIDTH), F32),
            pltpu.VMEM((total_rows, WIDTH), BF16),
            pltpu.VMEM((3, finer, WIDTH), F32),
            pltpu.VMEM(rows.shape, BF16),
            pltpu.VMEM(w_out.shape, BF16),
            dma(17),
        ],
        cost=cost(10 * tokens * 384 * WIDTH + 2 * BLOCK * w_out.size, 24 << 20),
        name="head_backward",
    )(grad.reshape(tokens, WIDTH), att, lse, lev, rows, w_out, cot)


def tile_body(groups, per, grads_ref, att_ref, cot_ref, out_ref, lhs):
    rows = per * WIDTH
    chunk = rows // HEADS
    out_ref[:, : 3 * BLOCK, :] = grads_ref[...]
    for o in range(groups):
        for j in range(per):
            lhs[o * BLOCK : (o + 1) * BLOCK, j * WIDTH : (j + 1) * WIDTH] = att_ref[o * per + j]
    for first in range(0, cot_ref.shape[1], 512):
        part = tn(lhs[...], cot_ref[:, first : first + 512]).astype(BF16)
        for i in range(HEADS):
            for j in range(512 // WIDTH):
                at = 3 * BLOCK + (first // WIDTH + j) * chunk
                out_ref[i, at : at + chunk, :] = part[
                    i * chunk : (i + 1) * chunk, j * WIDTH : (j + 1) * WIDTH
                ]


def with_tile(grads, att, cot):
    groups = cot.shape[0] // BLOCK
    per = HEADS // groups
    chunk = per * WIDTH // HEADS
    extra = chunk * (cot.shape[1] // WIDTH)
    return kernel_call(
        functools.partial(tile_body, groups, per),
        [((HEADS, 3 * BLOCK + extra, WIDTH), BF16, "vmem")],
        ["vmem"] * 3,
        12,
        scratch=[pltpu.VMEM((groups * BLOCK, per * WIDTH), BF16)],
        cost=cost(2 * cot.shape[0] * per * WIDTH * cot.shape[1], 10 << 20),
        name="projection_tile",
    )(grads, att, cot)[0]


def unpack_body(scale, in_ref, q_ref, k_ref, v_ref, w_ref):
    chunk, width = w_ref.shape
    for h in range(HEADS):
        for x, ref in enumerate((q_ref, k_ref, v_ref)):
            ref[:, h * WIDTH : (h + 1) * WIDTH] = in_ref[h, x * BLOCK : (x + 1) * BLOCK, :]
    for c in range(width // WIDTH):
        at = 3 * BLOCK + c * chunk
        total = in_ref[0, at : at + chunk, :].astype(F32)
        for h in range(1, HEADS):
            total = total + in_ref[h, at : at + chunk, :].astype(F32)
        w_ref[:, c * WIDTH : (c + 1) * WIDTH] = total * scale


def unpack(got, scale):
    chunk = (got.shape[1] - 3 * BLOCK) // HEADS
    width = HEADS * WIDTH
    return kernel_call(
        functools.partial(unpack_body, scale),
        [((BLOCK, width), BF16, "vmem")] * 3 + [((chunk, width), F32, "vmem")],
        ["vmem"],
        8,
        cost=cost(0, 6 << 20),
        name="unpack_grads",
    )(got)


def split_body(got_ref, grad_ref, att_ref, sems):
    copies = [
        pltpu.make_async_copy(got_ref.at[:, BLOCK:, :], att_ref, sems.at[0]),
        pltpu.make_async_copy(got_ref.at[:, :BLOCK, :], grad_ref, sems.at[1]),
    ]
    for copy in copies:
        copy.start()
    for copy in copies:
        copy.wait()


def split(got):
    return kernel_call(
        split_body,
        [((HEADS, BLOCK, WIDTH), BF16, "hbm")] * 2,
        ["vmem"],
        2,
        scratch=[dma(2)],
        cost=cost(0, 2 << 20),
        name="split_attended",
    )(got)


def swap(value, axis):
    return lax.all_to_all(value, axis, 0, 0, tiled=True)


def on_device(query_in, key_in, value_in, w_out, cotangent):
    tokens = query_in.shape[0] * lax.axis_size(("outer", "inner"))
    cot_outer = lax.all_gather(cotangent, "outer", axis=0, tiled=True)
    qkv = swap(pack(query_in, key_in, value_in), "inner")
    att_grad = attended_gradient(cotangent, w_out)
    sent, att_own, lse, lev = forward(qkv, att_grad)
    grad, att = split(swap(sent, "inner"))
    att_outer = swap(att, "outer")
    grads, output, cot_near = backward(grad, att_own, lse, lev, att, w_out, cot_outer)
    last = swap(with_tile(grads, att_outer, cot_near), "inner")
    query_grad, key_grad, value_grad, w_out_grad = unpack(last, 1.0 / math.sqrt(tokens))
    return output, query_grad, key_grad, value_grad, w_out_grad


def solution(mesh):
    rows = P(("outer", "inner"), None)
    return jax.shard_map(
        on_device,
        mesh=mesh,
        in_specs=(rows, rows, rows, P(), rows),
        out_specs=(rows,) * 5,
        check_vma=False,
    )
```

```python
import functools
import math

import jax
import jax.numpy as jnp
from jax import lax
from jax.experimental import pallas as pl
from jax.experimental.pallas import tpu as pltpu
from jax.sharding import PartitionSpec as P

HEADS = 16
BLOCK = 128
LEVELS = 3
WIDTH = 128
BF16 = jnp.bfloat16
F32 = jnp.float32
CHUNK = 256
PAIRS = 8


def nt(a, b):
    return lax.dot_general(a, b, (((1,), (1,)), ((), ())), preferred_element_type=F32)


def nn(a, b):
    return lax.dot_general(a, b, (((1,), (0,)), ((), ())), preferred_element_type=F32)


def tn(a, b):
    return lax.dot_general(a, b, (((0,), (0,)), ((), ())), preferred_element_type=F32)


def wide(stat, columns=WIDTH):
    return jnp.broadcast_to(stat, (stat.shape[0], columns))


def evens(ref, base, rows):
    return ref[pl.ds(base, rows, stride=2), :]


def odds(ref, base, rows):
    return ref[pl.ds(base + 1, rows, stride=2), :]


def put_twice(ref, base, value):
    rows = value.shape[0]
    ref[pl.ds(base, rows, stride=2), :] = value
    ref[pl.ds(base + 1, rows, stride=2), :] = value


def across(stat, columns):
    return jnp.concatenate([stat] * (columns // WIDTH), axis=1)


def coarse_blocks(tokens):
    spans, _ = level_rows(tokens)
    out = []
    for height in range(LEVELS, 0, -1):
        base, rows = spans[height]
        for row in range(0, rows, BLOCK):
            near, far = base + row, base + (row ^ BLOCK)
            out.append((height, row, slice(near, near + BLOCK), slice(far, far + BLOCK)))
    return out


def level_rows(tokens):
    out, base = [], 0
    for height in range(LEVELS + 1):
        out.append((base, tokens >> height))
        base += tokens >> height
    return out, base


def kernel_call(body, outs, in_places, mib, scratch=(), cost=None, name=None):
    spec = {
        "vmem": pl.BlockSpec(memory_space=pltpu.VMEM),
        "hbm": pl.BlockSpec(memory_space=pl.ANY),
    }
    shapes = [
        pltpu.HBM(shape, dtype) if place == "hbm" else jax.ShapeDtypeStruct(shape, dtype)
        for shape, dtype, place in outs
    ]
    call = pl.pallas_call(
        body,
        out_shape=shapes,
        in_specs=[spec[place] for place in in_places],
        out_specs=[spec[place] for _, _, place in outs],
        scratch_shapes=list(scratch),
        compiler_params=pltpu.CompilerParams(vmem_limit_bytes=mib << 20),
        cost_estimate=cost,
        name=name,
    )

    def run(*operands):
        operands = [
            pltpu.with_memory_space_constraint(x, pltpu.HBM) if place == "hbm" else x
            for x, place in zip(operands, in_places)
        ]
        return call(*operands)

    return run


def dma(count):
    return pltpu.SemaphoreType.DMA((count,))


def cost(flops, nbytes):
    return pl.CostEstimate(flops=int(flops), bytes_accessed=int(nbytes), transcendentals=0)


def pack_body(q_ref, k_ref, v_ref, out_ref, held, packed, in_sems, out_sems):
    loads = [
        pltpu.make_async_copy(ref, held.at[x], in_sems.at[x])
        for x, ref in enumerate((q_ref, k_ref, v_ref))
    ]
    for load in loads:
        load.start()
    stores = []
    for x, load in enumerate(loads):
        load.wait()
        rows = slice(x * BLOCK, (x + 1) * BLOCK)
        for h in range(HEADS):
            packed[h, rows, :] = held[x, :, h * WIDTH : (h + 1) * WIDTH]
        stores.append(
            pltpu.make_async_copy(packed.at[:, rows, :], out_ref.at[:, rows, :], out_sems.at[x])
        )
        stores[-1].start()
    for store in stores:
        store.wait()


def pack(q, k, v):
    packed = (HEADS, 3 * BLOCK, WIDTH)
    return kernel_call(
        pack_body,
        [(packed, BF16, "hbm")],
        ["hbm"] * 3,
        6,
        scratch=[pltpu.VMEM((3,) + q.shape, BF16), pltpu.VMEM(packed, BF16), dma(3), dma(3)],
        cost=cost(0, 6 * q.size * 2),
        name="pack_qkv",
    )(q, k, v)[0]


def att_grad_body(chunks, cot_ref, w_ref, out_ref, held, sems):
    rows = held.shape[0] // chunks
    copies = []
    for c in range(chunks):
        at = slice(c * rows, (c + 1) * rows)
        copies.append(pltpu.make_async_copy(w_ref.at[at, :], held.at[at, :], sems.at[c]))
        copies[-1].start()
    for c, copy in enumerate(copies):
        at = slice(c * rows, (c + 1) * rows)
        copy.wait()
        out_ref[:, at] = nt(cot_ref[...], held[at, :]).astype(BF16)


def attended_gradient(cot, w_out):
    chunks = 4
    return kernel_call(
        functools.partial(att_grad_body, chunks),
        [(cot.shape, BF16, "vmem")],
        ["vmem", "hbm"],
        14,
        scratch=[pltpu.VMEM(w_out.shape, BF16), dma(chunks)],
        cost=cost(2 * cot.size * w_out.shape[0], 9 << 20),
        name="attended_gradient",
    )(cot, w_out)[0]


def forward_body(
    blocks, in_ref, grad_ref, out_ref, att_out, lse_out, lev_out,
    lse_ref, lev_ref, fq, mu, du, nu, sems,
):
    tokens = blocks * BLOCK
    spans, _ = level_rows(tokens)
    copies = []

    def send(source, target):
        copies.append(pltpu.make_async_copy(source, target, sems.at[len(copies)]))
        copies[-1].start()

    scale = 1.0 / math.sqrt(WIDTH)
    for b in range(blocks):
        out_ref[b, 0:BLOCK, :] = grad_ref[:, b * WIDTH : (b + 1) * WIDTH]
        for x in range(3):
            part = in_ref[b, x * BLOCK : (x + 1) * BLOCK, :]
            lev_ref[x, b * BLOCK : (b + 1) * BLOCK, :] = part
            fq[x, b * BLOCK : (b + 1) * BLOCK, :] = part.astype(F32)
    for height in range(1, LEVELS + 1):
        below, _ = spans[height - 1]
        base, rows = spans[height]
        step = min(CHUNK, rows)
        for x in range(3):
            for r in range(0, rows, step):
                mean = (
                    evens(fq.at[x], below + 2 * r, step) + odds(fq.at[x], below + 2 * r, step)
                ) * 0.5
                mean = mean.astype(BF16)
                lev_ref[x, base + r : base + r + step, :] = mean
                fq[x, base + r : base + r + step, :] = mean.astype(F32)

    send(lev_ref, lev_out)

    def attend(jobs):
        scores = [nt(lev_ref[0, q, :], lev_ref[1, k, :]) * scale for q, k, _ in jobs]
        tops = [wide(jnp.max(x, axis=1, keepdims=True)) for x in scores]
        expos = [jnp.exp(x - across(top, x.shape[1])) for x, top in zip(scores, tops)]
        numers = [nn(x.astype(BF16), lev_ref[2, k, :]) for x, (_, k, _) in zip(expos, jobs)]
        denoms = [wide(jnp.sum(x, axis=1, keepdims=True)) for x in expos]
        return [
            (top, denom * factor, numer * factor) if factor != 1 else (top, denom, numer)
            for top, denom, numer, (_, _, factor) in zip(tops, denoms, numers, jobs)
        ]

    def merge(at, stats):
        top, denom, numer = stats
        up = mu[at, :]
        peak = jnp.maximum(top, up)
        mine, theirs = jnp.exp(top - peak), jnp.exp(up - peak)
        return peak, mine * denom + theirs * du[at, :], mine * numer + theirs * nu[at, :]

    coarse = coarse_blocks(tokens)
    stats = attend([(near, far, float(2**height)) for height, _, near, far in coarse])
    for (height, row, near, _), one in zip(coarse, stats):
        if height < LEVELS:
            one = merge(near, one)
        for ref, value in zip((mu, du, nu), one):
            put_twice(ref, spans[height - 1][0] + 2 * row, value)
    for first in range(0, tokens, PAIRS * 2 * BLOCK):
        pairs = [
            slice(row, row + 2 * BLOCK)
            for row in range(first, min(first + PAIRS * 2 * BLOCK, tokens), 2 * BLOCK)
        ]
        for at, one in zip(pairs, attend([(at, at, 1) for at in pairs])):
            peak, total, summed = merge(at, one)
            attended = (summed / total).astype(BF16)
            lse_ref[at, :] = peak + jnp.log(total)
            pair = slice(at.start // BLOCK, at.stop // BLOCK)
            out_ref[pair, BLOCK:, :] = attended.reshape(2, BLOCK, WIDTH)
            send(lse_ref.at[at, :], lse_out.at[at, :])
            send(out_ref.at[pair, BLOCK:, :], att_out.at[pair, :, :])
    for copy in copies:
        copy.wait()


def forward(qkv, att_grad):
    blocks = qkv.shape[0]
    tokens = blocks * BLOCK
    spans, total_rows = level_rows(tokens)
    finer = total_rows - spans[LEVELS][1]
    outs = [
        ((blocks, 2 * BLOCK, WIDTH), BF16, "vmem"),
        ((blocks, BLOCK, WIDTH), BF16, "hbm"),
        ((tokens, WIDTH), F32, "hbm"),
        ((3, total_rows, WIDTH), BF16, "hbm"),
    ]
    return kernel_call(
        functools.partial(forward_body, blocks),
        outs,
        ["vmem"] * 2,
        32,
        scratch=[
            pltpu.VMEM((tokens, WIDTH), F32),
            pltpu.VMEM((3, total_rows, WIDTH), BF16),
            pltpu.VMEM((3, total_rows, WIDTH), F32),
            pltpu.VMEM((finer, WIDTH), F32),
            pltpu.VMEM((finer, WIDTH), F32),
            pltpu.VMEM((finer, WIDTH), F32),
            dma(1 + blocks),
        ],
        cost=cost(4 * tokens * 384 * WIDTH, 8 << 20),
        name="head_forward",
    )(qkv, att_grad)


def backward_body(
    blocks, grad_in, att_in, lse_in, lev_in, rows_in, w_in, out_ref, output_ref,
    att_ref, lev_ref, ys, ds, rs, cg, up, rows_ref, w_ref, sems,
):
    tokens = blocks * BLOCK
    spans, total_rows = level_rows(tokens)
    scale = 1.0 / math.sqrt(WIDTH)
    parts, count = 4, [0]

    def fetch(source, target):
        copy = pltpu.make_async_copy(source, target, sems.at[count[0]])
        count[0] += 1
        copy.start()
        return copy

    first_loads = []
    for p in range(parts):
        some = slice(p * blocks // parts, (p + 1) * blocks // parts)
        at = slice(p * tokens // parts, (p + 1) * tokens // parts)
        first_loads.append(
            [
                fetch(grad_in.at[at, :], cg.at[at, :]),
                fetch(att_in.at[some, :, :], att_ref.at[some, :, :]),
                fetch(lse_in.at[at, :], rs.at[at, :]),
            ]
        )
    coarse = slice(tokens, total_rows)
    later_loads = [
        fetch(lev_in.at[:, coarse, :], lev_ref.at[:, coarse, :]),
        fetch(lev_in.at[:, :tokens, :], lev_ref.at[:, :tokens, :]),
        fetch(rows_in, rows_ref),
        fetch(w_in, w_ref),
    ]
    for b in range(blocks):
        if b % (blocks // parts) == 0:
            for copy in first_loads[b // (blocks // parts)]:
                copy.wait()
        at = slice(b * BLOCK, (b + 1) * BLOCK)
        grad = cg[at, :].astype(F32)
        ys[at, :] = grad
        ds[at, :] = wide(jnp.sum(grad * att_ref[b].astype(F32), axis=1, keepdims=True))
    for height in range(1, LEVELS + 1):
        below, _ = spans[height - 1]
        base, rows = spans[height]
        for r in range(0, rows, BLOCK):
            at = slice(base + r, base + r + BLOCK)
            first = below + 2 * r
            lo, hi = evens(rs, first, BLOCK), odds(rs, first, BLOCK)
            low = jnp.minimum(lo, hi)
            lo, hi = jnp.exp(low - lo), jnp.exp(low - hi)
            grad = lo * evens(ys, first, BLOCK) + hi * odds(ys, first, BLOCK)
            delta = lo * evens(ds, first, BLOCK) + hi * odds(ds, first, BLOCK)
            ys[at, :], ds[at, :], rs[at, :] = grad, delta, low
            cg[at, :] = grad.astype(BF16)

    def gradients(jobs):
        scores = [nt(lev_ref[0, q, :], lev_ref[1, k, :]) * scale for q, k in jobs]
        inner = [nt(cg[q, :], lev_ref[2, k, :]) for q, k in jobs]
        expos = [
            jnp.exp(x - across(rs[q, :], x.shape[1])) for x, (q, _) in zip(scores, jobs)
        ]
        sgrads = [
            (expo * (x - across(ds[q, :], x.shape[1])) * scale).astype(BF16)
            for expo, x, (q, _) in zip(expos, inner, jobs)
        ]
        probs = [expo.astype(BF16) for expo in expos]
        q_parts = [nn(x, lev_ref[1, k, :]) for x, (_, k) in zip(sgrads, jobs)]
        k_parts = [tn(x, lev_ref[0, q, :]) for x, (q, _) in zip(sgrads, jobs)]
        v_parts = [tn(x, cg[q, :]) for x, (q, _) in zip(probs, jobs)]
        return list(zip(q_parts, k_parts, v_parts))

    later_loads[0].wait()
    coarse = coarse_blocks(tokens)
    for (height, row, near, far), parts in zip(
        coarse, gradients([(near, far) for _, _, near, far in coarse])
    ):
        for x, (at, first) in enumerate(((near, row), (far, row ^ BLOCK), (far, row ^ BLOCK))):
            value = parts[x]
            if height < LEVELS:
                value = value + up[x, at, :]
            put_twice(up.at[x], spans[height - 1][0] + 2 * first, value)
    later_loads[1].wait()
    for first in range(0, tokens, PAIRS * 2 * BLOCK):
        pairs = [
            slice(row, row + 2 * BLOCK)
            for row in range(first, min(first + PAIRS * 2 * BLOCK, tokens), 2 * BLOCK)
        ]
        for at, parts in zip(pairs, gradients([(at, at) for at in pairs])):
            pair = slice(at.start // BLOCK, at.stop // BLOCK)
            for x, value in enumerate(parts):
                value = (value + up[x, at, :]).astype(BF16)
                out_ref[pair, x * BLOCK : (x + 1) * BLOCK, :] = value.reshape(2, BLOCK, WIDTH)
    later_loads[2].wait()
    later_loads[3].wait()
    rows = jnp.concatenate([rows_ref[h] for h in range(HEADS)], axis=1)
    width = w_ref.shape[1]
    for first in range(0, width, 512):
        at = slice(first, first + 512)
        output_ref[:, at] = nn(rows, w_ref[:, at]).astype(BF16)


def backward(grad, att, lse, lev, rows, w_out):
    blocks = att.shape[0]
    tokens = blocks * BLOCK
    spans, total_rows = level_rows(tokens)
    finer = total_rows - spans[LEVELS][1]
    return kernel_call(
        functools.partial(backward_body, blocks),
        [
            ((blocks, 3 * BLOCK, WIDTH), BF16, "vmem"),
            ((BLOCK, w_out.shape[1]), BF16, "vmem"),
        ],
        ["hbm"] * 6,
        44,
        scratch=[
            pltpu.VMEM(att.shape, BF16),
            pltpu.VMEM(lev.shape, BF16),
            pltpu.VMEM((total_rows, WIDTH), F32),
            pltpu.VMEM((total_rows, WIDTH), F32),
            pltpu.VMEM((total_rows, WIDTH), F32),
            pltpu.VMEM((total_rows, WIDTH), BF16),
            pltpu.VMEM((3, finer, WIDTH), F32),
            pltpu.VMEM(rows.shape, BF16),
            pltpu.VMEM(w_out.shape, BF16),
            dma(16),
        ],
        cost=cost(10 * tokens * 384 * WIDTH + 2 * BLOCK * w_out.size, 24 << 20),
        name="head_backward",
    )(grad.reshape(tokens, WIDTH), att, lse, lev, rows, w_out)


def tile_body(groups, per, chunks, grads_ref, att_ref, cot_ref, out_ref, lhs, held, sems):
    rows = per * WIDTH
    chunk = rows // HEADS
    width = held.shape[2]
    copies = []
    for c in range(chunks):
        at = slice(c * width, (c + 1) * width)
        copies.append(pltpu.make_async_copy(cot_ref.at[:, at], held.at[c], sems.at[c]))
        copies[-1].start()
    out_ref[:, : 3 * BLOCK, :] = grads_ref[...]
    for o in range(groups):
        for j in range(per):
            lhs[o * BLOCK : (o + 1) * BLOCK, j * WIDTH : (j + 1) * WIDTH] = att_ref[o * per + j]
    for c, copy in enumerate(copies):
        copy.wait()
        part = tn(lhs[...], held[c]).astype(BF16)
        for i in range(HEADS):
            for j in range(width // WIDTH):
                at = 3 * BLOCK + (c * width // WIDTH + j) * chunk
                out_ref[i, at : at + chunk, :] = part[
                    i * chunk : (i + 1) * chunk, j * WIDTH : (j + 1) * WIDTH
                ]


def with_tile(grads, att, cot):
    chunks = 8
    groups = cot.shape[0] // BLOCK
    per = HEADS // groups
    chunk = per * WIDTH // HEADS
    extra = chunk * (cot.shape[1] // WIDTH)
    return kernel_call(
        functools.partial(tile_body, groups, per, chunks),
        [((HEADS, 3 * BLOCK + extra, WIDTH), BF16, "vmem")],
        ["vmem", "vmem", "hbm"],
        16,
        scratch=[
            pltpu.VMEM((groups * BLOCK, per * WIDTH), BF16),
            pltpu.VMEM((chunks, cot.shape[0], cot.shape[1] // chunks), BF16),
            dma(chunks),
        ],
        cost=cost(2 * cot.shape[0] * per * WIDTH * cot.shape[1], 10 << 20),
        name="projection_tile",
    )(grads, att, cot)[0]


def unpack_body(scale, in_ref, q_ref, k_ref, v_ref, w_ref):
    chunk, width = w_ref.shape
    for h in range(HEADS):
        for x, ref in enumerate((q_ref, k_ref, v_ref)):
            ref[:, h * WIDTH : (h + 1) * WIDTH] = in_ref[h, x * BLOCK : (x + 1) * BLOCK, :]
    for c in range(width // WIDTH):
        at = 3 * BLOCK + c * chunk
        total = in_ref[0, at : at + chunk, :].astype(F32)
        for h in range(1, HEADS):
            total = total + in_ref[h, at : at + chunk, :].astype(F32)
        w_ref[:, c * WIDTH : (c + 1) * WIDTH] = total * scale


def unpack(got, scale):
    chunk = (got.shape[1] - 3 * BLOCK) // HEADS
    width = HEADS * WIDTH
    return kernel_call(
        functools.partial(unpack_body, scale),
        [((BLOCK, width), BF16, "vmem")] * 3 + [((chunk, width), F32, "vmem")],
        ["vmem"],
        8,
        cost=cost(0, 6 << 20),
        name="unpack_grads",
    )(got)


def split_body(got_ref, grad_ref, att_ref, sems):
    copies = [
        pltpu.make_async_copy(got_ref.at[:, BLOCK:, :], att_ref, sems.at[0]),
        pltpu.make_async_copy(got_ref.at[:, :BLOCK, :], grad_ref, sems.at[1]),
    ]
    for copy in copies:
        copy.start()
    for copy in copies:
        copy.wait()


def split(got):
    return kernel_call(
        split_body,
        [((HEADS, BLOCK, WIDTH), BF16, "hbm")] * 2,
        ["vmem"],
        2,
        scratch=[dma(2)],
        cost=cost(0, 2 << 20),
        name="split_attended",
    )(got)


def swap(value, axis):
    return lax.all_to_all(value, axis, 0, 0, tiled=True)


def on_device(query_in, key_in, value_in, w_out, cotangent):
    tokens = query_in.shape[0] * lax.axis_size(("outer", "inner"))
    cot_outer = lax.all_gather(cotangent, "outer", axis=0, tiled=True)
    qkv = swap(pack(query_in, key_in, value_in), "inner")
    att_grad = attended_gradient(cotangent, w_out)
    sent, att_own, lse, lev = forward(qkv, att_grad)
    grad, att = split(swap(sent, "inner"))
    att_outer = swap(att, "outer")
    grads, output = backward(grad, att_own, lse, lev, att, w_out)
    last = swap(with_tile(grads, att_outer, cot_outer), "inner")
    query_grad, key_grad, value_grad, w_out_grad = unpack(last, 1.0 / math.sqrt(tokens))
    return output, query_grad, key_grad, value_grad, w_out_grad


def solution(mesh):
    rows = P(("outer", "inner"), None)
    return jax.shard_map(
        on_device,
        mesh=mesh,
        in_specs=(rows, rows, rows, P(), rows),
        out_specs=(rows,) * 5,
        check_vma=False,
    )
```

```python
import functools
import math

import jax
import jax.numpy as jnp
from jax import lax
from jax.experimental import pallas as pl
from jax.experimental.pallas import tpu as pltpu
from jax.sharding import PartitionSpec as P

HEADS = 16
BLOCK = 128
LEVELS = 3
WIDTH = 128
BF16 = jnp.bfloat16
F32 = jnp.float32
CHUNK = 256
PAIRS = 8


def nt(a, b):
    return lax.dot_general(a, b, (((1,), (1,)), ((), ())), preferred_element_type=F32)


def nn(a, b):
    return lax.dot_general(a, b, (((1,), (0,)), ((), ())), preferred_element_type=F32)


def tn(a, b):
    return lax.dot_general(a, b, (((0,), (0,)), ((), ())), preferred_element_type=F32)


def wide(stat, columns=WIDTH):
    return jnp.broadcast_to(stat, (stat.shape[0], columns))


def evens(ref, base, rows):
    return ref[pl.ds(base, rows, stride=2), :]


def odds(ref, base, rows):
    return ref[pl.ds(base + 1, rows, stride=2), :]


def put_twice(ref, base, value):
    rows = value.shape[0]
    ref[pl.ds(base, rows, stride=2), :] = value
    ref[pl.ds(base + 1, rows, stride=2), :] = value


def across(stat, columns):
    return jnp.concatenate([stat] * (columns // WIDTH), axis=1)


def coarse_blocks(tokens):
    spans, _ = level_rows(tokens)
    out = []
    for height in range(LEVELS, 0, -1):
        base, rows = spans[height]
        for row in range(0, rows, BLOCK):
            near, far = base + row, base + (row ^ BLOCK)
            out.append((height, row, slice(near, near + BLOCK), slice(far, far + BLOCK)))
    return out


def level_rows(tokens):
    out, base = [], 0
    for height in range(LEVELS + 1):
        out.append((base, tokens >> height))
        base += tokens >> height
    return out, base


def kernel_call(body, outs, in_places, mib, scratch=(), cost=None, name=None, after=()):
    count = len(in_places)
    in_places = list(in_places) + ["any"] * len(after)

    def ordered(*refs):
        body(*refs[:count], *refs[len(in_places) :])

    spec = {
        "vmem": pl.BlockSpec(memory_space=pltpu.VMEM),
        "hbm": pl.BlockSpec(memory_space=pl.ANY),
        "any": pl.BlockSpec(memory_space=pl.ANY),
    }
    shapes = [
        pltpu.HBM(shape, dtype) if place == "hbm" else jax.ShapeDtypeStruct(shape, dtype)
        for shape, dtype, place in outs
    ]
    call = pl.pallas_call(
        ordered,
        out_shape=shapes,
        in_specs=[spec[place] for place in in_places],
        out_specs=[spec[place] for _, _, place in outs],
        scratch_shapes=list(scratch),
        compiler_params=pltpu.CompilerParams(vmem_limit_bytes=mib << 20),
        cost_estimate=cost,
        name=name,
    )

    def run(*operands):
        operands = [
            pltpu.with_memory_space_constraint(x, pltpu.HBM) if place == "hbm" else x
            for x, place in zip((*operands, *after), in_places)
        ]
        return call(*operands)

    return run


def dma(count):
    return pltpu.SemaphoreType.DMA((count,))


def cost(flops, nbytes):
    return pl.CostEstimate(flops=int(flops), bytes_accessed=int(nbytes), transcendentals=0)


def pack_body(q_ref, k_ref, v_ref, out_ref, held, packed, in_sems, out_sems):
    loads = [
        pltpu.make_async_copy(ref, held.at[x], in_sems.at[x])
        for x, ref in enumerate((q_ref, k_ref, v_ref))
    ]
    for load in loads:
        load.start()
    stores = []
    for x, load in enumerate(loads):
        load.wait()
        rows = slice(x * BLOCK, (x + 1) * BLOCK)
        for h in range(HEADS):
            packed[h, rows, :] = held[x, :, h * WIDTH : (h + 1) * WIDTH]
        stores.append(
            pltpu.make_async_copy(packed.at[:, rows, :], out_ref.at[:, rows, :], out_sems.at[x])
        )
        stores[-1].start()
    for store in stores:
        store.wait()


def pack(q, k, v):
    packed = (HEADS, 3 * BLOCK, WIDTH)
    return kernel_call(
        pack_body,
        [(packed, BF16, "hbm")],
        ["hbm"] * 3,
        6,
        scratch=[pltpu.VMEM((3,) + q.shape, BF16), pltpu.VMEM(packed, BF16), dma(3), dma(3)],
        cost=cost(0, 6 * q.size * 2),
        name="pack_qkv",
    )(q, k, v)[0]


def att_grad_body(chunks, cot_ref, w_ref, out_ref, held, sems):
    rows = held.shape[0] // chunks
    copies = []
    for c in range(chunks):
        at = slice(c * rows, (c + 1) * rows)
        copies.append(pltpu.make_async_copy(w_ref.at[at, :], held.at[at, :], sems.at[c]))
        copies[-1].start()
    for c, copy in enumerate(copies):
        at = slice(c * rows, (c + 1) * rows)
        copy.wait()
        out_ref[:, at] = nt(cot_ref[...], held[at, :]).astype(BF16)


def attended_gradient(cot, w_out):
    chunks = 4
    return kernel_call(
        functools.partial(att_grad_body, chunks),
        [(cot.shape, BF16, "vmem")],
        ["vmem", "hbm"],
        14,
        scratch=[pltpu.VMEM(w_out.shape, BF16), dma(chunks)],
        cost=cost(2 * cot.size * w_out.shape[0], 9 << 20),
        name="attended_gradient",
    )(cot, w_out)[0]


def forward_body(
    blocks, in_ref, grad_ref, out_ref, att_out, lse_out, lev_out,
    lse_ref, lev_ref, fq, mu, du, nu, sems,
):
    tokens = blocks * BLOCK
    spans, _ = level_rows(tokens)
    copies = []

    def send(source, target):
        copies.append(pltpu.make_async_copy(source, target, sems.at[len(copies)]))
        copies[-1].start()

    scale = 1.0 / math.sqrt(WIDTH)
    for b in range(blocks):
        out_ref[b, 0:BLOCK, :] = grad_ref[:, b * WIDTH : (b + 1) * WIDTH]
        for x in range(3):
            part = in_ref[b, x * BLOCK : (x + 1) * BLOCK, :]
            lev_ref[x, b * BLOCK : (b + 1) * BLOCK, :] = part
            fq[x, b * BLOCK : (b + 1) * BLOCK, :] = part.astype(F32)
    for height in range(1, LEVELS + 1):
        below, _ = spans[height - 1]
        base, rows = spans[height]
        step = min(CHUNK, rows)
        for x in range(3):
            for r in range(0, rows, step):
                mean = (
                    evens(fq.at[x], below + 2 * r, step) + odds(fq.at[x], below + 2 * r, step)
                ) * 0.5
                mean = mean.astype(BF16)
                lev_ref[x, base + r : base + r + step, :] = mean
                fq[x, base + r : base + r + step, :] = mean.astype(F32)

    send(lev_ref, lev_out)

    def attend(jobs):
        scores = [nt(lev_ref[0, q, :], lev_ref[1, k, :]) * scale for q, k, _ in jobs]
        tops = [wide(jnp.max(x, axis=1, keepdims=True)) for x in scores]
        expos = [jnp.exp(x - across(top, x.shape[1])) for x, top in zip(scores, tops)]
        numers = [nn(x.astype(BF16), lev_ref[2, k, :]) for x, (_, k, _) in zip(expos, jobs)]
        denoms = [wide(jnp.sum(x, axis=1, keepdims=True)) for x in expos]
        return [
            (top, denom * factor, numer * factor) if factor != 1 else (top, denom, numer)
            for top, denom, numer, (_, _, factor) in zip(tops, denoms, numers, jobs)
        ]

    def merge(at, stats):
        top, denom, numer = stats
        up = mu[at, :]
        peak = jnp.maximum(top, up)
        mine, theirs = jnp.exp(top - peak), jnp.exp(up - peak)
        return peak, mine * denom + theirs * du[at, :], mine * numer + theirs * nu[at, :]

    coarse = coarse_blocks(tokens)
    stats = attend([(near, far, float(2**height)) for height, _, near, far in coarse])
    for (height, row, near, _), one in zip(coarse, stats):
        if height < LEVELS:
            one = merge(near, one)
        for ref, value in zip((mu, du, nu), one):
            put_twice(ref, spans[height - 1][0] + 2 * row, value)
    for first in range(0, tokens, PAIRS * 2 * BLOCK):
        pairs = [
            slice(row, row + 2 * BLOCK)
            for row in range(first, min(first + PAIRS * 2 * BLOCK, tokens), 2 * BLOCK)
        ]
        for at, one in zip(pairs, attend([(at, at, 1) for at in pairs])):
            peak, total, summed = merge(at, one)
            attended = (summed / total).astype(BF16)
            lse_ref[at, :] = peak + jnp.log(total)
            pair = slice(at.start // BLOCK, at.stop // BLOCK)
            out_ref[pair, BLOCK:, :] = attended.reshape(2, BLOCK, WIDTH)
            send(lse_ref.at[at, :], lse_out.at[at, :])
            send(out_ref.at[pair, BLOCK:, :], att_out.at[pair, :, :])
    for copy in copies:
        copy.wait()


def forward(qkv, att_grad, after=()):
    blocks = qkv.shape[0]
    tokens = blocks * BLOCK
    spans, total_rows = level_rows(tokens)
    finer = total_rows - spans[LEVELS][1]
    outs = [
        ((blocks, 2 * BLOCK, WIDTH), BF16, "vmem"),
        ((blocks, BLOCK, WIDTH), BF16, "hbm"),
        ((tokens, WIDTH), F32, "hbm"),
        ((3, total_rows, WIDTH), BF16, "hbm"),
    ]
    return kernel_call(
        functools.partial(forward_body, blocks),
        outs,
        ["vmem"] * 2,
        32,
        scratch=[
            pltpu.VMEM((tokens, WIDTH), F32),
            pltpu.VMEM((3, total_rows, WIDTH), BF16),
            pltpu.VMEM((3, total_rows, WIDTH), F32),
            pltpu.VMEM((finer, WIDTH), F32),
            pltpu.VMEM((finer, WIDTH), F32),
            pltpu.VMEM((finer, WIDTH), F32),
            dma(1 + blocks),
        ],
        cost=cost(4 * tokens * 384 * WIDTH, 8 << 20),
        name="head_forward",
        after=after,
    )(qkv, att_grad)


def backward_body(
    blocks, grad_in, att_in, lse_in, lev_in, rows_in, w_in, out_ref, output_ref,
    att_ref, lev_ref, ys, ds, rs, cg, up, rows_ref, w_ref, sems,
):
    tokens = blocks * BLOCK
    spans, total_rows = level_rows(tokens)
    scale = 1.0 / math.sqrt(WIDTH)
    parts, count = 4, [0]

    def fetch(source, target):
        copy = pltpu.make_async_copy(source, target, sems.at[count[0]])
        count[0] += 1
        copy.start()
        return copy

    first_loads = []
    for p in range(parts):
        some = slice(p * blocks // parts, (p + 1) * blocks // parts)
        at = slice(p * tokens // parts, (p + 1) * tokens // parts)
        first_loads.append(
            [
                fetch(grad_in.at[at, :], cg.at[at, :]),
                fetch(att_in.at[some, :, :], att_ref.at[some, :, :]),
                fetch(lse_in.at[at, :], rs.at[at, :]),
            ]
        )
    coarse = slice(tokens, total_rows)
    later_loads = [
        fetch(lev_in.at[:, coarse, :], lev_ref.at[:, coarse, :]),
        fetch(lev_in.at[:, :tokens, :], lev_ref.at[:, :tokens, :]),
        fetch(rows_in, rows_ref),
        fetch(w_in, w_ref),
    ]
    for b in range(blocks):
        if b % (blocks // parts) == 0:
            for copy in first_loads[b // (blocks // parts)]:
                copy.wait()
        at = slice(b * BLOCK, (b + 1) * BLOCK)
        grad = cg[at, :].astype(F32)
        ys[at, :] = grad
        ds[at, :] = wide(jnp.sum(grad * att_ref[b].astype(F32), axis=1, keepdims=True))
    for height in range(1, LEVELS + 1):
        below, _ = spans[height - 1]
        base, rows = spans[height]
        for r in range(0, rows, BLOCK):
            at = slice(base + r, base + r + BLOCK)
            first = below + 2 * r
            lo, hi = evens(rs, first, BLOCK), odds(rs, first, BLOCK)
            low = jnp.minimum(lo, hi)
            lo, hi = jnp.exp(low - lo), jnp.exp(low - hi)
            grad = lo * evens(ys, first, BLOCK) + hi * odds(ys, first, BLOCK)
            delta = lo * evens(ds, first, BLOCK) + hi * odds(ds, first, BLOCK)
            ys[at, :], ds[at, :], rs[at, :] = grad, delta, low
            cg[at, :] = grad.astype(BF16)

    def gradients(jobs):
        scores = [nt(lev_ref[0, q, :], lev_ref[1, k, :]) * scale for q, k in jobs]
        inner = [nt(cg[q, :], lev_ref[2, k, :]) for q, k in jobs]
        expos = [
            jnp.exp(x - across(rs[q, :], x.shape[1])) for x, (q, _) in zip(scores, jobs)
        ]
        sgrads = [
            (expo * (x - across(ds[q, :], x.shape[1])) * scale).astype(BF16)
            for expo, x, (q, _) in zip(expos, inner, jobs)
        ]
        probs = [expo.astype(BF16) for expo in expos]
        q_parts = [nn(x, lev_ref[1, k, :]) for x, (_, k) in zip(sgrads, jobs)]
        k_parts = [tn(x, lev_ref[0, q, :]) for x, (q, _) in zip(sgrads, jobs)]
        v_parts = [tn(x, cg[q, :]) for x, (q, _) in zip(probs, jobs)]
        return list(zip(q_parts, k_parts, v_parts))

    later_loads[0].wait()
    coarse = coarse_blocks(tokens)
    for (height, row, near, far), parts in zip(
        coarse, gradients([(near, far) for _, _, near, far in coarse])
    ):
        for x, (at, first) in enumerate(((near, row), (far, row ^ BLOCK), (far, row ^ BLOCK))):
            value = parts[x]
            if height < LEVELS:
                value = value + up[x, at, :]
            put_twice(up.at[x], spans[height - 1][0] + 2 * first, value)
    later_loads[1].wait()
    for first in range(0, tokens, PAIRS * 2 * BLOCK):
        pairs = [
            slice(row, row + 2 * BLOCK)
            for row in range(first, min(first + PAIRS * 2 * BLOCK, tokens), 2 * BLOCK)
        ]
        for at, parts in zip(pairs, gradients([(at, at) for at in pairs])):
            pair = slice(at.start // BLOCK, at.stop // BLOCK)
            for x, value in enumerate(parts):
                value = (value + up[x, at, :]).astype(BF16)
                out_ref[pair, x * BLOCK : (x + 1) * BLOCK, :] = value.reshape(2, BLOCK, WIDTH)
    later_loads[2].wait()
    later_loads[3].wait()
    rows = jnp.concatenate([rows_ref[h] for h in range(HEADS)], axis=1)
    width = w_ref.shape[1]
    for first in range(0, width, 512):
        at = slice(first, first + 512)
        output_ref[:, at] = nn(rows, w_ref[:, at]).astype(BF16)


def backward(grad, att, lse, lev, rows, w_out, after=()):
    blocks = att.shape[0]
    tokens = blocks * BLOCK
    spans, total_rows = level_rows(tokens)
    finer = total_rows - spans[LEVELS][1]
    return kernel_call(
        functools.partial(backward_body, blocks),
        [
            ((blocks, 3 * BLOCK, WIDTH), BF16, "vmem"),
            ((BLOCK, w_out.shape[1]), BF16, "vmem"),
        ],
        ["hbm"] * 6,
        44,
        scratch=[
            pltpu.VMEM(att.shape, BF16),
            pltpu.VMEM(lev.shape, BF16),
            pltpu.VMEM((total_rows, WIDTH), F32),
            pltpu.VMEM((total_rows, WIDTH), F32),
            pltpu.VMEM((total_rows, WIDTH), F32),
            pltpu.VMEM((total_rows, WIDTH), BF16),
            pltpu.VMEM((3, finer, WIDTH), F32),
            pltpu.VMEM(rows.shape, BF16),
            pltpu.VMEM(w_out.shape, BF16),
            dma(16),
        ],
        cost=cost(10 * tokens * 384 * WIDTH + 2 * BLOCK * w_out.size, 24 << 20),
        name="head_backward",
        after=after,
    )(grad.reshape(tokens, WIDTH), att, lse, lev, rows, w_out)


def tile_body(groups, per, grads_ref, att_ref, *refs):
    cot_refs = refs[:groups]
    out_ref, lhs, held, total, sems = refs[groups:]
    rows, depth = lhs.shape
    chunk = rows // HEADS
    copies = []
    for k, ref in enumerate(cot_refs):
        at = slice(k * BLOCK, (k + 1) * BLOCK)
        copies.append(pltpu.make_async_copy(ref, held.at[at, :], sems.at[k]))
        copies[-1].start()
    out_ref[:, : 3 * BLOCK, :] = grads_ref[...]
    mine = lax.axis_index("outer")
    for k in range(groups):
        for j in range(per):
            lhs[j * WIDTH : (j + 1) * WIDTH, k * BLOCK : (k + 1) * BLOCK] = att_ref[
                (mine ^ k) * per + j
            ].T
    half, step = depth // 2, 512
    for copy in copies[: groups // 2]:
        copy.wait()
    for first in range(0, held.shape[1], step):
        at = slice(first, first + step)
        total[:, at] = nn(lhs[:, :half], held[:half, at])
    for copy in copies[groups // 2 :]:
        copy.wait()
    for first in range(0, held.shape[1], step):
        at = slice(first, first + step)
        part = (total[:, at] + nn(lhs[:, half:], held[half:, at])).astype(BF16)
        for i in range(HEADS):
            for j in range(step // WIDTH):
                to = 3 * BLOCK + (first // WIDTH + j) * chunk
                out_ref[i, to : to + chunk, :] = part[
                    i * chunk : (i + 1) * chunk, j * WIDTH : (j + 1) * WIDTH
                ]


def with_tile(grads, att, pieces):
    groups, width = len(pieces), pieces[0].shape[1]
    per = HEADS // groups
    chunk = per * WIDTH // HEADS
    extra = chunk * (width // WIDTH)
    return kernel_call(
        functools.partial(tile_body, groups, per),
        [((HEADS, 3 * BLOCK + extra, WIDTH), BF16, "vmem")],
        ["vmem", "vmem"] + ["any"] * groups,
        18,
        scratch=[
            pltpu.VMEM((per * WIDTH, groups * BLOCK), BF16),
            pltpu.VMEM((groups * BLOCK, width), BF16),
            pltpu.VMEM((per * WIDTH, width), F32),
            dma(groups),
        ],
        cost=cost(2 * groups * BLOCK * per * WIDTH * width, 10 << 20),
        name="projection_tile",
    )(grads, att, *pieces)[0]


def unpack_body(scale, in_ref, q_ref, k_ref, v_ref, w_ref):
    chunk, width = w_ref.shape
    for h in range(HEADS):
        for x, ref in enumerate((q_ref, k_ref, v_ref)):
            ref[:, h * WIDTH : (h + 1) * WIDTH] = in_ref[h, x * BLOCK : (x + 1) * BLOCK, :]
    for c in range(width // WIDTH):
        at = 3 * BLOCK + c * chunk
        total = in_ref[0, at : at + chunk, :].astype(F32)
        for h in range(1, HEADS):
            total = total + in_ref[h, at : at + chunk, :].astype(F32)
        w_ref[:, c * WIDTH : (c + 1) * WIDTH] = total * scale


def unpack(got, scale):
    chunk = (got.shape[1] - 3 * BLOCK) // HEADS
    width = HEADS * WIDTH
    return kernel_call(
        functools.partial(unpack_body, scale),
        [((BLOCK, width), BF16, "vmem")] * 3 + [((chunk, width), F32, "vmem")],
        ["vmem"],
        8,
        cost=cost(0, 6 << 20),
        name="unpack_grads",
    )(got)


def split_body(got_ref, grad_ref, att_ref, sems):
    copies = [
        pltpu.make_async_copy(got_ref.at[:, BLOCK:, :], att_ref, sems.at[0]),
        pltpu.make_async_copy(got_ref.at[:, :BLOCK, :], grad_ref, sems.at[1]),
    ]
    for copy in copies:
        copy.start()
    for copy in copies:
        copy.wait()


def split(got):
    return kernel_call(
        split_body,
        [((HEADS, BLOCK, WIDTH), BF16, "hbm")] * 2,
        ["vmem"],
        2,
        scratch=[dma(2)],
        cost=cost(0, 2 << 20),
        name="split_attended",
    )(got)


def swap(value, axis):
    return lax.all_to_all(value, axis, 0, 0, tiled=True)


def from_outer(value, apart):
    size = lax.axis_size("outer")
    return lax.ppermute(value, "outer", [(i, i ^ apart) for i in range(size)])


def on_device(query_in, key_in, value_in, w_out, cotangent):
    groups = lax.axis_size("outer")
    tokens = query_in.shape[0] * lax.axis_size(("outer", "inner"))
    pieces = {0: cotangent, 1: from_outer(cotangent, 1)}
    for k in range(2, groups, 2):
        pieces[k] = from_outer(cotangent, k)
    far = [pieces[k] for k in range(2, groups, 2)]
    qkv = swap(pack(query_in, key_in, value_in), "inner")
    att_grad = attended_gradient(cotangent, w_out)
    sent, att_own, lse, lev = forward(qkv, att_grad, after=[pieces[1]] + far)
    for k in range(2, groups, 2):
        pieces[k + 1] = from_outer(pieces[k], 1)
    near = [pieces[k + 1] for k in range(2, groups, 2)]
    grad, att = split(swap(sent, "inner"))
    att_outer = swap(att, "outer")
    grads, output = backward(grad, att_own, lse, lev, att, w_out, after=near)
    pieces = [pieces[k] for k in range(groups)]
    last = swap(with_tile(grads, att_outer, pieces), "inner")
    query_grad, key_grad, value_grad, w_out_grad = unpack(last, 1.0 / math.sqrt(tokens))
    return output, query_grad, key_grad, value_grad, w_out_grad


def solution(mesh):
    rows = P(("outer", "inner"), None)
    return jax.shard_map(
        on_device,
        mesh=mesh,
        in_specs=(rows, rows, rows, P(), rows),
        out_specs=(rows,) * 5,
        check_vma=False,
    )
```

```python
import functools
import math

import jax
import jax.numpy as jnp
from jax import lax
from jax.experimental import pallas as pl
from jax.experimental.pallas import tpu as pltpu
from jax.sharding import PartitionSpec as P

HEADS = 16
BLOCK = 128
LEVELS = 3
WIDTH = 128
BF16 = jnp.bfloat16
F32 = jnp.float32
CHUNK = 256
PAIRS = 8


def nt(a, b):
    return lax.dot_general(a, b, (((1,), (1,)), ((), ())), preferred_element_type=F32)


def nn(a, b):
    return lax.dot_general(a, b, (((1,), (0,)), ((), ())), preferred_element_type=F32)


def tn(a, b):
    return lax.dot_general(a, b, (((0,), (0,)), ((), ())), preferred_element_type=F32)


def wide(stat, columns=WIDTH):
    return jnp.broadcast_to(stat, (stat.shape[0], columns))


def evens(ref, base, rows):
    return ref[pl.ds(base, rows, stride=2), :]


def odds(ref, base, rows):
    return ref[pl.ds(base + 1, rows, stride=2), :]


def put_twice(ref, base, value):
    rows = value.shape[0]
    ref[pl.ds(base, rows, stride=2), :] = value
    ref[pl.ds(base + 1, rows, stride=2), :] = value


def across(stat, columns):
    return jnp.concatenate([stat] * (columns // WIDTH), axis=1)


def coarse_blocks(tokens):
    spans, _ = level_rows(tokens)
    out = []
    for height in range(LEVELS, 0, -1):
        base, rows = spans[height]
        for row in range(0, rows, BLOCK):
            near, far = base + row, base + (row ^ BLOCK)
            out.append((height, row, slice(near, near + BLOCK), slice(far, far + BLOCK)))
    return out


def level_rows(tokens):
    out, base = [], 0
    for height in range(LEVELS + 1):
        out.append((base, tokens >> height))
        base += tokens >> height
    return out, base


def kernel_call(body, outs, in_places, mib, scratch=(), cost=None, name=None, after=()):
    count = len(in_places)
    in_places = list(in_places) + ["any"] * len(after)

    def ordered(*refs):
        body(*refs[:count], *refs[len(in_places) :])

    spec = {
        "vmem": pl.BlockSpec(memory_space=pltpu.VMEM),
        "hbm": pl.BlockSpec(memory_space=pl.ANY),
        "any": pl.BlockSpec(memory_space=pl.ANY),
    }
    shapes = [
        pltpu.HBM(shape, dtype) if place == "hbm" else jax.ShapeDtypeStruct(shape, dtype)
        for shape, dtype, place in outs
    ]
    call = pl.pallas_call(
        ordered,
        out_shape=shapes,
        in_specs=[spec[place] for place in in_places],
        out_specs=[spec[place] for _, _, place in outs],
        scratch_shapes=list(scratch),
        compiler_params=pltpu.CompilerParams(vmem_limit_bytes=mib << 20),
        cost_estimate=cost,
        name=name,
    )

    def run(*operands):
        operands = [
            pltpu.with_memory_space_constraint(x, pltpu.HBM) if place == "hbm" else x
            for x, place in zip((*operands, *after), in_places)
        ]
        return call(*operands)

    return run


def dma(count):
    return pltpu.SemaphoreType.DMA((count,))


def cost(flops, nbytes):
    return pl.CostEstimate(flops=int(flops), bytes_accessed=int(nbytes), transcendentals=0)


def pack_body(q_ref, k_ref, v_ref, out_ref, held, packed, in_sems, out_sems):
    loads = [
        pltpu.make_async_copy(ref, held.at[x], in_sems.at[x])
        for x, ref in enumerate((q_ref, k_ref, v_ref))
    ]
    for load in loads:
        load.start()
    stores = []
    for x, load in enumerate(loads):
        load.wait()
        rows = slice(x * BLOCK, (x + 1) * BLOCK)
        for h in range(HEADS):
            packed[h, rows, :] = held[x, :, h * WIDTH : (h + 1) * WIDTH]
        stores.append(
            pltpu.make_async_copy(packed.at[:, rows, :], out_ref.at[:, rows, :], out_sems.at[x])
        )
        stores[-1].start()
    for store in stores:
        store.wait()


def pack(q, k, v):
    packed = (HEADS, 3 * BLOCK, WIDTH)
    return kernel_call(
        pack_body,
        [(packed, BF16, "hbm")],
        ["hbm"] * 3,
        6,
        scratch=[pltpu.VMEM((3,) + q.shape, BF16), pltpu.VMEM(packed, BF16), dma(3), dma(3)],
        cost=cost(0, 6 * q.size * 2),
        name="pack_qkv",
    )(q, k, v)[0]


def att_grad_body(chunks, cot_ref, w_ref, out_ref, held, sems):
    rows = held.shape[0] // chunks
    copies = []
    for c in range(chunks):
        at = slice(c * rows, (c + 1) * rows)
        copies.append(pltpu.make_async_copy(w_ref.at[at, :], held.at[at, :], sems.at[c]))
        copies[-1].start()
    for c, copy in enumerate(copies):
        at = slice(c * rows, (c + 1) * rows)
        copy.wait()
        out_ref[:, at] = nt(cot_ref[...], held[at, :]).astype(BF16)


def attended_gradient(cot, w_out):
    chunks = 4
    return kernel_call(
        functools.partial(att_grad_body, chunks),
        [(cot.shape, BF16, "vmem")],
        ["vmem", "hbm"],
        14,
        scratch=[pltpu.VMEM(w_out.shape, BF16), dma(chunks)],
        cost=cost(2 * cot.size * w_out.shape[0], 9 << 20),
        name="attended_gradient",
    )(cot, w_out)[0]


def forward_body(
    blocks, in_ref, grad_ref, out_ref, att_out, lse_out, lev_out,
    lse_ref, lev_ref, fq, mu, du, nu, sems,
):
    tokens = blocks * BLOCK
    spans, _ = level_rows(tokens)
    copies = []

    def send(source, target):
        copies.append(pltpu.make_async_copy(source, target, sems.at[len(copies)]))
        copies[-1].start()

    scale = 1.0 / math.sqrt(WIDTH)
    for b in range(blocks):
        out_ref[b, 0:BLOCK, :] = grad_ref[:, b * WIDTH : (b + 1) * WIDTH]
        for x in range(3):
            part = in_ref[b, x * BLOCK : (x + 1) * BLOCK, :]
            lev_ref[x, b * BLOCK : (b + 1) * BLOCK, :] = part
            fq[x, b * BLOCK : (b + 1) * BLOCK, :] = part.astype(F32)
    for height in range(1, LEVELS + 1):
        below, _ = spans[height - 1]
        base, rows = spans[height]
        step = min(CHUNK, rows)
        for x in range(3):
            for r in range(0, rows, step):
                mean = (
                    evens(fq.at[x], below + 2 * r, step) + odds(fq.at[x], below + 2 * r, step)
                ) * 0.5
                mean = mean.astype(BF16)
                lev_ref[x, base + r : base + r + step, :] = mean
                fq[x, base + r : base + r + step, :] = mean.astype(F32)

    send(lev_ref, lev_out)

    def attend(jobs):
        scores = [nt(lev_ref[0, q, :], lev_ref[1, k, :]) * scale for q, k, _ in jobs]
        tops = [wide(jnp.max(x, axis=1, keepdims=True)) for x in scores]
        expos = [jnp.exp(x - across(top, x.shape[1])) for x, top in zip(scores, tops)]
        numers = [nn(x.astype(BF16), lev_ref[2, k, :]) for x, (_, k, _) in zip(expos, jobs)]
        denoms = [wide(jnp.sum(x, axis=1, keepdims=True)) for x in expos]
        return [
            (top, denom * factor, numer * factor) if factor != 1 else (top, denom, numer)
            for top, denom, numer, (_, _, factor) in zip(tops, denoms, numers, jobs)
        ]

    def merge(at, stats):
        top, denom, numer = stats
        up = mu[at, :]
        peak = jnp.maximum(top, up)
        mine, theirs = jnp.exp(top - peak), jnp.exp(up - peak)
        return peak, mine * denom + theirs * du[at, :], mine * numer + theirs * nu[at, :]

    coarse = coarse_blocks(tokens)
    stats = attend([(near, far, float(2**height)) for height, _, near, far in coarse])
    for (height, row, near, _), one in zip(coarse, stats):
        if height < LEVELS:
            one = merge(near, one)
        for ref, value in zip((mu, du, nu), one):
            put_twice(ref, spans[height - 1][0] + 2 * row, value)
    for first in range(0, tokens, PAIRS * 2 * BLOCK):
        pairs = [
            slice(row, row + 2 * BLOCK)
            for row in range(first, min(first + PAIRS * 2 * BLOCK, tokens), 2 * BLOCK)
        ]
        for at, one in zip(pairs, attend([(at, at, 1) for at in pairs])):
            peak, total, summed = merge(at, one)
            attended = (summed / total).astype(BF16)
            lse_ref[at, :] = peak + jnp.log(total)
            pair = slice(at.start // BLOCK, at.stop // BLOCK)
            out_ref[pair, BLOCK:, :] = attended.reshape(2, BLOCK, WIDTH)
            send(lse_ref.at[at, :], lse_out.at[at, :])
            send(out_ref.at[pair, BLOCK:, :], att_out.at[pair, :, :])
    for copy in copies:
        copy.wait()


def forward(qkv, att_grad):
    blocks = qkv.shape[0]
    tokens = blocks * BLOCK
    spans, total_rows = level_rows(tokens)
    finer = total_rows - spans[LEVELS][1]
    outs = [
        ((blocks, 2 * BLOCK, WIDTH), BF16, "vmem"),
        ((blocks, BLOCK, WIDTH), BF16, "hbm"),
        ((tokens, WIDTH), F32, "hbm"),
        ((3, total_rows, WIDTH), BF16, "hbm"),
    ]
    return kernel_call(
        functools.partial(forward_body, blocks),
        outs,
        ["vmem"] * 2,
        32,
        scratch=[
            pltpu.VMEM((tokens, WIDTH), F32),
            pltpu.VMEM((3, total_rows, WIDTH), BF16),
            pltpu.VMEM((3, total_rows, WIDTH), F32),
            pltpu.VMEM((finer, WIDTH), F32),
            pltpu.VMEM((finer, WIDTH), F32),
            pltpu.VMEM((finer, WIDTH), F32),
            dma(1 + blocks),
        ],
        cost=cost(4 * tokens * 384 * WIDTH, 8 << 20),
        name="head_forward",
    )(qkv, att_grad)


def backward_body(
    blocks, grad_in, att_in, lse_in, lev_in, rows_in, w_in, out_ref, output_ref,
    att_ref, lev_ref, ys, ds, rs, cg, up, rows_ref, w_ref, sems,
):
    tokens = blocks * BLOCK
    spans, total_rows = level_rows(tokens)
    scale = 1.0 / math.sqrt(WIDTH)
    parts, count = 4, [0]

    def fetch(source, target):
        copy = pltpu.make_async_copy(source, target, sems.at[count[0]])
        count[0] += 1
        copy.start()
        return copy

    first_loads = []
    for p in range(parts):
        some = slice(p * blocks // parts, (p + 1) * blocks // parts)
        at = slice(p * tokens // parts, (p + 1) * tokens // parts)
        first_loads.append(
            [
                fetch(grad_in.at[at, :], cg.at[at, :]),
                fetch(att_in.at[some, :, :], att_ref.at[some, :, :]),
                fetch(lse_in.at[at, :], rs.at[at, :]),
            ]
        )
    coarse = slice(tokens, total_rows)
    later_loads = [
        fetch(lev_in.at[:, coarse, :], lev_ref.at[:, coarse, :]),
        fetch(lev_in.at[:, :tokens, :], lev_ref.at[:, :tokens, :]),
        fetch(rows_in, rows_ref),
        fetch(w_in, w_ref),
    ]
    for b in range(blocks):
        if b % (blocks // parts) == 0:
            for copy in first_loads[b // (blocks // parts)]:
                copy.wait()
        at = slice(b * BLOCK, (b + 1) * BLOCK)
        grad = cg[at, :].astype(F32)
        ys[at, :] = grad
        ds[at, :] = wide(jnp.sum(grad * att_ref[b].astype(F32), axis=1, keepdims=True))
    for height in range(1, LEVELS + 1):
        below, _ = spans[height - 1]
        base, rows = spans[height]
        for r in range(0, rows, BLOCK):
            at = slice(base + r, base + r + BLOCK)
            first = below + 2 * r
            lo, hi = evens(rs, first, BLOCK), odds(rs, first, BLOCK)
            low = jnp.minimum(lo, hi)
            lo, hi = jnp.exp(low - lo), jnp.exp(low - hi)
            grad = lo * evens(ys, first, BLOCK) + hi * odds(ys, first, BLOCK)
            delta = lo * evens(ds, first, BLOCK) + hi * odds(ds, first, BLOCK)
            ys[at, :], ds[at, :], rs[at, :] = grad, delta, low
            cg[at, :] = grad.astype(BF16)

    def gradients(jobs):
        scores = [nt(lev_ref[0, q, :], lev_ref[1, k, :]) * scale for q, k in jobs]
        inner = [nt(cg[q, :], lev_ref[2, k, :]) for q, k in jobs]
        expos = [
            jnp.exp(x - across(rs[q, :], x.shape[1])) for x, (q, _) in zip(scores, jobs)
        ]
        sgrads = [
            (expo * (x - across(ds[q, :], x.shape[1])) * scale).astype(BF16)
            for expo, x, (q, _) in zip(expos, inner, jobs)
        ]
        probs = [expo.astype(BF16) for expo in expos]
        q_parts = [nn(x, lev_ref[1, k, :]) for x, (_, k) in zip(sgrads, jobs)]
        k_parts = [tn(x, lev_ref[0, q, :]) for x, (q, _) in zip(sgrads, jobs)]
        v_parts = [tn(x, cg[q, :]) for x, (q, _) in zip(probs, jobs)]
        return list(zip(q_parts, k_parts, v_parts))

    later_loads[0].wait()
    coarse = coarse_blocks(tokens)
    for (height, row, near, far), parts in zip(
        coarse, gradients([(near, far) for _, _, near, far in coarse])
    ):
        for x, (at, first) in enumerate(((near, row), (far, row ^ BLOCK), (far, row ^ BLOCK))):
            value = parts[x]
            if height < LEVELS:
                value = value + up[x, at, :]
            put_twice(up.at[x], spans[height - 1][0] + 2 * first, value)
    later_loads[1].wait()
    for first in range(0, tokens, PAIRS * 2 * BLOCK):
        pairs = [
            slice(row, row + 2 * BLOCK)
            for row in range(first, min(first + PAIRS * 2 * BLOCK, tokens), 2 * BLOCK)
        ]
        for at, parts in zip(pairs, gradients([(at, at) for at in pairs])):
            pair = slice(at.start // BLOCK, at.stop // BLOCK)
            for x, value in enumerate(parts):
                value = (value + up[x, at, :]).astype(BF16)
                out_ref[pair, x * BLOCK : (x + 1) * BLOCK, :] = value.reshape(2, BLOCK, WIDTH)
    later_loads[2].wait()
    later_loads[3].wait()
    rows = jnp.concatenate([rows_ref[h] for h in range(HEADS)], axis=1)
    width = w_ref.shape[1]
    for first in range(0, width, 512):
        at = slice(first, first + 512)
        output_ref[:, at] = nn(rows, w_ref[:, at]).astype(BF16)


def backward(grad, att, lse, lev, rows, w_out):
    blocks = att.shape[0]
    tokens = blocks * BLOCK
    spans, total_rows = level_rows(tokens)
    finer = total_rows - spans[LEVELS][1]
    return kernel_call(
        functools.partial(backward_body, blocks),
        [
            ((blocks, 3 * BLOCK, WIDTH), BF16, "vmem"),
            ((BLOCK, w_out.shape[1]), BF16, "vmem"),
        ],
        ["hbm"] * 6,
        44,
        scratch=[
            pltpu.VMEM(att.shape, BF16),
            pltpu.VMEM(lev.shape, BF16),
            pltpu.VMEM((total_rows, WIDTH), F32),
            pltpu.VMEM((total_rows, WIDTH), F32),
            pltpu.VMEM((total_rows, WIDTH), F32),
            pltpu.VMEM((total_rows, WIDTH), BF16),
            pltpu.VMEM((3, finer, WIDTH), F32),
            pltpu.VMEM(rows.shape, BF16),
            pltpu.VMEM(w_out.shape, BF16),
            dma(16),
        ],
        cost=cost(10 * tokens * 384 * WIDTH + 2 * BLOCK * w_out.size, 24 << 20),
        name="head_backward",
    )(grad.reshape(tokens, WIDTH), att, lse, lev, rows, w_out)


def tile_body(groups, per, grads_ref, att_ref, *refs):
    cot_refs = refs[:groups]
    out_ref, lhs, held, total, sems = refs[groups:]
    rows, depth = lhs.shape
    chunk = rows // HEADS
    copies = []
    for k, ref in enumerate(cot_refs):
        at = slice(k * BLOCK, (k + 1) * BLOCK)
        copies.append(pltpu.make_async_copy(ref, held.at[at, :], sems.at[k]))
        copies[-1].start()
    out_ref[:, : 3 * BLOCK, :] = grads_ref[...]
    mine = lax.axis_index("outer")
    for k in range(groups):
        for j in range(per):
            lhs[j * WIDTH : (j + 1) * WIDTH, k * BLOCK : (k + 1) * BLOCK] = att_ref[
                (mine ^ k) * per + j
            ].T
    half, step = depth // 2, 512
    for copy in copies[: groups // 2]:
        copy.wait()
    for first in range(0, held.shape[1], step):
        at = slice(first, first + step)
        total[:, at] = nn(lhs[:, :half], held[:half, at])
    for copy in copies[groups // 2 :]:
        copy.wait()
    for first in range(0, held.shape[1], step):
        at = slice(first, first + step)
        part = (total[:, at] + nn(lhs[:, half:], held[half:, at])).astype(BF16)
        for i in range(HEADS):
            for j in range(step // WIDTH):
                to = 3 * BLOCK + (first // WIDTH + j) * chunk
                out_ref[i, to : to + chunk, :] = part[
                    i * chunk : (i + 1) * chunk, j * WIDTH : (j + 1) * WIDTH
                ]


def with_tile(grads, att, pieces):
    groups, width = len(pieces), pieces[0].shape[1]
    per = HEADS // groups
    chunk = per * WIDTH // HEADS
    extra = chunk * (width // WIDTH)
    return kernel_call(
        functools.partial(tile_body, groups, per),
        [((HEADS, 3 * BLOCK + extra, WIDTH), BF16, "vmem")],
        ["vmem", "vmem"] + ["hbm"] * groups,
        18,
        scratch=[
            pltpu.VMEM((per * WIDTH, groups * BLOCK), BF16),
            pltpu.VMEM((groups * BLOCK, width), BF16),
            pltpu.VMEM((per * WIDTH, width), F32),
            dma(groups),
        ],
        cost=cost(2 * groups * BLOCK * per * WIDTH * width, 10 << 20),
        name="projection_tile",
    )(grads, att, *pieces)[0]


def unpack_body(scale, in_ref, q_ref, k_ref, v_ref, w_ref):
    chunk, width = w_ref.shape
    for h in range(HEADS):
        for x, ref in enumerate((q_ref, k_ref, v_ref)):
            ref[:, h * WIDTH : (h + 1) * WIDTH] = in_ref[h, x * BLOCK : (x + 1) * BLOCK, :]
    for c in range(width // WIDTH):
        at = 3 * BLOCK + c * chunk
        total = in_ref[0, at : at + chunk, :].astype(F32)
        for h in range(1, HEADS):
            total = total + in_ref[h, at : at + chunk, :].astype(F32)
        w_ref[:, c * WIDTH : (c + 1) * WIDTH] = total * scale


def unpack(got, scale):
    chunk = (got.shape[1] - 3 * BLOCK) // HEADS
    width = HEADS * WIDTH
    return kernel_call(
        functools.partial(unpack_body, scale),
        [((BLOCK, width), BF16, "vmem")] * 3 + [((chunk, width), F32, "vmem")],
        ["vmem"],
        8,
        cost=cost(0, 6 << 20),
        name="unpack_grads",
    )(got)


def split_body(got_ref, grad_ref, att_ref, sems):
    copies = [
        pltpu.make_async_copy(got_ref.at[:, BLOCK:, :], att_ref, sems.at[0]),
        pltpu.make_async_copy(got_ref.at[:, :BLOCK, :], grad_ref, sems.at[1]),
    ]
    for copy in copies:
        copy.start()
    for copy in copies:
        copy.wait()


def split(got, after):
    return kernel_call(
        split_body,
        [((HEADS, BLOCK, WIDTH), BF16, "hbm")] * 2,
        ["vmem"],
        2,
        scratch=[dma(2)],
        cost=cost(0, 2 << 20),
        name="split_attended",
        after=after,
    )(got)


def swap(value, axis):
    return lax.all_to_all(value, axis, 0, 0, tiled=True)


def from_outer(value, apart):
    size = lax.axis_size("outer")
    return lax.ppermute(value, "outer", [(i, i ^ apart) for i in range(size)])


def on_device(query_in, key_in, value_in, w_out, cotangent):
    groups = lax.axis_size("outer")
    tokens = query_in.shape[0] * lax.axis_size(("outer", "inner"))
    pieces = {0: cotangent, 1: from_outer(cotangent, 1)}
    for k in range(2, groups, 2):
        pieces[k] = from_outer(cotangent, k)
    far = [pieces[k] for k in range(2, groups, 2)]
    qkv = swap(pack(query_in, key_in, value_in), "inner")
    att_grad = attended_gradient(cotangent, w_out)
    sent, att_own, lse, lev = forward(qkv, att_grad)
    grad, att = split(swap(sent, "inner"), after=[pieces[1]] + far)
    for k in range(2, groups, 2):
        pieces[k + 1] = from_outer(pieces[k], 1)
    att_outer = swap(att, "outer")
    grads, output = backward(grad, att_own, lse, lev, att, w_out)
    pieces = [pieces[k] for k in range(groups)]
    last = swap(with_tile(grads, att_outer, pieces), "inner")
    query_grad, key_grad, value_grad, w_out_grad = unpack(last, 1.0 / math.sqrt(tokens))
    return output, query_grad, key_grad, value_grad, w_out_grad


def solution(mesh):
    rows = P(("outer", "inner"), None)
    return jax.shard_map(
        on_device,
        mesh=mesh,
        in_specs=(rows, rows, rows, P(), rows),
        out_specs=(rows,) * 5,
        check_vma=False,
    )
```

```python
import functools
import math

import jax
import jax.numpy as jnp
from jax import lax
from jax.experimental import pallas as pl
from jax.experimental.pallas import tpu as pltpu
from jax.sharding import PartitionSpec as P

HEADS = 16
BLOCK = 128
LEVELS = 3
WIDTH = 128
BF16 = jnp.bfloat16
F32 = jnp.float32
CHUNK = 256
PAIRS = 8


def nt(a, b):
    return lax.dot_general(a, b, (((1,), (1,)), ((), ())), preferred_element_type=F32)


def nn(a, b):
    return lax.dot_general(a, b, (((1,), (0,)), ((), ())), preferred_element_type=F32)


def tn(a, b):
    return lax.dot_general(a, b, (((0,), (0,)), ((), ())), preferred_element_type=F32)


def wide(stat, columns=WIDTH):
    return jnp.broadcast_to(stat, (stat.shape[0], columns))


def evens(ref, base, rows):
    return ref[pl.ds(base, rows, stride=2), :]


def odds(ref, base, rows):
    return ref[pl.ds(base + 1, rows, stride=2), :]


def put_twice(ref, base, value):
    rows = value.shape[0]
    ref[pl.ds(base, rows, stride=2), :] = value
    ref[pl.ds(base + 1, rows, stride=2), :] = value


def across(stat, columns):
    return jnp.concatenate([stat] * (columns // WIDTH), axis=1)


def coarse_blocks(tokens):
    spans, _ = level_rows(tokens)
    out = []
    for height in range(LEVELS, 0, -1):
        base, rows = spans[height]
        for row in range(0, rows, BLOCK):
            near, far = base + row, base + (row ^ BLOCK)
            out.append((height, row, slice(near, near + BLOCK), slice(far, far + BLOCK)))
    return out


def level_rows(tokens):
    out, base = [], 0
    for height in range(LEVELS + 1):
        out.append((base, tokens >> height))
        base += tokens >> height
    return out, base


def kernel_call(body, outs, in_places, mib, scratch=(), cost=None, name=None, after=()):
    count = len(in_places)
    in_places = list(in_places) + ["hbm"] * len(after)

    def ordered(*refs):
        body(*refs[:count], *refs[len(in_places) :])

    spec = {
        "vmem": pl.BlockSpec(memory_space=pltpu.VMEM),
        "hbm": pl.BlockSpec(memory_space=pl.ANY),
    }
    shapes = [
        pltpu.HBM(shape, dtype) if place == "hbm" else jax.ShapeDtypeStruct(shape, dtype)
        for shape, dtype, place in outs
    ]
    call = pl.pallas_call(
        ordered,
        out_shape=shapes,
        in_specs=[spec[place] for place in in_places],
        out_specs=[spec[place] for _, _, place in outs],
        scratch_shapes=list(scratch),
        compiler_params=pltpu.CompilerParams(vmem_limit_bytes=int(mib * 2**20)),
        cost_estimate=cost,
        name=name,
    )

    def run(*operands):
        operands = [
            pltpu.with_memory_space_constraint(x, pltpu.HBM) if place == "hbm" else x
            for x, place in zip((*operands, *after), in_places)
        ]
        return call(*operands)

    return run


def dma(count):
    return pltpu.SemaphoreType.DMA((count,))


def cost(flops, nbytes):
    return pl.CostEstimate(flops=int(flops), bytes_accessed=int(nbytes), transcendentals=0)


def pack_body(q_ref, k_ref, v_ref, out_ref, held, packed, in_sems, out_sems):
    loads = [
        pltpu.make_async_copy(ref, held.at[x], in_sems.at[x])
        for x, ref in enumerate((q_ref, k_ref, v_ref))
    ]
    for load in loads:
        load.start()
    stores = []
    for x, load in enumerate(loads):
        load.wait()
        rows = slice(x * BLOCK, (x + 1) * BLOCK)
        for h in range(HEADS):
            packed[h, rows, :] = held[x, :, h * WIDTH : (h + 1) * WIDTH]
        stores.append(
            pltpu.make_async_copy(packed.at[:, rows, :], out_ref.at[:, rows, :], out_sems.at[x])
        )
        stores[-1].start()
    for store in stores:
        store.wait()


def pack(q, k, v):
    packed = (HEADS, 3 * BLOCK, WIDTH)
    return kernel_call(
        pack_body,
        [(packed, BF16, "hbm")],
        ["hbm"] * 3,
        6,
        scratch=[pltpu.VMEM((3,) + q.shape, BF16), pltpu.VMEM(packed, BF16), dma(3), dma(3)],
        cost=cost(0, 6 * q.size * 2),
        name="pack_qkv",
    )(q, k, v)[0]


def att_grad_body(chunks, cot_ref, w_ref, out_ref, held, sems):
    rows = held.shape[0] // chunks
    copies = []
    for c in range(chunks):
        at = slice(c * rows, (c + 1) * rows)
        copies.append(pltpu.make_async_copy(w_ref.at[at, :], held.at[at, :], sems.at[c]))
        copies[-1].start()
    for c, copy in enumerate(copies):
        at = slice(c * rows, (c + 1) * rows)
        copy.wait()
        out_ref[:, at] = nt(cot_ref[...], held[at, :]).astype(BF16)


def attended_gradient(cot, w_out):
    chunks = 4
    return kernel_call(
        functools.partial(att_grad_body, chunks),
        [(cot.shape, BF16, "vmem")],
        ["vmem", "hbm"],
        63.6,
        scratch=[pltpu.VMEM(w_out.shape, BF16), dma(chunks)],
        cost=cost(0, 1 << 20),
        name="attended_gradient",
    )(cot, w_out)[0]


def forward_body(
    blocks, in_ref, grad_ref, sent_out, att_out, lse_out, lev_out,
    out_ref, lse_ref, lev_ref, fq, mu, du, nu, sems,
):
    tokens = blocks * BLOCK
    spans, _ = level_rows(tokens)
    copies = []

    def send(source, target):
        copies.append(pltpu.make_async_copy(source, target, sems.at[len(copies)]))
        copies[-1].start()

    scale = 1.0 / math.sqrt(WIDTH)
    for b in range(blocks):
        out_ref[b, 0:BLOCK, :] = grad_ref[:, b * WIDTH : (b + 1) * WIDTH]
        for x in range(3):
            part = in_ref[b, x * BLOCK : (x + 1) * BLOCK, :]
            lev_ref[x, b * BLOCK : (b + 1) * BLOCK, :] = part
            fq[x, b * BLOCK : (b + 1) * BLOCK, :] = part.astype(F32)
    for height in range(1, LEVELS + 1):
        below, _ = spans[height - 1]
        base, rows = spans[height]
        step = min(CHUNK, rows)
        for x in range(3):
            for r in range(0, rows, step):
                mean = (
                    evens(fq.at[x], below + 2 * r, step) + odds(fq.at[x], below + 2 * r, step)
                ) * 0.5
                mean = mean.astype(BF16)
                lev_ref[x, base + r : base + r + step, :] = mean
                fq[x, base + r : base + r + step, :] = mean.astype(F32)

    send(lev_ref, lev_out)

    def attend(jobs):
        scores = [nt(lev_ref[0, q, :], lev_ref[1, k, :]) * scale for q, k, _ in jobs]
        tops = [wide(jnp.max(x, axis=1, keepdims=True)) for x in scores]
        expos = [jnp.exp(x - across(top, x.shape[1])) for x, top in zip(scores, tops)]
        numers = [nn(x.astype(BF16), lev_ref[2, k, :]) for x, (_, k, _) in zip(expos, jobs)]
        denoms = [wide(jnp.sum(x, axis=1, keepdims=True)) for x in expos]
        return [
            (top, denom * factor, numer * factor) if factor != 1 else (top, denom, numer)
            for top, denom, numer, (_, _, factor) in zip(tops, denoms, numers, jobs)
        ]

    def merge(at, stats):
        top, denom, numer = stats
        up = mu[at, :]
        peak = jnp.maximum(top, up)
        mine, theirs = jnp.exp(top - peak), jnp.exp(up - peak)
        return peak, mine * denom + theirs * du[at, :], mine * numer + theirs * nu[at, :]

    coarse = coarse_blocks(tokens)
    stats = attend([(near, far, float(2**height)) for height, _, near, far in coarse])
    for (height, row, near, _), one in zip(coarse, stats):
        if height < LEVELS:
            one = merge(near, one)
        for ref, value in zip((mu, du, nu), one):
            put_twice(ref, spans[height - 1][0] + 2 * row, value)
    for first in range(0, tokens, PAIRS * 2 * BLOCK):
        pairs = [
            slice(row, row + 2 * BLOCK)
            for row in range(first, min(first + PAIRS * 2 * BLOCK, tokens), 2 * BLOCK)
        ]
        for at, one in zip(pairs, attend([(at, at, 1) for at in pairs])):
            peak, total, summed = merge(at, one)
            attended = (summed / total).astype(BF16)
            lse_ref[at, :] = peak + jnp.log(total)
            pair = slice(at.start // BLOCK, at.stop // BLOCK)
            out_ref[pair, BLOCK:, :] = attended.reshape(2, BLOCK, WIDTH)
            send(lse_ref.at[at, :], lse_out.at[at, :])
            send(out_ref.at[pair, BLOCK:, :], att_out.at[pair, :, :])
            send(out_ref.at[pair, :, :], sent_out.at[pair, :, :])
    for copy in copies:
        copy.wait()


def forward(qkv, att_grad, after=()):
    blocks = qkv.shape[0]
    tokens = blocks * BLOCK
    spans, total_rows = level_rows(tokens)
    finer = total_rows - spans[LEVELS][1]
    outs = [
        ((blocks, 2 * BLOCK, WIDTH), BF16, "hbm"),
        ((blocks, BLOCK, WIDTH), BF16, "hbm"),
        ((tokens, WIDTH), F32, "hbm"),
        ((3, total_rows, WIDTH), BF16, "hbm"),
    ]
    return kernel_call(
        functools.partial(forward_body, blocks),
        outs,
        ["vmem"] * 2,
        32,
        scratch=[
            pltpu.VMEM((blocks, 2 * BLOCK, WIDTH), BF16),
            pltpu.VMEM((tokens, WIDTH), F32),
            pltpu.VMEM((3, total_rows, WIDTH), BF16),
            pltpu.VMEM((3, total_rows, WIDTH), F32),
            pltpu.VMEM((finer, WIDTH), F32),
            pltpu.VMEM((finer, WIDTH), F32),
            pltpu.VMEM((finer, WIDTH), F32),
            dma(1 + 3 * blocks // 2),
        ],
        cost=cost(4 * tokens * 384 * WIDTH, 8 << 20),
        name="head_forward",
        after=after,
    )(qkv, att_grad)


def backward_body(
    blocks, grad_in, att_in, lse_in, lev_in, rows_in, w_in, grads_out, output_ref,
    out_ref, att_ref, lev_ref, ys, ds, rs, cg, up, rows_ref, w_ref, sems,
):
    tokens = blocks * BLOCK
    spans, total_rows = level_rows(tokens)
    scale = 1.0 / math.sqrt(WIDTH)
    parts, count = 4, [0]

    def fetch(source, target):
        copy = pltpu.make_async_copy(source, target, sems.at[count[0]])
        count[0] += 1
        copy.start()
        return copy

    first_loads = []
    for p in range(parts):
        some = slice(p * blocks // parts, (p + 1) * blocks // parts)
        at = slice(p * tokens // parts, (p + 1) * tokens // parts)
        first_loads.append(
            [
                fetch(grad_in.at[at, :], cg.at[at, :]),
                fetch(att_in.at[some, :, :], att_ref.at[some, :, :]),
                fetch(lse_in.at[at, :], rs.at[at, :]),
            ]
        )
    coarse = slice(tokens, total_rows)
    later_loads = [
        fetch(lev_in.at[:, coarse, :], lev_ref.at[:, coarse, :]),
        fetch(lev_in.at[:, :tokens, :], lev_ref.at[:, :tokens, :]),
        fetch(rows_in, rows_ref),
        fetch(w_in, w_ref),
    ]
    for b in range(blocks):
        if b % (blocks // parts) == 0:
            for copy in first_loads[b // (blocks // parts)]:
                copy.wait()
        at = slice(b * BLOCK, (b + 1) * BLOCK)
        grad = cg[at, :].astype(F32)
        ys[at, :] = grad
        ds[at, :] = wide(jnp.sum(grad * att_ref[b].astype(F32), axis=1, keepdims=True))
    for height in range(1, LEVELS + 1):
        below, _ = spans[height - 1]
        base, rows = spans[height]
        for r in range(0, rows, BLOCK):
            at = slice(base + r, base + r + BLOCK)
            first = below + 2 * r
            lo, hi = evens(rs, first, BLOCK), odds(rs, first, BLOCK)
            low = jnp.minimum(lo, hi)
            lo, hi = jnp.exp(low - lo), jnp.exp(low - hi)
            grad = lo * evens(ys, first, BLOCK) + hi * odds(ys, first, BLOCK)
            delta = lo * evens(ds, first, BLOCK) + hi * odds(ds, first, BLOCK)
            ys[at, :], ds[at, :], rs[at, :] = grad, delta, low
            cg[at, :] = grad.astype(BF16)

    def gradients(jobs):
        scores = [nt(lev_ref[0, q, :], lev_ref[1, k, :]) * scale for q, k in jobs]
        inner = [nt(cg[q, :], lev_ref[2, k, :]) for q, k in jobs]
        expos = [
            jnp.exp(x - across(rs[q, :], x.shape[1])) for x, (q, _) in zip(scores, jobs)
        ]
        sgrads = [
            (expo * (x - across(ds[q, :], x.shape[1])) * scale).astype(BF16)
            for expo, x, (q, _) in zip(expos, inner, jobs)
        ]
        probs = [expo.astype(BF16) for expo in expos]
        q_parts = [nn(x, lev_ref[1, k, :]) for x, (_, k) in zip(sgrads, jobs)]
        k_parts = [tn(x, lev_ref[0, q, :]) for x, (q, _) in zip(sgrads, jobs)]
        v_parts = [tn(x, cg[q, :]) for x, (q, _) in zip(probs, jobs)]
        return list(zip(q_parts, k_parts, v_parts))

    later_loads[0].wait()
    coarse = coarse_blocks(tokens)
    for (height, row, near, far), parts in zip(
        coarse, gradients([(near, far) for _, _, near, far in coarse])
    ):
        for x, (at, first) in enumerate(((near, row), (far, row ^ BLOCK), (far, row ^ BLOCK))):
            value = parts[x]
            if height < LEVELS:
                value = value + up[x, at, :]
            put_twice(up.at[x], spans[height - 1][0] + 2 * first, value)
    later_loads[1].wait()
    stores = []
    for first in range(0, tokens, PAIRS * 2 * BLOCK):
        pairs = [
            slice(row, row + 2 * BLOCK)
            for row in range(first, min(first + PAIRS * 2 * BLOCK, tokens), 2 * BLOCK)
        ]
        for at, parts in zip(pairs, gradients([(at, at) for at in pairs])):
            pair = slice(at.start // BLOCK, at.stop // BLOCK)
            for x, value in enumerate(parts):
                value = (value + up[x, at, :]).astype(BF16)
                out_ref[pair, x * BLOCK : (x + 1) * BLOCK, :] = value.reshape(2, BLOCK, WIDTH)
            stores.append(fetch(out_ref.at[pair, :, :], grads_out.at[pair, :, :]))
    later_loads[2].wait()
    later_loads[3].wait()
    rows = jnp.concatenate([rows_ref[h] for h in range(HEADS)], axis=1)
    width = w_ref.shape[1]
    for first in range(0, width, 512):
        at = slice(first, first + 512)
        output_ref[:, at] = nn(rows, w_ref[:, at]).astype(BF16)
    for store in stores:
        store.wait()


def backward(grad, att, lse, lev, rows, w_out):
    blocks = att.shape[0]
    tokens = blocks * BLOCK
    spans, total_rows = level_rows(tokens)
    finer = total_rows - spans[LEVELS][1]
    return kernel_call(
        functools.partial(backward_body, blocks),
        [
            ((blocks, 3 * BLOCK, WIDTH), BF16, "hbm"),
            ((BLOCK, w_out.shape[1]), BF16, "vmem"),
        ],
        ["hbm"] * 6,
        63.6,
        scratch=[
            pltpu.VMEM((blocks, 3 * BLOCK, WIDTH), BF16),
            pltpu.VMEM(att.shape, BF16),
            pltpu.VMEM(lev.shape, BF16),
            pltpu.VMEM((total_rows, WIDTH), F32),
            pltpu.VMEM((total_rows, WIDTH), F32),
            pltpu.VMEM((total_rows, WIDTH), F32),
            pltpu.VMEM((total_rows, WIDTH), BF16),
            pltpu.VMEM((3, finer, WIDTH), F32),
            pltpu.VMEM(rows.shape, BF16),
            pltpu.VMEM(w_out.shape, BF16),
            dma(16 + blocks // 2),
        ],
        cost=cost(10 * tokens * 384 * WIDTH + 2 * BLOCK * w_out.size, 24 << 20),
        name="head_backward",
    )(grad.reshape(tokens, WIDTH), att, lse, lev, rows, w_out)


def tile_body(groups, per, grads_ref, att_ref, *refs):
    cot_refs = refs[:groups]
    out_ref, lhs, held, total, sems = refs[groups:]
    rows, depth = lhs.shape
    chunk = rows // HEADS
    copies = []
    for k, ref in enumerate(cot_refs):
        at = slice(k * BLOCK, (k + 1) * BLOCK)
        copies.append(pltpu.make_async_copy(ref, held.at[at, :], sems.at[k]))
        copies[-1].start()
    pass_on = pltpu.make_async_copy(grads_ref, out_ref.at[:, : 3 * BLOCK, :], sems.at[groups])
    pass_on.start()
    mine = lax.axis_index("outer")
    for k in range(groups):
        for j in range(per):
            lhs[j * WIDTH : (j + 1) * WIDTH, k * BLOCK : (k + 1) * BLOCK] = att_ref[
                (mine ^ k) * per + j
            ].T
    half, step = depth // 2, 512
    for copy in copies[: groups // 2]:
        copy.wait()
    for first in range(0, held.shape[1], step):
        at = slice(first, first + step)
        total[:, at] = nn(lhs[:, :half], held[:half, at])
    for copy in copies[groups // 2 :]:
        copy.wait()
    for first in range(0, held.shape[1], step):
        at = slice(first, first + step)
        part = (total[:, at] + nn(lhs[:, half:], held[half:, at])).astype(BF16)
        for i in range(HEADS):
            for j in range(step // WIDTH):
                to = 3 * BLOCK + (first // WIDTH + j) * chunk
                out_ref[i, to : to + chunk, :] = part[
                    i * chunk : (i + 1) * chunk, j * WIDTH : (j + 1) * WIDTH
                ]
    pass_on.wait()


def with_tile(grads, att, pieces):
    groups, width = len(pieces), pieces[0].shape[1]
    per = HEADS // groups
    chunk = per * WIDTH // HEADS
    extra = chunk * (width // WIDTH)
    return kernel_call(
        functools.partial(tile_body, groups, per),
        [((HEADS, 3 * BLOCK + extra, WIDTH), BF16, "vmem")],
        ["hbm", "vmem"] + ["hbm"] * groups,
        18,
        scratch=[
            pltpu.VMEM((per * WIDTH, groups * BLOCK), BF16),
            pltpu.VMEM((groups * BLOCK, width), BF16),
            pltpu.VMEM((per * WIDTH, width), F32),
            dma(groups + 1),
        ],
        cost=cost(2 * groups * BLOCK * per * WIDTH * width, 10 << 20),
        name="projection_tile",
    )(grads, att, *pieces)[0]


def unpack_body(scale, in_ref, q_ref, k_ref, v_ref, w_ref):
    chunk, width = w_ref.shape
    for h in range(HEADS):
        for x, ref in enumerate((q_ref, k_ref, v_ref)):
            ref[:, h * WIDTH : (h + 1) * WIDTH] = in_ref[h, x * BLOCK : (x + 1) * BLOCK, :]
    for c in range(width // WIDTH):
        at = 3 * BLOCK + c * chunk
        total = in_ref[0, at : at + chunk, :].astype(F32)
        for h in range(1, HEADS):
            total = total + in_ref[h, at : at + chunk, :].astype(F32)
        w_ref[:, c * WIDTH : (c + 1) * WIDTH] = total * scale


def unpack(got, scale):
    chunk = (got.shape[1] - 3 * BLOCK) // HEADS
    width = HEADS * WIDTH
    return kernel_call(
        functools.partial(unpack_body, scale),
        [((BLOCK, width), BF16, "vmem")] * 3 + [((chunk, width), F32, "vmem")],
        ["vmem"],
        8,
        cost=cost(0, 6 << 20),
        name="unpack_grads",
    )(got)


def split_body(got_ref, grad_ref, att_ref, sems):
    copies = [
        pltpu.make_async_copy(got_ref.at[:, BLOCK:, :], att_ref, sems.at[0]),
        pltpu.make_async_copy(got_ref.at[:, :BLOCK, :], grad_ref, sems.at[1]),
    ]
    for copy in copies:
        copy.start()
    for copy in copies:
        copy.wait()


def split(got):
    return kernel_call(
        split_body,
        [((HEADS, BLOCK, WIDTH), BF16, "hbm")] * 2,
        ["vmem"],
        2,
        scratch=[dma(2)],
        cost=cost(0, 2 << 20),
        name="split_attended",
    )(got)


def swap(value, axis):
    return lax.all_to_all(value, axis, 0, 0, tiled=True)


def from_outer(value, apart):
    size = lax.axis_size("outer")
    return lax.ppermute(value, "outer", [(i, i ^ apart) for i in range(size)])


def on_device(query_in, key_in, value_in, w_out, cotangent):
    groups = lax.axis_size("outer")
    tokens = query_in.shape[0] * lax.axis_size(("outer", "inner"))
    pieces = {0: cotangent, 1: from_outer(cotangent, 1)}
    for k in range(2, groups, 2):
        pieces[k] = from_outer(cotangent, k)
    far = [pieces[k] for k in range(2, groups, 2)]
    qkv = swap(pack(query_in, key_in, value_in), "inner")
    att_grad = attended_gradient(cotangent, w_out)
    sent, att_own, lse, lev = forward(qkv, att_grad, after=[pieces[1]] + far)
    for k in range(2, groups, 2):
        pieces[k + 1] = from_outer(pieces[k], 1)
    grad, att = split(swap(sent, "inner"))
    att_outer = swap(att, "outer")
    grads, output = backward(grad, att_own, lse, lev, att, w_out)
    pieces = [pieces[k] for k in range(groups)]
    last = swap(with_tile(grads, att_outer, pieces), "inner")
    query_grad, key_grad, value_grad, w_out_grad = unpack(last, 1.0 / math.sqrt(tokens))
    return output, query_grad, key_grad, value_grad, w_out_grad


def solution(mesh):
    rows = P(("outer", "inner"), None)
    return jax.shard_map(
        on_device,
        mesh=mesh,
        in_specs=(rows, rows, rows, P(), rows),
        out_specs=(rows,) * 5,
        check_vma=False,
    )
```

```python
import functools
import math

import jax
import jax.numpy as jnp
from jax import lax
from jax.experimental import pallas as pl
from jax.experimental.pallas import tpu as pltpu
from jax.sharding import PartitionSpec as P

HEADS = 16
BLOCK = 128
LEVELS = 3
WIDTH = 128
BF16 = jnp.bfloat16
F32 = jnp.float32
CHUNK = 256
PAIRS = 4


def nt(a, b):
    return lax.dot_general(a, b, (((1,), (1,)), ((), ())), preferred_element_type=F32)


def nn(a, b):
    return lax.dot_general(a, b, (((1,), (0,)), ((), ())), preferred_element_type=F32)


def tn(a, b):
    return lax.dot_general(a, b, (((0,), (0,)), ((), ())), preferred_element_type=F32)


def wide(stat, columns=WIDTH):
    return jnp.broadcast_to(stat, (stat.shape[0], columns))


def evens(ref, base, rows):
    return ref[pl.ds(base, rows, stride=2), :]


def odds(ref, base, rows):
    return ref[pl.ds(base + 1, rows, stride=2), :]


def put_twice(ref, base, value):
    rows = value.shape[0]
    ref[pl.ds(base, rows, stride=2), :] = value
    ref[pl.ds(base + 1, rows, stride=2), :] = value


def across(stat, columns):
    return jnp.concatenate([stat] * (columns // WIDTH), axis=1)


def coarse_blocks(tokens):
    spans, _ = level_rows(tokens)
    out = []
    for height in range(LEVELS, 0, -1):
        base, rows = spans[height]
        for row in range(0, rows, BLOCK):
            near, far = base + row, base + (row ^ BLOCK)
            out.append((height, row, slice(near, near + BLOCK), slice(far, far + BLOCK)))
    return out


def level_rows(tokens):
    out, base = [], 0
    for height in range(LEVELS + 1):
        out.append((base, tokens >> height))
        base += tokens >> height
    return out, base


def kernel_call(body, outs, in_places, mib, scratch=(), cost=None, name=None, after=(), aliases=None):
    count = len(in_places)
    in_places = list(in_places) + ["hbm"] * len(after)

    def ordered(*refs):
        body(*refs[:count], *refs[len(in_places) :])

    spec = {
        "vmem": pl.BlockSpec(memory_space=pltpu.VMEM),
        "hbm": pl.BlockSpec(memory_space=pl.ANY),
    }
    shapes = [
        pltpu.HBM(shape, dtype) if place == "hbm" else jax.ShapeDtypeStruct(shape, dtype)
        for shape, dtype, place in outs
    ]
    call = pl.pallas_call(
        ordered,
        out_shape=shapes,
        in_specs=[spec[place] for place in in_places],
        out_specs=[spec[place] for _, _, place in outs],
        scratch_shapes=list(scratch),
        compiler_params=pltpu.CompilerParams(vmem_limit_bytes=int(mib * 2**20)),
        cost_estimate=cost,
        name=name,
        input_output_aliases=aliases or {},
    )

    def run(*operands):
        operands = [
            pltpu.with_memory_space_constraint(x, pltpu.HBM) if place == "hbm" else x
            for x, place in zip((*operands, *after), in_places)
        ]
        return call(*operands)

    return run


def dma(count):
    return pltpu.SemaphoreType.DMA((count,))


def cost(flops, nbytes):
    return pl.CostEstimate(flops=int(flops), bytes_accessed=int(nbytes), transcendentals=0)


def pack_body(q_ref, k_ref, v_ref, out_ref, held, packed, in_sems, out_sems):
    loads = [
        pltpu.make_async_copy(ref, held.at[x], in_sems.at[x])
        for x, ref in enumerate((q_ref, k_ref, v_ref))
    ]
    for load in loads:
        load.start()
    stores = []
    for x, load in enumerate(loads):
        load.wait()
        rows = slice(x * BLOCK, (x + 1) * BLOCK)
        for h in range(HEADS):
            packed[h, rows, :] = held[x, :, h * WIDTH : (h + 1) * WIDTH]
        stores.append(
            pltpu.make_async_copy(packed.at[:, rows, :], out_ref.at[:, rows, :], out_sems.at[x])
        )
        stores[-1].start()
    for store in stores:
        store.wait()


def pack(q, k, v):
    packed = (HEADS, 3 * BLOCK, WIDTH)
    return kernel_call(
        pack_body,
        [(packed, BF16, "hbm")],
        ["hbm"] * 3,
        6,
        scratch=[pltpu.VMEM((3,) + q.shape, BF16), pltpu.VMEM(packed, BF16), dma(3), dma(3)],
        cost=cost(0, 6 * q.size * 2),
        name="pack_qkv",
    )(q, k, v)[0]


def att_grad_body(chunks, cot_ref, w_ref, out_ref, held, sems):
    rows = held.shape[0] // chunks
    copies = []
    for c in range(chunks):
        at = slice(c * rows, (c + 1) * rows)
        copies.append(pltpu.make_async_copy(w_ref.at[at, :], held.at[at, :], sems.at[c]))
        copies[-1].start()
    for c, copy in enumerate(copies):
        at = slice(c * rows, (c + 1) * rows)
        copy.wait()
        out_ref[:, at] = nt(cot_ref[...], held[at, :]).astype(BF16)


def attended_gradient(cot, w_out):
    chunks = 4
    return kernel_call(
        functools.partial(att_grad_body, chunks),
        [(cot.shape, BF16, "vmem")],
        ["vmem", "hbm"],
        63.6,
        scratch=[pltpu.VMEM(w_out.shape, BF16), dma(chunks)],
        cost=cost(0, 1 << 20),
        name="attended_gradient",
    )(cot, w_out)[0]


def forward_body(
    blocks, qkv_in, grad_in, sent_out, lse_out, lev_out,
    in_ref, grad_ref, out_ref, lse_ref, lev_ref, fq, mu, du, nu, sems,
):
    tokens = blocks * BLOCK
    spans, _ = level_rows(tokens)
    copies, count = [], [0]

    def send(source, target):
        copies.append(pltpu.make_async_copy(source, target, sems.at[count[0]]))
        copies[-1].start()
        count[0] += 1

    scale = 1.0 / math.sqrt(WIDTH)
    parts = 4
    for p in range(parts):
        some = slice(p * blocks // parts, (p + 1) * blocks // parts)
        send(qkv_in.at[some, :, :], in_ref.at[some, :, :])
    send(grad_in, grad_ref)
    loads, copies[:] = copies[:], []
    for b in range(blocks):
        if b % (blocks // parts) == 0:
            loads[b // (blocks // parts)].wait()
        for x in range(3):
            part = in_ref[b, x * BLOCK : (x + 1) * BLOCK, :]
            lev_ref[x, b * BLOCK : (b + 1) * BLOCK, :] = part
            fq[x, b * BLOCK : (b + 1) * BLOCK, :] = part.astype(F32)
    for height in range(1, LEVELS + 1):
        below, _ = spans[height - 1]
        base, rows = spans[height]
        step = min(CHUNK, rows)
        for x in range(3):
            for r in range(0, rows, step):
                mean = (
                    evens(fq.at[x], below + 2 * r, step) + odds(fq.at[x], below + 2 * r, step)
                ) * 0.5
                mean = mean.astype(BF16)
                lev_ref[x, base + r : base + r + step, :] = mean
                fq[x, base + r : base + r + step, :] = mean.astype(F32)

    send(lev_ref, lev_out)

    def attend(jobs):
        scores = [nt(lev_ref[0, q, :], lev_ref[1, k, :]) * scale for q, k, _ in jobs]
        tops = [wide(jnp.max(x, axis=1, keepdims=True)) for x in scores]
        expos = [jnp.exp(x - across(top, x.shape[1])) for x, top in zip(scores, tops)]
        numers = [nn(x.astype(BF16), lev_ref[2, k, :]) for x, (_, k, _) in zip(expos, jobs)]
        denoms = [wide(jnp.sum(x, axis=1, keepdims=True)) for x in expos]
        return [
            (top, denom * factor, numer * factor) if factor != 1 else (top, denom, numer)
            for top, denom, numer, (_, _, factor) in zip(tops, denoms, numers, jobs)
        ]

    def merge(at, stats):
        top, denom, numer = stats
        up = mu[at, :]
        peak = jnp.maximum(top, up)
        mine, theirs = jnp.exp(top - peak), jnp.exp(up - peak)
        return peak, mine * denom + theirs * du[at, :], mine * numer + theirs * nu[at, :]

    coarse = coarse_blocks(tokens)
    stats = attend([(near, far, float(2**height)) for height, _, near, far in coarse])
    for (height, row, near, _), one in zip(coarse, stats):
        if height < LEVELS:
            one = merge(near, one)
        for ref, value in zip((mu, du, nu), one):
            put_twice(ref, spans[height - 1][0] + 2 * row, value)
    loads[parts].wait()
    for b in range(blocks):
        out_ref[b, :BLOCK, :] = grad_ref[:, b * WIDTH : (b + 1) * WIDTH]
    for first in range(0, tokens, PAIRS * 2 * BLOCK):
        pairs = [
            slice(row, row + 2 * BLOCK)
            for row in range(first, min(first + PAIRS * 2 * BLOCK, tokens), 2 * BLOCK)
        ]
        for at, one in zip(pairs, attend([(at, at, 1) for at in pairs])):
            peak, total, summed = merge(at, one)
            attended = (summed / total).astype(BF16)
            lse_ref[at, :] = peak + jnp.log(total)
            pair = slice(at.start // BLOCK, at.stop // BLOCK)
            out_ref[pair, BLOCK:, :] = attended.reshape(2, BLOCK, WIDTH)
            send(lse_ref.at[at, :], lse_out.at[at, :])
            send(out_ref.at[pair, :, :], sent_out.at[pair, :, :])
    for copy in copies:
        copy.wait()


def forward(qkv, att_grad, after=()):
    blocks = qkv.shape[0]
    tokens = blocks * BLOCK
    spans, total_rows = level_rows(tokens)
    finer = total_rows - spans[LEVELS][1]
    outs = [
        ((blocks, 2 * BLOCK, WIDTH), BF16, "hbm"),
        ((tokens, WIDTH), F32, "hbm"),
        ((3, total_rows, WIDTH), BF16, "hbm"),
    ]
    return kernel_call(
        functools.partial(forward_body, blocks),
        outs,
        ["hbm"] * 2,
        32,
        scratch=[
            pltpu.VMEM(qkv.shape, BF16),
            pltpu.VMEM(att_grad.shape, BF16),
            pltpu.VMEM((blocks, 2 * BLOCK, WIDTH), BF16),
            pltpu.VMEM((tokens, WIDTH), F32),
            pltpu.VMEM((3, total_rows, WIDTH), BF16),
            pltpu.VMEM((3, total_rows, WIDTH), F32),
            pltpu.VMEM((finer, WIDTH), F32),
            pltpu.VMEM((finer, WIDTH), F32),
            pltpu.VMEM((finer, WIDTH), F32),
            dma(6 + blocks),
        ],
        cost=cost(4 * tokens * 384 * WIDTH, 8 << 20),
        name="head_forward",
        after=after,
    )(qkv, att_grad)


def backward_body(
    blocks, grad_in, sent_in, lse_in, lev_in, rows_in, w_in, grads_out, output_ref,
    out_ref, att_ref, lev_ref, ys, ds, rs, cg, up, rows_ref, w_ref, sems,
):
    tokens = blocks * BLOCK
    spans, total_rows = level_rows(tokens)
    scale = 1.0 / math.sqrt(WIDTH)
    parts, count = 4, [0]

    def fetch(source, target):
        copy = pltpu.make_async_copy(source, target, sems.at[count[0]])
        count[0] += 1
        copy.start()
        return copy

    first_loads = []
    for p in range(parts):
        some = slice(p * blocks // parts, (p + 1) * blocks // parts)
        at = slice(p * tokens // parts, (p + 1) * tokens // parts)
        first_loads.append(
            [
                fetch(grad_in.at[at, :], cg.at[at, :]),
                fetch(sent_in.at[some, BLOCK:, :], att_ref.at[some, :, :]),
                fetch(lse_in.at[at, :], rs.at[at, :]),
            ]
        )
    coarse = slice(tokens, total_rows)
    later_loads = [
        fetch(lev_in.at[:, coarse, :], lev_ref.at[:, coarse, :]),
        fetch(lev_in.at[:, :tokens, :], lev_ref.at[:, :tokens, :]),
        fetch(rows_in, rows_ref),
        fetch(w_in, w_ref),
    ]
    for b in range(blocks):
        if b % (blocks // parts) == 0:
            for copy in first_loads[b // (blocks // parts)]:
                copy.wait()
        at = slice(b * BLOCK, (b + 1) * BLOCK)
        grad = cg[at, :].astype(F32)
        ys[at, :] = grad
        ds[at, :] = wide(jnp.sum(grad * att_ref[b].astype(F32), axis=1, keepdims=True))
    for height in range(1, LEVELS + 1):
        below, _ = spans[height - 1]
        base, rows = spans[height]
        for r in range(0, rows, BLOCK):
            at = slice(base + r, base + r + BLOCK)
            first = below + 2 * r
            lo, hi = evens(rs, first, BLOCK), odds(rs, first, BLOCK)
            low = jnp.minimum(lo, hi)
            lo, hi = jnp.exp(low - lo), jnp.exp(low - hi)
            grad = lo * evens(ys, first, BLOCK) + hi * odds(ys, first, BLOCK)
            delta = lo * evens(ds, first, BLOCK) + hi * odds(ds, first, BLOCK)
            ys[at, :], ds[at, :], rs[at, :] = grad, delta, low
            cg[at, :] = grad.astype(BF16)

    def gradients(jobs):
        scores = [nt(lev_ref[0, q, :], lev_ref[1, k, :]) * scale for q, k in jobs]
        inner = [nt(cg[q, :], lev_ref[2, k, :]) for q, k in jobs]
        expos = [
            jnp.exp(x - across(rs[q, :], x.shape[1])) for x, (q, _) in zip(scores, jobs)
        ]
        sgrads = [
            (expo * (x - across(ds[q, :], x.shape[1])) * scale).astype(BF16)
            for expo, x, (q, _) in zip(expos, inner, jobs)
        ]
        probs = [expo.astype(BF16) for expo in expos]
        q_parts = [nn(x, lev_ref[1, k, :]) for x, (_, k) in zip(sgrads, jobs)]
        k_parts = [tn(x, lev_ref[0, q, :]) for x, (q, _) in zip(sgrads, jobs)]
        v_parts = [tn(x, cg[q, :]) for x, (q, _) in zip(probs, jobs)]
        return list(zip(q_parts, k_parts, v_parts))

    later_loads[0].wait()
    coarse = coarse_blocks(tokens)
    for (height, row, near, far), parts in zip(
        coarse, gradients([(near, far) for _, _, near, far in coarse])
    ):
        for x, (at, first) in enumerate(((near, row), (far, row ^ BLOCK), (far, row ^ BLOCK))):
            value = parts[x]
            if height < LEVELS:
                value = value + up[x, at, :]
            put_twice(up.at[x], spans[height - 1][0] + 2 * first, value)
    later_loads[1].wait()
    stores = []
    for first in range(0, tokens, PAIRS * 2 * BLOCK):
        pairs = [
            slice(row, row + 2 * BLOCK)
            for row in range(first, min(first + PAIRS * 2 * BLOCK, tokens), 2 * BLOCK)
        ]
        for at, parts in zip(pairs, gradients([(at, at) for at in pairs])):
            pair = slice(at.start // BLOCK, at.stop // BLOCK)
            for x, value in enumerate(parts):
                value = (value + up[x, at, :]).astype(BF16)
                out_ref[pair, x * BLOCK : (x + 1) * BLOCK, :] = value.reshape(2, BLOCK, WIDTH)
            stores.append(fetch(out_ref.at[pair, :, :], grads_out.at[pair, : 3 * BLOCK, :]))
    later_loads[2].wait()
    later_loads[3].wait()
    rows = jnp.concatenate([rows_ref[h] for h in range(HEADS)], axis=1)
    width = w_ref.shape[1]
    for first in range(0, width, 512):
        at = slice(first, first + 512)
        output_ref[:, at] = nn(rows, w_ref[:, at]).astype(BF16)
    for store in stores:
        store.wait()


def backward(grad, sent, lse, lev, rows, w_out):
    blocks = sent.shape[0]
    tokens = blocks * BLOCK
    spans, total_rows = level_rows(tokens)
    finer = total_rows - spans[LEVELS][1]
    extra = w_out.size // lax.axis_size("outer") // blocks // WIDTH
    return kernel_call(
        functools.partial(backward_body, blocks),
        [
            ((blocks, 3 * BLOCK + extra, WIDTH), BF16, "hbm"),
            ((BLOCK, w_out.shape[1]), BF16, "vmem"),
        ],
        ["hbm"] * 6,
        63.6,
        scratch=[
            pltpu.VMEM((blocks, 3 * BLOCK, WIDTH), BF16),
            pltpu.VMEM(rows.shape, BF16),
            pltpu.VMEM(lev.shape, BF16),
            pltpu.VMEM((total_rows, WIDTH), F32),
            pltpu.VMEM((total_rows, WIDTH), F32),
            pltpu.VMEM((total_rows, WIDTH), F32),
            pltpu.VMEM((total_rows, WIDTH), BF16),
            pltpu.VMEM((3, finer, WIDTH), F32),
            pltpu.VMEM(rows.shape, BF16),
            pltpu.VMEM(w_out.shape, BF16),
            dma(16 + blocks // 2),
        ],
        cost=cost(10 * tokens * 384 * WIDTH + 2 * BLOCK * w_out.size, 24 << 20),
        name="head_backward",
    )(grad.reshape(tokens, WIDTH), sent, lse, lev, rows, w_out)


def tile_body(groups, per, _, att_ref, *refs):
    cot_refs = refs[:groups]
    out_ref, lhs, held, total, tile, sems = refs[groups:]
    rows, depth = lhs.shape
    chunk = rows // HEADS
    copies = []
    for k, ref in enumerate(cot_refs):
        at = slice(k * BLOCK, (k + 1) * BLOCK)
        copies.append(pltpu.make_async_copy(ref, held.at[at, :], sems.at[k]))
        copies[-1].start()
    mine = lax.axis_index("outer")
    for k in range(groups):
        for j in range(per):
            lhs[j * WIDTH : (j + 1) * WIDTH, k * BLOCK : (k + 1) * BLOCK] = att_ref[
                (mine ^ k) * per + j
            ].T
    half, step, stores = depth // 2, 512, []
    for copy in copies[: groups // 2]:
        copy.wait()
    for first in range(0, held.shape[1], step):
        at = slice(first, first + step)
        total[:, at] = nn(lhs[:, :half], held[:half, at])
    for copy in copies[groups // 2 :]:
        copy.wait()
    for first in range(0, held.shape[1], step):
        at = slice(first, first + step)
        part = (total[:, at] + nn(lhs[:, half:], held[half:, at])).astype(BF16)
        for i in range(HEADS):
            for j in range(step // WIDTH):
                to = (first // WIDTH + j) * chunk
                tile[i, to : to + chunk, :] = part[
                    i * chunk : (i + 1) * chunk, j * WIDTH : (j + 1) * WIDTH
                ]
        done = slice(first // WIDTH * chunk, (first + step) // WIDTH * chunk)
        to = slice(3 * BLOCK + done.start, 3 * BLOCK + done.stop)
        stores.append(
            pltpu.make_async_copy(
                tile.at[:, done, :], out_ref.at[:, to, :], sems.at[groups + len(stores)]
            )
        )
        stores[-1].start()
    for store in stores:
        store.wait()


def with_tile(grads, att, pieces):
    groups, width = len(pieces), pieces[0].shape[1]
    per = HEADS // groups
    chunk = per * WIDTH // HEADS
    extra = chunk * (width // WIDTH)
    return kernel_call(
        functools.partial(tile_body, groups, per),
        [(grads.shape, BF16, "hbm")],
        ["hbm", "vmem"] + ["hbm"] * groups,
        18,
        scratch=[
            pltpu.VMEM((per * WIDTH, groups * BLOCK), BF16),
            pltpu.VMEM((groups * BLOCK, width), BF16),
            pltpu.VMEM((per * WIDTH, width), F32),
            pltpu.VMEM((HEADS, extra, WIDTH), BF16),
            dma(groups + width // 512),
        ],
        aliases={0: 0},
        cost=cost(2 * groups * BLOCK * per * WIDTH * width, 10 << 20),
        name="projection_tile",
    )(grads, att, *pieces)[0]


def unpack_body(scale, in_ref, q_ref, k_ref, v_ref, w_ref):
    chunk, width = w_ref.shape
    for h in range(HEADS):
        for x, ref in enumerate((q_ref, k_ref, v_ref)):
            ref[:, h * WIDTH : (h + 1) * WIDTH] = in_ref[h, x * BLOCK : (x + 1) * BLOCK, :]
    for c in range(width // WIDTH):
        at = 3 * BLOCK + c * chunk
        total = in_ref[0, at : at + chunk, :].astype(F32)
        for h in range(1, HEADS):
            total = total + in_ref[h, at : at + chunk, :].astype(F32)
        w_ref[:, c * WIDTH : (c + 1) * WIDTH] = total * scale


def unpack(got, scale):
    chunk = (got.shape[1] - 3 * BLOCK) // HEADS
    width = HEADS * WIDTH
    return kernel_call(
        functools.partial(unpack_body, scale),
        [((BLOCK, width), BF16, "vmem")] * 3 + [((chunk, width), F32, "vmem")],
        ["vmem"],
        8,
        cost=cost(0, 6 << 20),
        name="unpack_grads",
    )(got)


def split_body(got_ref, grad_ref, att_ref, sems):
    copies = [
        pltpu.make_async_copy(got_ref.at[:, BLOCK:, :], att_ref, sems.at[0]),
        pltpu.make_async_copy(got_ref.at[:, :BLOCK, :], grad_ref, sems.at[1]),
    ]
    for copy in copies:
        copy.start()
    for copy in copies:
        copy.wait()


def split(got, after):
    return kernel_call(
        split_body,
        [((HEADS, BLOCK, WIDTH), BF16, "hbm")] * 2,
        ["vmem"],
        2,
        scratch=[dma(2)],
        cost=cost(0, 2 << 20),
        name="split_attended",
        after=after,
    )(got)


def swap(value, axis):
    return lax.all_to_all(value, axis, 0, 0, tiled=True)


def from_outer(value, apart):
    size = lax.axis_size("outer")
    return lax.ppermute(value, "outer", [(i, i ^ apart) for i in range(size)])


def on_device(query_in, key_in, value_in, w_out, cotangent):
    groups = lax.axis_size("outer")
    tokens = query_in.shape[0] * lax.axis_size(("outer", "inner"))
    pieces = {0: cotangent, 1: from_outer(cotangent, 1)}
    for k in range(2, groups, 2):
        pieces[k] = from_outer(cotangent, k)
    late = [pieces[k] for k in range(2, groups, 2) if k & 6 == 4]
    soon = [pieces[k] for k in range(1, groups) if k in pieces and k & 6 != 4]
    qkv = swap(pack(query_in, key_in, value_in), "inner")
    att_grad = attended_gradient(cotangent, w_out)
    sent, lse, lev = forward(qkv, att_grad, after=soon)
    for k in range(2, groups, 2):
        pieces[k + 1] = from_outer(pieces[k], 1)
    grad, att = split(swap(sent, "inner"), late)
    att_outer = swap(att, "outer")
    grads, output = backward(grad, sent, lse, lev, att, w_out)
    pieces = [pieces[k] for k in range(groups)]
    last = swap(with_tile(grads, att_outer, pieces), "inner")
    query_grad, key_grad, value_grad, w_out_grad = unpack(last, 1.0 / math.sqrt(tokens))
    return output, query_grad, key_grad, value_grad, w_out_grad


def solution(mesh):
    rows = P(("outer", "inner"), None)
    return jax.shard_map(
        on_device,
        mesh=mesh,
        in_specs=(rows, rows, rows, P(), rows),
        out_specs=(rows,) * 5,
        check_vma=False,
    )
```

```python
import functools
import math

import jax
import jax.numpy as jnp
from jax import lax
from jax.experimental import pallas as pl
from jax.experimental.pallas import tpu as pltpu
from jax.sharding import PartitionSpec as P

HEADS = 16
BLOCK = 128
LEVELS = 3
WIDTH = 128
BF16 = jnp.bfloat16
F32 = jnp.float32
CHUNK = 256
PAIRS = 4


def nt(a, b):
    return lax.dot_general(a, b, (((1,), (1,)), ((), ())), preferred_element_type=F32)


def nn(a, b):
    return lax.dot_general(a, b, (((1,), (0,)), ((), ())), preferred_element_type=F32)


def tn(a, b):
    return lax.dot_general(a, b, (((0,), (0,)), ((), ())), preferred_element_type=F32)


def wide(stat, columns=WIDTH):
    return jnp.broadcast_to(stat, (stat.shape[0], columns))


def evens(ref, base, rows):
    return ref[pl.ds(base, rows, stride=2), :]


def odds(ref, base, rows):
    return ref[pl.ds(base + 1, rows, stride=2), :]


def put_twice(ref, base, value):
    rows = value.shape[0]
    ref[pl.ds(base, rows, stride=2), :] = value
    ref[pl.ds(base + 1, rows, stride=2), :] = value


def across(stat, columns):
    return jnp.concatenate([stat] * (columns // WIDTH), axis=1)


def coarse_blocks(tokens):
    spans, _ = level_rows(tokens)
    out = []
    for height in range(LEVELS, 0, -1):
        base, rows = spans[height]
        for row in range(0, rows, BLOCK):
            near, far = base + row, base + (row ^ BLOCK)
            out.append((height, row, slice(near, near + BLOCK), slice(far, far + BLOCK)))
    return out


def rows_of(token_ref, coarse_ref, x, at):
    tokens = token_ref.shape[0] * BLOCK
    if at.start >= tokens:
        return coarse_ref[x, at.start - tokens : at.stop - tokens, :]
    some = slice(at.start // BLOCK, at.stop // BLOCK)
    return token_ref[some, x * BLOCK : (x + 1) * BLOCK, :].reshape(at.stop - at.start, WIDTH)


def level_rows(tokens):
    out, base = [], 0
    for height in range(LEVELS + 1):
        out.append((base, tokens >> height))
        base += tokens >> height
    return out, base


def kernel_call(body, outs, in_places, mib, scratch=(), cost=None, name=None, after=(), aliases=None):
    count = len(in_places)
    in_places = list(in_places) + ["hbm"] * len(after)

    def ordered(*refs):
        body(*refs[:count], *refs[len(in_places) :])

    spec = {
        "vmem": pl.BlockSpec(memory_space=pltpu.VMEM),
        "hbm": pl.BlockSpec(memory_space=pl.ANY),
    }
    shapes = [
        pltpu.HBM(shape, dtype) if place == "hbm" else jax.ShapeDtypeStruct(shape, dtype)
        for shape, dtype, place in outs
    ]
    call = pl.pallas_call(
        ordered,
        out_shape=shapes,
        in_specs=[spec[place] for place in in_places],
        out_specs=[spec[place] for _, _, place in outs],
        scratch_shapes=list(scratch),
        compiler_params=pltpu.CompilerParams(vmem_limit_bytes=int(mib * 2**20)),
        cost_estimate=cost,
        name=name,
        input_output_aliases=aliases or {},
    )

    def run(*operands):
        operands = [
            pltpu.with_memory_space_constraint(x, pltpu.HBM) if place == "hbm" else x
            for x, place in zip((*operands, *after), in_places)
        ]
        return call(*operands)

    return run


def dma(count):
    return pltpu.SemaphoreType.DMA((count,))


def cost(flops, nbytes):
    return pl.CostEstimate(flops=int(flops), bytes_accessed=int(nbytes), transcendentals=0)


def pack_body(q_ref, k_ref, v_ref, out_ref, held, packed, in_sems, out_sems):
    loads = [
        pltpu.make_async_copy(ref, held.at[x], in_sems.at[x])
        for x, ref in enumerate((q_ref, k_ref, v_ref))
    ]
    for load in loads:
        load.start()
    stores = []
    for x, load in enumerate(loads):
        load.wait()
        rows = slice(x * BLOCK, (x + 1) * BLOCK)
        for h in range(HEADS):
            packed[h, rows, :] = held[x, :, h * WIDTH : (h + 1) * WIDTH]
        stores.append(
            pltpu.make_async_copy(packed.at[:, rows, :], out_ref.at[:, rows, :], out_sems.at[x])
        )
        stores[-1].start()
    for store in stores:
        store.wait()


def pack(q, k, v):
    packed = (HEADS, 3 * BLOCK, WIDTH)
    return kernel_call(
        pack_body,
        [(packed, BF16, "hbm")],
        ["hbm"] * 3,
        6,
        scratch=[pltpu.VMEM((3,) + q.shape, BF16), pltpu.VMEM(packed, BF16), dma(3), dma(3)],
        cost=cost(0, 6 * q.size * 2),
        name="pack_qkv",
    )(q, k, v)[0]


def att_grad_body(chunks, cot_ref, w_ref, out_ref, held, sems):
    rows = held.shape[0] // chunks
    copies = []
    for c in range(chunks):
        at = slice(c * rows, (c + 1) * rows)
        copies.append(pltpu.make_async_copy(w_ref.at[at, :], held.at[at, :], sems.at[c]))
        copies[-1].start()
    for c, copy in enumerate(copies):
        at = slice(c * rows, (c + 1) * rows)
        copy.wait()
        out_ref[:, at] = nt(cot_ref[...], held[at, :]).astype(BF16)


def attended_gradient(cot, w_out):
    chunks = 4
    return kernel_call(
        functools.partial(att_grad_body, chunks),
        [(cot.shape, BF16, "vmem")],
        ["vmem", "hbm"],
        63.6,
        scratch=[pltpu.VMEM(w_out.shape, BF16), dma(chunks)],
        cost=cost(0, 1 << 20),
        name="attended_gradient",
    )(cot, w_out)[0]


def forward_body(
    blocks, qkv_in, grad_in, sent_out, lse_out, lev_out,
    in_ref, grad_ref, out_ref, lse_ref, lev_ref, fq, mu, du, nu, sems,
):
    tokens = blocks * BLOCK
    spans, _ = level_rows(tokens)
    copies, count = [], [0]

    def send(source, target):
        copies.append(pltpu.make_async_copy(source, target, sems.at[count[0]]))
        copies[-1].start()
        count[0] += 1

    scale = 1.0 / math.sqrt(WIDTH)
    parts = 4
    for p in range(parts):
        some = slice(p * blocks // parts, (p + 1) * blocks // parts)
        send(qkv_in.at[some, :, :], in_ref.at[some, :, :])
    send(grad_in, grad_ref)
    loads, copies[:] = copies[:], []
    for b in range(blocks):
        if b % (blocks // parts) == 0:
            loads[b // (blocks // parts)].wait()
        for x in range(3):
            part = in_ref[b, x * BLOCK : (x + 1) * BLOCK, :]
            fq[x, b * BLOCK : (b + 1) * BLOCK, :] = part.astype(F32)
    for height in range(1, LEVELS + 1):
        below, _ = spans[height - 1]
        base, rows = spans[height]
        step = min(CHUNK, rows)
        for x in range(3):
            for r in range(0, rows, step):
                mean = (
                    evens(fq.at[x], below + 2 * r, step) + odds(fq.at[x], below + 2 * r, step)
                ) * 0.5
                mean = mean.astype(BF16)
                lev_ref[x, base - tokens + r : base - tokens + r + step, :] = mean
                fq[x, base + r : base + r + step, :] = mean.astype(F32)

    send(lev_ref, lev_out)

    level = functools.partial(rows_of, in_ref, lev_ref)

    def attend(jobs):
        scores = [nt(level(0, q), level(1, k)) * scale for q, k, _ in jobs]
        tops = [wide(jnp.max(x, axis=1, keepdims=True)) for x in scores]
        expos = [jnp.exp(x - across(top, x.shape[1])) for x, top in zip(scores, tops)]
        numers = [nn(x.astype(BF16), level(2, k)) for x, (_, k, _) in zip(expos, jobs)]
        denoms = [wide(jnp.sum(x, axis=1, keepdims=True)) for x in expos]
        return [
            (top, denom * factor, numer * factor) if factor != 1 else (top, denom, numer)
            for top, denom, numer, (_, _, factor) in zip(tops, denoms, numers, jobs)
        ]

    def merge(at, stats):
        top, denom, numer = stats
        up = mu[at, :]
        peak = jnp.maximum(top, up)
        mine, theirs = jnp.exp(top - peak), jnp.exp(up - peak)
        return peak, mine * denom + theirs * du[at, :], mine * numer + theirs * nu[at, :]

    coarse = coarse_blocks(tokens)
    stats = attend([(near, far, float(2**height)) for height, _, near, far in coarse])
    for (height, row, near, _), one in zip(coarse, stats):
        if height < LEVELS:
            one = merge(near, one)
        for ref, value in zip((mu, du, nu), one):
            put_twice(ref, spans[height - 1][0] + 2 * row, value)
    loads[parts].wait()
    for b in range(blocks):
        out_ref[b, :BLOCK, :] = grad_ref[:, b * WIDTH : (b + 1) * WIDTH]
    for first in range(0, tokens, PAIRS * 2 * BLOCK):
        pairs = [
            slice(row, row + 2 * BLOCK)
            for row in range(first, min(first + PAIRS * 2 * BLOCK, tokens), 2 * BLOCK)
        ]
        for at, one in zip(pairs, attend([(at, at, 1) for at in pairs])):
            peak, total, summed = merge(at, one)
            attended = (summed / total).astype(BF16)
            lse_ref[at, :] = peak + jnp.log(total)
            pair = slice(at.start // BLOCK, at.stop // BLOCK)
            out_ref[pair, BLOCK:, :] = attended.reshape(2, BLOCK, WIDTH)
            send(lse_ref.at[at, :], lse_out.at[at, :])
            send(out_ref.at[pair, :, :], sent_out.at[pair, :, :])
    for copy in copies:
        copy.wait()


def forward(qkv, att_grad, after=()):
    blocks = qkv.shape[0]
    tokens = blocks * BLOCK
    spans, total_rows = level_rows(tokens)
    finer = total_rows - spans[LEVELS][1]
    outs = [
        ((blocks, 2 * BLOCK, WIDTH), BF16, "hbm"),
        ((tokens, WIDTH), F32, "hbm"),
        ((3, total_rows - tokens, WIDTH), BF16, "hbm"),
    ]
    return kernel_call(
        functools.partial(forward_body, blocks),
        outs,
        ["hbm"] * 2,
        32,
        scratch=[
            pltpu.VMEM(qkv.shape, BF16),
            pltpu.VMEM(att_grad.shape, BF16),
            pltpu.VMEM((blocks, 2 * BLOCK, WIDTH), BF16),
            pltpu.VMEM((tokens, WIDTH), F32),
            pltpu.VMEM((3, total_rows - tokens, WIDTH), BF16),
            pltpu.VMEM((3, total_rows, WIDTH), F32),
            pltpu.VMEM((finer, WIDTH), F32),
            pltpu.VMEM((finer, WIDTH), F32),
            pltpu.VMEM((finer, WIDTH), F32),
            dma(6 + blocks),
        ],
        cost=cost(4 * tokens * 384 * WIDTH, 8 << 20),
        name="head_forward",
        after=after,
    )(qkv, att_grad)


def backward_body(
    blocks, grad_in, sent_in, lse_in, lev_in, qkv_in, rows_in, w_in, grads_out, output_ref,
    out_ref, att_ref, lev_ref, qkv_ref, ys, ds, rs, cg, up, rows_ref, w_ref, sems,
):
    tokens = blocks * BLOCK
    spans, _ = level_rows(tokens)
    scale = 1.0 / math.sqrt(WIDTH)
    parts, count = 4, [0]

    def fetch(source, target):
        copy = pltpu.make_async_copy(source, target, sems.at[count[0]])
        count[0] += 1
        copy.start()
        return copy

    first_loads = []
    for p in range(parts):
        some = slice(p * blocks // parts, (p + 1) * blocks // parts)
        at = slice(p * tokens // parts, (p + 1) * tokens // parts)
        first_loads.append(
            [
                fetch(grad_in.at[at, :], cg.at[at, :]),
                fetch(sent_in.at[some, BLOCK:, :], att_ref.at[some, :, :]),
                fetch(lse_in.at[at, :], rs.at[at, :]),
            ]
        )
    later_loads = [
        fetch(lev_in, lev_ref),
        fetch(qkv_in, qkv_ref),
        fetch(rows_in, rows_ref),
        fetch(w_in, w_ref),
    ]
    for b in range(blocks):
        if b % (blocks // parts) == 0:
            for copy in first_loads[b // (blocks // parts)]:
                copy.wait()
        at = slice(b * BLOCK, (b + 1) * BLOCK)
        grad = cg[at, :].astype(F32)
        ys[at, :] = grad
        ds[at, :] = wide(jnp.sum(grad * att_ref[b].astype(F32), axis=1, keepdims=True))
    for height in range(1, LEVELS + 1):
        below, _ = spans[height - 1]
        base, rows = spans[height]
        for r in range(0, rows, BLOCK):
            at = slice(base + r, base + r + BLOCK)
            first = below + 2 * r
            lo, hi = evens(rs, first, BLOCK), odds(rs, first, BLOCK)
            low = jnp.minimum(lo, hi)
            lo, hi = jnp.exp(low - lo), jnp.exp(low - hi)
            grad = lo * evens(ys, first, BLOCK) + hi * odds(ys, first, BLOCK)
            delta = lo * evens(ds, first, BLOCK) + hi * odds(ds, first, BLOCK)
            ys[at, :], ds[at, :], rs[at, :] = grad, delta, low
            cg[at, :] = grad.astype(BF16)

    level = functools.partial(rows_of, qkv_ref, lev_ref)

    def gradients(jobs):
        scores = [nt(level(0, q), level(1, k)) * scale for q, k in jobs]
        inner = [nt(cg[q, :], level(2, k)) for q, k in jobs]
        expos = [
            jnp.exp(x - across(rs[q, :], x.shape[1])) for x, (q, _) in zip(scores, jobs)
        ]
        sgrads = [
            (expo * (x - across(ds[q, :], x.shape[1])) * scale).astype(BF16)
            for expo, x, (q, _) in zip(expos, inner, jobs)
        ]
        probs = [expo.astype(BF16) for expo in expos]
        q_parts = [nn(x, level(1, k)) for x, (_, k) in zip(sgrads, jobs)]
        k_parts = [tn(x, level(0, q)) for x, (q, _) in zip(sgrads, jobs)]
        v_parts = [tn(x, cg[q, :]) for x, (q, _) in zip(probs, jobs)]
        return list(zip(q_parts, k_parts, v_parts))

    later_loads[0].wait()
    coarse = coarse_blocks(tokens)
    for (height, row, near, far), parts in zip(
        coarse, gradients([(near, far) for _, _, near, far in coarse])
    ):
        for x, (at, first) in enumerate(((near, row), (far, row ^ BLOCK), (far, row ^ BLOCK))):
            value = parts[x]
            if height < LEVELS:
                value = value + up[x, at, :]
            put_twice(up.at[x], spans[height - 1][0] + 2 * first, value)
    later_loads[1].wait()
    stores = []
    for first in range(0, tokens, PAIRS * 2 * BLOCK):
        pairs = [
            slice(row, row + 2 * BLOCK)
            for row in range(first, min(first + PAIRS * 2 * BLOCK, tokens), 2 * BLOCK)
        ]
        for at, parts in zip(pairs, gradients([(at, at) for at in pairs])):
            pair = slice(at.start // BLOCK, at.stop // BLOCK)
            for x, value in enumerate(parts):
                value = (value + up[x, at, :]).astype(BF16)
                out_ref[pair, x * BLOCK : (x + 1) * BLOCK, :] = value.reshape(2, BLOCK, WIDTH)
            stores.append(fetch(out_ref.at[pair, :, :], grads_out.at[pair, : 3 * BLOCK, :]))
    later_loads[2].wait()
    later_loads[3].wait()
    rows = jnp.concatenate([rows_ref[h] for h in range(HEADS)], axis=1)
    width = w_ref.shape[1]
    for first in range(0, width, 512):
        at = slice(first, first + 512)
        output_ref[:, at] = nn(rows, w_ref[:, at]).astype(BF16)
    for store in stores:
        store.wait()


def backward(grad, sent, lse, lev, qkv, rows, w_out):
    blocks = sent.shape[0]
    tokens = blocks * BLOCK
    spans, total_rows = level_rows(tokens)
    finer = total_rows - spans[LEVELS][1]
    extra = w_out.size // lax.axis_size("outer") // blocks // WIDTH
    return kernel_call(
        functools.partial(backward_body, blocks),
        [
            ((blocks, 3 * BLOCK + extra, WIDTH), BF16, "hbm"),
            ((BLOCK, w_out.shape[1]), BF16, "vmem"),
        ],
        ["hbm"] * 7,
        63.6,
        scratch=[
            pltpu.VMEM((blocks, 3 * BLOCK, WIDTH), BF16),
            pltpu.VMEM(rows.shape, BF16),
            pltpu.VMEM(lev.shape, BF16),
            pltpu.VMEM(qkv.shape, BF16),
            pltpu.VMEM((total_rows, WIDTH), F32),
            pltpu.VMEM((total_rows, WIDTH), F32),
            pltpu.VMEM((total_rows, WIDTH), F32),
            pltpu.VMEM((total_rows, WIDTH), BF16),
            pltpu.VMEM((3, finer, WIDTH), F32),
            pltpu.VMEM(rows.shape, BF16),
            pltpu.VMEM(w_out.shape, BF16),
            dma(16 + blocks // 2),
        ],
        cost=cost(10 * tokens * 384 * WIDTH + 2 * BLOCK * w_out.size, 24 << 20),
        name="head_backward",
    )(grad.reshape(tokens, WIDTH), sent, lse, lev, qkv, rows, w_out)


def tile_body(groups, per, _, att_in, *refs):
    cot_refs = refs[:groups]
    out_ref, att_ref, lhs, held, tile, sems = refs[groups:]
    chunk = lhs.shape[0] // HEADS
    chunks, step = held.shape[0], held.shape[2]
    att_copy = pltpu.make_async_copy(att_in, att_ref, sems.at[0])
    att_copy.start()
    copies, stores = [], []
    for c in range(chunks):
        for k, ref in enumerate(cot_refs):
            copies.append(
                pltpu.make_async_copy(
                    ref.at[:, c * step : (c + 1) * step],
                    held.at[c, k * BLOCK : (k + 1) * BLOCK, :],
                    sems.at[1 + c * groups + k],
                )
            )
            copies[-1].start()
    att_copy.wait()
    mine = lax.axis_index("outer")
    for k in range(groups):
        for j in range(per):
            lhs[j * WIDTH : (j + 1) * WIDTH, k * BLOCK : (k + 1) * BLOCK] = att_ref[
                (mine ^ k) * per + j
            ].T
    for c in range(chunks):
        for copy in copies[c * groups : (c + 1) * groups]:
            copy.wait()
        part = nn(lhs[...], held[c]).astype(BF16)
        first = c * step
        for i in range(HEADS):
            for j in range(step // WIDTH):
                to = (first // WIDTH + j) * chunk
                tile[i, to : to + chunk, :] = part[
                    i * chunk : (i + 1) * chunk, j * WIDTH : (j + 1) * WIDTH
                ]
        done = slice(first // WIDTH * chunk, (first + step) // WIDTH * chunk)
        to = slice(3 * BLOCK + done.start, 3 * BLOCK + done.stop)
        stores.append(
            pltpu.make_async_copy(
                tile.at[:, done, :], out_ref.at[:, to, :], sems.at[1 + chunks * groups + c]
            )
        )
        stores[-1].start()
    for store in stores:
        store.wait()


def with_tile(grads, att, pieces):
    groups, width = len(pieces), pieces[0].shape[1]
    per = HEADS // groups
    chunk = per * WIDTH // HEADS
    extra = chunk * (width // WIDTH)
    chunks = 4
    return kernel_call(
        functools.partial(tile_body, groups, per),
        [(grads.shape, BF16, "hbm")],
        ["hbm"] * (2 + groups),
        18,
        scratch=[
            pltpu.VMEM(att.shape, BF16),
            pltpu.VMEM((per * WIDTH, groups * BLOCK), BF16),
            pltpu.VMEM((chunks, groups * BLOCK, width // chunks), BF16),
            pltpu.VMEM((HEADS, extra, WIDTH), BF16),
            dma(1 + chunks * (groups + 1)),
        ],
        aliases={0: 0},
        cost=cost(2 * groups * BLOCK * per * WIDTH * width, 10 << 20),
        name="projection_tile",
    )(grads, att, *pieces)[0]


def unpack_body(scale, in_ref, q_ref, k_ref, v_ref, w_ref):
    chunk, width = w_ref.shape
    for h in range(HEADS):
        for x, ref in enumerate((q_ref, k_ref, v_ref)):
            ref[:, h * WIDTH : (h + 1) * WIDTH] = in_ref[h, x * BLOCK : (x + 1) * BLOCK, :]
    for c in range(width // WIDTH):
        at = 3 * BLOCK + c * chunk
        total = in_ref[0, at : at + chunk, :].astype(F32)
        for h in range(1, HEADS):
            total = total + in_ref[h, at : at + chunk, :].astype(F32)
        w_ref[:, c * WIDTH : (c + 1) * WIDTH] = total * scale


def unpack(got, scale):
    chunk = (got.shape[1] - 3 * BLOCK) // HEADS
    width = HEADS * WIDTH
    return kernel_call(
        functools.partial(unpack_body, scale),
        [((BLOCK, width), BF16, "vmem")] * 3 + [((chunk, width), F32, "vmem")],
        ["vmem"],
        8,
        cost=cost(0, 6 << 20),
        name="unpack_grads",
    )(got)


def split_body(got_ref, grad_ref, att_ref, sems):
    copies = [
        pltpu.make_async_copy(got_ref.at[:, BLOCK:, :], att_ref, sems.at[0]),
        pltpu.make_async_copy(got_ref.at[:, :BLOCK, :], grad_ref, sems.at[1]),
    ]
    for copy in copies:
        copy.start()
    for copy in copies:
        copy.wait()


def split(got, after):
    return kernel_call(
        split_body,
        [((HEADS, BLOCK, WIDTH), BF16, "hbm")] * 2,
        ["vmem"],
        2,
        scratch=[dma(2)],
        cost=cost(0, 2 << 20),
        name="split_attended",
        after=after,
    )(got)


def swap(value, axis):
    return lax.all_to_all(value, axis, 0, 0, tiled=True)


def from_outer(value, apart):
    size = lax.axis_size("outer")
    return lax.ppermute(value, "outer", [(i, i ^ apart) for i in range(size)])


def on_device(query_in, key_in, value_in, w_out, cotangent):
    groups = lax.axis_size("outer")
    tokens = query_in.shape[0] * lax.axis_size(("outer", "inner"))
    pieces = {k: from_outer(cotangent, k) if k else cotangent for k in range(groups) if k < 2 or k & 3 == 2}
    soon = [pieces[k] for k in pieces if k]
    qkv = swap(pack(query_in, key_in, value_in), "inner")
    att_grad = attended_gradient(cotangent, w_out)
    sent, lse, lev = forward(qkv, att_grad, after=soon)
    late = {k: from_outer(pieces[k + 2], 2) for k in range(4, groups, 4)}
    pieces.update(late)
    for k in range(2, groups, 2):
        pieces[k + 1] = from_outer(pieces[k], 1)
    grad, att = split(swap(sent, "inner"), list(late.values()))
    att_outer = swap(att, "outer")
    grads, output = backward(grad, sent, lse, lev, qkv, att, w_out)
    pieces = [pieces[k] for k in range(groups)]
    last = swap(with_tile(grads, att_outer, pieces), "inner")
    query_grad, key_grad, value_grad, w_out_grad = unpack(last, 1.0 / math.sqrt(tokens))
    return output, query_grad, key_grad, value_grad, w_out_grad


def solution(mesh):
    rows = P(("outer", "inner"), None)
    return jax.shard_map(
        on_device,
        mesh=mesh,
        in_specs=(rows, rows, rows, P(), rows),
        out_specs=(rows,) * 5,
        check_vma=False,
    )
```

```python
import functools
import math

import jax
import jax.numpy as jnp
from jax import lax
from jax.experimental import pallas as pl
from jax.experimental.pallas import tpu as pltpu
from jax.sharding import PartitionSpec as P

HEADS = 16
BLOCK = 128
LEVELS = 3
WIDTH = 128
BF16 = jnp.bfloat16
F32 = jnp.float32
CHUNK = 256
PAIRS = 4


def nt(a, b):
    return lax.dot_general(a, b, (((1,), (1,)), ((), ())), preferred_element_type=F32)


def nn(a, b):
    return lax.dot_general(a, b, (((1,), (0,)), ((), ())), preferred_element_type=F32)


def tn(a, b):
    return lax.dot_general(a, b, (((0,), (0,)), ((), ())), preferred_element_type=F32)


def wide(stat, columns=WIDTH):
    return jnp.broadcast_to(stat, (stat.shape[0], columns))


def evens(ref, base, rows):
    return ref[pl.ds(base, rows, stride=2), :]


def odds(ref, base, rows):
    return ref[pl.ds(base + 1, rows, stride=2), :]


def put_twice(ref, base, value):
    rows = value.shape[0]
    ref[pl.ds(base, rows, stride=2), :] = value
    ref[pl.ds(base + 1, rows, stride=2), :] = value


def across(stat, columns):
    return jnp.concatenate([stat] * (columns // WIDTH), axis=1)


def coarse_blocks(tokens):
    spans, _ = level_rows(tokens)
    out = []
    for height in range(LEVELS, 0, -1):
        base, rows = spans[height]
        for row in range(0, rows, BLOCK):
            near, far = base + row, base + (row ^ BLOCK)
            out.append((height, row, slice(near, near + BLOCK), slice(far, far + BLOCK)))
    return out


def rows_of(token_ref, coarse_ref, x, at):
    tokens = token_ref.shape[0] * BLOCK
    if at.start >= tokens:
        return coarse_ref[x, at.start - tokens : at.stop - tokens, :]
    some = slice(at.start // BLOCK, at.stop // BLOCK)
    return token_ref[some, x * BLOCK : (x + 1) * BLOCK, :].reshape(at.stop - at.start, WIDTH)


def level_rows(tokens):
    out, base = [], 0
    for height in range(LEVELS + 1):
        out.append((base, tokens >> height))
        base += tokens >> height
    return out, base


def kernel_call(body, outs, in_places, mib, scratch=(), cost=None, name=None, after=(), aliases=None):
    count = len(in_places)
    in_places = list(in_places) + ["hbm"] * len(after)

    def ordered(*refs):
        body(*refs[:count], *refs[len(in_places) :])

    spec = {
        "vmem": pl.BlockSpec(memory_space=pltpu.VMEM),
        "hbm": pl.BlockSpec(memory_space=pl.ANY),
    }
    shapes = [
        pltpu.HBM(shape, dtype) if place == "hbm" else jax.ShapeDtypeStruct(shape, dtype)
        for shape, dtype, place in outs
    ]
    call = pl.pallas_call(
        ordered,
        out_shape=shapes,
        in_specs=[spec[place] for place in in_places],
        out_specs=[spec[place] for _, _, place in outs],
        scratch_shapes=list(scratch),
        compiler_params=pltpu.CompilerParams(vmem_limit_bytes=int(mib * 2**20)),
        cost_estimate=cost,
        name=name,
        input_output_aliases=aliases or {},
    )

    def run(*operands):
        operands = [
            pltpu.with_memory_space_constraint(x, pltpu.HBM) if place == "hbm" else x
            for x, place in zip((*operands, *after), in_places)
        ]
        return call(*operands)

    return run


def dma(count):
    return pltpu.SemaphoreType.DMA((count,))


def cost(flops, nbytes):
    return pl.CostEstimate(flops=int(flops), bytes_accessed=int(nbytes), transcendentals=0)


def pack_body(q_ref, k_ref, v_ref, out_ref, held, packed, in_sems, out_sems):
    loads = [
        pltpu.make_async_copy(ref, held.at[x], in_sems.at[x])
        for x, ref in enumerate((q_ref, k_ref, v_ref))
    ]
    for load in loads:
        load.start()
    stores = []
    for x, load in enumerate(loads):
        load.wait()
        rows = slice(x * BLOCK, (x + 1) * BLOCK)
        for h in range(HEADS):
            packed[h, rows, :] = held[x, :, h * WIDTH : (h + 1) * WIDTH]
        stores.append(
            pltpu.make_async_copy(packed.at[:, rows, :], out_ref.at[:, rows, :], out_sems.at[x])
        )
        stores[-1].start()
    for store in stores:
        store.wait()


def pack(q, k, v):
    packed = (HEADS, 3 * BLOCK, WIDTH)
    return kernel_call(
        pack_body,
        [(packed, BF16, "hbm")],
        ["hbm"] * 3,
        6,
        scratch=[pltpu.VMEM((3,) + q.shape, BF16), pltpu.VMEM(packed, BF16), dma(3), dma(3)],
        cost=cost(0, 6 * q.size * 2),
        name="pack_qkv",
    )(q, k, v)[0]


def att_grad_body(chunks, cot_ref, w_ref, out_ref, held, sems):
    rows = held.shape[0] // chunks
    copies = []
    for c in range(chunks):
        at = slice(c * rows, (c + 1) * rows)
        copies.append(pltpu.make_async_copy(w_ref.at[at, :], held.at[at, :], sems.at[c]))
        copies[-1].start()
    for c, copy in enumerate(copies):
        at = slice(c * rows, (c + 1) * rows)
        copy.wait()
        out_ref[:, at] = nt(cot_ref[...], held[at, :]).astype(BF16)


def attended_gradient(cot, w_out):
    chunks = 4
    return kernel_call(
        functools.partial(att_grad_body, chunks),
        [(cot.shape, BF16, "vmem")],
        ["vmem", "hbm"],
        63.6,
        scratch=[pltpu.VMEM(w_out.shape, BF16), dma(chunks)],
        cost=cost(0, 1 << 20),
        name="attended_gradient",
    )(cot, w_out)[0]


def forward_body(
    blocks, qkv_in, grad_in, sent_out, lse_out, lev_out,
    in_ref, grad_ref, out_ref, lse_ref, lev_ref, fq, mu, du, nu, sems,
):
    tokens = blocks * BLOCK
    spans, _ = level_rows(tokens)
    copies, count = [], [0]

    def send(source, target):
        copies.append(pltpu.make_async_copy(source, target, sems.at[count[0]]))
        copies[-1].start()
        count[0] += 1

    scale = 1.0 / math.sqrt(WIDTH)
    parts = 4
    for p in range(parts):
        some = slice(p * blocks // parts, (p + 1) * blocks // parts)
        send(qkv_in.at[some, :, :], in_ref.at[some, :, :])
    send(grad_in, grad_ref)
    loads, copies[:] = copies[:], []
    for b in range(blocks):
        if b % (blocks // parts) == 0:
            loads[b // (blocks // parts)].wait()
        for x in range(3):
            part = in_ref[b, x * BLOCK : (x + 1) * BLOCK, :]
            fq[x, b * BLOCK : (b + 1) * BLOCK, :] = part.astype(F32)
    for height in range(1, LEVELS + 1):
        below, _ = spans[height - 1]
        base, rows = spans[height]
        step = min(CHUNK, rows)
        for x in range(3):
            for r in range(0, rows, step):
                mean = (
                    evens(fq.at[x], below + 2 * r, step) + odds(fq.at[x], below + 2 * r, step)
                ) * 0.5
                mean = mean.astype(BF16)
                lev_ref[x, base - tokens + r : base - tokens + r + step, :] = mean
                fq[x, base + r : base + r + step, :] = mean.astype(F32)

    send(lev_ref, lev_out)

    level = functools.partial(rows_of, in_ref, lev_ref)

    def attend(jobs):
        scores = [nt(level(0, q), level(1, k)) * scale for q, k, _ in jobs]
        tops = [wide(jnp.max(x, axis=1, keepdims=True)) for x in scores]
        expos = [jnp.exp(x - across(top, x.shape[1])) for x, top in zip(scores, tops)]
        numers = [nn(x.astype(BF16), level(2, k)) for x, (_, k, _) in zip(expos, jobs)]
        denoms = [wide(jnp.sum(x, axis=1, keepdims=True)) for x in expos]
        return [
            (top, denom * factor, numer * factor) if factor != 1 else (top, denom, numer)
            for top, denom, numer, (_, _, factor) in zip(tops, denoms, numers, jobs)
        ]

    def merge(at, stats):
        top, denom, numer = stats
        up = mu[at, :]
        peak = jnp.maximum(top, up)
        mine, theirs = jnp.exp(top - peak), jnp.exp(up - peak)
        return peak, mine * denom + theirs * du[at, :], mine * numer + theirs * nu[at, :]

    coarse = coarse_blocks(tokens)
    stats = attend([(near, far, float(2**height)) for height, _, near, far in coarse])
    for (height, row, near, _), one in zip(coarse, stats):
        if height < LEVELS:
            one = merge(near, one)
        for ref, value in zip((mu, du, nu), one):
            put_twice(ref, spans[height - 1][0] + 2 * row, value)
    loads[parts].wait()
    for b in range(blocks):
        out_ref[b, :BLOCK, :] = grad_ref[:, b * WIDTH : (b + 1) * WIDTH]
    for first in range(0, tokens, PAIRS * 2 * BLOCK):
        pairs = [
            slice(row, row + 2 * BLOCK)
            for row in range(first, min(first + PAIRS * 2 * BLOCK, tokens), 2 * BLOCK)
        ]
        for at, one in zip(pairs, attend([(at, at, 1) for at in pairs])):
            peak, total, summed = merge(at, one)
            attended = (summed / total).astype(BF16)
            lse_ref[at, :] = peak + jnp.log(total)
            pair = slice(at.start // BLOCK, at.stop // BLOCK)
            out_ref[pair, BLOCK:, :] = attended.reshape(2, BLOCK, WIDTH)
            send(lse_ref.at[at, :], lse_out.at[at, :])
            send(out_ref.at[pair, :, :], sent_out.at[pair, :, :])
    for copy in copies:
        copy.wait()


def forward(qkv, att_grad, after=()):
    blocks = qkv.shape[0]
    tokens = blocks * BLOCK
    spans, total_rows = level_rows(tokens)
    finer = total_rows - spans[LEVELS][1]
    outs = [
        ((blocks, 2 * BLOCK, WIDTH), BF16, "hbm"),
        ((tokens, WIDTH), F32, "hbm"),
        ((3, total_rows - tokens, WIDTH), BF16, "hbm"),
    ]
    return kernel_call(
        functools.partial(forward_body, blocks),
        outs,
        ["hbm"] * 2,
        32,
        scratch=[
            pltpu.VMEM(qkv.shape, BF16),
            pltpu.VMEM(att_grad.shape, BF16),
            pltpu.VMEM((blocks, 2 * BLOCK, WIDTH), BF16),
            pltpu.VMEM((tokens, WIDTH), F32),
            pltpu.VMEM((3, total_rows - tokens, WIDTH), BF16),
            pltpu.VMEM((3, total_rows, WIDTH), F32),
            pltpu.VMEM((finer, WIDTH), F32),
            pltpu.VMEM((finer, WIDTH), F32),
            pltpu.VMEM((finer, WIDTH), F32),
            dma(6 + blocks),
        ],
        cost=cost(4 * tokens * 384 * WIDTH, 8 << 20),
        name="head_forward",
        after=after,
    )(qkv, att_grad)


def backward_body(
    blocks, grad_in, sent_in, lse_in, lev_in, qkv_in, rows_in, w_in, grads_out, output_ref,
    out_ref, att_ref, lev_ref, qkv_ref, ys, ds, rs, cg, up, rows_ref, w_ref, sems,
):
    tokens = blocks * BLOCK
    spans, _ = level_rows(tokens)
    scale = 1.0 / math.sqrt(WIDTH)
    parts, count = 4, [0]

    def fetch(source, target):
        copy = pltpu.make_async_copy(source, target, sems.at[count[0]])
        count[0] += 1
        copy.start()
        return copy

    first_loads = []
    for p in range(parts):
        some = slice(p * blocks // parts, (p + 1) * blocks // parts)
        at = slice(p * tokens // parts, (p + 1) * tokens // parts)
        first_loads.append(
            [
                fetch(grad_in.at[at, :], cg.at[at, :]),
                fetch(sent_in.at[some, BLOCK:, :], att_ref.at[some, :, :]),
                fetch(lse_in.at[at, :], rs.at[at, :]),
            ]
        )
    later_loads = [
        fetch(lev_in, lev_ref),
        fetch(qkv_in, qkv_ref),
        fetch(rows_in, rows_ref),
        fetch(w_in, w_ref),
    ]
    for b in range(blocks):
        if b % (blocks // parts) == 0:
            for copy in first_loads[b // (blocks // parts)]:
                copy.wait()
        at = slice(b * BLOCK, (b + 1) * BLOCK)
        grad = cg[at, :].astype(F32)
        ys[at, :] = grad
        ds[at, :] = wide(jnp.sum(grad * att_ref[b].astype(F32), axis=1, keepdims=True))
    for height in range(1, LEVELS + 1):
        below, _ = spans[height - 1]
        base, rows = spans[height]
        for r in range(0, rows, BLOCK):
            at = slice(base + r, base + r + BLOCK)
            first = below + 2 * r
            lo, hi = evens(rs, first, BLOCK), odds(rs, first, BLOCK)
            low = jnp.minimum(lo, hi)
            lo, hi = jnp.exp(low - lo), jnp.exp(low - hi)
            grad = lo * evens(ys, first, BLOCK) + hi * odds(ys, first, BLOCK)
            delta = lo * evens(ds, first, BLOCK) + hi * odds(ds, first, BLOCK)
            ys[at, :], ds[at, :], rs[at, :] = grad, delta, low
            cg[at, :] = grad.astype(BF16)

    level = functools.partial(rows_of, qkv_ref, lev_ref)

    def gradients(jobs):
        scores = [nt(level(0, q), level(1, k)) * scale for q, k in jobs]
        inner = [nt(cg[q, :], level(2, k)) for q, k in jobs]
        expos = [
            jnp.exp(x - across(rs[q, :], x.shape[1])) for x, (q, _) in zip(scores, jobs)
        ]
        sgrads = [
            (expo * (x - across(ds[q, :], x.shape[1])) * scale).astype(BF16)
            for expo, x, (q, _) in zip(expos, inner, jobs)
        ]
        probs = [expo.astype(BF16) for expo in expos]
        q_parts = [nn(x, level(1, k)) for x, (_, k) in zip(sgrads, jobs)]
        k_parts = [tn(x, level(0, q)) for x, (q, _) in zip(sgrads, jobs)]
        v_parts = [tn(x, cg[q, :]) for x, (q, _) in zip(probs, jobs)]
        return list(zip(q_parts, k_parts, v_parts))

    later_loads[0].wait()
    coarse = coarse_blocks(tokens)
    for (height, row, near, far), parts in zip(
        coarse, gradients([(near, far) for _, _, near, far in coarse])
    ):
        for x, (at, first) in enumerate(((near, row), (far, row ^ BLOCK), (far, row ^ BLOCK))):
            value = parts[x]
            if height < LEVELS:
                value = value + up[x, at, :]
            put_twice(up.at[x], spans[height - 1][0] + 2 * first, value)
    later_loads[1].wait()
    stores = []
    for first in range(0, tokens, PAIRS * 2 * BLOCK):
        pairs = [
            slice(row, row + 2 * BLOCK)
            for row in range(first, min(first + PAIRS * 2 * BLOCK, tokens), 2 * BLOCK)
        ]
        for at, parts in zip(pairs, gradients([(at, at) for at in pairs])):
            pair = slice(at.start // BLOCK, at.stop // BLOCK)
            for x, value in enumerate(parts):
                value = (value + up[x, at, :]).astype(BF16)
                out_ref[pair, x * BLOCK : (x + 1) * BLOCK, :] = value.reshape(2, BLOCK, WIDTH)
            stores.append(fetch(out_ref.at[pair, :, :], grads_out.at[pair, : 3 * BLOCK, :]))
    later_loads[2].wait()
    later_loads[3].wait()
    rows = jnp.concatenate([rows_ref[h] for h in range(HEADS)], axis=1)
    width = w_ref.shape[1]
    for first in range(0, width, 512):
        at = slice(first, first + 512)
        output_ref[:, at] = nn(rows, w_ref[:, at]).astype(BF16)
    for store in stores:
        store.wait()


def backward(grad, sent, lse, lev, qkv, rows, w_out, after):
    blocks = sent.shape[0]
    tokens = blocks * BLOCK
    spans, total_rows = level_rows(tokens)
    finer = total_rows - spans[LEVELS][1]
    extra = w_out.size // lax.axis_size("outer") // blocks // WIDTH
    return kernel_call(
        functools.partial(backward_body, blocks),
        [
            ((blocks, 3 * BLOCK + extra, WIDTH), BF16, "hbm"),
            ((BLOCK, w_out.shape[1]), BF16, "vmem"),
        ],
        ["hbm"] * 7,
        63.6,
        scratch=[
            pltpu.VMEM((blocks, 3 * BLOCK, WIDTH), BF16),
            pltpu.VMEM(rows.shape, BF16),
            pltpu.VMEM(lev.shape, BF16),
            pltpu.VMEM(qkv.shape, BF16),
            pltpu.VMEM((total_rows, WIDTH), F32),
            pltpu.VMEM((total_rows, WIDTH), F32),
            pltpu.VMEM((total_rows, WIDTH), F32),
            pltpu.VMEM((total_rows, WIDTH), BF16),
            pltpu.VMEM((3, finer, WIDTH), F32),
            pltpu.VMEM(rows.shape, BF16),
            pltpu.VMEM(w_out.shape, BF16),
            dma(16 + blocks // 2),
        ],
        cost=cost(10 * tokens * 384 * WIDTH + 2 * BLOCK * w_out.size, 24 << 20),
        name="head_backward",
        after=after,
    )(grad.reshape(tokens, WIDTH), sent, lse, lev, qkv, rows, w_out)


def tile_body(groups, per, _, att_in, *refs):
    cot_refs = refs[:groups]
    out_ref, att_ref, lhs, held, tile, sems = refs[groups:]
    chunk = lhs.shape[0] // HEADS
    chunks, step = held.shape[0], held.shape[2]
    att_copy = pltpu.make_async_copy(att_in, att_ref, sems.at[0])
    att_copy.start()
    copies, stores = [], []
    for c in range(chunks):
        for k, ref in enumerate(cot_refs):
            copies.append(
                pltpu.make_async_copy(
                    ref.at[:, c * step : (c + 1) * step],
                    held.at[c, k * BLOCK : (k + 1) * BLOCK, :],
                    sems.at[1 + c * groups + k],
                )
            )
            copies[-1].start()
    att_copy.wait()
    mine = lax.axis_index("outer")
    for k in range(groups):
        for j in range(per):
            lhs[j * WIDTH : (j + 1) * WIDTH, k * BLOCK : (k + 1) * BLOCK] = att_ref[
                (mine ^ k) * per + j
            ].T
    for c in range(chunks):
        for copy in copies[c * groups : (c + 1) * groups]:
            copy.wait()
        part = nn(lhs[...], held[c]).astype(BF16)
        first = c * step
        for i in range(HEADS):
            for j in range(step // WIDTH):
                to = (first // WIDTH + j) * chunk
                tile[i, to : to + chunk, :] = part[
                    i * chunk : (i + 1) * chunk, j * WIDTH : (j + 1) * WIDTH
                ]
        done = slice(first // WIDTH * chunk, (first + step) // WIDTH * chunk)
        to = slice(3 * BLOCK + done.start, 3 * BLOCK + done.stop)
        stores.append(
            pltpu.make_async_copy(
                tile.at[:, done, :], out_ref.at[:, to, :], sems.at[1 + chunks * groups + c]
            )
        )
        stores[-1].start()
    for store in stores:
        store.wait()


def with_tile(grads, att, pieces):
    groups, width = len(pieces), pieces[0].shape[1]
    per = HEADS // groups
    chunk = per * WIDTH // HEADS
    extra = chunk * (width // WIDTH)
    chunks = 4
    return kernel_call(
        functools.partial(tile_body, groups, per),
        [(grads.shape, BF16, "hbm")],
        ["hbm"] * (2 + groups),
        18,
        scratch=[
            pltpu.VMEM(att.shape, BF16),
            pltpu.VMEM((per * WIDTH, groups * BLOCK), BF16),
            pltpu.VMEM((chunks, groups * BLOCK, width // chunks), BF16),
            pltpu.VMEM((HEADS, extra, WIDTH), BF16),
            dma(1 + chunks * (groups + 1)),
        ],
        aliases={0: 0},
        cost=cost(2 * groups * BLOCK * per * WIDTH * width, 10 << 20),
        name="projection_tile",
    )(grads, att, *pieces)[0]


def unpack_body(scale, in_ref, q_out, k_out, v_out, w_out, grads, w_ref, sems):
    chunk, width = w_ref.shape
    stores = []

    def send(source, target):
        stores.append(pltpu.make_async_copy(source, target, sems.at[len(stores)]))
        stores[-1].start()

    for x, target in enumerate((q_out, k_out, v_out)):
        for h in range(HEADS):
            grads[x, :, h * WIDTH : (h + 1) * WIDTH] = in_ref[h, x * BLOCK : (x + 1) * BLOCK, :]
        send(grads.at[x], target)
    for c in range(width // WIDTH):
        at = 3 * BLOCK + c * chunk
        total = in_ref[0, at : at + chunk, :].astype(F32)
        for h in range(1, HEADS):
            total = total + in_ref[h, at : at + chunk, :].astype(F32)
        w_ref[:, c * WIDTH : (c + 1) * WIDTH] = total * scale
    send(w_ref, w_out)
    for store in stores:
        store.wait()


def unpack(got, scale):
    chunk = (got.shape[1] - 3 * BLOCK) // HEADS
    width = HEADS * WIDTH
    return kernel_call(
        functools.partial(unpack_body, scale),
        [((BLOCK, width), BF16, "hbm")] * 3 + [((chunk, width), F32, "hbm")],
        ["vmem"],
        8,
        scratch=[
            pltpu.VMEM((3, BLOCK, width), BF16),
            pltpu.VMEM((chunk, width), F32),
            dma(4),
        ],
        cost=cost(0, 6 << 20),
        name="unpack_grads",
    )(got)


def split_body(got_ref, grad_ref, att_ref, sems):
    copies = [
        pltpu.make_async_copy(got_ref.at[:, BLOCK:, :], att_ref, sems.at[0]),
        pltpu.make_async_copy(got_ref.at[:, :BLOCK, :], grad_ref, sems.at[1]),
    ]
    for copy in copies:
        copy.start()
    for copy in copies:
        copy.wait()


def split(got):
    return kernel_call(
        split_body,
        [((HEADS, BLOCK, WIDTH), BF16, "hbm")] * 2,
        ["vmem"],
        2,
        scratch=[dma(2)],
        cost=cost(0, 2 << 20),
        name="split_attended",
    )(got)


def swap(value, axis):
    return lax.all_to_all(value, axis, 0, 0, tiled=True)


def from_outer(value, apart):
    size = lax.axis_size("outer")
    return lax.ppermute(value, "outer", [(i, i ^ apart) for i in range(size)])


def on_device(query_in, key_in, value_in, w_out, cotangent):
    groups = lax.axis_size("outer")
    tokens = query_in.shape[0] * lax.axis_size(("outer", "inner"))
    pieces = {k: from_outer(cotangent, k) if k else cotangent for k in range(groups) if k < 2 or k & 3 == 2}
    soon = [pieces[k] for k in pieces if k]
    qkv = swap(pack(query_in, key_in, value_in), "inner")
    att_grad = attended_gradient(cotangent, w_out)
    sent, lse, lev = forward(qkv, att_grad, after=soon)
    late = {k: from_outer(pieces[k + 2], 2) for k in range(4, groups, 4)}
    pieces.update(late)
    for k in range(2, groups, 2):
        pieces[k + 1] = from_outer(pieces[k], 1)
    grad, att = split(swap(sent, "inner"))
    att_outer = swap(att, "outer")
    grads, output = backward(grad, sent, lse, lev, qkv, att, w_out, list(late.values()))
    pieces = [pieces[k] for k in range(groups)]
    last = swap(with_tile(grads, att_outer, pieces), "inner")
    query_grad, key_grad, value_grad, w_out_grad = unpack(last, 1.0 / math.sqrt(tokens))
    return output, query_grad, key_grad, value_grad, w_out_grad


def solution(mesh):
    rows = P(("outer", "inner"), None)
    return jax.shard_map(
        on_device,
        mesh=mesh,
        in_specs=(rows, rows, rows, P(), rows),
        out_specs=(rows,) * 5,
        check_vma=False,
    )
```

```python
import functools
import math

import jax
import jax.numpy as jnp
from jax import lax
from jax.experimental import pallas as pl
from jax.experimental.pallas import tpu as pltpu
from jax.sharding import PartitionSpec as P

HEADS = 16
BLOCK = 128
LEVELS = 3
WIDTH = 128
BF16 = jnp.bfloat16
F32 = jnp.float32
CHUNK = 256
PAIRS = 4


def nt(a, b):
    return lax.dot_general(a, b, (((1,), (1,)), ((), ())), preferred_element_type=F32)


def nn(a, b):
    return lax.dot_general(a, b, (((1,), (0,)), ((), ())), preferred_element_type=F32)


def tn(a, b):
    return lax.dot_general(a, b, (((0,), (0,)), ((), ())), preferred_element_type=F32)


def wide(stat, columns=WIDTH):
    return jnp.broadcast_to(stat, (stat.shape[0], columns))


def evens(ref, base, rows):
    return ref[pl.ds(base, rows, stride=2), :]


def odds(ref, base, rows):
    return ref[pl.ds(base + 1, rows, stride=2), :]


def put_twice(ref, base, value):
    rows = value.shape[0]
    ref[pl.ds(base, rows, stride=2), :] = value
    ref[pl.ds(base + 1, rows, stride=2), :] = value


def diagonal(matrix):
    rows = lax.broadcasted_iota(jnp.int32, matrix.shape, 0)
    columns = lax.broadcasted_iota(jnp.int32, matrix.shape, 1)
    return jnp.where(rows == columns, matrix, 0.0)


def across(stat, columns):
    return jnp.concatenate([stat] * (columns // WIDTH), axis=1)


def coarse_blocks(tokens):
    spans, _ = level_rows(tokens)
    out = []
    for height in range(LEVELS, 0, -1):
        base, rows = spans[height]
        for row in range(0, rows, BLOCK):
            near, far = base + row, base + (row ^ BLOCK)
            out.append((height, row, slice(near, near + BLOCK), slice(far, far + BLOCK)))
    return out


def rows_of(token_ref, coarse_ref, x, at):
    tokens = token_ref.shape[0] * BLOCK
    if at.start >= tokens:
        return coarse_ref[x, at.start - tokens : at.stop - tokens, :]
    some = slice(at.start // BLOCK, at.stop // BLOCK)
    return token_ref[some, x * BLOCK : (x + 1) * BLOCK, :].reshape(at.stop - at.start, WIDTH)


def level_rows(tokens):
    out, base = [], 0
    for height in range(LEVELS + 1):
        out.append((base, tokens >> height))
        base += tokens >> height
    return out, base


def kernel_call(body, outs, in_places, mib, scratch=(), cost=None, name=None, after=(), aliases=None):
    count = len(in_places)
    in_places = list(in_places) + ["hbm"] * len(after)

    def ordered(*refs):
        body(*refs[:count], *refs[len(in_places) :])

    spec = {
        "vmem": pl.BlockSpec(memory_space=pltpu.VMEM),
        "hbm": pl.BlockSpec(memory_space=pl.ANY),
    }
    shapes = [
        pltpu.HBM(shape, dtype) if place == "hbm" else jax.ShapeDtypeStruct(shape, dtype)
        for shape, dtype, place in outs
    ]
    call = pl.pallas_call(
        ordered,
        out_shape=shapes,
        in_specs=[spec[place] for place in in_places],
        out_specs=[spec[place] for _, _, place in outs],
        scratch_shapes=list(scratch),
        compiler_params=pltpu.CompilerParams(vmem_limit_bytes=int(mib * 2**20)),
        cost_estimate=cost,
        name=name,
        input_output_aliases=aliases or {},
    )

    def run(*operands):
        operands = [
            pltpu.with_memory_space_constraint(x, pltpu.HBM) if place == "hbm" else x
            for x, place in zip((*operands, *after), in_places)
        ]
        return call(*operands)

    return run


def dma(count):
    return pltpu.SemaphoreType.DMA((count,))


def cost(flops, nbytes):
    return pl.CostEstimate(flops=int(flops), bytes_accessed=int(nbytes), transcendentals=0)


def pack_body(q_ref, k_ref, v_ref, out_ref, held, packed, in_sems, out_sems):
    loads = [
        pltpu.make_async_copy(ref, held.at[x], in_sems.at[x])
        for x, ref in enumerate((q_ref, k_ref, v_ref))
    ]
    for load in loads:
        load.start()
    stores = []
    for x, load in enumerate(loads):
        load.wait()
        rows = slice(x * BLOCK, (x + 1) * BLOCK)
        for h in range(HEADS):
            packed[h, rows, :] = held[x, :, h * WIDTH : (h + 1) * WIDTH]
        stores.append(
            pltpu.make_async_copy(packed.at[:, rows, :], out_ref.at[:, rows, :], out_sems.at[x])
        )
        stores[-1].start()
    for store in stores:
        store.wait()


def pack(q, k, v):
    packed = (HEADS, 3 * BLOCK, WIDTH)
    return kernel_call(
        pack_body,
        [(packed, BF16, "hbm")],
        ["hbm"] * 3,
        6,
        scratch=[pltpu.VMEM((3,) + q.shape, BF16), pltpu.VMEM(packed, BF16), dma(3), dma(3)],
        cost=cost(0, 6 * q.size * 2),
        name="pack_qkv",
    )(q, k, v)[0]


def att_grad_body(chunks, cot_ref, w_ref, out_ref, held, sems):
    rows = held.shape[0] // chunks
    copies = []
    for c in range(chunks):
        at = slice(c * rows, (c + 1) * rows)
        copies.append(pltpu.make_async_copy(w_ref.at[at, :], held.at[at, :], sems.at[c]))
        copies[-1].start()
    for c, copy in enumerate(copies):
        at = slice(c * rows, (c + 1) * rows)
        copy.wait()
        out_ref[:, at] = nt(cot_ref[...], held[at, :]).astype(BF16)


def attended_gradient(cot, w_out):
    chunks = 4
    return kernel_call(
        functools.partial(att_grad_body, chunks),
        [(cot.shape, BF16, "vmem")],
        ["vmem", "hbm"],
        63.6,
        scratch=[pltpu.VMEM(w_out.shape, BF16), dma(chunks)],
        cost=cost(0, 1 << 20),
        name="attended_gradient",
    )(cot, w_out)[0]


def forward_body(
    blocks, qkv_in, grad_in, sent_out, lse_out, lev_out,
    in_ref, grad_ref, out_ref, lse_ref, lev_ref, fq, mu, du, nu, sems,
):
    tokens = blocks * BLOCK
    spans, _ = level_rows(tokens)
    copies, count = [], [0]

    def send(source, target):
        copies.append(pltpu.make_async_copy(source, target, sems.at[count[0]]))
        copies[-1].start()
        count[0] += 1

    scale = 1.0 / math.sqrt(WIDTH)
    parts = 4
    for p in range(parts):
        some = slice(p * blocks // parts, (p + 1) * blocks // parts)
        send(qkv_in.at[some, :, :], in_ref.at[some, :, :])
    send(grad_in, grad_ref)
    loads, copies[:] = copies[:], []
    for b in range(blocks):
        if b % (blocks // parts) == 0:
            loads[b // (blocks // parts)].wait()
        for x in range(3):
            part = in_ref[b, x * BLOCK : (x + 1) * BLOCK, :]
            fq[x, b * BLOCK : (b + 1) * BLOCK, :] = part.astype(F32)
    for height in range(1, LEVELS + 1):
        below, _ = spans[height - 1]
        base, rows = spans[height]
        step = min(CHUNK, rows)
        for x in range(3):
            for r in range(0, rows, step):
                mean = (
                    evens(fq.at[x], below + 2 * r, step) + odds(fq.at[x], below + 2 * r, step)
                ) * 0.5
                mean = mean.astype(BF16)
                lev_ref[x, base - tokens + r : base - tokens + r + step, :] = mean
                fq[x, base + r : base + r + step, :] = mean.astype(F32)

    send(lev_ref, lev_out)

    level = functools.partial(rows_of, in_ref, lev_ref)

    def attend(jobs):
        scores = [nt(level(0, q), level(1, k)) * scale for q, k, _ in jobs]
        tops = [wide(jnp.max(x, axis=1, keepdims=True)) for x in scores]
        expos = [jnp.exp(x - across(top, x.shape[1])) for x, top in zip(scores, tops)]
        numers = [nn(x.astype(BF16), level(2, k)) for x, (_, k, _) in zip(expos, jobs)]
        denoms = [wide(jnp.sum(x, axis=1, keepdims=True)) for x in expos]
        return [
            (top, denom * factor, numer * factor) if factor != 1 else (top, denom, numer)
            for top, denom, numer, (_, _, factor) in zip(tops, denoms, numers, jobs)
        ]

    def merge(at, stats):
        top, denom, numer = stats
        up = mu[at, :]
        peak = jnp.maximum(top, up)
        mine, theirs = jnp.exp(top - peak), jnp.exp(up - peak)
        return peak, mine * denom + theirs * du[at, :], mine * numer + theirs * nu[at, :]

    coarse = coarse_blocks(tokens)
    stats = attend([(near, far, float(2**height)) for height, _, near, far in coarse])
    for (height, row, near, _), one in zip(coarse, stats):
        if height < LEVELS:
            one = merge(near, one)
        for ref, value in zip((mu, du, nu), one):
            put_twice(ref, spans[height - 1][0] + 2 * row, value)
    loads[parts].wait()
    for b in range(blocks):
        out_ref[b, :BLOCK, :] = grad_ref[:, b * WIDTH : (b + 1) * WIDTH]
    send(out_ref.at[:, :BLOCK, :], sent_out.at[:, :BLOCK, :])
    for first in range(0, tokens, PAIRS * 2 * BLOCK):
        pairs = [
            slice(row, row + 2 * BLOCK)
            for row in range(first, min(first + PAIRS * 2 * BLOCK, tokens), 2 * BLOCK)
        ]
        for at, one in zip(pairs, attend([(at, at, 1) for at in pairs])):
            peak, total, summed = merge(at, one)
            attended = (summed / total).astype(BF16)
            lse = peak + jnp.log(total)
            for half in range(2):
                b = at.start // BLOCK + half
                part = lse[half * BLOCK : (half + 1) * BLOCK]
                lse_ref[b : b + 1, :] = jnp.sum(diagonal(part), axis=0, keepdims=True)
            pair = slice(at.start // BLOCK, at.stop // BLOCK)
            out_ref[pair, BLOCK:, :] = attended.reshape(2, BLOCK, WIDTH)
            send(out_ref.at[pair, BLOCK:, :], sent_out.at[pair, BLOCK:, :])
    send(lse_ref, lse_out)
    for copy in copies:
        copy.wait()


def forward(qkv, att_grad, after=()):
    blocks = qkv.shape[0]
    tokens = blocks * BLOCK
    spans, total_rows = level_rows(tokens)
    finer = total_rows - spans[LEVELS][1]
    outs = [
        ((blocks, 2 * BLOCK, WIDTH), BF16, "hbm"),
        ((blocks, BLOCK), F32, "hbm"),
        ((3, total_rows - tokens, WIDTH), BF16, "hbm"),
    ]
    return kernel_call(
        functools.partial(forward_body, blocks),
        outs,
        ["hbm"] * 2,
        32,
        scratch=[
            pltpu.VMEM(qkv.shape, BF16),
            pltpu.VMEM(att_grad.shape, BF16),
            pltpu.VMEM((blocks, 2 * BLOCK, WIDTH), BF16),
            pltpu.VMEM((blocks, BLOCK), F32),
            pltpu.VMEM((3, total_rows - tokens, WIDTH), BF16),
            pltpu.VMEM((3, total_rows, WIDTH), F32),
            pltpu.VMEM((finer, WIDTH), F32),
            pltpu.VMEM((finer, WIDTH), F32),
            pltpu.VMEM((finer, WIDTH), F32),
            dma(8 + blocks // 2),
        ],
        cost=cost(4 * tokens * 384 * WIDTH, 8 << 20),
        name="head_forward",
        after=after,
    )(qkv, att_grad)


def backward_body(
    blocks, grad_in, sent_in, lse_in, lev_in, qkv_in, rows_in, w_in, grads_out, output_ref,
    out_ref, att_ref, lse_ref, lev_ref, qkv_ref, ys, ds, rs, cg, up, rows_ref, w_ref, sems,
):
    tokens = blocks * BLOCK
    spans, _ = level_rows(tokens)
    scale = 1.0 / math.sqrt(WIDTH)
    parts, count = 4, [0]

    def fetch(source, target):
        copy = pltpu.make_async_copy(source, target, sems.at[count[0]])
        count[0] += 1
        copy.start()
        return copy

    first_loads = []
    lse_load = fetch(lse_in, lse_ref)
    for p in range(parts):
        some = slice(p * blocks // parts, (p + 1) * blocks // parts)
        at = slice(p * tokens // parts, (p + 1) * tokens // parts)
        first_loads.append(
            [
                fetch(grad_in.at[at, :], cg.at[at, :]),
                fetch(sent_in.at[some, BLOCK:, :], att_ref.at[some, :, :]),
            ]
        )
    later_loads = [
        fetch(lev_in, lev_ref),
        fetch(qkv_in, qkv_ref),
        fetch(rows_in, rows_ref),
        fetch(w_in, w_ref),
    ]
    lse_load.wait()
    for b in range(blocks):
        if b % (blocks // parts) == 0:
            for copy in first_loads[b // (blocks // parts)]:
                copy.wait()
        at = slice(b * BLOCK, (b + 1) * BLOCK)
        lse = jnp.broadcast_to(lse_ref[b : b + 1, :], (BLOCK, BLOCK))
        rs[at, :] = wide(jnp.sum(diagonal(lse), axis=1, keepdims=True))
        grad = cg[at, :].astype(F32)
        ys[at, :] = grad
        ds[at, :] = wide(jnp.sum(grad * att_ref[b].astype(F32), axis=1, keepdims=True))
    for height in range(1, LEVELS + 1):
        below, _ = spans[height - 1]
        base, rows = spans[height]
        for r in range(0, rows, BLOCK):
            at = slice(base + r, base + r + BLOCK)
            first = below + 2 * r
            lo, hi = evens(rs, first, BLOCK), odds(rs, first, BLOCK)
            low = jnp.minimum(lo, hi)
            lo, hi = jnp.exp(low - lo), jnp.exp(low - hi)
            grad = lo * evens(ys, first, BLOCK) + hi * odds(ys, first, BLOCK)
            delta = lo * evens(ds, first, BLOCK) + hi * odds(ds, first, BLOCK)
            ys[at, :], ds[at, :], rs[at, :] = grad, delta, low
            cg[at, :] = grad.astype(BF16)

    level = functools.partial(rows_of, qkv_ref, lev_ref)

    def gradients(jobs):
        scores = [nt(level(0, q), level(1, k)) * scale for q, k in jobs]
        inner = [nt(cg[q, :], level(2, k)) for q, k in jobs]
        expos = [
            jnp.exp(x - across(rs[q, :], x.shape[1])) for x, (q, _) in zip(scores, jobs)
        ]
        sgrads = [
            (expo * (x - across(ds[q, :], x.shape[1])) * scale).astype(BF16)
            for expo, x, (q, _) in zip(expos, inner, jobs)
        ]
        probs = [expo.astype(BF16) for expo in expos]
        q_parts = [nn(x, level(1, k)) for x, (_, k) in zip(sgrads, jobs)]
        k_parts = [tn(x, level(0, q)) for x, (q, _) in zip(sgrads, jobs)]
        v_parts = [tn(x, cg[q, :]) for x, (q, _) in zip(probs, jobs)]
        return list(zip(q_parts, k_parts, v_parts))

    later_loads[0].wait()
    coarse = coarse_blocks(tokens)
    for (height, row, near, far), parts in zip(
        coarse, gradients([(near, far) for _, _, near, far in coarse])
    ):
        for x, (at, first) in enumerate(((near, row), (far, row ^ BLOCK), (far, row ^ BLOCK))):
            value = parts[x]
            if height < LEVELS:
                value = value + up[x, at, :]
            put_twice(up.at[x], spans[height - 1][0] + 2 * first, value)
    later_loads[1].wait()
    stores = []
    for first in range(0, tokens, PAIRS * 2 * BLOCK):
        pairs = [
            slice(row, row + 2 * BLOCK)
            for row in range(first, min(first + PAIRS * 2 * BLOCK, tokens), 2 * BLOCK)
        ]
        for at, parts in zip(pairs, gradients([(at, at) for at in pairs])):
            pair = slice(at.start // BLOCK, at.stop // BLOCK)
            for x, value in enumerate(parts):
                value = (value + up[x, at, :]).astype(BF16)
                out_ref[pair, x * BLOCK : (x + 1) * BLOCK, :] = value.reshape(2, BLOCK, WIDTH)
            stores.append(fetch(out_ref.at[pair, :, :], grads_out.at[pair, : 3 * BLOCK, :]))
    later_loads[2].wait()
    later_loads[3].wait()
    rows = jnp.concatenate([rows_ref[h] for h in range(HEADS)], axis=1)
    width = w_ref.shape[1]
    for first in range(0, width, 512):
        at = slice(first, first + 512)
        output_ref[:, at] = nn(rows, w_ref[:, at]).astype(BF16)
    for store in stores:
        store.wait()


def backward(grad, sent, lse, lev, qkv, rows, w_out, after):
    blocks = sent.shape[0]
    tokens = blocks * BLOCK
    spans, total_rows = level_rows(tokens)
    finer = total_rows - spans[LEVELS][1]
    extra = w_out.size // lax.axis_size("outer") // blocks // WIDTH
    return kernel_call(
        functools.partial(backward_body, blocks),
        [
            ((blocks, 3 * BLOCK + extra, WIDTH), BF16, "hbm"),
            ((BLOCK, w_out.shape[1]), BF16, "vmem"),
        ],
        ["hbm"] * 7,
        63.6,
        scratch=[
            pltpu.VMEM((blocks, 3 * BLOCK, WIDTH), BF16),
            pltpu.VMEM(rows.shape, BF16),
            pltpu.VMEM(lse.shape, F32),
            pltpu.VMEM(lev.shape, BF16),
            pltpu.VMEM(qkv.shape, BF16),
            pltpu.VMEM((total_rows, WIDTH), F32),
            pltpu.VMEM((total_rows, WIDTH), F32),
            pltpu.VMEM((total_rows, WIDTH), F32),
            pltpu.VMEM((total_rows, WIDTH), BF16),
            pltpu.VMEM((3, finer, WIDTH), F32),
            pltpu.VMEM(rows.shape, BF16),
            pltpu.VMEM(w_out.shape, BF16),
            dma(16 + blocks // 2),
        ],
        cost=cost(10 * tokens * 384 * WIDTH + 2 * BLOCK * w_out.size, 24 << 20),
        name="head_backward",
        after=after,
    )(grad.reshape(tokens, WIDTH), sent, lse, lev, qkv, rows, w_out)


def tile_body(groups, per, _, att_in, *refs):
    cot_refs = refs[:groups]
    out_ref, att_ref, lhs, held, tile, sems = refs[groups:]
    chunk = lhs.shape[0] // HEADS
    chunks, step = held.shape[0], held.shape[2]
    att_copy = pltpu.make_async_copy(att_in, att_ref, sems.at[0])
    att_copy.start()
    copies, stores = [], []
    for c in range(chunks):
        for k, ref in enumerate(cot_refs):
            copies.append(
                pltpu.make_async_copy(
                    ref.at[:, c * step : (c + 1) * step],
                    held.at[c, k * BLOCK : (k + 1) * BLOCK, :],
                    sems.at[1 + c * groups + k],
                )
            )
            copies[-1].start()
    att_copy.wait()
    mine = lax.axis_index("outer")
    for k in range(groups):
        for j in range(per):
            lhs[j * WIDTH : (j + 1) * WIDTH, k * BLOCK : (k + 1) * BLOCK] = att_ref[
                (mine ^ k) * per + j
            ].T
    for c in range(chunks):
        for copy in copies[c * groups : (c + 1) * groups]:
            copy.wait()
        part = nn(lhs[...], held[c]).astype(BF16)
        first = c * step
        for i in range(HEADS):
            for j in range(step // WIDTH):
                to = (first // WIDTH + j) * chunk
                tile[i, to : to + chunk, :] = part[
                    i * chunk : (i + 1) * chunk, j * WIDTH : (j + 1) * WIDTH
                ]
        done = slice(first // WIDTH * chunk, (first + step) // WIDTH * chunk)
        to = slice(3 * BLOCK + done.start, 3 * BLOCK + done.stop)
        stores.append(
            pltpu.make_async_copy(
                tile.at[:, done, :], out_ref.at[:, to, :], sems.at[1 + chunks * groups + c]
            )
        )
        stores[-1].start()
    for store in stores:
        store.wait()


def with_tile(grads, att, pieces):
    groups, width = len(pieces), pieces[0].shape[1]
    per = HEADS // groups
    chunk = per * WIDTH // HEADS
    extra = chunk * (width // WIDTH)
    chunks = 4
    return kernel_call(
        functools.partial(tile_body, groups, per),
        [(grads.shape, BF16, "hbm")],
        ["hbm"] * (2 + groups),
        18,
        scratch=[
            pltpu.VMEM(att.shape, BF16),
            pltpu.VMEM((per * WIDTH, groups * BLOCK), BF16),
            pltpu.VMEM((chunks, groups * BLOCK, width // chunks), BF16),
            pltpu.VMEM((HEADS, extra, WIDTH), BF16),
            dma(1 + chunks * (groups + 1)),
        ],
        aliases={0: 0},
        cost=cost(2 * groups * BLOCK * per * WIDTH * width, 10 << 20),
        name="projection_tile",
    )(grads, att, *pieces)[0]


def unpack_body(scale, in_ref, q_out, k_out, v_out, w_out, grads, w_ref, sems):
    chunk, width = w_ref.shape
    stores = []

    def send(source, target):
        stores.append(pltpu.make_async_copy(source, target, sems.at[len(stores)]))
        stores[-1].start()

    for x, target in enumerate((q_out, k_out, v_out)):
        for h in range(HEADS):
            grads[x, :, h * WIDTH : (h + 1) * WIDTH] = in_ref[h, x * BLOCK : (x + 1) * BLOCK, :]
        send(grads.at[x], target)
    for c in range(width // WIDTH):
        at = 3 * BLOCK + c * chunk
        total = in_ref[0, at : at + chunk, :].astype(F32)
        for h in range(1, HEADS):
            total = total + in_ref[h, at : at + chunk, :].astype(F32)
        w_ref[:, c * WIDTH : (c + 1) * WIDTH] = total * scale
    send(w_ref, w_out)
    for store in stores:
        store.wait()


def unpack(got, scale):
    chunk = (got.shape[1] - 3 * BLOCK) // HEADS
    width = HEADS * WIDTH
    return kernel_call(
        functools.partial(unpack_body, scale),
        [((BLOCK, width), BF16, "hbm")] * 3 + [((chunk, width), F32, "hbm")],
        ["vmem"],
        8,
        scratch=[
            pltpu.VMEM((3, BLOCK, width), BF16),
            pltpu.VMEM((chunk, width), F32),
            dma(4),
        ],
        cost=cost(0, 6 << 20),
        name="unpack_grads",
    )(got)


def split_body(got_ref, grad_ref, att_ref, sems):
    copies = [
        pltpu.make_async_copy(got_ref.at[:, BLOCK:, :], att_ref, sems.at[0]),
        pltpu.make_async_copy(got_ref.at[:, :BLOCK, :], grad_ref, sems.at[1]),
    ]
    for copy in copies:
        copy.start()
    for copy in copies:
        copy.wait()


def split(got):
    return kernel_call(
        split_body,
        [((HEADS, BLOCK, WIDTH), BF16, "hbm")] * 2,
        ["vmem"],
        2,
        scratch=[dma(2)],
        cost=cost(0, 2 << 20),
        name="split_attended",
    )(got)


def swap(value, axis):
    return lax.all_to_all(value, axis, 0, 0, tiled=True)


def from_outer(value, apart):
    size = lax.axis_size("outer")
    return lax.ppermute(value, "outer", [(i, i ^ apart) for i in range(size)])


def on_device(query_in, key_in, value_in, w_out, cotangent):
    groups = lax.axis_size("outer")
    tokens = query_in.shape[0] * lax.axis_size(("outer", "inner"))
    pieces = {k: from_outer(cotangent, k) if k else cotangent for k in range(groups) if k < 2 or k & 3 == 2}
    soon = [pieces[k] for k in pieces if k]
    qkv = swap(pack(query_in, key_in, value_in), "inner")
    att_grad = attended_gradient(cotangent, w_out)
    sent, lse, lev = forward(qkv, att_grad, after=soon)
    late = {k: from_outer(pieces[k + 2], 2) for k in range(4, groups, 4)}
    pieces.update(late)
    for k in range(2, groups, 2):
        pieces[k + 1] = from_outer(pieces[k], 1)
    grad, att = split(swap(sent, "inner"))
    att_outer = swap(att, "outer")
    grads, output = backward(grad, sent, lse, lev, qkv, att, w_out, list(late.values()))
    pieces = [pieces[k] for k in range(groups)]
    last = swap(with_tile(grads, att_outer, pieces), "inner")
    query_grad, key_grad, value_grad, w_out_grad = unpack(last, 1.0 / math.sqrt(tokens))
    return output, query_grad, key_grad, value_grad, w_out_grad


def solution(mesh):
    rows = P(("outer", "inner"), None)
    return jax.shard_map(
        on_device,
        mesh=mesh,
        in_specs=(rows, rows, rows, P(), rows),
        out_specs=(rows,) * 5,
        check_vma=False,
    )
```

```python
import functools
import math

import jax
import jax.numpy as jnp
from jax import lax
from jax.experimental import pallas as pl
from jax.experimental.pallas import tpu as pltpu
from jax.sharding import PartitionSpec as P

HEADS = 16
BLOCK = 128
LEVELS = 3
WIDTH = 128
BF16 = jnp.bfloat16
F32 = jnp.float32
CHUNK = 256
PAIRS = 4
GRAD_CHUNKS = 4


def nt(a, b):
    return lax.dot_general(a, b, (((1,), (1,)), ((), ())), preferred_element_type=F32)


def nn(a, b):
    return lax.dot_general(a, b, (((1,), (0,)), ((), ())), preferred_element_type=F32)


def tn(a, b):
    return lax.dot_general(a, b, (((0,), (0,)), ((), ())), preferred_element_type=F32)


def wide(stat, columns=WIDTH):
    return jnp.broadcast_to(stat, (stat.shape[0], columns))


def evens(ref, base, rows):
    return ref[pl.ds(base, rows, stride=2), :]


def odds(ref, base, rows):
    return ref[pl.ds(base + 1, rows, stride=2), :]


def put_twice(ref, base, value):
    rows = value.shape[0]
    ref[pl.ds(base, rows, stride=2), :] = value
    ref[pl.ds(base + 1, rows, stride=2), :] = value


def diagonal(matrix):
    rows = lax.broadcasted_iota(jnp.int32, matrix.shape, 0)
    columns = lax.broadcasted_iota(jnp.int32, matrix.shape, 1)
    return jnp.where(rows == columns, matrix, 0.0)


def across(stat, columns):
    return jnp.concatenate([stat] * (columns // WIDTH), axis=1)


def coarse_blocks(tokens):
    spans, _ = level_rows(tokens)
    out = []
    for height in range(LEVELS, 0, -1):
        base, rows = spans[height]
        for row in range(0, rows, BLOCK):
            near, far = base + row, base + (row ^ BLOCK)
            out.append((height, row, slice(near, near + BLOCK), slice(far, far + BLOCK)))
    return out


def rows_of(token_ref, coarse_ref, x, at):
    tokens = token_ref.shape[0] * BLOCK
    if at.start >= tokens:
        return coarse_ref[x, at.start - tokens : at.stop - tokens, :]
    some = slice(at.start // BLOCK, at.stop // BLOCK)
    return token_ref[some, x * BLOCK : (x + 1) * BLOCK, :].reshape(at.stop - at.start, WIDTH)


def level_rows(tokens):
    out, base = [], 0
    for height in range(LEVELS + 1):
        out.append((base, tokens >> height))
        base += tokens >> height
    return out, base


def kernel_call(body, outs, in_places, mib, scratch=(), cost=None, name=None, after=(), aliases=None):
    count = len(in_places)
    in_places = list(in_places) + ["hbm"] * len(after)

    def ordered(*refs):
        body(*refs[:count], *refs[len(in_places) :])

    spec = {
        "vmem": pl.BlockSpec(memory_space=pltpu.VMEM),
        "hbm": pl.BlockSpec(memory_space=pl.ANY),
    }
    shapes = [
        pltpu.HBM(shape, dtype) if place == "hbm" else jax.ShapeDtypeStruct(shape, dtype)
        for shape, dtype, place in outs
    ]
    call = pl.pallas_call(
        ordered,
        out_shape=shapes,
        in_specs=[spec[place] for place in in_places],
        out_specs=[spec[place] for _, _, place in outs],
        scratch_shapes=list(scratch),
        compiler_params=pltpu.CompilerParams(vmem_limit_bytes=int(mib * 2**20)),
        cost_estimate=cost,
        name=name,
        input_output_aliases=aliases or {},
    )

    def run(*operands):
        operands = [
            pltpu.with_memory_space_constraint(x, pltpu.HBM) if place == "hbm" else x
            for x, place in zip((*operands, *after), in_places)
        ]
        return call(*operands)

    return run


def dma(count):
    return pltpu.SemaphoreType.DMA((count,))


def cost(flops, nbytes):
    return pl.CostEstimate(flops=int(flops), bytes_accessed=int(nbytes), transcendentals=0)


def odd_core():
    return lax.axis_index("outer") & 1 == 1


def gradient(cot_ref, w_ref, grad_out, cot, held, grad, sems):
    rows = held.shape[0] // GRAD_CHUNKS
    load = pltpu.make_async_copy(cot_ref, cot, sems.at[GRAD_CHUNKS])
    load.start()
    copies = []
    for c in range(GRAD_CHUNKS):
        at = slice(c * rows, (c + 1) * rows)
        copies.append(pltpu.make_async_copy(w_ref.at[at, :], held.at[at, :], sems.at[c]))
        copies[-1].start()
    load.wait()
    for c, copy in enumerate(copies):
        at = slice(c * rows, (c + 1) * rows)
        copy.wait()
        grad[:, at] = nt(cot[...], held[at, :]).astype(BF16)
    store = pltpu.make_async_copy(grad, grad_out, sems.at[GRAD_CHUNKS + 1])
    store.start()
    store.wait()


def gradient_scratch(cot, w_out):
    return [
        pltpu.VMEM(cot.shape, BF16),
        pltpu.VMEM(w_out.shape, BF16),
        pltpu.VMEM(cot.shape, BF16),
        dma(GRAD_CHUNKS + 2),
    ]


def pack_body(
    q_ref, k_ref, v_ref, cot_ref, w_ref, out_ref, grad_out, held, packed, in_sems, out_sems, *room
):
    loads = [
        pltpu.make_async_copy(ref, held.at[x], in_sems.at[x])
        for x, ref in enumerate((q_ref, k_ref, v_ref))
    ]
    for load in loads:
        load.start()

    @pl.when(odd_core())
    def _():
        gradient(cot_ref, w_ref, grad_out, *room)

    stores = []
    for x, load in enumerate(loads):
        load.wait()
        rows = slice(x * BLOCK, (x + 1) * BLOCK)
        for h in range(HEADS):
            packed[h, rows, :] = held[x, :, h * WIDTH : (h + 1) * WIDTH]
        stores.append(
            pltpu.make_async_copy(packed.at[:, rows, :], out_ref.at[:, rows, :], out_sems.at[x])
        )
        stores[-1].start()
    for store in stores:
        store.wait()


def pack(q, k, v, cot, w_out):
    packed = (HEADS, 3 * BLOCK, WIDTH)
    return kernel_call(
        pack_body,
        [(packed, BF16, "hbm"), (cot.shape, BF16, "hbm")],
        ["hbm"] * 5,
        18,
        scratch=[pltpu.VMEM((3,) + q.shape, BF16), pltpu.VMEM(packed, BF16), dma(3), dma(3)]
        + gradient_scratch(cot, w_out),
        cost=cost(0, 6 * q.size * 2),
        name="pack_qkv",
    )(q, k, v, cot, w_out)


def late_gradient_body(_, cot_ref, w_ref, grad_out, *room):
    @pl.when(jnp.logical_not(odd_core()))
    def _():
        gradient(cot_ref, w_ref, grad_out, *room)


def late_gradient(grad, cot, w_out):
    return kernel_call(
        late_gradient_body,
        [(grad.shape, BF16, "hbm")],
        ["hbm"] * 3,
        63.6,
        scratch=gradient_scratch(cot, w_out),
        cost=cost(0, 1 << 20),
        name="attended_gradient",
        aliases={0: 0},
    )(grad, cot, w_out)[0]


def forward_body(
    blocks, qkv_in, grad_in, sent_out, lse_out, lev_out,
    in_ref, grad_ref, out_ref, lse_ref, lev_ref, fq, mu, du, nu, sems,
):
    tokens = blocks * BLOCK
    spans, _ = level_rows(tokens)
    copies, count = [], [0]

    def send(source, target):
        copies.append(pltpu.make_async_copy(source, target, sems.at[count[0]]))
        copies[-1].start()
        count[0] += 1

    scale = 1.0 / math.sqrt(WIDTH)
    parts = 4
    for p in range(parts):
        some = slice(p * blocks // parts, (p + 1) * blocks // parts)
        send(qkv_in.at[some, :, :], in_ref.at[some, :, :])
    send(grad_in, grad_ref)
    loads, copies[:] = copies[:], []
    for b in range(blocks):
        if b % (blocks // parts) == 0:
            loads[b // (blocks // parts)].wait()
        for x in range(3):
            part = in_ref[b, x * BLOCK : (x + 1) * BLOCK, :]
            fq[x, b * BLOCK : (b + 1) * BLOCK, :] = part.astype(F32)
    for height in range(1, LEVELS + 1):
        below, _ = spans[height - 1]
        base, rows = spans[height]
        step = min(CHUNK, rows)
        for x in range(3):
            for r in range(0, rows, step):
                mean = (
                    evens(fq.at[x], below + 2 * r, step) + odds(fq.at[x], below + 2 * r, step)
                ) * 0.5
                mean = mean.astype(BF16)
                lev_ref[x, base - tokens + r : base - tokens + r + step, :] = mean
                fq[x, base + r : base + r + step, :] = mean.astype(F32)

    send(lev_ref, lev_out)

    level = functools.partial(rows_of, in_ref, lev_ref)

    def attend(jobs):
        scores = [nt(level(0, q), level(1, k)) * scale for q, k, _ in jobs]
        tops = [wide(jnp.max(x, axis=1, keepdims=True)) for x in scores]
        expos = [jnp.exp(x - across(top, x.shape[1])) for x, top in zip(scores, tops)]
        numers = [nn(x.astype(BF16), level(2, k)) for x, (_, k, _) in zip(expos, jobs)]
        denoms = [wide(jnp.sum(x, axis=1, keepdims=True)) for x in expos]
        return [
            (top, denom * factor, numer * factor) if factor != 1 else (top, denom, numer)
            for top, denom, numer, (_, _, factor) in zip(tops, denoms, numers, jobs)
        ]

    def merge(at, stats):
        top, denom, numer = stats
        up = mu[at, :]
        peak = jnp.maximum(top, up)
        mine, theirs = jnp.exp(top - peak), jnp.exp(up - peak)
        return peak, mine * denom + theirs * du[at, :], mine * numer + theirs * nu[at, :]

    coarse = coarse_blocks(tokens)
    stats = attend([(near, far, float(2**height)) for height, _, near, far in coarse])
    for (height, row, near, _), one in zip(coarse, stats):
        if height < LEVELS:
            one = merge(near, one)
        for ref, value in zip((mu, du, nu), one):
            put_twice(ref, spans[height - 1][0] + 2 * row, value)
    loads[parts].wait()
    for b in range(blocks):
        out_ref[b, :BLOCK, :] = grad_ref[:, b * WIDTH : (b + 1) * WIDTH]
    send(out_ref.at[:, :BLOCK, :], sent_out.at[:, :BLOCK, :])
    for first in range(0, tokens, PAIRS * 2 * BLOCK):
        pairs = [
            slice(row, row + 2 * BLOCK)
            for row in range(first, min(first + PAIRS * 2 * BLOCK, tokens), 2 * BLOCK)
        ]
        for at, one in zip(pairs, attend([(at, at, 1) for at in pairs])):
            peak, total, summed = merge(at, one)
            attended = (summed / total).astype(BF16)
            lse = peak + jnp.log(total)
            for half in range(2):
                b = at.start // BLOCK + half
                part = lse[half * BLOCK : (half + 1) * BLOCK]
                lse_ref[b : b + 1, :] = jnp.sum(diagonal(part), axis=0, keepdims=True)
            pair = slice(at.start // BLOCK, at.stop // BLOCK)
            out_ref[pair, BLOCK:, :] = attended.reshape(2, BLOCK, WIDTH)
            send(out_ref.at[pair, BLOCK:, :], sent_out.at[pair, BLOCK:, :])
    send(lse_ref, lse_out)
    for copy in copies:
        copy.wait()


def forward(qkv, att_grad, after=()):
    blocks = qkv.shape[0]
    tokens = blocks * BLOCK
    spans, total_rows = level_rows(tokens)
    finer = total_rows - spans[LEVELS][1]
    outs = [
        ((blocks, 2 * BLOCK, WIDTH), BF16, "hbm"),
        ((blocks, BLOCK), F32, "hbm"),
        ((3, total_rows - tokens, WIDTH), BF16, "hbm"),
    ]
    return kernel_call(
        functools.partial(forward_body, blocks),
        outs,
        ["hbm"] * 2,
        32,
        scratch=[
            pltpu.VMEM(qkv.shape, BF16),
            pltpu.VMEM(att_grad.shape, BF16),
            pltpu.VMEM((blocks, 2 * BLOCK, WIDTH), BF16),
            pltpu.VMEM((blocks, BLOCK), F32),
            pltpu.VMEM((3, total_rows - tokens, WIDTH), BF16),
            pltpu.VMEM((3, total_rows, WIDTH), F32),
            pltpu.VMEM((finer, WIDTH), F32),
            pltpu.VMEM((finer, WIDTH), F32),
            pltpu.VMEM((finer, WIDTH), F32),
            dma(8 + blocks // 2),
        ],
        cost=cost(4 * tokens * 384 * WIDTH, 8 << 20),
        name="head_forward",
        after=after,
    )(qkv, att_grad)


def backward_body(
    blocks, grad_in, sent_in, lse_in, lev_in, qkv_in, rows_in, w_in, grads_out, output_ref,
    out_ref, att_ref, lse_ref, lev_ref, qkv_ref, ys, ds, rs, cg, up, rows_ref, w_ref, sems,
):
    tokens = blocks * BLOCK
    spans, _ = level_rows(tokens)
    scale = 1.0 / math.sqrt(WIDTH)
    parts, count = 4, [0]

    def fetch(source, target):
        copy = pltpu.make_async_copy(source, target, sems.at[count[0]])
        count[0] += 1
        copy.start()
        return copy

    first_loads = []
    lse_load = fetch(lse_in, lse_ref)
    for p in range(parts):
        some = slice(p * blocks // parts, (p + 1) * blocks // parts)
        at = slice(p * tokens // parts, (p + 1) * tokens // parts)
        first_loads.append(
            [
                fetch(grad_in.at[at, :], cg.at[at, :]),
                fetch(sent_in.at[some, BLOCK:, :], att_ref.at[some, :, :]),
            ]
        )
    later_loads = [
        fetch(lev_in, lev_ref),
        fetch(qkv_in, qkv_ref),
        fetch(rows_in, rows_ref),
        fetch(w_in, w_ref),
    ]
    lse_load.wait()
    for b in range(blocks):
        if b % (blocks // parts) == 0:
            for copy in first_loads[b // (blocks // parts)]:
                copy.wait()
        at = slice(b * BLOCK, (b + 1) * BLOCK)
        lse = jnp.broadcast_to(lse_ref[b : b + 1, :], (BLOCK, BLOCK))
        rs[at, :] = wide(jnp.sum(diagonal(lse), axis=1, keepdims=True))
        grad = cg[at, :].astype(F32)
        ys[at, :] = grad
        ds[at, :] = wide(jnp.sum(grad * att_ref[b].astype(F32), axis=1, keepdims=True))
    for height in range(1, LEVELS + 1):
        below, _ = spans[height - 1]
        base, rows = spans[height]
        for r in range(0, rows, BLOCK):
            at = slice(base + r, base + r + BLOCK)
            first = below + 2 * r
            lo, hi = evens(rs, first, BLOCK), odds(rs, first, BLOCK)
            low = jnp.minimum(lo, hi)
            lo, hi = jnp.exp(low - lo), jnp.exp(low - hi)
            grad = lo * evens(ys, first, BLOCK) + hi * odds(ys, first, BLOCK)
            delta = lo * evens(ds, first, BLOCK) + hi * odds(ds, first, BLOCK)
            ys[at, :], ds[at, :], rs[at, :] = grad, delta, low
            cg[at, :] = grad.astype(BF16)

    level = functools.partial(rows_of, qkv_ref, lev_ref)

    def gradients(jobs):
        scores = [nt(level(0, q), level(1, k)) * scale for q, k in jobs]
        inner = [nt(cg[q, :], level(2, k)) for q, k in jobs]
        expos = [
            jnp.exp(x - across(rs[q, :], x.shape[1])) for x, (q, _) in zip(scores, jobs)
        ]
        sgrads = [
            (expo * (x - across(ds[q, :], x.shape[1])) * scale).astype(BF16)
            for expo, x, (q, _) in zip(expos, inner, jobs)
        ]
        probs = [expo.astype(BF16) for expo in expos]
        q_parts = [nn(x, level(1, k)) for x, (_, k) in zip(sgrads, jobs)]
        k_parts = [tn(x, level(0, q)) for x, (q, _) in zip(sgrads, jobs)]
        v_parts = [tn(x, cg[q, :]) for x, (q, _) in zip(probs, jobs)]
        return list(zip(q_parts, k_parts, v_parts))

    later_loads[0].wait()
    coarse = coarse_blocks(tokens)
    for (height, row, near, far), parts in zip(
        coarse, gradients([(near, far) for _, _, near, far in coarse])
    ):
        for x, (at, first) in enumerate(((near, row), (far, row ^ BLOCK), (far, row ^ BLOCK))):
            value = parts[x]
            if height < LEVELS:
                value = value + up[x, at, :]
            put_twice(up.at[x], spans[height - 1][0] + 2 * first, value)
    later_loads[1].wait()
    stores = []
    for first in range(0, tokens, PAIRS * 2 * BLOCK):
        pairs = [
            slice(row, row + 2 * BLOCK)
            for row in range(first, min(first + PAIRS * 2 * BLOCK, tokens), 2 * BLOCK)
        ]
        for at, parts in zip(pairs, gradients([(at, at) for at in pairs])):
            pair = slice(at.start // BLOCK, at.stop // BLOCK)
            for x, value in enumerate(parts):
                value = (value + up[x, at, :]).astype(BF16)
                out_ref[pair, x * BLOCK : (x + 1) * BLOCK, :] = value.reshape(2, BLOCK, WIDTH)
            stores.append(fetch(out_ref.at[pair, :, :], grads_out.at[pair, : 3 * BLOCK, :]))
    later_loads[2].wait()
    later_loads[3].wait()
    rows = jnp.concatenate([rows_ref[h] for h in range(HEADS)], axis=1)
    width = w_ref.shape[1]
    for first in range(0, width, 512):
        at = slice(first, first + 512)
        output_ref[:, at] = nn(rows, w_ref[:, at]).astype(BF16)
    for store in stores:
        store.wait()


def backward(grad, sent, lse, lev, qkv, rows, w_out, after):
    blocks = sent.shape[0]
    tokens = blocks * BLOCK
    spans, total_rows = level_rows(tokens)
    finer = total_rows - spans[LEVELS][1]
    extra = w_out.size // lax.axis_size("outer") // blocks // WIDTH
    return kernel_call(
        functools.partial(backward_body, blocks),
        [
            ((blocks, 3 * BLOCK + extra, WIDTH), BF16, "hbm"),
            ((BLOCK, w_out.shape[1]), BF16, "vmem"),
        ],
        ["hbm"] * 7,
        63.6,
        scratch=[
            pltpu.VMEM((blocks, 3 * BLOCK, WIDTH), BF16),
            pltpu.VMEM(rows.shape, BF16),
            pltpu.VMEM(lse.shape, F32),
            pltpu.VMEM(lev.shape, BF16),
            pltpu.VMEM(qkv.shape, BF16),
            pltpu.VMEM((total_rows, WIDTH), F32),
            pltpu.VMEM((total_rows, WIDTH), F32),
            pltpu.VMEM((total_rows, WIDTH), F32),
            pltpu.VMEM((total_rows, WIDTH), BF16),
            pltpu.VMEM((3, finer, WIDTH), F32),
            pltpu.VMEM(rows.shape, BF16),
            pltpu.VMEM(w_out.shape, BF16),
            dma(16 + blocks // 2),
        ],
        cost=cost(10 * tokens * 384 * WIDTH + 2 * BLOCK * w_out.size, 24 << 20),
        name="head_backward",
        after=after,
    )(grad.reshape(tokens, WIDTH), sent, lse, lev, qkv, rows, w_out)


def tile_body(groups, per, _, att_in, *refs):
    cot_refs = refs[:groups]
    out_ref, att_ref, lhs, held, tile, sems = refs[groups:]
    chunk = lhs.shape[0] // HEADS
    chunks, step = held.shape[0], held.shape[2]
    att_copy = pltpu.make_async_copy(att_in, att_ref, sems.at[0])
    att_copy.start()
    copies, stores = [], []
    for c in range(chunks):
        for k, ref in enumerate(cot_refs):
            copies.append(
                pltpu.make_async_copy(
                    ref.at[:, c * step : (c + 1) * step],
                    held.at[c, k * BLOCK : (k + 1) * BLOCK, :],
                    sems.at[1 + c * groups + k],
                )
            )
            copies[-1].start()
    att_copy.wait()
    mine = lax.axis_index("outer")
    for k in range(groups):
        for j in range(per):
            lhs[j * WIDTH : (j + 1) * WIDTH, k * BLOCK : (k + 1) * BLOCK] = att_ref[
                (mine ^ k) * per + j
            ].T
    for c in range(chunks):
        for copy in copies[c * groups : (c + 1) * groups]:
            copy.wait()
        part = nn(lhs[...], held[c]).astype(BF16)
        first = c * step
        for i in range(HEADS):
            for j in range(step // WIDTH):
                to = (first // WIDTH + j) * chunk
                tile[i, to : to + chunk, :] = part[
                    i * chunk : (i + 1) * chunk, j * WIDTH : (j + 1) * WIDTH
                ]
        done = slice(first // WIDTH * chunk, (first + step) // WIDTH * chunk)
        to = slice(3 * BLOCK + done.start, 3 * BLOCK + done.stop)
        stores.append(
            pltpu.make_async_copy(
                tile.at[:, done, :], out_ref.at[:, to, :], sems.at[1 + chunks * groups + c]
            )
        )
        stores[-1].start()
    for store in stores:
        store.wait()


def with_tile(grads, att, pieces):
    groups, width = len(pieces), pieces[0].shape[1]
    per = HEADS // groups
    chunk = per * WIDTH // HEADS
    extra = chunk * (width // WIDTH)
    chunks = 4
    return kernel_call(
        functools.partial(tile_body, groups, per),
        [(grads.shape, BF16, "hbm")],
        ["hbm"] * (2 + groups),
        18,
        scratch=[
            pltpu.VMEM(att.shape, BF16),
            pltpu.VMEM((per * WIDTH, groups * BLOCK), BF16),
            pltpu.VMEM((chunks, groups * BLOCK, width // chunks), BF16),
            pltpu.VMEM((HEADS, extra, WIDTH), BF16),
            dma(1 + chunks * (groups + 1)),
        ],
        aliases={0: 0},
        cost=cost(2 * groups * BLOCK * per * WIDTH * width, 10 << 20),
        name="projection_tile",
    )(grads, att, *pieces)[0]


def unpack_body(scale, in_ref, q_out, k_out, v_out, w_out, grads, w_ref, sems):
    chunk, width = w_ref.shape
    stores = []

    def send(source, target):
        stores.append(pltpu.make_async_copy(source, target, sems.at[len(stores)]))
        stores[-1].start()

    for x, target in enumerate((q_out, k_out, v_out)):
        for h in range(HEADS):
            grads[x, :, h * WIDTH : (h + 1) * WIDTH] = in_ref[h, x * BLOCK : (x + 1) * BLOCK, :]
        send(grads.at[x], target)
    for c in range(width // WIDTH):
        at = 3 * BLOCK + c * chunk
        total = in_ref[0, at : at + chunk, :].astype(F32)
        for h in range(1, HEADS):
            total = total + in_ref[h, at : at + chunk, :].astype(F32)
        w_ref[:, c * WIDTH : (c + 1) * WIDTH] = total * scale
    send(w_ref, w_out)
    for store in stores:
        store.wait()


def unpack(got, scale):
    chunk = (got.shape[1] - 3 * BLOCK) // HEADS
    width = HEADS * WIDTH
    return kernel_call(
        functools.partial(unpack_body, scale),
        [((BLOCK, width), BF16, "hbm")] * 3 + [((chunk, width), F32, "hbm")],
        ["vmem"],
        8,
        scratch=[
            pltpu.VMEM((3, BLOCK, width), BF16),
            pltpu.VMEM((chunk, width), F32),
            dma(4),
        ],
        cost=cost(0, 6 << 20),
        name="unpack_grads",
    )(got)


def split_body(got_ref, grad_ref, att_ref, sems):
    copies = [
        pltpu.make_async_copy(got_ref.at[:, BLOCK:, :], att_ref, sems.at[0]),
        pltpu.make_async_copy(got_ref.at[:, :BLOCK, :], grad_ref, sems.at[1]),
    ]
    for copy in copies:
        copy.start()
    for copy in copies:
        copy.wait()


def split(got):
    return kernel_call(
        split_body,
        [((HEADS, BLOCK, WIDTH), BF16, "hbm")] * 2,
        ["vmem"],
        2,
        scratch=[dma(2)],
        cost=cost(0, 2 << 20),
        name="split_attended",
    )(got)


def swap(value, axis):
    return lax.all_to_all(value, axis, 0, 0, tiled=True)


def from_outer(value, apart):
    size = lax.axis_size("outer")
    return lax.ppermute(value, "outer", [(i, i ^ apart) for i in range(size)])


def on_device(query_in, key_in, value_in, w_out, cotangent):
    groups = lax.axis_size("outer")
    tokens = query_in.shape[0] * lax.axis_size(("outer", "inner"))
    pieces = {k: from_outer(cotangent, k) if k else cotangent for k in range(groups) if k < 2 or k & 3 == 2}
    soon = [pieces[k] for k in pieces if k]
    packed, att_grad = pack(query_in, key_in, value_in, cotangent, w_out)
    qkv = swap(packed, "inner")
    att_grad = late_gradient(att_grad, cotangent, w_out)
    sent, lse, lev = forward(qkv, att_grad, after=soon)
    late = {k: from_outer(pieces[k + 2], 2) for k in range(4, groups, 4)}
    pieces.update(late)
    for k in range(2, groups, 2):
        pieces[k + 1] = from_outer(pieces[k], 1)
    grad, att = split(swap(sent, "inner"))
    att_outer = swap(att, "outer")
    grads, output = backward(grad, sent, lse, lev, qkv, att, w_out, list(late.values()))
    pieces = [pieces[k] for k in range(groups)]
    last = swap(with_tile(grads, att_outer, pieces), "inner")
    query_grad, key_grad, value_grad, w_out_grad = unpack(last, 1.0 / math.sqrt(tokens))
    return output, query_grad, key_grad, value_grad, w_out_grad


def solution(mesh):
    rows = P(("outer", "inner"), None)
    return jax.shard_map(
        on_device,
        mesh=mesh,
        in_specs=(rows, rows, rows, P(), rows),
        out_specs=(rows,) * 5,
        check_vma=False,
    )
```

```python
import functools
import math

import jax
import jax.numpy as jnp
from jax import lax
from jax.experimental import pallas as pl
from jax.experimental.pallas import tpu as pltpu
from jax.sharding import PartitionSpec as P

HEADS = 16
BLOCK = 128
LEVELS = 3
WIDTH = 128
BF16 = jnp.bfloat16
F32 = jnp.float32
CHUNK = 256
PAIRS = 4
GRAD_CHUNKS = 4


def nt(a, b):
    return lax.dot_general(a, b, (((1,), (1,)), ((), ())), preferred_element_type=F32)


def nn(a, b):
    return lax.dot_general(a, b, (((1,), (0,)), ((), ())), preferred_element_type=F32)


def tn(a, b):
    return lax.dot_general(a, b, (((0,), (0,)), ((), ())), preferred_element_type=F32)


def wide(stat, columns=WIDTH):
    return jnp.broadcast_to(stat, (stat.shape[0], columns))


def evens(ref, base, rows):
    return ref[pl.ds(base, rows, stride=2), :]


def odds(ref, base, rows):
    return ref[pl.ds(base + 1, rows, stride=2), :]


def put_twice(ref, base, value):
    rows = value.shape[0]
    ref[pl.ds(base, rows, stride=2), :] = value
    ref[pl.ds(base + 1, rows, stride=2), :] = value


def diagonal(matrix):
    rows = lax.broadcasted_iota(jnp.int32, matrix.shape, 0)
    columns = lax.broadcasted_iota(jnp.int32, matrix.shape, 1)
    return jnp.where(rows == columns, matrix, 0.0)


def across(stat, columns):
    return jnp.concatenate([stat] * (columns // WIDTH), axis=1)


def coarse_blocks(tokens):
    spans, _ = level_rows(tokens)
    out = []
    for height in range(LEVELS, 0, -1):
        base, rows = spans[height]
        for row in range(0, rows, BLOCK):
            near, far = base + row, base + (row ^ BLOCK)
            out.append((height, row, slice(near, near + BLOCK), slice(far, far + BLOCK)))
    return out


def rows_of(token_ref, coarse_ref, x, at):
    tokens = token_ref.shape[0] * BLOCK
    if at.start >= tokens:
        return coarse_ref[x, at.start - tokens : at.stop - tokens, :]
    some = slice(at.start // BLOCK, at.stop // BLOCK)
    return token_ref[some, x * BLOCK : (x + 1) * BLOCK, :].reshape(at.stop - at.start, WIDTH)


def level_rows(tokens):
    out, base = [], 0
    for height in range(LEVELS + 1):
        out.append((base, tokens >> height))
        base += tokens >> height
    return out, base


def kernel_call(body, outs, in_places, mib, scratch=(), cost=None, name=None, after=(), aliases=None):
    count = len(in_places)
    in_places = list(in_places) + ["hbm"] * len(after)

    def ordered(*refs):
        body(*refs[:count], *refs[len(in_places) :])

    spec = {
        "vmem": pl.BlockSpec(memory_space=pltpu.VMEM),
        "hbm": pl.BlockSpec(memory_space=pl.ANY),
    }
    shapes = [
        pltpu.HBM(shape, dtype) if place == "hbm" else jax.ShapeDtypeStruct(shape, dtype)
        for shape, dtype, place in outs
    ]
    call = pl.pallas_call(
        ordered,
        out_shape=shapes,
        in_specs=[spec[place] for place in in_places],
        out_specs=[spec[place] for _, _, place in outs],
        scratch_shapes=list(scratch),
        compiler_params=pltpu.CompilerParams(vmem_limit_bytes=int(mib * 2**20)),
        cost_estimate=cost,
        name=name,
        input_output_aliases=aliases or {},
    )

    def run(*operands):
        operands = [
            pltpu.with_memory_space_constraint(x, pltpu.HBM) if place == "hbm" else x
            for x, place in zip((*operands, *after), in_places)
        ]
        return call(*operands)

    return run


def dma(count):
    return pltpu.SemaphoreType.DMA((count,))


def cost(flops, nbytes):
    return pl.CostEstimate(flops=int(flops), bytes_accessed=int(nbytes), transcendentals=0)


def odd_core():
    return lax.axis_index("outer") & 1 == 1


def gradient(cot_ref, w_ref, grad_out, cot, held, grad, sems):
    rows = held.shape[0] // GRAD_CHUNKS
    load = pltpu.make_async_copy(cot_ref, cot, sems.at[GRAD_CHUNKS])
    load.start()
    copies = []
    for c in range(GRAD_CHUNKS):
        at = slice(c * rows, (c + 1) * rows)
        copies.append(pltpu.make_async_copy(w_ref.at[at, :], held.at[at, :], sems.at[c]))
        copies[-1].start()
    load.wait()
    for c, copy in enumerate(copies):
        at = slice(c * rows, (c + 1) * rows)
        copy.wait()
        grad[:, at] = nt(cot[...], held[at, :]).astype(BF16)
    store = pltpu.make_async_copy(grad, grad_out, sems.at[GRAD_CHUNKS + 1])
    store.start()
    store.wait()


def gradient_scratch(cot, w_out):
    return [
        pltpu.VMEM(cot.shape, BF16),
        pltpu.VMEM(w_out.shape, BF16),
        pltpu.VMEM(cot.shape, BF16),
        dma(GRAD_CHUNKS + 2),
    ]


def pack_body(
    q_ref, k_ref, v_ref, cot_ref, w_ref, out_ref, grad_out, held, packed, in_sems, out_sems, *room
):
    loads = [
        pltpu.make_async_copy(ref, held.at[x], in_sems.at[x])
        for x, ref in enumerate((q_ref, k_ref, v_ref))
    ]
    for load in loads:
        load.start()

    @pl.when(odd_core())
    def _():
        gradient(cot_ref, w_ref, grad_out, *room)

    stores = []
    for x, load in enumerate(loads):
        load.wait()
        rows = slice(x * BLOCK, (x + 1) * BLOCK)
        for h in range(HEADS):
            packed[h, rows, :] = held[x, :, h * WIDTH : (h + 1) * WIDTH]
        stores.append(
            pltpu.make_async_copy(packed.at[:, rows, :], out_ref.at[:, rows, :], out_sems.at[x])
        )
        stores[-1].start()
    for store in stores:
        store.wait()


def pack(q, k, v, cot, w_out):
    packed = (HEADS, 3 * BLOCK, WIDTH)
    return kernel_call(
        pack_body,
        [(packed, BF16, "hbm"), (cot.shape, BF16, "hbm")],
        ["hbm"] * 5,
        18,
        scratch=[pltpu.VMEM((3,) + q.shape, BF16), pltpu.VMEM(packed, BF16), dma(3), dma(3)]
        + gradient_scratch(cot, w_out),
        cost=cost(0, 6 * q.size * 2),
        name="pack_qkv",
    )(q, k, v, cot, w_out)


def late_gradient_body(_, cot_ref, w_ref, grad_out, *room):
    @pl.when(jnp.logical_not(odd_core()))
    def _():
        gradient(cot_ref, w_ref, grad_out, *room)


def late_gradient(grad, cot, w_out):
    return kernel_call(
        late_gradient_body,
        [(grad.shape, BF16, "hbm")],
        ["hbm"] * 3,
        63.6,
        scratch=gradient_scratch(cot, w_out),
        cost=cost(0, 1 << 20),
        name="attended_gradient",
        aliases={0: 0},
    )(grad, cot, w_out)[0]


def forward_body(
    blocks, qkv_in, grad_in, sent_out, lse_out, lev_out,
    in_ref, grad_ref, out_ref, lse_ref, lev_ref, fq, mu, du, nu, sems,
):
    tokens = blocks * BLOCK
    spans, _ = level_rows(tokens)
    copies, count = [], [0]

    def send(source, target):
        copies.append(pltpu.make_async_copy(source, target, sems.at[count[0]]))
        copies[-1].start()
        count[0] += 1

    scale = 1.0 / math.sqrt(WIDTH)
    parts = 4
    for p in range(parts):
        some = slice(p * blocks // parts, (p + 1) * blocks // parts)
        send(qkv_in.at[some, :, :], in_ref.at[some, :, :])
    send(grad_in, grad_ref)
    loads, copies[:] = copies[:], []
    for b in range(blocks):
        if b % (blocks // parts) == 0:
            loads[b // (blocks // parts)].wait()
        for x in range(3):
            part = in_ref[b, x * BLOCK : (x + 1) * BLOCK, :]
            fq[x, b * BLOCK : (b + 1) * BLOCK, :] = part.astype(F32)
    for height in range(1, LEVELS + 1):
        below, _ = spans[height - 1]
        base, rows = spans[height]
        step = min(CHUNK, rows)
        for x in range(3):
            for r in range(0, rows, step):
                mean = (
                    evens(fq.at[x], below + 2 * r, step) + odds(fq.at[x], below + 2 * r, step)
                ) * 0.5
                mean = mean.astype(BF16)
                lev_ref[x, base - tokens + r : base - tokens + r + step, :] = mean
                fq[x, base + r : base + r + step, :] = mean.astype(F32)

    send(lev_ref, lev_out)

    level = functools.partial(rows_of, in_ref, lev_ref)

    def attend(jobs):
        scores = [nt(level(0, q), level(1, k)) * scale for q, k, _ in jobs]
        tops = [wide(jnp.max(x, axis=1, keepdims=True)) for x in scores]
        expos = [jnp.exp(x - across(top, x.shape[1])) for x, top in zip(scores, tops)]
        numers = [nn(x.astype(BF16), level(2, k)) for x, (_, k, _) in zip(expos, jobs)]
        denoms = [wide(jnp.sum(x, axis=1, keepdims=True)) for x in expos]
        return [
            (top, denom * factor, numer * factor) if factor != 1 else (top, denom, numer)
            for top, denom, numer, (_, _, factor) in zip(tops, denoms, numers, jobs)
        ]

    def merge(at, stats):
        top, denom, numer = stats
        up = mu[at, :]
        peak = jnp.maximum(top, up)
        mine, theirs = jnp.exp(top - peak), jnp.exp(up - peak)
        return peak, mine * denom + theirs * du[at, :], mine * numer + theirs * nu[at, :]

    coarse = coarse_blocks(tokens)
    stats = attend([(near, far, float(2**height)) for height, _, near, far in coarse])
    for (height, row, near, _), one in zip(coarse, stats):
        if height < LEVELS:
            one = merge(near, one)
        for ref, value in zip((mu, du, nu), one):
            put_twice(ref, spans[height - 1][0] + 2 * row, value)
    loads[parts].wait()
    for b in range(blocks):
        out_ref[b, :BLOCK, :] = grad_ref[:, b * WIDTH : (b + 1) * WIDTH]
    send(out_ref.at[:, :BLOCK, :], sent_out.at[:, :BLOCK, :])
    for first in range(0, tokens, PAIRS * 2 * BLOCK):
        pairs = [
            slice(row, row + 2 * BLOCK)
            for row in range(first, min(first + PAIRS * 2 * BLOCK, tokens), 2 * BLOCK)
        ]
        for at, one in zip(pairs, attend([(at, at, 1) for at in pairs])):
            peak, total, summed = merge(at, one)
            attended = (summed / total).astype(BF16)
            lse = peak + jnp.log(total)
            for half in range(2):
                b = at.start // BLOCK + half
                part = lse[half * BLOCK : (half + 1) * BLOCK]
                lse_ref[b : b + 1, :] = jnp.sum(diagonal(part), axis=0, keepdims=True)
            pair = slice(at.start // BLOCK, at.stop // BLOCK)
            out_ref[pair, BLOCK:, :] = attended.reshape(2, BLOCK, WIDTH)
            send(out_ref.at[pair, BLOCK:, :], sent_out.at[pair, BLOCK:, :])
    send(lse_ref, lse_out)
    for copy in copies:
        copy.wait()


def forward(qkv, att_grad, after=()):
    blocks = qkv.shape[0]
    tokens = blocks * BLOCK
    spans, total_rows = level_rows(tokens)
    finer = total_rows - spans[LEVELS][1]
    outs = [
        ((blocks, 2 * BLOCK, WIDTH), BF16, "hbm"),
        ((blocks, BLOCK), F32, "hbm"),
        ((3, total_rows - tokens, WIDTH), BF16, "hbm"),
    ]
    return kernel_call(
        functools.partial(forward_body, blocks),
        outs,
        ["hbm"] * 2,
        32,
        scratch=[
            pltpu.VMEM(qkv.shape, BF16),
            pltpu.VMEM(att_grad.shape, BF16),
            pltpu.VMEM((blocks, 2 * BLOCK, WIDTH), BF16),
            pltpu.VMEM((blocks, BLOCK), F32),
            pltpu.VMEM((3, total_rows - tokens, WIDTH), BF16),
            pltpu.VMEM((3, total_rows, WIDTH), F32),
            pltpu.VMEM((finer, WIDTH), F32),
            pltpu.VMEM((finer, WIDTH), F32),
            pltpu.VMEM((finer, WIDTH), F32),
            dma(8 + blocks // 2),
        ],
        cost=cost(4 * tokens * 384 * WIDTH, 8 << 20),
        name="head_forward",
        after=after,
    )(qkv, att_grad)


def backward_body(
    blocks, grad_in, sent_in, lse_in, lev_in, qkv_in, rows_in, w_in, grads_out, output_ref,
    out_ref, att_ref, lse_ref, lev_ref, qkv_ref, ys, ds, rs, cg, up, rows_ref, w_ref, sems,
):
    tokens = blocks * BLOCK
    spans, _ = level_rows(tokens)
    scale = 1.0 / math.sqrt(WIDTH)
    parts, count = 4, [0]

    def fetch(source, target):
        copy = pltpu.make_async_copy(source, target, sems.at[count[0]])
        count[0] += 1
        copy.start()
        return copy

    first_loads = []
    lse_load = fetch(lse_in, lse_ref)
    for p in range(parts):
        some = slice(p * blocks // parts, (p + 1) * blocks // parts)
        at = slice(p * tokens // parts, (p + 1) * tokens // parts)
        first_loads.append(
            [
                fetch(grad_in.at[at, :], cg.at[at, :]),
                fetch(sent_in.at[some, BLOCK:, :], att_ref.at[some, :, :]),
            ]
        )
    later_loads = [
        fetch(lev_in, lev_ref),
        fetch(qkv_in, qkv_ref),
        fetch(rows_in, rows_ref),
        fetch(w_in, w_ref),
    ]
    lse_load.wait()
    for b in range(blocks):
        if b % (blocks // parts) == 0:
            for copy in first_loads[b // (blocks // parts)]:
                copy.wait()
        at = slice(b * BLOCK, (b + 1) * BLOCK)
        lse = jnp.broadcast_to(lse_ref[b : b + 1, :], (BLOCK, BLOCK))
        rs[at, :] = wide(jnp.sum(diagonal(lse), axis=1, keepdims=True))
        grad = cg[at, :].astype(F32)
        ys[at, :] = grad
        ds[at, :] = wide(jnp.sum(grad * att_ref[b].astype(F32), axis=1, keepdims=True))
    for height in range(1, LEVELS + 1):
        below, _ = spans[height - 1]
        base, rows = spans[height]
        for r in range(0, rows, BLOCK):
            at = slice(base + r, base + r + BLOCK)
            first = below + 2 * r
            lo, hi = evens(rs, first, BLOCK), odds(rs, first, BLOCK)
            low = jnp.minimum(lo, hi)
            lo, hi = jnp.exp(low - lo), jnp.exp(low - hi)
            grad = lo * evens(ys, first, BLOCK) + hi * odds(ys, first, BLOCK)
            delta = lo * evens(ds, first, BLOCK) + hi * odds(ds, first, BLOCK)
            ys[at, :], ds[at, :], rs[at, :] = grad, delta, low
            cg[at, :] = grad.astype(BF16)

    level = functools.partial(rows_of, qkv_ref, lev_ref)

    def gradients(jobs):
        scores = [nt(level(0, q), level(1, k)) * scale for q, k in jobs]
        inner = [nt(cg[q, :], level(2, k)) for q, k in jobs]
        expos = [
            jnp.exp(x - across(rs[q, :], x.shape[1])) for x, (q, _) in zip(scores, jobs)
        ]
        sgrads = [
            (expo * (x - across(ds[q, :], x.shape[1])) * scale).astype(BF16)
            for expo, x, (q, _) in zip(expos, inner, jobs)
        ]
        probs = [expo.astype(BF16) for expo in expos]
        q_parts = [nn(x, level(1, k)) for x, (_, k) in zip(sgrads, jobs)]
        k_parts = [tn(x, level(0, q)) for x, (q, _) in zip(sgrads, jobs)]
        v_parts = [tn(x, cg[q, :]) for x, (q, _) in zip(probs, jobs)]
        return list(zip(q_parts, k_parts, v_parts))

    later_loads[0].wait()
    coarse = coarse_blocks(tokens)
    for (height, row, near, far), parts in zip(
        coarse, gradients([(near, far) for _, _, near, far in coarse])
    ):
        for x, (at, first) in enumerate(((near, row), (far, row ^ BLOCK), (far, row ^ BLOCK))):
            value = parts[x]
            if height < LEVELS:
                value = value + up[x, at, :]
            put_twice(up.at[x], spans[height - 1][0] + 2 * first, value)
    later_loads[1].wait()
    stores = []
    for first in range(0, tokens, PAIRS * 2 * BLOCK):
        pairs = [
            slice(row, row + 2 * BLOCK)
            for row in range(first, min(first + PAIRS * 2 * BLOCK, tokens), 2 * BLOCK)
        ]
        for at, parts in zip(pairs, gradients([(at, at) for at in pairs])):
            pair = slice(at.start // BLOCK, at.stop // BLOCK)
            for x, value in enumerate(parts):
                value = (value + up[x, at, :]).astype(BF16)
                out_ref[pair, x * BLOCK : (x + 1) * BLOCK, :] = value.reshape(2, BLOCK, WIDTH)
            stores.append(fetch(out_ref.at[pair, :, :], grads_out.at[pair, : 3 * BLOCK, :]))
    later_loads[2].wait()
    later_loads[3].wait()
    rows = jnp.concatenate([rows_ref[h] for h in range(HEADS)], axis=1)
    width = w_ref.shape[1]
    for first in range(0, width, 512):
        at = slice(first, first + 512)
        output_ref[:, at] = nn(rows, w_ref[:, at]).astype(BF16)
    for store in stores:
        store.wait()


def backward(grad, sent, lse, lev, qkv, rows, w_out, after):
    blocks = sent.shape[0]
    tokens = blocks * BLOCK
    spans, total_rows = level_rows(tokens)
    finer = total_rows - spans[LEVELS][1]
    extra = w_out.size // lax.axis_size("outer") // blocks // WIDTH
    return kernel_call(
        functools.partial(backward_body, blocks),
        [
            ((blocks, 3 * BLOCK + extra, WIDTH), BF16, "hbm"),
            ((BLOCK, w_out.shape[1]), BF16, "vmem"),
        ],
        ["hbm"] * 7,
        63.6,
        scratch=[
            pltpu.VMEM((blocks, 3 * BLOCK, WIDTH), BF16),
            pltpu.VMEM(rows.shape, BF16),
            pltpu.VMEM(lse.shape, F32),
            pltpu.VMEM(lev.shape, BF16),
            pltpu.VMEM(qkv.shape, BF16),
            pltpu.VMEM((total_rows, WIDTH), F32),
            pltpu.VMEM((total_rows, WIDTH), F32),
            pltpu.VMEM((total_rows, WIDTH), F32),
            pltpu.VMEM((total_rows, WIDTH), BF16),
            pltpu.VMEM((3, finer, WIDTH), F32),
            pltpu.VMEM(rows.shape, BF16),
            pltpu.VMEM(w_out.shape, BF16),
            dma(16 + blocks // 2),
        ],
        cost=cost(10 * tokens * 384 * WIDTH + 2 * BLOCK * w_out.size, 24 << 20),
        name="head_backward",
        after=after,
    )(grad.reshape(tokens, WIDTH), sent, lse, lev, qkv, rows, w_out)


def tile_body(groups, per, places, _, att_in, *refs):
    count = len(places)
    cot_refs = refs[:count]
    out_ref, att_ref, lhs, held, tile, sems = refs[count:]
    chunk = lhs.shape[0] // HEADS
    chunks, step = held.shape[0], held.shape[2]
    att_copy = pltpu.make_async_copy(att_in, att_ref, sems.at[0])
    att_copy.start()
    copies, stores = [], []
    for c in range(chunks):
        for i, ((k, first), ref) in enumerate(zip(places, cot_refs)):
            row = k * BLOCK + first
            copies.append(
                pltpu.make_async_copy(
                    ref.at[:, c * step : (c + 1) * step],
                    held.at[c, row : row + ref.shape[0], :],
                    sems.at[1 + c * count + i],
                )
            )
            copies[-1].start()
    att_copy.wait()
    mine = lax.axis_index("outer")
    for k in range(groups):
        for j in range(per):
            lhs[j * WIDTH : (j + 1) * WIDTH, k * BLOCK : (k + 1) * BLOCK] = att_ref[
                (mine ^ k) * per + j
            ].T
    for c in range(chunks):
        for copy in copies[c * count : (c + 1) * count]:
            copy.wait()
        part = nn(lhs[...], held[c]).astype(BF16)
        first = c * step
        for i in range(HEADS):
            for j in range(step // WIDTH):
                to = (first // WIDTH + j) * chunk
                tile[i, to : to + chunk, :] = part[
                    i * chunk : (i + 1) * chunk, j * WIDTH : (j + 1) * WIDTH
                ]
        done = slice(first // WIDTH * chunk, (first + step) // WIDTH * chunk)
        to = slice(3 * BLOCK + done.start, 3 * BLOCK + done.stop)
        stores.append(
            pltpu.make_async_copy(
                tile.at[:, done, :], out_ref.at[:, to, :], sems.at[1 + chunks * count + c]
            )
        )
        stores[-1].start()
    for store in stores:
        store.wait()


def with_tile(grads, att, parts, groups):
    places = [(k, first) for k, first, _ in parts]
    pieces = [part for _, _, part in parts]
    width = pieces[0].shape[1]
    per = HEADS // groups
    chunk = per * WIDTH // HEADS
    extra = chunk * (width // WIDTH)
    chunks = 4
    return kernel_call(
        functools.partial(tile_body, groups, per, places),
        [(grads.shape, BF16, "hbm")],
        ["hbm"] * (2 + len(places)),
        18,
        scratch=[
            pltpu.VMEM(att.shape, BF16),
            pltpu.VMEM((per * WIDTH, groups * BLOCK), BF16),
            pltpu.VMEM((chunks, groups * BLOCK, width // chunks), BF16),
            pltpu.VMEM((HEADS, extra, WIDTH), BF16),
            dma(1 + chunks * (len(places) + 1)),
        ],
        aliases={0: 0},
        cost=cost(2 * groups * BLOCK * per * WIDTH * width, 10 << 20),
        name="projection_tile",
    )(grads, att, *pieces)[0]


def unpack_body(scale, in_ref, q_out, k_out, v_out, w_out, grads, w_ref, sems):
    chunk, width = w_ref.shape
    stores = []

    def send(source, target):
        stores.append(pltpu.make_async_copy(source, target, sems.at[len(stores)]))
        stores[-1].start()

    for x, target in enumerate((q_out, k_out, v_out)):
        for h in range(HEADS):
            grads[x, :, h * WIDTH : (h + 1) * WIDTH] = in_ref[h, x * BLOCK : (x + 1) * BLOCK, :]
        send(grads.at[x], target)
    for c in range(width // WIDTH):
        at = 3 * BLOCK + c * chunk
        total = in_ref[0, at : at + chunk, :].astype(F32)
        for h in range(1, HEADS):
            total = total + in_ref[h, at : at + chunk, :].astype(F32)
        w_ref[:, c * WIDTH : (c + 1) * WIDTH] = total * scale
    send(w_ref, w_out)
    for store in stores:
        store.wait()


def unpack(got, scale):
    chunk = (got.shape[1] - 3 * BLOCK) // HEADS
    width = HEADS * WIDTH
    return kernel_call(
        functools.partial(unpack_body, scale),
        [((BLOCK, width), BF16, "hbm")] * 3 + [((chunk, width), F32, "hbm")],
        ["vmem"],
        8,
        scratch=[
            pltpu.VMEM((3, BLOCK, width), BF16),
            pltpu.VMEM((chunk, width), F32),
            dma(4),
        ],
        cost=cost(0, 6 << 20),
        name="unpack_grads",
    )(got)


def split_body(got_ref, grad_ref, att_ref, sems):
    copies = [
        pltpu.make_async_copy(got_ref.at[:, BLOCK:, :], att_ref, sems.at[0]),
        pltpu.make_async_copy(got_ref.at[:, :BLOCK, :], grad_ref, sems.at[1]),
    ]
    for copy in copies:
        copy.start()
    for copy in copies:
        copy.wait()


def split(got):
    return kernel_call(
        split_body,
        [((HEADS, BLOCK, WIDTH), BF16, "hbm")] * 2,
        ["vmem"],
        2,
        scratch=[dma(2)],
        cost=cost(0, 2 << 20),
        name="split_attended",
    )(got)


def swap(value, axis):
    return lax.all_to_all(value, axis, 0, 0, tiled=True)


def from_outer(value, apart):
    size = lax.axis_size("outer")
    return lax.ppermute(value, "outer", [(i, i ^ apart) for i in range(size)])


def on_device(query_in, key_in, value_in, w_out, cotangent):
    groups = lax.axis_size("outer")
    tokens = query_in.shape[0] * lax.axis_size(("outer", "inner"))
    pieces = {k: from_outer(cotangent, k) if k else cotangent for k in range(groups) if k < 2 or k & 3 == 2}
    soon = [pieces[k] for k in pieces if k]
    packed, att_grad = pack(query_in, key_in, value_in, cotangent, w_out)
    qkv = swap(packed, "inner")
    att_grad = late_gradient(att_grad, cotangent, w_out)
    sent, lse, lev = forward(qkv, att_grad, after=soon)
    half = BLOCK // 2
    late = []
    for k in range(4, groups, 4):
        late.append((k, 0, from_outer(pieces[k + 2][:half], 2)))
        late.append((k, half, from_outer(pieces[k - 2][half:], 6)))
    parts = [(k, 0, piece) for k, piece in pieces.items()] + late
    parts += [(k + 1, first, from_outer(part, 1)) for k, first, part in parts if k > 1]
    grad, att = split(swap(sent, "inner"))
    att_outer = swap(att, "outer")
    grads, output = backward(
        grad, sent, lse, lev, qkv, att, w_out, [part for _, _, part in late]
    )
    last = swap(with_tile(grads, att_outer, parts, groups), "inner")
    query_grad, key_grad, value_grad, w_out_grad = unpack(last, 1.0 / math.sqrt(tokens))
    return output, query_grad, key_grad, value_grad, w_out_grad


def solution(mesh):
    rows = P(("outer", "inner"), None)
    return jax.shard_map(
        on_device,
        mesh=mesh,
        in_specs=(rows, rows, rows, P(), rows),
        out_specs=(rows,) * 5,
        check_vma=False,
    )
```

```python
import functools
import math

import jax
import jax.numpy as jnp
from jax import lax
from jax.experimental import pallas as pl
from jax.experimental.pallas import tpu as pltpu
from jax.sharding import PartitionSpec as P

HEADS = 16
BLOCK = 128
LEVELS = 3
WIDTH = 128
BF16 = jnp.bfloat16
F32 = jnp.float32
CHUNK = 256
PAIRS = 4


def nt(a, b):
    return lax.dot_general(a, b, (((1,), (1,)), ((), ())), preferred_element_type=F32)


def nn(a, b):
    return lax.dot_general(a, b, (((1,), (0,)), ((), ())), preferred_element_type=F32)


def tn(a, b):
    return lax.dot_general(a, b, (((0,), (0,)), ((), ())), preferred_element_type=F32)


def wide(stat, columns=WIDTH):
    return jnp.broadcast_to(stat, (stat.shape[0], columns))


def evens(ref, base, rows):
    return ref[pl.ds(base, rows, stride=2), :]


def odds(ref, base, rows):
    return ref[pl.ds(base + 1, rows, stride=2), :]


def put_twice(ref, base, value):
    rows = value.shape[0]
    ref[pl.ds(base, rows, stride=2), :] = value
    ref[pl.ds(base + 1, rows, stride=2), :] = value


def diagonal(matrix):
    rows = lax.broadcasted_iota(jnp.int32, matrix.shape, 0)
    columns = lax.broadcasted_iota(jnp.int32, matrix.shape, 1)
    return jnp.where(rows == columns, matrix, 0.0)


def across(stat, columns):
    return jnp.concatenate([stat] * (columns // WIDTH), axis=1)


def coarse_blocks(tokens):
    spans, _ = level_rows(tokens)
    out = []
    for height in range(LEVELS, 0, -1):
        base, rows = spans[height]
        for row in range(0, rows, BLOCK):
            near, far = base + row, base + (row ^ BLOCK)
            out.append((height, row, slice(near, near + BLOCK), slice(far, far + BLOCK)))
    return out


def rows_of(token_ref, coarse_ref, x, at):
    tokens = token_ref.shape[0] * BLOCK
    if at.start >= tokens:
        return coarse_ref[x, at.start - tokens : at.stop - tokens, :]
    some = slice(at.start // BLOCK, at.stop // BLOCK)
    return token_ref[some, x * BLOCK : (x + 1) * BLOCK, :].reshape(at.stop - at.start, WIDTH)


def level_rows(tokens):
    out, base = [], 0
    for height in range(LEVELS + 1):
        out.append((base, tokens >> height))
        base += tokens >> height
    return out, base


def kernel_call(body, outs, in_places, mib, scratch=(), cost=None, name=None, after=(), aliases=None):
    count = len(in_places)
    in_places = list(in_places) + ["hbm"] * len(after)

    def ordered(*refs):
        body(*refs[:count], *refs[len(in_places) :])

    spec = {
        "vmem": pl.BlockSpec(memory_space=pltpu.VMEM),
        "hbm": pl.BlockSpec(memory_space=pl.ANY),
    }
    shapes = [
        pltpu.HBM(shape, dtype) if place == "hbm" else jax.ShapeDtypeStruct(shape, dtype)
        for shape, dtype, place in outs
    ]
    call = pl.pallas_call(
        ordered,
        out_shape=shapes,
        in_specs=[spec[place] for place in in_places],
        out_specs=[spec[place] for _, _, place in outs],
        scratch_shapes=list(scratch),
        compiler_params=pltpu.CompilerParams(vmem_limit_bytes=int(mib * 2**20)),
        cost_estimate=cost,
        name=name,
        input_output_aliases=aliases or {},
    )

    def run(*operands):
        operands = [
            pltpu.with_memory_space_constraint(x, pltpu.HBM) if place == "hbm" else x
            for x, place in zip((*operands, *after), in_places)
        ]
        return call(*operands)

    return run


def dma(count):
    return pltpu.SemaphoreType.DMA((count,))


def cost(flops, nbytes):
    return pl.CostEstimate(flops=int(flops), bytes_accessed=int(nbytes), transcendentals=0)


def pack_body(q_ref, k_ref, v_ref, out_ref, held, packed, in_sems, out_sems):
    loads = [
        pltpu.make_async_copy(ref, held.at[x], in_sems.at[x])
        for x, ref in enumerate((q_ref, k_ref, v_ref))
    ]
    for load in loads:
        load.start()
    stores = []
    for x, load in enumerate(loads):
        load.wait()
        rows = slice(x * BLOCK, (x + 1) * BLOCK)
        for h in range(HEADS):
            packed[h, rows, :] = held[x, :, h * WIDTH : (h + 1) * WIDTH]
        stores.append(
            pltpu.make_async_copy(packed.at[:, rows, :], out_ref.at[:, rows, :], out_sems.at[x])
        )
        stores[-1].start()
    for store in stores:
        store.wait()


def pack(q, k, v):
    packed = (HEADS, 3 * BLOCK, WIDTH)
    return kernel_call(
        pack_body,
        [(packed, BF16, "hbm")],
        ["hbm"] * 3,
        6,
        scratch=[pltpu.VMEM((3,) + q.shape, BF16), pltpu.VMEM(packed, BF16), dma(3), dma(3)],
        cost=cost(0, 6 * q.size * 2),
        name="pack_qkv",
    )(q, k, v)[0]


def att_grad_body(chunks, cot_ref, w_ref, out_ref, held, sems):
    rows = held.shape[0] // chunks
    copies = []
    for c in range(chunks):
        at = slice(c * rows, (c + 1) * rows)
        copies.append(pltpu.make_async_copy(w_ref.at[at, :], held.at[at, :], sems.at[c]))
        copies[-1].start()
    for c, copy in enumerate(copies):
        at = slice(c * rows, (c + 1) * rows)
        copy.wait()
        out_ref[:, at] = nt(cot_ref[...], held[at, :]).astype(BF16)


def attended_gradient(cot, w_out):
    chunks = 4
    return kernel_call(
        functools.partial(att_grad_body, chunks),
        [(cot.shape, BF16, "vmem")],
        ["vmem", "hbm"],
        63.6,
        scratch=[pltpu.VMEM(w_out.shape, BF16), dma(chunks)],
        cost=cost(0, 1 << 20),
        name="attended_gradient",
    )(cot, w_out)[0]


def forward_body(
    blocks, qkv_in, grad_in, sent_out, lse_out, lev_out,
    in_ref, grad_ref, out_ref, lse_ref, lev_ref, fq, mu, du, nu, sems,
):
    tokens = blocks * BLOCK
    spans, _ = level_rows(tokens)
    copies, count = [], [0]

    def send(source, target):
        copies.append(pltpu.make_async_copy(source, target, sems.at[count[0]]))
        copies[-1].start()
        count[0] += 1

    scale = 1.0 / math.sqrt(WIDTH)
    parts = 4
    for p in range(parts):
        some = slice(p * blocks // parts, (p + 1) * blocks // parts)
        send(qkv_in.at[some, :, :], in_ref.at[some, :, :])
    send(grad_in, grad_ref)
    loads, copies[:] = copies[:], []
    for b in range(blocks):
        if b % (blocks // parts) == 0:
            loads[b // (blocks // parts)].wait()
        for x in range(3):
            part = in_ref[b, x * BLOCK : (x + 1) * BLOCK, :]
            fq[x, b * BLOCK : (b + 1) * BLOCK, :] = part.astype(F32)
    for height in range(1, LEVELS + 1):
        below, _ = spans[height - 1]
        base, rows = spans[height]
        step = min(CHUNK, rows)
        for x in range(3):
            for r in range(0, rows, step):
                mean = (
                    evens(fq.at[x], below + 2 * r, step) + odds(fq.at[x], below + 2 * r, step)
                ) * 0.5
                mean = mean.astype(BF16)
                lev_ref[x, base - tokens + r : base - tokens + r + step, :] = mean
                fq[x, base + r : base + r + step, :] = mean.astype(F32)

    send(lev_ref, lev_out)

    level = functools.partial(rows_of, in_ref, lev_ref)

    def attend(jobs):
        scores = [nt(level(0, q), level(1, k)) * scale for q, k, _ in jobs]
        tops = [wide(jnp.max(x, axis=1, keepdims=True)) for x in scores]
        expos = [jnp.exp(x - across(top, x.shape[1])) for x, top in zip(scores, tops)]
        numers = [nn(x.astype(BF16), level(2, k)) for x, (_, k, _) in zip(expos, jobs)]
        denoms = [wide(jnp.sum(x, axis=1, keepdims=True)) for x in expos]
        return [
            (top, denom * factor, numer * factor) if factor != 1 else (top, denom, numer)
            for top, denom, numer, (_, _, factor) in zip(tops, denoms, numers, jobs)
        ]

    def merge(at, stats):
        top, denom, numer = stats
        up = mu[at, :]
        peak = jnp.maximum(top, up)
        mine, theirs = jnp.exp(top - peak), jnp.exp(up - peak)
        return peak, mine * denom + theirs * du[at, :], mine * numer + theirs * nu[at, :]

    coarse = coarse_blocks(tokens)
    stats = attend([(near, far, float(2**height)) for height, _, near, far in coarse])
    for (height, row, near, _), one in zip(coarse, stats):
        if height < LEVELS:
            one = merge(near, one)
        for ref, value in zip((mu, du, nu), one):
            put_twice(ref, spans[height - 1][0] + 2 * row, value)
    loads[parts].wait()
    for b in range(blocks):
        out_ref[b, :BLOCK, :] = grad_ref[:, b * WIDTH : (b + 1) * WIDTH]
    send(out_ref.at[:, :BLOCK, :], sent_out.at[:, :BLOCK, :])
    for first in range(0, tokens, PAIRS * 2 * BLOCK):
        pairs = [
            slice(row, row + 2 * BLOCK)
            for row in range(first, min(first + PAIRS * 2 * BLOCK, tokens), 2 * BLOCK)
        ]
        for at, one in zip(pairs, attend([(at, at, 1) for at in pairs])):
            peak, total, summed = merge(at, one)
            attended = (summed / total).astype(BF16)
            lse = peak + jnp.log(total)
            for half in range(2):
                b = at.start // BLOCK + half
                part = lse[half * BLOCK : (half + 1) * BLOCK]
                lse_ref[b : b + 1, :] = jnp.sum(diagonal(part), axis=0, keepdims=True)
            pair = slice(at.start // BLOCK, at.stop // BLOCK)
            out_ref[pair, BLOCK:, :] = attended.reshape(2, BLOCK, WIDTH)
            send(out_ref.at[pair, BLOCK:, :], sent_out.at[pair, BLOCK:, :])
    send(lse_ref, lse_out)
    for copy in copies:
        copy.wait()


def forward(qkv, att_grad, after=()):
    blocks = qkv.shape[0]
    tokens = blocks * BLOCK
    spans, total_rows = level_rows(tokens)
    finer = total_rows - spans[LEVELS][1]
    outs = [
        ((blocks, 2 * BLOCK, WIDTH), BF16, "hbm"),
        ((blocks, BLOCK), F32, "hbm"),
        ((3, total_rows - tokens, WIDTH), BF16, "hbm"),
    ]
    return kernel_call(
        functools.partial(forward_body, blocks),
        outs,
        ["hbm"] * 2,
        32,
        scratch=[
            pltpu.VMEM(qkv.shape, BF16),
            pltpu.VMEM(att_grad.shape, BF16),
            pltpu.VMEM((blocks, 2 * BLOCK, WIDTH), BF16),
            pltpu.VMEM((blocks, BLOCK), F32),
            pltpu.VMEM((3, total_rows - tokens, WIDTH), BF16),
            pltpu.VMEM((3, total_rows, WIDTH), F32),
            pltpu.VMEM((finer, WIDTH), F32),
            pltpu.VMEM((finer, WIDTH), F32),
            pltpu.VMEM((finer, WIDTH), F32),
            dma(8 + blocks // 2),
        ],
        cost=cost(4 * tokens * 384 * WIDTH, 8 << 20),
        name="head_forward",
        after=after,
    )(qkv, att_grad)


def backward_body(
    blocks, grad_in, sent_in, lse_in, lev_in, qkv_in, rows_in, w_in, grads_out, output_ref,
    out_ref, att_ref, lse_ref, lev_ref, qkv_ref, ys, ds, rs, cg, up, rows_ref, w_ref, sems,
):
    tokens = blocks * BLOCK
    spans, _ = level_rows(tokens)
    scale = 1.0 / math.sqrt(WIDTH)
    parts, count = 4, [0]

    def fetch(source, target):
        copy = pltpu.make_async_copy(source, target, sems.at[count[0]])
        count[0] += 1
        copy.start()
        return copy

    first_loads = []
    lse_load = fetch(lse_in, lse_ref)
    for p in range(parts):
        some = slice(p * blocks // parts, (p + 1) * blocks // parts)
        at = slice(p * tokens // parts, (p + 1) * tokens // parts)
        first_loads.append(
            [
                fetch(grad_in.at[at, :], cg.at[at, :]),
                fetch(sent_in.at[some, BLOCK:, :], att_ref.at[some, :, :]),
            ]
        )
    later_loads = [
        fetch(lev_in, lev_ref),
        fetch(qkv_in, qkv_ref),
        fetch(rows_in, rows_ref),
        fetch(w_in, w_ref),
    ]
    lse_load.wait()
    for b in range(blocks):
        if b % (blocks // parts) == 0:
            for copy in first_loads[b // (blocks // parts)]:
                copy.wait()
        at = slice(b * BLOCK, (b + 1) * BLOCK)
        lse = jnp.broadcast_to(lse_ref[b : b + 1, :], (BLOCK, BLOCK))
        rs[at, :] = wide(jnp.sum(diagonal(lse), axis=1, keepdims=True))
        grad = cg[at, :].astype(F32)
        ys[at, :] = grad
        ds[at, :] = wide(jnp.sum(grad * att_ref[b].astype(F32), axis=1, keepdims=True))
    for height in range(1, LEVELS + 1):
        below, _ = spans[height - 1]
        base, rows = spans[height]
        for r in range(0, rows, BLOCK):
            at = slice(base + r, base + r + BLOCK)
            first = below + 2 * r
            lo, hi = evens(rs, first, BLOCK), odds(rs, first, BLOCK)
            low = jnp.minimum(lo, hi)
            lo, hi = jnp.exp(low - lo), jnp.exp(low - hi)
            grad = lo * evens(ys, first, BLOCK) + hi * odds(ys, first, BLOCK)
            delta = lo * evens(ds, first, BLOCK) + hi * odds(ds, first, BLOCK)
            ys[at, :], ds[at, :], rs[at, :] = grad, delta, low
            cg[at, :] = grad.astype(BF16)

    level = functools.partial(rows_of, qkv_ref, lev_ref)

    def gradients(jobs):
        scores = [nt(level(0, q), level(1, k)) * scale for q, k in jobs]
        inner = [nt(cg[q, :], level(2, k)) for q, k in jobs]
        expos = [
            jnp.exp(x - across(rs[q, :], x.shape[1])) for x, (q, _) in zip(scores, jobs)
        ]
        sgrads = [
            (expo * (x - across(ds[q, :], x.shape[1])) * scale).astype(BF16)
            for expo, x, (q, _) in zip(expos, inner, jobs)
        ]
        probs = [expo.astype(BF16) for expo in expos]
        q_parts = [nn(x, level(1, k)) for x, (_, k) in zip(sgrads, jobs)]
        k_parts = [tn(x, level(0, q)) for x, (q, _) in zip(sgrads, jobs)]
        v_parts = [tn(x, cg[q, :]) for x, (q, _) in zip(probs, jobs)]
        return list(zip(q_parts, k_parts, v_parts))

    later_loads[0].wait()
    coarse = coarse_blocks(tokens)
    for (height, row, near, far), parts in zip(
        coarse, gradients([(near, far) for _, _, near, far in coarse])
    ):
        for x, (at, first) in enumerate(((near, row), (far, row ^ BLOCK), (far, row ^ BLOCK))):
            value = parts[x]
            if height < LEVELS:
                value = value + up[x, at, :]
            put_twice(up.at[x], spans[height - 1][0] + 2 * first, value)
    later_loads[1].wait()
    stores = []
    for first in range(0, tokens, PAIRS * 2 * BLOCK):
        pairs = [
            slice(row, row + 2 * BLOCK)
            for row in range(first, min(first + PAIRS * 2 * BLOCK, tokens), 2 * BLOCK)
        ]
        for at, parts in zip(pairs, gradients([(at, at) for at in pairs])):
            pair = slice(at.start // BLOCK, at.stop // BLOCK)
            for x, value in enumerate(parts):
                value = (value + up[x, at, :]).astype(BF16)
                out_ref[pair, x * BLOCK : (x + 1) * BLOCK, :] = value.reshape(2, BLOCK, WIDTH)
            stores.append(fetch(out_ref.at[pair, :, :], grads_out.at[pair, : 3 * BLOCK, :]))
    later_loads[2].wait()
    later_loads[3].wait()
    rows = jnp.concatenate([rows_ref[h] for h in range(HEADS)], axis=1)
    width = w_ref.shape[1]
    for first in range(0, width, 512):
        at = slice(first, first + 512)
        output_ref[:, at] = nn(rows, w_ref[:, at]).astype(BF16)
    for store in stores:
        store.wait()


def backward(grad, sent, lse, lev, qkv, rows, w_out, after):
    blocks = sent.shape[0]
    tokens = blocks * BLOCK
    spans, total_rows = level_rows(tokens)
    finer = total_rows - spans[LEVELS][1]
    extra = w_out.size // lax.axis_size("outer") // blocks // WIDTH
    return kernel_call(
        functools.partial(backward_body, blocks),
        [
            ((blocks, 3 * BLOCK + extra, WIDTH), BF16, "hbm"),
            ((BLOCK, w_out.shape[1]), BF16, "vmem"),
        ],
        ["hbm"] * 7,
        63.4,
        scratch=[
            pltpu.VMEM((blocks, 3 * BLOCK, WIDTH), BF16),
            pltpu.VMEM(rows.shape, BF16),
            pltpu.VMEM(lse.shape, F32),
            pltpu.VMEM(lev.shape, BF16),
            pltpu.VMEM(qkv.shape, BF16),
            pltpu.VMEM((total_rows, WIDTH), F32),
            pltpu.VMEM((total_rows, WIDTH), F32),
            pltpu.VMEM((total_rows, WIDTH), F32),
            pltpu.VMEM((total_rows, WIDTH), BF16),
            pltpu.VMEM((3, finer, WIDTH), F32),
            pltpu.VMEM(rows.shape, BF16),
            pltpu.VMEM(w_out.shape, BF16),
            dma(16 + blocks // 2),
        ],
        cost=cost(10 * tokens * 384 * WIDTH + 2 * BLOCK * w_out.size, 24 << 20),
        name="head_backward",
        after=after,
    )(grad.reshape(tokens, WIDTH), sent, lse, lev, qkv, rows, w_out)


def tile_body(groups, per, _, att_ref, *refs):
    cot_refs = refs[:groups]
    out_ref, lhs, held, tile, sems = refs[groups:]
    chunk = lhs.shape[0] // HEADS
    chunks, step = held.shape[0], held.shape[2]
    copies, stores = [], []
    for c in range(chunks):
        for k, ref in enumerate(cot_refs):
            copies.append(
                pltpu.make_async_copy(
                    ref.at[:, c * step : (c + 1) * step],
                    held.at[c, k * BLOCK : (k + 1) * BLOCK, :],
                    sems.at[1 + c * groups + k],
                )
            )
            copies[-1].start()
    mine = lax.axis_index("outer")
    for k in range(groups):
        for j in range(per):
            lhs[j * WIDTH : (j + 1) * WIDTH, k * BLOCK : (k + 1) * BLOCK] = att_ref[
                (mine ^ k) * per + j
            ].T
    for c in range(chunks):
        for copy in copies[c * groups : (c + 1) * groups]:
            copy.wait()
        part = nn(lhs[...], held[c]).astype(BF16)
        first = c * step
        for i in range(HEADS):
            for j in range(step // WIDTH):
                to = (first // WIDTH + j) * chunk
                tile[i, to : to + chunk, :] = part[
                    i * chunk : (i + 1) * chunk, j * WIDTH : (j + 1) * WIDTH
                ]
        done = slice(first // WIDTH * chunk, (first + step) // WIDTH * chunk)
        to = slice(3 * BLOCK + done.start, 3 * BLOCK + done.stop)
        stores.append(
            pltpu.make_async_copy(
                tile.at[:, done, :], out_ref.at[:, to, :], sems.at[1 + chunks * groups + c]
            )
        )
        stores[-1].start()
    for store in stores:
        store.wait()


def with_tile(grads, att, pieces):
    groups, width = len(pieces), pieces[0].shape[1]
    per = HEADS // groups
    chunk = per * WIDTH // HEADS
    extra = chunk * (width // WIDTH)
    chunks = 4
    return kernel_call(
        functools.partial(tile_body, groups, per),
        [(grads.shape, BF16, "hbm")],
        ["hbm", "vmem"] + ["hbm"] * groups,
        18,
        scratch=[
            pltpu.VMEM((per * WIDTH, groups * BLOCK), BF16),
            pltpu.VMEM((chunks, groups * BLOCK, width // chunks), BF16),
            pltpu.VMEM((HEADS, extra, WIDTH), BF16),
            dma(1 + chunks * (groups + 1)),
        ],
        aliases={0: 0},
        cost=cost(2 * groups * BLOCK * per * WIDTH * width, 10 << 20),
        name="projection_tile",
    )(grads, att, *pieces)[0]


def unpack_body(scale, in_ref, q_out, k_out, v_out, w_out, grads, w_ref, sems):
    chunk, width = w_ref.shape
    stores = []

    def send(source, target):
        stores.append(pltpu.make_async_copy(source, target, sems.at[len(stores)]))
        stores[-1].start()

    for x, target in enumerate((q_out, k_out, v_out)):
        for h in range(HEADS):
            grads[x, :, h * WIDTH : (h + 1) * WIDTH] = in_ref[h, x * BLOCK : (x + 1) * BLOCK, :]
        send(grads.at[x], target)
    for c in range(width // WIDTH):
        at = 3 * BLOCK + c * chunk
        total = in_ref[0, at : at + chunk, :].astype(F32)
        for h in range(1, HEADS):
            total = total + in_ref[h, at : at + chunk, :].astype(F32)
        w_ref[:, c * WIDTH : (c + 1) * WIDTH] = total * scale
    send(w_ref, w_out)
    for store in stores:
        store.wait()


def unpack(got, scale):
    chunk = (got.shape[1] - 3 * BLOCK) // HEADS
    width = HEADS * WIDTH
    return kernel_call(
        functools.partial(unpack_body, scale),
        [((BLOCK, width), BF16, "hbm")] * 3 + [((chunk, width), F32, "hbm")],
        ["vmem"],
        8,
        scratch=[
            pltpu.VMEM((3, BLOCK, width), BF16),
            pltpu.VMEM((chunk, width), F32),
            dma(4),
        ],
        cost=cost(0, 6 << 20),
        name="unpack_grads",
    )(got)


def split_body(got_ref, grad_ref, att_ref, sems):
    copies = [
        pltpu.make_async_copy(got_ref.at[:, BLOCK:, :], att_ref, sems.at[0]),
        pltpu.make_async_copy(got_ref.at[:, :BLOCK, :], grad_ref, sems.at[1]),
    ]
    for copy in copies:
        copy.start()
    for copy in copies:
        copy.wait()


def split(got):
    return kernel_call(
        split_body,
        [((HEADS, BLOCK, WIDTH), BF16, "hbm")] * 2,
        ["vmem"],
        2,
        scratch=[dma(2)],
        cost=cost(0, 2 << 20),
        name="split_attended",
    )(got)


def swap(value, axis):
    return lax.all_to_all(value, axis, 0, 0, tiled=True)


def from_outer(value, apart):
    size = lax.axis_size("outer")
    return lax.ppermute(value, "outer", [(i, i ^ apart) for i in range(size)])


def on_device(query_in, key_in, value_in, w_out, cotangent):
    groups = lax.axis_size("outer")
    tokens = query_in.shape[0] * lax.axis_size(("outer", "inner"))
    pieces = {k: from_outer(cotangent, k) if k else cotangent for k in range(groups) if k < 2 or k & 3 == 2}
    soon = [pieces[k] for k in pieces if k]
    qkv = swap(pack(query_in, key_in, value_in), "inner")
    att_grad = attended_gradient(cotangent, w_out)
    sent, lse, lev = forward(qkv, att_grad, after=soon)
    late = {k: from_outer(pieces[k + 2], 2) for k in range(4, groups, 4)}
    pieces.update(late)
    for k in range(2, groups, 2):
        pieces[k + 1] = from_outer(pieces[k], 1)
    grad, att = split(swap(sent, "inner"))
    att_outer = swap(att, "outer")
    grads, output = backward(grad, sent, lse, lev, qkv, att, w_out, list(late.values()))
    pieces = [pieces[k] for k in range(groups)]
    last = swap(with_tile(grads, att_outer, pieces), "inner")
    query_grad, key_grad, value_grad, w_out_grad = unpack(last, 1.0 / math.sqrt(tokens))
    return output, query_grad, key_grad, value_grad, w_out_grad


def solution(mesh):
    rows = P(("outer", "inner"), None)
    return jax.shard_map(
        on_device,
        mesh=mesh,
        in_specs=(rows, rows, rows, P(), rows),
        out_specs=(rows,) * 5,
        check_vma=False,
    )
```

```python
import functools
import math

import jax
import jax.numpy as jnp
from jax import lax
from jax.experimental import pallas as pl
from jax.experimental.pallas import tpu as pltpu
from jax.sharding import PartitionSpec as P

HEADS = 16
BLOCK = 128
LEVELS = 3
WIDTH = 128
BF16 = jnp.bfloat16
F32 = jnp.float32
CHUNK = 256
PAIRS = 4


def nt(a, b):
    return lax.dot_general(a, b, (((1,), (1,)), ((), ())), preferred_element_type=F32)


def nn(a, b):
    return lax.dot_general(a, b, (((1,), (0,)), ((), ())), preferred_element_type=F32)


def tn(a, b):
    return lax.dot_general(a, b, (((0,), (0,)), ((), ())), preferred_element_type=F32)


def wide(stat, columns=WIDTH):
    return jnp.broadcast_to(stat, (stat.shape[0], columns))


def evens(ref, base, rows):
    return ref[pl.ds(base, rows, stride=2), :]


def odds(ref, base, rows):
    return ref[pl.ds(base + 1, rows, stride=2), :]


def put_twice(ref, base, value):
    rows = value.shape[0]
    ref[pl.ds(base, rows, stride=2), :] = value
    ref[pl.ds(base + 1, rows, stride=2), :] = value


def diagonal(matrix):
    rows = lax.broadcasted_iota(jnp.int32, matrix.shape, 0)
    columns = lax.broadcasted_iota(jnp.int32, matrix.shape, 1)
    return jnp.where(rows == columns, matrix, 0.0)


def across(stat, columns):
    return jnp.concatenate([stat] * (columns // WIDTH), axis=1)


def coarse_blocks(tokens):
    spans, _ = level_rows(tokens)
    out = []
    for height in range(LEVELS, 0, -1):
        base, rows = spans[height]
        for row in range(0, rows, BLOCK):
            near, far = base + row, base + (row ^ BLOCK)
            out.append((height, row, slice(near, near + BLOCK), slice(far, far + BLOCK)))
    return out


def rows_of(token_ref, coarse_ref, x, at):
    tokens = token_ref.shape[0] * BLOCK
    if at.start >= tokens:
        return coarse_ref[x, at.start - tokens : at.stop - tokens, :]
    some = slice(at.start // BLOCK, at.stop // BLOCK)
    return token_ref[some, x * BLOCK : (x + 1) * BLOCK, :].reshape(at.stop - at.start, WIDTH)


def level_rows(tokens):
    out, base = [], 0
    for height in range(LEVELS + 1):
        out.append((base, tokens >> height))
        base += tokens >> height
    return out, base


def kernel_call(body, outs, in_places, mib, scratch=(), cost=None, name=None, after=(), aliases=None):
    count = len(in_places)
    in_places = list(in_places) + ["hbm"] * len(after)

    def ordered(*refs):
        body(*refs[:count], *refs[len(in_places) :])

    spec = {
        "vmem": pl.BlockSpec(memory_space=pltpu.VMEM),
        "kept": pl.BlockSpec(memory_space=pltpu.VMEM),
        "hbm": pl.BlockSpec(memory_space=pl.ANY),
    }
    kinds = {"hbm": pltpu.HBM, "kept": pltpu.VMEM}
    shapes = [
        kinds.get(place, jax.ShapeDtypeStruct)(shape, dtype) for shape, dtype, place in outs
    ]
    call = pl.pallas_call(
        ordered,
        out_shape=shapes,
        in_specs=[spec[place] for place in in_places],
        out_specs=[spec[place] for _, _, place in outs],
        scratch_shapes=list(scratch),
        compiler_params=pltpu.CompilerParams(vmem_limit_bytes=int(mib * 2**20)),
        cost_estimate=cost,
        name=name,
        input_output_aliases=aliases or {},
    )

    def run(*operands):
        operands = [
            pltpu.with_memory_space_constraint(x, pltpu.HBM) if place == "hbm" else x
            for x, place in zip((*operands, *after), in_places)
        ]
        return call(*operands)

    return run


def dma(count):
    return pltpu.SemaphoreType.DMA((count,))


def cost(flops, nbytes):
    return pl.CostEstimate(flops=int(flops), bytes_accessed=int(nbytes), transcendentals=0)


def pack_body(q_ref, k_ref, v_ref, out_ref, held, packed, in_sems, out_sems):
    loads = [
        pltpu.make_async_copy(ref, held.at[x], in_sems.at[x])
        for x, ref in enumerate((q_ref, k_ref, v_ref))
    ]
    for load in loads:
        load.start()
    stores = []
    for x, load in enumerate(loads):
        load.wait()
        rows = slice(x * BLOCK, (x + 1) * BLOCK)
        for h in range(HEADS):
            packed[h, rows, :] = held[x, :, h * WIDTH : (h + 1) * WIDTH]
        stores.append(
            pltpu.make_async_copy(packed.at[:, rows, :], out_ref.at[:, rows, :], out_sems.at[x])
        )
        stores[-1].start()
    for store in stores:
        store.wait()


def pack(q, k, v):
    packed = (HEADS, 3 * BLOCK, WIDTH)
    return kernel_call(
        pack_body,
        [(packed, BF16, "hbm")],
        ["hbm"] * 3,
        6,
        scratch=[pltpu.VMEM((3,) + q.shape, BF16), pltpu.VMEM(packed, BF16), dma(3), dma(3)],
        cost=cost(0, 6 * q.size * 2),
        name="pack_qkv",
    )(q, k, v)[0]


def att_grad_body(chunks, cot_ref, w_ref, out_ref, held, sems):
    rows = held.shape[0] // chunks
    copies = []
    for c in range(chunks):
        at = slice(c * rows, (c + 1) * rows)
        copies.append(pltpu.make_async_copy(w_ref.at[at, :], held.at[at, :], sems.at[c]))
        copies[-1].start()
    for c, copy in enumerate(copies):
        at = slice(c * rows, (c + 1) * rows)
        copy.wait()
        out_ref[:, at] = nt(cot_ref[...], held[at, :]).astype(BF16)


def attended_gradient(cot, w_out):
    chunks = 4
    return kernel_call(
        functools.partial(att_grad_body, chunks),
        [(cot.shape, BF16, "vmem")],
        ["vmem", "hbm"],
        63.6,
        scratch=[pltpu.VMEM(w_out.shape, BF16), dma(chunks)],
        cost=cost(0, 1 << 20),
        name="attended_gradient",
    )(cot, w_out)[0]


def forward_body(
    blocks, qkv_in, grad_in, sent_out, lse_out, lev_out,
    in_ref, grad_ref, out_ref, lse_ref, lev_ref, fq, mu, du, nu, sems,
):
    tokens = blocks * BLOCK
    spans, _ = level_rows(tokens)
    copies, count = [], [0]

    def send(source, target):
        copies.append(pltpu.make_async_copy(source, target, sems.at[count[0]]))
        copies[-1].start()
        count[0] += 1

    scale = 1.0 / math.sqrt(WIDTH)
    parts = 4
    for p in range(parts):
        some = slice(p * blocks // parts, (p + 1) * blocks // parts)
        send(qkv_in.at[some, :, :], in_ref.at[some, :, :])
    send(grad_in, grad_ref)
    loads, copies[:] = copies[:], []
    for b in range(blocks):
        if b % (blocks // parts) == 0:
            loads[b // (blocks // parts)].wait()
        for x in range(3):
            part = in_ref[b, x * BLOCK : (x + 1) * BLOCK, :]
            fq[x, b * BLOCK : (b + 1) * BLOCK, :] = part.astype(F32)
    for height in range(1, LEVELS + 1):
        below, _ = spans[height - 1]
        base, rows = spans[height]
        step = min(CHUNK, rows)
        for x in range(3):
            for r in range(0, rows, step):
                mean = (
                    evens(fq.at[x], below + 2 * r, step) + odds(fq.at[x], below + 2 * r, step)
                ) * 0.5
                mean = mean.astype(BF16)
                lev_ref[x, base - tokens + r : base - tokens + r + step, :] = mean
                fq[x, base + r : base + r + step, :] = mean.astype(F32)

    send(lev_ref, lev_out)

    level = functools.partial(rows_of, in_ref, lev_ref)

    def attend(jobs):
        scores = [nt(level(0, q), level(1, k)) * scale for q, k, _ in jobs]
        tops = [wide(jnp.max(x, axis=1, keepdims=True)) for x in scores]
        expos = [jnp.exp(x - across(top, x.shape[1])) for x, top in zip(scores, tops)]
        numers = [nn(x.astype(BF16), level(2, k)) for x, (_, k, _) in zip(expos, jobs)]
        denoms = [wide(jnp.sum(x, axis=1, keepdims=True)) for x in expos]
        return [
            (top, denom * factor, numer * factor) if factor != 1 else (top, denom, numer)
            for top, denom, numer, (_, _, factor) in zip(tops, denoms, numers, jobs)
        ]

    def merge(at, stats):
        top, denom, numer = stats
        up = mu[at, :]
        peak = jnp.maximum(top, up)
        mine, theirs = jnp.exp(top - peak), jnp.exp(up - peak)
        return peak, mine * denom + theirs * du[at, :], mine * numer + theirs * nu[at, :]

    coarse = coarse_blocks(tokens)
    stats = attend([(near, far, float(2**height)) for height, _, near, far in coarse])
    for (height, row, near, _), one in zip(coarse, stats):
        if height < LEVELS:
            one = merge(near, one)
        for ref, value in zip((mu, du, nu), one):
            put_twice(ref, spans[height - 1][0] + 2 * row, value)
    loads[parts].wait()
    for b in range(blocks):
        out_ref[b, :BLOCK, :] = grad_ref[:, b * WIDTH : (b + 1) * WIDTH]
    send(out_ref.at[:, :BLOCK, :], sent_out.at[:, :BLOCK, :])
    for first in range(0, tokens, PAIRS * 2 * BLOCK):
        pairs = [
            slice(row, row + 2 * BLOCK)
            for row in range(first, min(first + PAIRS * 2 * BLOCK, tokens), 2 * BLOCK)
        ]
        for at, one in zip(pairs, attend([(at, at, 1) for at in pairs])):
            peak, total, summed = merge(at, one)
            attended = (summed / total).astype(BF16)
            lse = peak + jnp.log(total)
            for half in range(2):
                b = at.start // BLOCK + half
                part = lse[half * BLOCK : (half + 1) * BLOCK]
                lse_ref[b : b + 1, :] = jnp.sum(diagonal(part), axis=0, keepdims=True)
            pair = slice(at.start // BLOCK, at.stop // BLOCK)
            out_ref[pair, BLOCK:, :] = attended.reshape(2, BLOCK, WIDTH)
            send(out_ref.at[pair, BLOCK:, :], sent_out.at[pair, BLOCK:, :])
    send(lse_ref, lse_out)
    for copy in copies:
        copy.wait()


def forward(qkv, att_grad, after=()):
    blocks = qkv.shape[0]
    tokens = blocks * BLOCK
    spans, total_rows = level_rows(tokens)
    finer = total_rows - spans[LEVELS][1]
    outs = [
        ((blocks, 2 * BLOCK, WIDTH), BF16, "hbm"),
        ((blocks, BLOCK), F32, "hbm"),
        ((3, total_rows - tokens, WIDTH), BF16, "hbm"),
    ]
    return kernel_call(
        functools.partial(forward_body, blocks),
        outs,
        ["hbm"] * 2,
        32,
        scratch=[
            pltpu.VMEM(qkv.shape, BF16),
            pltpu.VMEM(att_grad.shape, BF16),
            pltpu.VMEM((blocks, 2 * BLOCK, WIDTH), BF16),
            pltpu.VMEM((blocks, BLOCK), F32),
            pltpu.VMEM((3, total_rows - tokens, WIDTH), BF16),
            pltpu.VMEM((3, total_rows, WIDTH), F32),
            pltpu.VMEM((finer, WIDTH), F32),
            pltpu.VMEM((finer, WIDTH), F32),
            pltpu.VMEM((finer, WIDTH), F32),
            dma(8 + blocks // 2),
        ],
        cost=cost(4 * tokens * 384 * WIDTH, 8 << 20),
        name="head_forward",
        after=after,
    )(qkv, att_grad)


def backward_body(
    blocks, held, grad_in, sent_in, lse_in, lev_in, qkv_in, rows_in, w_in, *refs
):
    cot_in = refs[:held]
    grads_out, output_ref, cot_ref = refs[held : held + 3]
    (
        out_ref, att_ref, lse_ref, lev_ref, qkv_ref, ys, ds, rs, cg, up, rows_ref, w_ref, sems
    ) = refs[held + 3 :]
    tokens = blocks * BLOCK
    spans, _ = level_rows(tokens)
    scale = 1.0 / math.sqrt(WIDTH)
    parts, count = 4, [0]

    def fetch(source, target):
        copy = pltpu.make_async_copy(source, target, sems.at[count[0]])
        count[0] += 1
        copy.start()
        return copy

    first_loads = []
    lse_load = fetch(lse_in, lse_ref)
    for p in range(parts):
        some = slice(p * blocks // parts, (p + 1) * blocks // parts)
        at = slice(p * tokens // parts, (p + 1) * tokens // parts)
        first_loads.append(
            [
                fetch(grad_in.at[at, :], cg.at[at, :]),
                fetch(sent_in.at[some, BLOCK:, :], att_ref.at[some, :, :]),
            ]
        )
    later_loads = [
        fetch(lev_in, lev_ref),
        fetch(qkv_in, qkv_ref),
        fetch(rows_in, rows_ref),
        fetch(w_in, w_ref),
    ] + [
        fetch(ref, cot_ref.at[k * BLOCK : (k + 1) * BLOCK, :]) for k, ref in enumerate(cot_in)
    ]
    lse_load.wait()
    for b in range(blocks):
        if b % (blocks // parts) == 0:
            for copy in first_loads[b // (blocks // parts)]:
                copy.wait()
        at = slice(b * BLOCK, (b + 1) * BLOCK)
        lse = jnp.broadcast_to(lse_ref[b : b + 1, :], (BLOCK, BLOCK))
        rs[at, :] = wide(jnp.sum(diagonal(lse), axis=1, keepdims=True))
        grad = cg[at, :].astype(F32)
        ys[at, :] = grad
        ds[at, :] = wide(jnp.sum(grad * att_ref[b].astype(F32), axis=1, keepdims=True))
    for height in range(1, LEVELS + 1):
        below, _ = spans[height - 1]
        base, rows = spans[height]
        for r in range(0, rows, BLOCK):
            at = slice(base + r, base + r + BLOCK)
            first = below + 2 * r
            lo, hi = evens(rs, first, BLOCK), odds(rs, first, BLOCK)
            low = jnp.minimum(lo, hi)
            lo, hi = jnp.exp(low - lo), jnp.exp(low - hi)
            grad = lo * evens(ys, first, BLOCK) + hi * odds(ys, first, BLOCK)
            delta = lo * evens(ds, first, BLOCK) + hi * odds(ds, first, BLOCK)
            ys[at, :], ds[at, :], rs[at, :] = grad, delta, low
            cg[at, :] = grad.astype(BF16)

    level = functools.partial(rows_of, qkv_ref, lev_ref)

    def gradients(jobs):
        scores = [nt(level(0, q), level(1, k)) * scale for q, k in jobs]
        inner = [nt(cg[q, :], level(2, k)) for q, k in jobs]
        expos = [
            jnp.exp(x - across(rs[q, :], x.shape[1])) for x, (q, _) in zip(scores, jobs)
        ]
        sgrads = [
            (expo * (x - across(ds[q, :], x.shape[1])) * scale).astype(BF16)
            for expo, x, (q, _) in zip(expos, inner, jobs)
        ]
        probs = [expo.astype(BF16) for expo in expos]
        q_parts = [nn(x, level(1, k)) for x, (_, k) in zip(sgrads, jobs)]
        k_parts = [tn(x, level(0, q)) for x, (q, _) in zip(sgrads, jobs)]
        v_parts = [tn(x, cg[q, :]) for x, (q, _) in zip(probs, jobs)]
        return list(zip(q_parts, k_parts, v_parts))

    later_loads[0].wait()
    coarse = coarse_blocks(tokens)
    for (height, row, near, far), parts in zip(
        coarse, gradients([(near, far) for _, _, near, far in coarse])
    ):
        for x, (at, first) in enumerate(((near, row), (far, row ^ BLOCK), (far, row ^ BLOCK))):
            value = parts[x]
            if height < LEVELS:
                value = value + up[x, at, :]
            put_twice(up.at[x], spans[height - 1][0] + 2 * first, value)
    later_loads[1].wait()
    stores = []
    for first in range(0, tokens, PAIRS * 2 * BLOCK):
        pairs = [
            slice(row, row + 2 * BLOCK)
            for row in range(first, min(first + PAIRS * 2 * BLOCK, tokens), 2 * BLOCK)
        ]
        for at, parts in zip(pairs, gradients([(at, at) for at in pairs])):
            pair = slice(at.start // BLOCK, at.stop // BLOCK)
            for x, value in enumerate(parts):
                value = (value + up[x, at, :]).astype(BF16)
                out_ref[pair, x * BLOCK : (x + 1) * BLOCK, :] = value.reshape(2, BLOCK, WIDTH)
            stores.append(fetch(out_ref.at[pair, :, :], grads_out.at[pair, : 3 * BLOCK, :]))
    later_loads[2].wait()
    later_loads[3].wait()
    rows = jnp.concatenate([rows_ref[h] for h in range(HEADS)], axis=1)
    width = w_ref.shape[1]
    for first in range(0, width, 512):
        at = slice(first, first + 512)
        output_ref[:, at] = nn(rows, w_ref[:, at]).astype(BF16)
    for store in stores + later_loads[4:]:
        store.wait()


def backward(grad, sent, lse, lev, qkv, rows, w_out, pieces):
    blocks = sent.shape[0]
    tokens = blocks * BLOCK
    spans, total_rows = level_rows(tokens)
    finer = total_rows - spans[LEVELS][1]
    extra = w_out.size // lax.axis_size("outer") // blocks // WIDTH
    return kernel_call(
        functools.partial(backward_body, blocks, len(pieces)),
        [
            ((blocks, 3 * BLOCK + extra, WIDTH), BF16, "hbm"),
            ((BLOCK, w_out.shape[1]), BF16, "vmem"),
            ((len(pieces) * BLOCK, w_out.shape[1]), BF16, "kept"),
        ],
        ["hbm"] * (7 + len(pieces)),
        61.2,
        scratch=[
            pltpu.VMEM((blocks, 3 * BLOCK, WIDTH), BF16),
            pltpu.VMEM(rows.shape, BF16),
            pltpu.VMEM(lse.shape, F32),
            pltpu.VMEM(lev.shape, BF16),
            pltpu.VMEM(qkv.shape, BF16),
            pltpu.VMEM((total_rows, WIDTH), F32),
            pltpu.VMEM((total_rows, WIDTH), F32),
            pltpu.VMEM((total_rows, WIDTH), F32),
            pltpu.VMEM((total_rows, WIDTH), BF16),
            pltpu.VMEM((3, finer, WIDTH), F32),
            pltpu.VMEM(rows.shape, BF16),
            pltpu.VMEM(w_out.shape, BF16),
            dma(16 + blocks // 2 + len(pieces)),
        ],
        cost=cost(10 * tokens * 384 * WIDTH + 2 * BLOCK * w_out.size, 24 << 20),
        name="head_backward",
    )(grad.reshape(tokens, WIDTH), sent, lse, lev, qkv, rows, w_out, *pieces)


def tile_body(order, per, _, att_in, near_ref, *refs):
    count = len(order) - near_ref.shape[0] // BLOCK
    out_ref, att_ref, lhs, held, tile, sems = refs[count:]
    deep = near_ref.shape[0]
    chunk = lhs.shape[0] // HEADS
    chunks, step = held.shape[0], held.shape[2]
    att_copy = pltpu.make_async_copy(att_in, att_ref, sems.at[0])
    att_copy.start()
    copies, stores = [], []
    for c in range(chunks):
        for k, ref in enumerate(refs[:count]):
            copies.append(
                pltpu.make_async_copy(
                    ref.at[:, c * step : (c + 1) * step],
                    held.at[c, k * BLOCK : (k + 1) * BLOCK, :],
                    sems.at[1 + c * count + k],
                )
            )
            copies[-1].start()
    att_copy.wait()
    mine = lax.axis_index("outer")
    for place, k in enumerate(order):
        for j in range(per):
            lhs[j * WIDTH : (j + 1) * WIDTH, place * BLOCK : (place + 1) * BLOCK] = att_ref[
                (mine ^ k) * per + j
            ].T
    for c in range(chunks):
        first = c * step
        part = nn(lhs[:, :deep], near_ref[:, first : first + step])
        for copy in copies[c * count : (c + 1) * count]:
            copy.wait()
        part = (part + nn(lhs[:, deep:], held[c])).astype(BF16)
        for i in range(HEADS):
            for j in range(step // WIDTH):
                to = (first // WIDTH + j) * chunk
                tile[i, to : to + chunk, :] = part[
                    i * chunk : (i + 1) * chunk, j * WIDTH : (j + 1) * WIDTH
                ]
        done = slice(first // WIDTH * chunk, (first + step) // WIDTH * chunk)
        to = slice(3 * BLOCK + done.start, 3 * BLOCK + done.stop)
        stores.append(
            pltpu.make_async_copy(
                tile.at[:, done, :], out_ref.at[:, to, :], sems.at[1 + chunks * count + c]
            )
        )
        stores[-1].start()
    for store in stores:
        store.wait()


def with_tile(grads, att, near, pieces, order):
    groups, width, count = len(order), near.shape[1], len(pieces)
    per = HEADS // groups
    chunk = per * WIDTH // HEADS
    extra = chunk * (width // WIDTH)
    chunks = 4
    return kernel_call(
        functools.partial(tile_body, order, per),
        [(grads.shape, BF16, "hbm")],
        ["hbm", "hbm", "vmem"] + ["hbm"] * count,
        18,
        scratch=[
            pltpu.VMEM(att.shape, BF16),
            pltpu.VMEM((per * WIDTH, groups * BLOCK), BF16),
            pltpu.VMEM((chunks, count * BLOCK, width // chunks), BF16),
            pltpu.VMEM((HEADS, extra, WIDTH), BF16),
            dma(1 + chunks * (count + 1)),
        ],
        aliases={0: 0},
        cost=cost(2 * groups * BLOCK * per * WIDTH * width, 10 << 20),
        name="projection_tile",
    )(grads, att, near, *pieces)[0]


def unpack_body(scale, in_ref, q_out, k_out, v_out, w_out, grads, w_ref, sems):
    chunk, width = w_ref.shape
    stores = []

    def send(source, target):
        stores.append(pltpu.make_async_copy(source, target, sems.at[len(stores)]))
        stores[-1].start()

    for x, target in enumerate((q_out, k_out, v_out)):
        for h in range(HEADS):
            grads[x, :, h * WIDTH : (h + 1) * WIDTH] = in_ref[h, x * BLOCK : (x + 1) * BLOCK, :]
        send(grads.at[x], target)
    for c in range(width // WIDTH):
        at = 3 * BLOCK + c * chunk
        total = in_ref[0, at : at + chunk, :].astype(F32)
        for h in range(1, HEADS):
            total = total + in_ref[h, at : at + chunk, :].astype(F32)
        w_ref[:, c * WIDTH : (c + 1) * WIDTH] = total * scale
    send(w_ref, w_out)
    for store in stores:
        store.wait()


def unpack(got, scale):
    chunk = (got.shape[1] - 3 * BLOCK) // HEADS
    width = HEADS * WIDTH
    return kernel_call(
        functools.partial(unpack_body, scale),
        [((BLOCK, width), BF16, "hbm")] * 3 + [((chunk, width), F32, "hbm")],
        ["vmem"],
        8,
        scratch=[
            pltpu.VMEM((3, BLOCK, width), BF16),
            pltpu.VMEM((chunk, width), F32),
            dma(4),
        ],
        cost=cost(0, 6 << 20),
        name="unpack_grads",
    )(got)


def split_body(got_ref, grad_ref, att_ref, sems):
    copies = [
        pltpu.make_async_copy(got_ref.at[:, BLOCK:, :], att_ref, sems.at[0]),
        pltpu.make_async_copy(got_ref.at[:, :BLOCK, :], grad_ref, sems.at[1]),
    ]
    for copy in copies:
        copy.start()
    for copy in copies:
        copy.wait()


def split(got):
    return kernel_call(
        split_body,
        [((HEADS, BLOCK, WIDTH), BF16, "hbm")] * 2,
        ["vmem"],
        2,
        scratch=[dma(2)],
        cost=cost(0, 2 << 20),
        name="split_attended",
    )(got)


def swap(value, axis):
    return lax.all_to_all(value, axis, 0, 0, tiled=True)


def from_outer(value, apart):
    size = lax.axis_size("outer")
    return lax.ppermute(value, "outer", [(i, i ^ apart) for i in range(size)])


def on_device(query_in, key_in, value_in, w_out, cotangent):
    groups = lax.axis_size("outer")
    tokens = query_in.shape[0] * lax.axis_size(("outer", "inner"))
    pieces = {k: from_outer(cotangent, k) if k else cotangent for k in range(groups) if k < 2 or k & 3 == 2}
    soon = [pieces[k] for k in pieces if k]
    qkv = swap(pack(query_in, key_in, value_in), "inner")
    att_grad = attended_gradient(cotangent, w_out)
    sent, lse, lev = forward(qkv, att_grad, after=soon)
    late = {k: from_outer(pieces[k + 2], 2) for k in range(4, groups, 4)}
    pieces.update(late)
    for k in range(2, groups, 2):
        pieces[k + 1] = from_outer(pieces[k], 1)
    grad, att = split(swap(sent, "inner"))
    att_outer = swap(att, "outer")
    first = [k for k in range(groups) if k < 2 or k % 2 == 0]
    rest = [k for k in range(groups) if k not in first]
    grads, output, near = backward(
        grad, sent, lse, lev, qkv, att, w_out, [pieces[k] for k in first]
    )
    tile = with_tile(grads, att_outer, near, [pieces[k] for k in rest], first + rest)
    last = swap(tile, "inner")
    query_grad, key_grad, value_grad, w_out_grad = unpack(last, 1.0 / math.sqrt(tokens))
    return output, query_grad, key_grad, value_grad, w_out_grad


def solution(mesh):
    rows = P(("outer", "inner"), None)
    return jax.shard_map(
        on_device,
        mesh=mesh,
        in_specs=(rows, rows, rows, P(), rows),
        out_specs=(rows,) * 5,
        check_vma=False,
    )
```

```python
import functools
import math

import jax
import jax.numpy as jnp
from jax import lax
from jax.experimental import pallas as pl
from jax.experimental.pallas import tpu as pltpu
from jax.sharding import PartitionSpec as P

HEADS = 16
BLOCK = 128
LEVELS = 3
WIDTH = 128
BF16 = jnp.bfloat16
F32 = jnp.float32
CHUNK = 256
PAIRS = 4


def nt(a, b):
    return lax.dot_general(a, b, (((1,), (1,)), ((), ())), preferred_element_type=F32)


def nn(a, b):
    return lax.dot_general(a, b, (((1,), (0,)), ((), ())), preferred_element_type=F32)


def tn(a, b):
    return lax.dot_general(a, b, (((0,), (0,)), ((), ())), preferred_element_type=F32)


def wide(stat, columns=WIDTH):
    return jnp.broadcast_to(stat, (stat.shape[0], columns))


def evens(ref, base, rows):
    return ref[pl.ds(base, rows, stride=2), :]


def odds(ref, base, rows):
    return ref[pl.ds(base + 1, rows, stride=2), :]


def put_twice(ref, base, value):
    rows = value.shape[0]
    ref[pl.ds(base, rows, stride=2), :] = value
    ref[pl.ds(base + 1, rows, stride=2), :] = value


def diagonal(matrix):
    rows = lax.broadcasted_iota(jnp.int32, matrix.shape, 0)
    columns = lax.broadcasted_iota(jnp.int32, matrix.shape, 1)
    return jnp.where(rows == columns, matrix, 0.0)


def across(stat, columns):
    return jnp.concatenate([stat] * (columns // WIDTH), axis=1)


def coarse_blocks(tokens):
    spans, _ = level_rows(tokens)
    out = []
    for height in range(LEVELS, 0, -1):
        base, rows = spans[height]
        for row in range(0, rows, BLOCK):
            near, far = base + row, base + (row ^ BLOCK)
            out.append((height, row, slice(near, near + BLOCK), slice(far, far + BLOCK)))
    return out


def rows_of(token_ref, coarse_ref, x, at):
    tokens = token_ref.shape[0] * BLOCK
    if at.start >= tokens:
        return coarse_ref[x, at.start - tokens : at.stop - tokens, :]
    some = slice(at.start // BLOCK, at.stop // BLOCK)
    return token_ref[some, x * BLOCK : (x + 1) * BLOCK, :].reshape(at.stop - at.start, WIDTH)


def level_rows(tokens):
    out, base = [], 0
    for height in range(LEVELS + 1):
        out.append((base, tokens >> height))
        base += tokens >> height
    return out, base


def kernel_call(body, outs, in_places, mib, scratch=(), cost=None, name=None, after=(), aliases=None):
    count = len(in_places)
    in_places = list(in_places) + ["hbm"] * len(after)

    def ordered(*refs):
        body(*refs[:count], *refs[len(in_places) :])

    spec = {
        "vmem": pl.BlockSpec(memory_space=pltpu.VMEM),
        "hbm": pl.BlockSpec(memory_space=pl.ANY),
    }
    shapes = [
        pltpu.HBM(shape, dtype) if place == "hbm" else jax.ShapeDtypeStruct(shape, dtype)
        for shape, dtype, place in outs
    ]
    call = pl.pallas_call(
        ordered,
        out_shape=shapes,
        in_specs=[spec[place] for place in in_places],
        out_specs=[spec[place] for _, _, place in outs],
        scratch_shapes=list(scratch),
        compiler_params=pltpu.CompilerParams(vmem_limit_bytes=int(mib * 2**20)),
        cost_estimate=cost,
        name=name,
        input_output_aliases=aliases or {},
    )

    def run(*operands):
        operands = [
            pltpu.with_memory_space_constraint(x, pltpu.HBM) if place == "hbm" else x
            for x, place in zip((*operands, *after), in_places)
        ]
        return call(*operands)

    return run


def dma(count):
    return pltpu.SemaphoreType.DMA((count,))


def cost(flops, nbytes):
    return pl.CostEstimate(flops=int(flops), bytes_accessed=int(nbytes), transcendentals=0)


def pack_body(q_ref, k_ref, v_ref, out_ref, held, packed, in_sems, out_sems):
    half = BLOCK // 2
    jobs = [(x, first) for x in range(3) for first in (0, half)]
    loads, stores = [], []
    for i, (x, first) in enumerate(jobs):
        rows = slice(first, first + half)
        ref = (q_ref, k_ref, v_ref)[x]
        loads.append(
            pltpu.make_async_copy(ref.at[rows, :], held.at[x, rows, :], in_sems.at[i])
        )
        loads[-1].start()
    for i, (x, first) in enumerate(jobs):
        loads[i].wait()
        rows = slice(x * BLOCK + first, x * BLOCK + first + half)
        for h in range(HEADS):
            packed[h, rows, :] = held[x, first : first + half, h * WIDTH : (h + 1) * WIDTH]
        stores.append(
            pltpu.make_async_copy(packed.at[:, rows, :], out_ref.at[:, rows, :], out_sems.at[i])
        )
        stores[-1].start()
    for store in stores:
        store.wait()


def pack(q, k, v):
    packed = (HEADS, 3 * BLOCK, WIDTH)
    return kernel_call(
        pack_body,
        [(packed, BF16, "hbm")],
        ["hbm"] * 3,
        6,
        scratch=[pltpu.VMEM((3,) + q.shape, BF16), pltpu.VMEM(packed, BF16), dma(6), dma(6)],
        cost=cost(0, 6 * q.size * 2),
        name="pack_qkv",
    )(q, k, v)[0]


def att_grad_body(chunks, cot_ref, w_ref, out_ref, held, sems):
    rows = held.shape[0] // chunks
    copies = []
    for c in range(chunks):
        at = slice(c * rows, (c + 1) * rows)
        copies.append(pltpu.make_async_copy(w_ref.at[at, :], held.at[at, :], sems.at[c]))
        copies[-1].start()
    for c, copy in enumerate(copies):
        at = slice(c * rows, (c + 1) * rows)
        copy.wait()
        out_ref[:, at] = nt(cot_ref[...], held[at, :]).astype(BF16)


def attended_gradient(cot, w_out):
    chunks = 4
    return kernel_call(
        functools.partial(att_grad_body, chunks),
        [(cot.shape, BF16, "vmem")],
        ["vmem", "hbm"],
        63.6,
        scratch=[pltpu.VMEM(w_out.shape, BF16), dma(chunks)],
        cost=cost(0, 1 << 20),
        name="attended_gradient",
    )(cot, w_out)[0]


def forward_body(
    blocks, qkv_in, grad_in, sent_out, lse_out, lev_out,
    in_ref, grad_ref, out_ref, lse_ref, lev_ref, fq, mu, du, nu, sems,
):
    tokens = blocks * BLOCK
    spans, _ = level_rows(tokens)
    copies, count = [], [0]

    def send(source, target):
        copies.append(pltpu.make_async_copy(source, target, sems.at[count[0]]))
        copies[-1].start()
        count[0] += 1

    scale = 1.0 / math.sqrt(WIDTH)
    parts = 4
    for p in range(parts):
        some = slice(p * blocks // parts, (p + 1) * blocks // parts)
        send(qkv_in.at[some, :, :], in_ref.at[some, :, :])
    send(grad_in, grad_ref)
    loads, copies[:] = copies[:], []
    for b in range(blocks):
        if b % (blocks // parts) == 0:
            loads[b // (blocks // parts)].wait()
        for x in range(3):
            part = in_ref[b, x * BLOCK : (x + 1) * BLOCK, :]
            fq[x, b * BLOCK : (b + 1) * BLOCK, :] = part.astype(F32)
    for height in range(1, LEVELS + 1):
        below, _ = spans[height - 1]
        base, rows = spans[height]
        step = min(CHUNK, rows)
        for x in range(3):
            for r in range(0, rows, step):
                mean = (
                    evens(fq.at[x], below + 2 * r, step) + odds(fq.at[x], below + 2 * r, step)
                ) * 0.5
                mean = mean.astype(BF16)
                lev_ref[x, base - tokens + r : base - tokens + r + step, :] = mean
                fq[x, base + r : base + r + step, :] = mean.astype(F32)

    send(lev_ref, lev_out)

    level = functools.partial(rows_of, in_ref, lev_ref)

    def attend(jobs):
        scores = [nt(level(0, q), level(1, k)) * scale for q, k, _ in jobs]
        tops = [wide(jnp.max(x, axis=1, keepdims=True)) for x in scores]
        expos = [jnp.exp(x - across(top, x.shape[1])) for x, top in zip(scores, tops)]
        numers = [nn(x.astype(BF16), level(2, k)) for x, (_, k, _) in zip(expos, jobs)]
        denoms = [wide(jnp.sum(x, axis=1, keepdims=True)) for x in expos]
        return [
            (top, denom * factor, numer * factor) if factor != 1 else (top, denom, numer)
            for top, denom, numer, (_, _, factor) in zip(tops, denoms, numers, jobs)
        ]

    def merge(at, stats):
        top, denom, numer = stats
        up = mu[at, :]
        peak = jnp.maximum(top, up)
        mine, theirs = jnp.exp(top - peak), jnp.exp(up - peak)
        return peak, mine * denom + theirs * du[at, :], mine * numer + theirs * nu[at, :]

    coarse = coarse_blocks(tokens)
    stats = attend([(near, far, float(2**height)) for height, _, near, far in coarse])
    for (height, row, near, _), one in zip(coarse, stats):
        if height < LEVELS:
            one = merge(near, one)
        for ref, value in zip((mu, du, nu), one):
            put_twice(ref, spans[height - 1][0] + 2 * row, value)
    loads[parts].wait()
    for b in range(blocks):
        out_ref[b, :BLOCK, :] = grad_ref[:, b * WIDTH : (b + 1) * WIDTH]
    send(out_ref.at[:, :BLOCK, :], sent_out.at[:, :BLOCK, :])
    for first in range(0, tokens, PAIRS * 2 * BLOCK):
        pairs = [
            slice(row, row + 2 * BLOCK)
            for row in range(first, min(first + PAIRS * 2 * BLOCK, tokens), 2 * BLOCK)
        ]
        for at, one in zip(pairs, attend([(at, at, 1) for at in pairs])):
            peak, total, summed = merge(at, one)
            attended = (summed / total).astype(BF16)
            lse = peak + jnp.log(total)
            for half in range(2):
                b = at.start // BLOCK + half
                part = lse[half * BLOCK : (half + 1) * BLOCK]
                lse_ref[b : b + 1, :] = jnp.sum(diagonal(part), axis=0, keepdims=True)
            pair = slice(at.start // BLOCK, at.stop // BLOCK)
            out_ref[pair, BLOCK:, :] = attended.reshape(2, BLOCK, WIDTH)
            send(out_ref.at[pair, BLOCK:, :], sent_out.at[pair, BLOCK:, :])
    send(lse_ref, lse_out)
    for copy in copies:
        copy.wait()


def forward(qkv, att_grad, after=()):
    blocks = qkv.shape[0]
    tokens = blocks * BLOCK
    spans, total_rows = level_rows(tokens)
    finer = total_rows - spans[LEVELS][1]
    outs = [
        ((blocks, 2 * BLOCK, WIDTH), BF16, "hbm"),
        ((blocks, BLOCK), F32, "hbm"),
        ((3, total_rows - tokens, WIDTH), BF16, "hbm"),
    ]
    return kernel_call(
        functools.partial(forward_body, blocks),
        outs,
        ["hbm"] * 2,
        32,
        scratch=[
            pltpu.VMEM(qkv.shape, BF16),
            pltpu.VMEM(att_grad.shape, BF16),
            pltpu.VMEM((blocks, 2 * BLOCK, WIDTH), BF16),
            pltpu.VMEM((blocks, BLOCK), F32),
            pltpu.VMEM((3, total_rows - tokens, WIDTH), BF16),
            pltpu.VMEM((3, total_rows, WIDTH), F32),
            pltpu.VMEM((finer, WIDTH), F32),
            pltpu.VMEM((finer, WIDTH), F32),
            pltpu.VMEM((finer, WIDTH), F32),
            dma(8 + blocks // 2),
        ],
        cost=cost(4 * tokens * 384 * WIDTH, 8 << 20),
        name="head_forward",
        after=after,
    )(qkv, att_grad)


def backward_body(
    blocks, grad_in, sent_in, lse_in, lev_in, qkv_in, rows_in, w_in, grads_out, output_ref,
    out_ref, att_ref, lse_ref, lev_ref, qkv_ref, ys, ds, rs, cg, up, rows_ref, w_ref, sems,
):
    tokens = blocks * BLOCK
    spans, _ = level_rows(tokens)
    scale = 1.0 / math.sqrt(WIDTH)
    parts, count = 4, [0]

    def fetch(source, target):
        copy = pltpu.make_async_copy(source, target, sems.at[count[0]])
        count[0] += 1
        copy.start()
        return copy

    first_loads = []
    lse_load = fetch(lse_in, lse_ref)
    for p in range(parts):
        some = slice(p * blocks // parts, (p + 1) * blocks // parts)
        at = slice(p * tokens // parts, (p + 1) * tokens // parts)
        first_loads.append(
            [
                fetch(grad_in.at[at, :], cg.at[at, :]),
                fetch(sent_in.at[some, BLOCK:, :], att_ref.at[some, :, :]),
            ]
        )
    later_loads = [
        fetch(lev_in, lev_ref),
        fetch(qkv_in, qkv_ref),
        fetch(rows_in, rows_ref),
        fetch(w_in, w_ref),
    ]
    lse_load.wait()
    for b in range(blocks):
        if b % (blocks // parts) == 0:
            for copy in first_loads[b // (blocks // parts)]:
                copy.wait()
        at = slice(b * BLOCK, (b + 1) * BLOCK)
        lse = jnp.broadcast_to(lse_ref[b : b + 1, :], (BLOCK, BLOCK))
        rs[at, :] = wide(jnp.sum(diagonal(lse), axis=1, keepdims=True))
        grad = cg[at, :].astype(F32)
        ys[at, :] = grad
        ds[at, :] = wide(jnp.sum(grad * att_ref[b].astype(F32), axis=1, keepdims=True))
    for height in range(1, LEVELS + 1):
        below, _ = spans[height - 1]
        base, rows = spans[height]
        for r in range(0, rows, BLOCK):
            at = slice(base + r, base + r + BLOCK)
            first = below + 2 * r
            lo, hi = evens(rs, first, BLOCK), odds(rs, first, BLOCK)
            low = jnp.minimum(lo, hi)
            lo, hi = jnp.exp(low - lo), jnp.exp(low - hi)
            grad = lo * evens(ys, first, BLOCK) + hi * odds(ys, first, BLOCK)
            delta = lo * evens(ds, first, BLOCK) + hi * odds(ds, first, BLOCK)
            ys[at, :], ds[at, :], rs[at, :] = grad, delta, low
            cg[at, :] = grad.astype(BF16)

    level = functools.partial(rows_of, qkv_ref, lev_ref)

    def gradients(jobs):
        scores = [nt(level(0, q), level(1, k)) * scale for q, k in jobs]
        inner = [nt(cg[q, :], level(2, k)) for q, k in jobs]
        expos = [
            jnp.exp(x - across(rs[q, :], x.shape[1])) for x, (q, _) in zip(scores, jobs)
        ]
        sgrads = [
            (expo * (x - across(ds[q, :], x.shape[1])) * scale).astype(BF16)
            for expo, x, (q, _) in zip(expos, inner, jobs)
        ]
        probs = [expo.astype(BF16) for expo in expos]
        q_parts = [nn(x, level(1, k)) for x, (_, k) in zip(sgrads, jobs)]
        k_parts = [tn(x, level(0, q)) for x, (q, _) in zip(sgrads, jobs)]
        v_parts = [tn(x, cg[q, :]) for x, (q, _) in zip(probs, jobs)]
        return list(zip(q_parts, k_parts, v_parts))

    later_loads[0].wait()
    coarse = coarse_blocks(tokens)
    for (height, row, near, far), parts in zip(
        coarse, gradients([(near, far) for _, _, near, far in coarse])
    ):
        for x, (at, first) in enumerate(((near, row), (far, row ^ BLOCK), (far, row ^ BLOCK))):
            value = parts[x]
            if height < LEVELS:
                value = value + up[x, at, :]
            put_twice(up.at[x], spans[height - 1][0] + 2 * first, value)
    later_loads[1].wait()
    stores = []
    for first in range(0, tokens, PAIRS * 2 * BLOCK):
        pairs = [
            slice(row, row + 2 * BLOCK)
            for row in range(first, min(first + PAIRS * 2 * BLOCK, tokens), 2 * BLOCK)
        ]
        for at, parts in zip(pairs, gradients([(at, at) for at in pairs])):
            pair = slice(at.start // BLOCK, at.stop // BLOCK)
            for x, value in enumerate(parts):
                value = (value + up[x, at, :]).astype(BF16)
                out_ref[pair, x * BLOCK : (x + 1) * BLOCK, :] = value.reshape(2, BLOCK, WIDTH)
            stores.append(fetch(out_ref.at[pair, :, :], grads_out.at[pair, : 3 * BLOCK, :]))
    later_loads[2].wait()
    later_loads[3].wait()
    rows = jnp.concatenate([rows_ref[h] for h in range(HEADS)], axis=1)
    width = w_ref.shape[1]
    for first in range(0, width, 512):
        at = slice(first, first + 512)
        output_ref[:, at] = nn(rows, w_ref[:, at]).astype(BF16)
    for store in stores:
        store.wait()


def backward(grad, sent, lse, lev, qkv, rows, w_out, after):
    blocks = sent.shape[0]
    tokens = blocks * BLOCK
    spans, total_rows = level_rows(tokens)
    finer = total_rows - spans[LEVELS][1]
    extra = w_out.size // lax.axis_size("outer") // blocks // WIDTH
    return kernel_call(
        functools.partial(backward_body, blocks),
        [
            ((blocks, 3 * BLOCK + extra, WIDTH), BF16, "hbm"),
            ((BLOCK, w_out.shape[1]), BF16, "vmem"),
        ],
        ["hbm"] * 7,
        63.6,
        scratch=[
            pltpu.VMEM((blocks, 3 * BLOCK, WIDTH), BF16),
            pltpu.VMEM(rows.shape, BF16),
            pltpu.VMEM(lse.shape, F32),
            pltpu.VMEM(lev.shape, BF16),
            pltpu.VMEM(qkv.shape, BF16),
            pltpu.VMEM((total_rows, WIDTH), F32),
            pltpu.VMEM((total_rows, WIDTH), F32),
            pltpu.VMEM((total_rows, WIDTH), F32),
            pltpu.VMEM((total_rows, WIDTH), BF16),
            pltpu.VMEM((3, finer, WIDTH), F32),
            pltpu.VMEM(rows.shape, BF16),
            pltpu.VMEM(w_out.shape, BF16),
            dma(16 + blocks // 2),
        ],
        cost=cost(10 * tokens * 384 * WIDTH + 2 * BLOCK * w_out.size, 24 << 20),
        name="head_backward",
        after=after,
    )(grad.reshape(tokens, WIDTH), sent, lse, lev, qkv, rows, w_out)


def tile_body(groups, per, _, att_in, *refs):
    cot_refs = refs[:groups]
    out_ref, att_ref, lhs, held, tile, sems = refs[groups:]
    chunk = lhs.shape[0] // HEADS
    chunks, step = held.shape[0], held.shape[2]
    att_copy = pltpu.make_async_copy(att_in, att_ref, sems.at[0])
    att_copy.start()
    copies, stores = [], []
    for c in range(chunks):
        for k, ref in enumerate(cot_refs):
            copies.append(
                pltpu.make_async_copy(
                    ref.at[:, c * step : (c + 1) * step],
                    held.at[c, k * BLOCK : (k + 1) * BLOCK, :],
                    sems.at[1 + c * groups + k],
                )
            )
            copies[-1].start()
    att_copy.wait()
    mine = lax.axis_index("outer")
    for k in range(groups):
        for j in range(per):
            lhs[j * WIDTH : (j + 1) * WIDTH, k * BLOCK : (k + 1) * BLOCK] = att_ref[
                (mine ^ k) * per + j
            ].T
    for c in range(chunks):
        for copy in copies[c * groups : (c + 1) * groups]:
            copy.wait()
        part = nn(lhs[...], held[c]).astype(BF16)
        first = c * step
        for i in range(HEADS):
            for j in range(step // WIDTH):
                to = (first // WIDTH + j) * chunk
                tile[i, to : to + chunk, :] = part[
                    i * chunk : (i + 1) * chunk, j * WIDTH : (j + 1) * WIDTH
                ]
        done = slice(first // WIDTH * chunk, (first + step) // WIDTH * chunk)
        to = slice(3 * BLOCK + done.start, 3 * BLOCK + done.stop)
        stores.append(
            pltpu.make_async_copy(
                tile.at[:, done, :], out_ref.at[:, to, :], sems.at[1 + chunks * groups + c]
            )
        )
        stores[-1].start()
    for store in stores:
        store.wait()


def with_tile(grads, att, pieces):
    groups, width = len(pieces), pieces[0].shape[1]
    per = HEADS // groups
    chunk = per * WIDTH // HEADS
    extra = chunk * (width // WIDTH)
    chunks = 4
    return kernel_call(
        functools.partial(tile_body, groups, per),
        [(grads.shape, BF16, "hbm")],
        ["hbm"] * (2 + groups),
        18,
        scratch=[
            pltpu.VMEM(att.shape, BF16),
            pltpu.VMEM((per * WIDTH, groups * BLOCK), BF16),
            pltpu.VMEM((chunks, groups * BLOCK, width // chunks), BF16),
            pltpu.VMEM((HEADS, extra, WIDTH), BF16),
            dma(1 + chunks * (groups + 1)),
        ],
        aliases={0: 0},
        cost=cost(2 * groups * BLOCK * per * WIDTH * width, 10 << 20),
        name="projection_tile",
    )(grads, att, *pieces)[0]


def unpack_body(scale, in_ref, q_out, k_out, v_out, w_out, grads, w_ref, sems):
    chunk, width = w_ref.shape
    stores = []

    def send(source, target):
        stores.append(pltpu.make_async_copy(source, target, sems.at[len(stores)]))
        stores[-1].start()

    for x, target in enumerate((q_out, k_out, v_out)):
        for h in range(HEADS):
            grads[x, :, h * WIDTH : (h + 1) * WIDTH] = in_ref[h, x * BLOCK : (x + 1) * BLOCK, :]
        send(grads.at[x], target)
    for c in range(width // WIDTH):
        at = 3 * BLOCK + c * chunk
        total = in_ref[0, at : at + chunk, :].astype(F32)
        for h in range(1, HEADS):
            total = total + in_ref[h, at : at + chunk, :].astype(F32)
        w_ref[:, c * WIDTH : (c + 1) * WIDTH] = total * scale
    send(w_ref, w_out)
    for store in stores:
        store.wait()


def unpack(got, scale):
    chunk = (got.shape[1] - 3 * BLOCK) // HEADS
    width = HEADS * WIDTH
    return kernel_call(
        functools.partial(unpack_body, scale),
        [((BLOCK, width), BF16, "hbm")] * 3 + [((chunk, width), F32, "hbm")],
        ["vmem"],
        8,
        scratch=[
            pltpu.VMEM((3, BLOCK, width), BF16),
            pltpu.VMEM((chunk, width), F32),
            dma(4),
        ],
        cost=cost(0, 6 << 20),
        name="unpack_grads",
    )(got)


def split_body(got_ref, grad_ref, att_ref, sems):
    copies = [
        pltpu.make_async_copy(got_ref.at[:, BLOCK:, :], att_ref, sems.at[0]),
        pltpu.make_async_copy(got_ref.at[:, :BLOCK, :], grad_ref, sems.at[1]),
    ]
    for copy in copies:
        copy.start()
    for copy in copies:
        copy.wait()


def split(got):
    return kernel_call(
        split_body,
        [((HEADS, BLOCK, WIDTH), BF16, "hbm")] * 2,
        ["vmem"],
        2,
        scratch=[dma(2)],
        cost=cost(0, 2 << 20),
        name="split_attended",
    )(got)


def swap(value, axis):
    return lax.all_to_all(value, axis, 0, 0, tiled=True)


def from_outer(value, apart):
    size = lax.axis_size("outer")
    return lax.ppermute(value, "outer", [(i, i ^ apart) for i in range(size)])


def on_device(query_in, key_in, value_in, w_out, cotangent):
    groups = lax.axis_size("outer")
    tokens = query_in.shape[0] * lax.axis_size(("outer", "inner"))
    pieces = {k: from_outer(cotangent, k) if k else cotangent for k in range(groups) if k < 2 or k & 3 == 2}
    soon = [pieces[k] for k in pieces if k]
    qkv = swap(pack(query_in, key_in, value_in), "inner")
    att_grad = attended_gradient(cotangent, w_out)
    sent, lse, lev = forward(qkv, att_grad, after=soon)
    late = {k: from_outer(pieces[k + 2], 2) for k in range(4, groups, 4)}
    pieces.update(late)
    for k in range(2, groups, 2):
        pieces[k + 1] = from_outer(pieces[k], 1)
    grad, att = split(swap(sent, "inner"))
    att_outer = swap(att, "outer")
    grads, output = backward(grad, sent, lse, lev, qkv, att, w_out, list(late.values()))
    pieces = [pieces[k] for k in range(groups)]
    last = swap(with_tile(grads, att_outer, pieces), "inner")
    query_grad, key_grad, value_grad, w_out_grad = unpack(last, 1.0 / math.sqrt(tokens))
    return output, query_grad, key_grad, value_grad, w_out_grad


def solution(mesh):
    rows = P(("outer", "inner"), None)
    return jax.shard_map(
        on_device,
        mesh=mesh,
        in_specs=(rows, rows, rows, P(), rows),
        out_specs=(rows,) * 5,
        check_vma=False,
    )
```
